32 devices in a mesh: grp: 4 (over y, x), exp: 4 (over z), mdl: 2 (over core).
Axes of the slice: x: 2, y: 2, z: 4, core: 2. Of those that a mesh axis runs over, the one named last changes fastest.
Arguments:
- images: bfloat16 [64, 197, 768], P(('grp', 'exp')), may hold values from -6 to 6
- counts: int32 [4, 4], P('grp', 'exp'), may hold values from 1 to 4, 10 in all within a row
- routes: int32 [64, 197, 2], P(('grp', 'exp')), may hold values from 0 to 3, all different within a row
- priority: int32 [16, 788], P(('grp', 'exp')), may hold values from 0 to 787, each once within a row
- gain_one: float32 [768], replicated, may hold values from 0.25 to 1.75
- qkv_one: bfloat16 [3, 768, 768], P(None, None, 'mdl'), may hold values from -0.21875 to 0.21875
- out_one: bfloat16 [768, 768], P('mdl'), may hold values from -0.625 to 0.625
- gain_two: float32 [768], replicated, may hold values from 0.25 to 1.75
- fc_in: bfloat16 [768, 3072], P(None, 'mdl'), may hold values from -0.21875 to 0.21875
- fc_out: bfloat16 [3072, 768], P('mdl'), may hold values from -0.109375 to 0.109375
- gain_three: float32 [768], replicated, may hold values from 0.25 to 1.75
- qkv_two: bfloat16 [3, 768, 768], P(None, None, 'mdl'), may hold values from -0.21875 to 0.21875
- out_two: bfloat16 [768, 768], P('mdl'), may hold values from -0.625 to 0.625
- gain_four: float32 [768], replicated, may hold values from 0.25 to 1.75
- router: bfloat16 [768, 4], replicated, may hold values from -0.15625 to 0.15625
- expert_in: bfloat16 [4, 768, 3072], P('exp', None, 'mdl'), may hold values from -0.21875 to 0.21875
- expert_out: bfloat16 [4, 3072, 768], P('exp', 'mdl'), may hold values from -1.75 to 1.75
- cotangent: bfloat16 [64, 197, 768], P(('grp', 'exp')), may hold values from -6 to 6
Outputs:
- output: bfloat16 [64, 197, 768], P(('grp', 'exp'))
- grad_images: bfloat16 [64, 197, 768], P(('grp', 'exp'))
- grad_gain_one: float32 [768], replicated
- grad_qkv_one: float32 [3, 768, 768], P(None, None, 'mdl')
- grad_out_one: float32 [768, 768], P('mdl')
- grad_gain_two: float32 [768], replicated
- grad_fc_in: float32 [768, 3072], P(None, 'mdl')
- grad_fc_out: float32 [3072, 768], P('mdl')
- grad_gain_three: float32 [768], replicated
- grad_qkv_two: float32 [3, 768, 768], P(None, None, 'mdl')
- grad_out_two: float32 [768, 768], P('mdl')
- grad_gain_four: float32 [768], replicated
- grad_router: float32 [768, 4], replicated
- grad_expert_in: float32 [4, 768, 3072], P('exp', 'grp', 'mdl')
- grad_expert_out: float32 [4, 3072, 768], P('exp', 'mdl', 'grp')
The draws below stay inside these ranges and needn't reach their ends.
Inputs may be any that keep to these rules, and one draw needn't show every extreme that they name: `counts`: each row sums to 10, and some device of every group holds 4 images. `routes`: the 2 experts of a token differ. `priority`: each row is a permutation of one device's token places.
All inputs are finite; a program needn't handle non-finite values.
Results may differ from the reference program's by a relative error of at most 0.029.
Values may be sent and summed in bfloat16 or wider, within the bound.
A program may use at most 192 MiB of HBM per device.

```python
import math
import jax
import jax.numpy as jnp
import numpy as np
from jax import lax

D = 768
HEADS = 12
HDIM = 64
FF = 3072
L = 197
TOPK = 2
SLOTS = 4
EXPERTS = 4
IMG_GRP = 10
SLOT_ALL = 64
CAP = 308
N_GRP = 4
N_EXP = 4


def levels(stream_key, dims, cuts, low, high):
    loudness, own = 1.0, jax.random.fold_in(stream_key, 6)
    for position, blocks in cuts:
        draws = jnp.exp(jax.random.uniform(jax.random.fold_in(own, position), (blocks,), jnp.float32, low / len(cuts), high / len(cuts)))
        loudness = loudness * jnp.repeat(draws, dims[position] // blocks).reshape([-1 if axis == position else 1 for axis in range(len(dims))])
    return loudness


def picks_of(key, rows, number_of, top, lift):
    ranking = jax.random.permutation(jax.random.fold_in(key, 1), number_of)
    favour = ranking
    for power in range(3):
        favour = favour * favour // number_of
    favour = favour * lift // number_of
    tickets = jax.random.randint(jax.random.fold_in(key, 2), (rows, number_of), 0, 4096) + favour
    holders = jax.random.permutation(jax.random.fold_in(key, 3), rows)[jnp.arange(number_of) % rows]
    tickets = jnp.where(jnp.arange(rows)[:, None] == holders[None, :], 1 << 14, tickets)
    score = tickets * number_of + jnp.arange(number_of)
    return lax.top_k(score.astype(jnp.int32), top)[1].astype(jnp.int32)


def profile(count, total, most, lean):
    weights = [(1 << 20) // math.isqrt(standing ** lean) + 1 for standing in range(2, count + 1)]
    rest, given = total - most - (count - 1), [1] * (count - 1)
    while rest > 0:
        movable = [i for i in range(count - 1) if given[i] < most]
        pool, left = sum([weights[i] for i in movable]), rest
        for i in movable:
            addition = min(most - given[i], max(1, left * weights[i] // pool), rest)
            given[i] = given[i] + addition
            rest = rest - addition
    return np.array([most] + given)


def uneven(key, count, total, limit, skew):
    if count == 2:
        one = jax.random.randint(key, (), max(1, total - limit), min(limit, total - 1) + 1)
        return jnp.stack([one, total - one])
    tallies = jnp.asarray(profile(count, total, limit, skew), jnp.int32)
    couples = (count - 1) // 2
    giver, sink = tallies[1:1 + 2 * couples:2], tallies[2:2 + 2 * couples:2]
    margin = jnp.minimum(giver - 1, limit - sink)
    shifted = jax.random.randint(jax.random.fold_in(key, 1), (couples,), 0, 1 << 20) % (margin + 1)
    tallies = tallies.at[1:1 + 2 * couples:2].set(giver - shifted).at[2:2 + 2 * couples:2].set(sink + shifted)
    return tallies[jax.random.permutation(jax.random.fold_in(key, 2), count)]


def normal_values(key, extent, scale, bound, pieces=(), kind=jnp.bfloat16):
    loudness = levels(key, extent, pieces, -0.22, 0.18) if pieces else 1.0
    array = jax.random.normal(key, extent, jnp.float32) * scale * loudness
    return jnp.minimum(jnp.maximum(array, -bound), bound).astype(kind)


def setup_inputs(seed: int = 0) -> dict:
    seeds = jax.random.split(jax.random.key(seed), 19)
    images = normal_values(seeds[0], (SLOT_ALL, L, D), 1.0, 6.0, ((0, 16),))
    counts = jax.vmap(lambda own: uneven(own, N_EXP, IMG_GRP, SLOTS, 2))(jax.random.split(seeds[1], N_GRP)).reshape((N_GRP, N_EXP)).astype(jnp.int32)
    routes = picks_of(seeds[2], SLOT_ALL * L, EXPERTS, TOPK, 4096).reshape((SLOT_ALL, L, TOPK))
    priority = jax.vmap(lambda own: jax.random.permutation(own, SLOTS * L))(jax.random.split(seeds[3], (N_GRP * N_EXP))).reshape((N_GRP * N_EXP, SLOTS * L)).astype(jnp.int32)
    gain_one = jnp.clip(1.0 + 0.15 * jax.random.normal(seeds[4], (D,), jnp.float32), 0.25, 1.75)
    qkv_one = normal_values(seeds[5], (3, D, D), D ** -0.5, 0.21875, ((2, 2),))
    out_one = normal_values(seeds[6], (D, D), (D // 8) ** -0.5, 0.625, ((0, 2),))
    gain_two = jnp.clip(1.0 + 0.15 * jax.random.normal(seeds[7], (D,), jnp.float32), 0.25, 1.75)
    fc_in = normal_values(seeds[8], (D, FF), D ** -0.5, 0.21875, ((1, 2),))
    fc_out = normal_values(seeds[9], (FF, D), FF ** -0.5, 0.109375, ((0, 2),))
    gain_three = jnp.clip(1.0 + 0.15 * jax.random.normal(seeds[10], (D,), jnp.float32), 0.25, 1.75)
    qkv_two = normal_values(seeds[11], (3, D, D), D ** -0.5, 0.21875, ((2, 2),))
    out_two = normal_values(seeds[12], (D, D), (D // 8) ** -0.5, 0.625, ((0, 2),))
    gain_four = jnp.clip(1.0 + 0.15 * jax.random.normal(seeds[13], (D,), jnp.float32), 0.25, 1.75)
    router = normal_values(seeds[14], (D, EXPERTS), (2 * D) ** -0.5, 0.15625)
    expert_in = normal_values(seeds[15], (EXPERTS, D, FF), D ** -0.5, 0.21875, ((0, 4), (2, 2)))
    expert_out = normal_values(seeds[16], (EXPERTS, FF, D), (max(FF // 256, 4)) ** -0.5, 1.75, ((0, 4), (1, 2)))
    cotangent = normal_values(seeds[17], (SLOT_ALL, L, D), 1.0, 6.0, ((0, 16),))
    return {"images": images, "counts": counts, "routes": routes, "priority": priority, "gain_one": gain_one, "qkv_one": qkv_one, "out_one": out_one, "gain_two": gain_two, "fc_in": fc_in, "fc_out": fc_out, "gain_three": gain_three, "qkv_two": qkv_two, "out_two": out_two, "gain_four": gain_four, "router": router, "expert_in": expert_in, "expert_out": expert_out, "cotangent": cotangent}


@jax.custom_vjp
def low(v):
    return lax.optimization_barrier(v.astype(jnp.bfloat16)).astype(jnp.float32)

@jax.custom_vjp
def low_back(v):
    return v

def low_keep(v):
    return (low(v), None)

def low_pass(kept, grad):
    return (grad,)

def back_keep(v):
    return (v, None)

def back_low(kept, grad):
    return (low(grad),)
low.defvjp(low_keep, low_pass)
low_back.defvjp(back_keep, back_low)
HIGH = lax.Precision.HIGHEST
EPSILON = 1e-06

def rounded(value):
    return low_back(low(value))

def norm_rows(values, weight):
    center = values - lax.optimization_barrier(jnp.mean(values, axis=-1, keepdims=True))
    variance = lax.optimization_barrier(jnp.mean(center * center, axis=-1, keepdims=True))
    return center * lax.rsqrt(variance + EPSILON) * weight

def attend(residual, weight, qkv_weight, out_weight):
    count_img = residual.shape[0]
    normed = low(norm_rows(residual, weight))
    queries = rounded(jnp.einsum('nld,dc->nlc', normed, qkv_weight[0], precision=HIGH)).reshape(count_img, L, HEADS, HDIM)
    key_rows = rounded(jnp.einsum('nld,dc->nlc', normed, qkv_weight[1], precision=HIGH)).reshape(count_img, L, HEADS, HDIM)
    values = rounded(jnp.einsum('nld,dc->nlc', normed, qkv_weight[2], precision=HIGH)).reshape(count_img, L, HEADS, HDIM)
    scores = low_back(jnp.einsum('nqhd,nkhd->nhqk', queries, key_rows, precision=HIGH) * HDIM ** (-0.5))
    soft_rows = low(jax.nn.softmax(scores, axis=-1))
    mixed_heads = rounded(jnp.einsum('nhqk,nkhd->nqhd', soft_rows, values, precision=HIGH)).reshape(count_img, L, D)
    branch = low_back(jnp.einsum('nlc,cd->nld', mixed_heads, out_weight, precision=HIGH))
    return residual + branch

def feed(residual, weight, in_weight, out_weight):
    normed = low(norm_rows(residual, weight))
    hidden = low_back(jnp.einsum('nld,df->nlf', normed, in_weight, precision=HIGH))
    active = low(jax.nn.gelu(hidden, approximate=False))
    branch = low_back(jnp.einsum('nlf,fd->nld', active, out_weight, precision=HIGH))
    return residual + branch

def pair_slots(route_block, priority_row, count_value, place):
    row_total = SLOTS * L
    total_slots = N_GRP * EXPERTS * N_EXP * CAP
    live_int = (jnp.arange(row_total, dtype=jnp.int32) // L < count_value).astype(jnp.int32)
    picked = (route_block[:, :, None] == jnp.arange(EXPERTS, dtype=jnp.int32)[None, None, :]).astype(jnp.int32)
    chosen = lax.optimization_barrier(jnp.sum(picked, axis=1, dtype=jnp.int32)) * live_int[:, None]
    inverse = jnp.zeros((row_total,), jnp.int32).at[priority_row].set(jnp.arange(row_total, dtype=jnp.int32))
    ordered = chosen[inverse]
    before = jnp.cumsum(ordered, axis=0, dtype=jnp.int32) - ordered
    rank_rows = jnp.take_along_axis(before[priority_row], route_block, axis=1)
    kept_pairs = (live_int[:, None] > 0) & (rank_rows < CAP)
    group = place // N_EXP
    source = place % N_EXP
    slot_index = ((group * EXPERTS + route_block) * N_EXP + source) * CAP + rank_rows
    return jnp.where(kept_pairs, slot_index, total_slots).astype(jnp.int32)

def mixture(residual, weight, router_weight, in_weight, out_weight, targets, route_rows):
    devices, row_total = (residual.shape[0], residual.shape[1])
    total_slots = N_GRP * EXPERTS * N_EXP * CAP
    normed = low(norm_rows(residual, weight))
    logits = low_back(jnp.einsum('trd,de->tre', normed, router_weight, precision=HIGH))
    soft_rows = jax.nn.softmax(logits, axis=-1)
    gate_values = jnp.take_along_axis(soft_rows, route_rows, axis=-1)
    spread_rows = jnp.broadcast_to(normed[:, :, None, :], (devices, row_total, TOPK, D)).reshape(-1, D)
    flat_targets = targets.reshape(-1)
    buffer = jnp.zeros((total_slots, D), jnp.float32).at[flat_targets].add(spread_rows, mode='drop')
    buffer = low_back(buffer).reshape(N_GRP, EXPERTS, N_EXP * CAP, D)
    hidden = low_back(jnp.einsum('gerd,edf->gerf', buffer, in_weight, precision=HIGH))
    active = low(jax.nn.gelu(hidden, approximate=False))
    expert_rows = rounded(jnp.einsum('gerf,efd->gerd', active, out_weight, precision=HIGH)).reshape(total_slots, D)
    fetched = jnp.take(expert_rows, flat_targets, axis=0, mode='fill', fill_value=0.0).reshape(devices, row_total, TOPK, D)
    return residual + lax.optimization_barrier(jnp.sum(gate_values[..., None] * fetched, axis=2))

def reference(images, counts, routes, priority, gain_one, qkv_one, out_one, gain_two, fc_in, fc_out, gain_three, qkv_two, out_two, gain_four, router, expert_in, expert_out, cotangent):
    devices = N_GRP * N_EXP
    row_total = SLOTS * L
    count_rows = counts.reshape(devices)
    route_rows = routes.reshape(devices, row_total, TOPK)
    places = jnp.arange(devices, dtype=jnp.int32)
    targets = jax.vmap(pair_slots)(route_rows, priority, count_rows, places)
    live_rows = ((jnp.arange(row_total, dtype=jnp.int32) // L)[None, :] < count_rows[:, None]).astype(jnp.float32)
    live_rows = live_rows.reshape(SLOT_ALL, L, 1)

    def forward(params):
        residual, g_one, q_one, o_one, g_two, f_in, f_out, g_three, q_two, o_two, g_four, r_weight, e_in, e_out = params
        first = attend(residual, g_one, q_one, o_one)
        second = feed(first, g_two, f_in, f_out)
        third = attend(second, g_three, q_two, o_two)
        mixed_out = mixture(third.reshape(devices, row_total, D), g_four, r_weight, e_in, e_out, targets, route_rows)
        return mixed_out.reshape(SLOT_ALL, L, D) * live_rows
    floats = (images.astype(jnp.float32), gain_one.astype(jnp.float32), qkv_one.astype(jnp.float32), out_one.astype(jnp.float32), gain_two.astype(jnp.float32), fc_in.astype(jnp.float32), fc_out.astype(jnp.float32), gain_three.astype(jnp.float32), qkv_two.astype(jnp.float32), out_two.astype(jnp.float32), gain_four.astype(jnp.float32), router.astype(jnp.float32), expert_in.astype(jnp.float32), expert_out.astype(jnp.float32))
    output, pull = jax.vjp(forward, floats)
    grads = pull(cotangent.astype(jnp.float32))[0]
    return (output.astype(jnp.bfloat16), grads[0].astype(jnp.bfloat16), grads[1], grads[2], grads[3], grads[4], grads[5], grads[6], grads[7], grads[8], grads[9], grads[10], grads[11], grads[12], grads[13])
```

```python
import functools
import math

import jax
import jax.numpy as jnp
from jax import lax
from jax.experimental import pallas as pl
from jax.experimental.pallas import tpu as pltpu
from jax.sharding import PartitionSpec as P

HDIM = 64
L = 197
TOPK = 2
LP = (L + 15) // 16 * 16
LANES = 128
BF = jnp.bfloat16
F32 = jnp.float32
I32 = jnp.int32

EPSILON = 1e-06
ROOT_HALF = 0.7071067811865476
DENSITY_FACTOR = 0.3989422804014327
VMEM_BYTES = 60 * 1024 * 1024


def nn(a, b):
    return lax.dot_general(a, b, (((1,), (0,)), ((), ())), preferred_element_type=F32)


def nt(a, b):
    return lax.dot_general(a, b, (((1,), (1,)), ((), ())), preferred_element_type=F32)


def tn(a, b):
    return lax.dot_general(a, b, (((0,), (0,)), ((), ())), preferred_element_type=F32)


def norm_forward(v, w):
    c = v - jnp.mean(v, axis=-1, keepdims=True)
    r = lax.rsqrt(jnp.mean(c * c, axis=-1, keepdims=True) + EPSILON)
    n = c * r
    return n, r, (n * w).astype(BF)


def norm_backward(n, r, w, dh):
    dn = dh * w
    dw = jnp.sum(dh * n, axis=0, keepdims=True)
    dv = r * (dn - jnp.mean(dn, axis=-1, keepdims=True) - n * jnp.mean(dn * n, axis=-1, keepdims=True))
    return dv, dw


def whole(shape):
    return pl.BlockSpec(shape, lambda *i: (0,) * len(shape))


def call(body, out_shape, *args, grid=(), in_specs=None, out_specs=None, scratch=(), flops=0):
    if in_specs is None:
        in_specs = [whole(a.shape) for a in args]
    if out_specs is None:
        out_specs = [whole(o.shape) for o in out_shape]
    moved = sum(math.prod(a.shape) * a.dtype.itemsize for a in args)
    moved += sum(math.prod(o.shape) * jnp.dtype(o.dtype).itemsize for o in out_shape)
    return pl.pallas_call(
        body,
        grid=grid,
        in_specs=in_specs,
        out_specs=out_specs,
        out_shape=out_shape,
        scratch_shapes=list(scratch),
        cost_estimate=pl.CostEstimate(flops=int(flops), bytes_accessed=int(moved), transcendentals=0),
        compiler_params=pltpu.CompilerParams(vmem_limit_bytes=VMEM_BYTES),
    )(*args)


def out(shape, dtype):
    return jax.ShapeDtypeStruct(shape, dtype)


def head_mask(dtype):
    lane = lax.broadcasted_iota(I32, (LP, LANES), 1)
    return (lane < HDIM).astype(dtype)


def attention_forward_body(n_img, tail, *refs):
    if tail:
        x_ref, w_ref, qm, qo, om, oo, w4_ref, y_ref, h_ref, qkv_ref, p_ref, o_ref, h4_ref = refs
    else:
        x_ref, w_ref, qm, qo, om, oo, y_ref, h_ref, qkv_ref, p_ref, o_ref = refs
    d = x_ref.shape[1]
    c = qm.shape[2]
    pairs = d // LANES
    _, _, h = norm_forward(x_ref[...].astype(F32), w_ref[...])
    h_ref[...] = h
    for k in range(3):
        for half, w in ((0, qm), (1, qo)):
            at = (2 * k + half) * c
            qkv_ref[:, at : at + c] = nn(h_ref[...], w[k]).astype(BF)
    mask = head_mask(BF)
    key_ok = lax.broadcasted_iota(I32, (LP, LP), 1) < L

    def one(i, _):
        rows = pl.ds(pl.multiple_of((i // pairs) * LP, LP), LP)
        col = (i % pairs) * LANES
        q = qkv_ref[rows, pl.ds(pl.multiple_of(col, LANES), LANES)]
        ke = qkv_ref[rows, pl.ds(pl.multiple_of(d + col, LANES), LANES)]
        u = qkv_ref[rows, pl.ds(pl.multiple_of(2 * d + col, LANES), LANES)]
        o = jnp.zeros((LP, LANES), F32)
        for hh in range(2):
            mk = mask if hh == 0 else 1 - mask
            s = nt(q * mk, ke) * HDIM ** (-0.5)
            s = jnp.where(key_ok, s, -1e30)
            e = jnp.exp(s - jnp.max(s, axis=-1, keepdims=True))
            p = (e / jnp.sum(e, axis=-1, keepdims=True)).astype(BF)
            p_ref[2 * i + hh] = p
            o = o + nn(p, u * mk)
        o_ref[rows, pl.ds(pl.multiple_of(col, LANES), LANES)] = o.astype(BF)
        return 0

    lax.fori_loop(0, n_img * pairs, one, 0, unroll=2)
    y = x_ref[...].astype(F32) + nn(o_ref[:, :c], om[...]) + nn(o_ref[:, c:], oo[...])
    y_ref[...] = y
    if tail:
        _, _, h4 = norm_forward(y, w4_ref[...])
        h4_ref[...] = h4


def attention_forward(x, gain, qm, qo, om, oo, gain4=None):
    r, d = x.shape
    n_img = r // LP
    heads = d // HDIM
    shapes = [out((r, d), F32), out((r, d), BF), out((r, 3 * d), BF), out((n_img * heads, LP, LP), BF), out((r, d), BF)]
    args = [x, gain, qm, qo, om, oo]
    if gain4 is not None:
        shapes.append(out((r, d), BF))
        args.append(gain4)
    return call(
        functools.partial(attention_forward_body, n_img, gain4 is not None),
        shapes, *args, flops=2 * r * d * d * 4 + 4 * n_img * heads * LP * LP * LANES,
    )


def attention_backward_body(n_img, dy_ref, x_ref, w_ref, h_ref, qkv_ref, p_ref, o_ref, qm, qo, om, oo,
                            dx_ref, dw_ref, gm_ref, go_ref, do_ref, dqkv_ref, tr_ref):
    d = x_ref.shape[1]
    c = qm.shape[2]
    pairs = d // LANES
    da = dy_ref[...].astype(BF)
    tr_ref[...] = o_ref[...].T
    for half, (w, g) in enumerate(((om, gm_ref), (oo, go_ref))):
        gw = nn(tr_ref[half * c : (half + 1) * c, :], da).astype(BF)
        for part in range(d // c):
            g[3 * d + part * c : 3 * d + (part + 1) * c, :] = gw[:, part * c : (part + 1) * c]
        do_ref[:, half * c : (half + 1) * c] = nt(da, w[...]).astype(BF)
    mask = head_mask(BF)

    def one(i, _):
        rows = pl.ds(pl.multiple_of((i // pairs) * LP, LP), LP)
        col = (i % pairs) * LANES
        cq = pl.ds(pl.multiple_of(col, LANES), LANES)
        ck = pl.ds(pl.multiple_of(d + col, LANES), LANES)
        cu = pl.ds(pl.multiple_of(2 * d + col, LANES), LANES)
        q, ke, u, do = qkv_ref[rows, cq], qkv_ref[rows, ck], qkv_ref[rows, cu], do_ref[rows, cq]
        dq = jnp.zeros((LP, LANES), F32)
        dk = jnp.zeros((LP, LANES), F32)
        du = jnp.zeros((LP, LANES), F32)
        for hh in range(2):
            mk = mask if hh == 0 else 1 - mask
            p = p_ref[2 * i + hh]
            du = du + tn(p, do * mk)
            dp = nt(do * mk, u)
            pf = p.astype(F32)
            ds = (pf * (dp - jnp.sum(dp * pf, axis=-1, keepdims=True))).astype(BF)
            dq = dq + nn(ds, ke * mk)
            dk = dk + tn(ds, q * mk)
        dqkv_ref[rows, cq] = (dq * HDIM ** (-0.5)).astype(BF)
        dqkv_ref[rows, ck] = (dk * HDIM ** (-0.5)).astype(BF)
        dqkv_ref[rows, cu] = du.astype(BF)
        return 0

    lax.fori_loop(0, n_img * pairs, one, 0, unroll=2)
    tr_ref[...] = h_ref[...].T
    dh = jnp.zeros(x_ref.shape, F32)
    for k in range(3):
        for half, (w, g) in enumerate(((qm, gm_ref), (qo, go_ref))):
            at = (2 * k + half) * c
            g[k * d : (k + 1) * d, :] = nn(tr_ref[...], dqkv_ref[:, at : at + c]).astype(BF)
            dh = dh + nt(dqkv_ref[:, at : at + c], w[k])
    n, rr, _ = norm_forward(x_ref[...].astype(F32), w_ref[...])
    dv, dw = norm_backward(n, rr, w_ref[...], dh)
    dx_ref[...] = dy_ref[...] + dv
    dw_ref[...] = dw


def attention_backward(dy, x, gain, kept, qm, qo, om, oo):
    r, d = x.shape
    c = qm.shape[2]
    n_img = r // LP
    heads = d // HDIM
    return call(
        functools.partial(attention_backward_body, n_img),
        [out((r, d), F32), out((1, d), F32), out((3 * d + d, c), BF), out((3 * d + d, c), BF)],
        dy, x, gain, *kept, qm, qo, om, oo,
        scratch=[pltpu.VMEM((r, d), BF), pltpu.VMEM((r, 3 * d), BF), pltpu.VMEM((d, r), BF)],
        flops=4 * r * d * d * 4 + 8 * n_img * heads * LP * LP * LANES,
    )


def gelu_parts(z):
    phi = 0.5 * (1.0 + lax.erf(z * ROOT_HALF))
    return z * phi, phi + z * jnp.exp(-0.5 * z * z) * DENSITY_FACTOR


def tile_of(f):
    for t in (512, 256, 128):
        if f % t == 0:
            return t
    return f


def mlp_forward_body(x_ref, w_ref, im, io, tm, to, y_ref, h_ref, act_ref, slope_ref, acc_ref):
    step = pl.program_id(0)

    @pl.when(step == 0)
    def _():
        x = x_ref[...]
        _, _, h = norm_forward(x, w_ref[...])
        h_ref[...] = h
        acc_ref[...] = x

    for half, (wi, wo) in enumerate(((im, tm), (io, to))):
        a, s = gelu_parts(nn(h_ref[...], wi[...]))
        act = a.astype(BF)
        act_ref[half] = act
        slope_ref[half] = s.astype(BF)
        acc_ref[...] += nn(act, wo[...])

    @pl.when(step == pl.num_programs(0) - 1)
    def _():
        y_ref[...] = acc_ref[...]


def mlp_forward(x, gain, im, io, tm, to):
    r, d = x.shape
    f = im.shape[1]
    t = tile_of(f)
    col = pl.BlockSpec((d, t), lambda i: (0, i))
    row = pl.BlockSpec((t, d), lambda i: (i, 0))
    hid = pl.BlockSpec((2, r, t), lambda i: (0, 0, i))
    return call(
        mlp_forward_body,
        [out((r, d), F32), out((r, d), BF), out((2, r, f), BF), out((2, r, f), BF)],
        x, gain, im, io, tm, to, grid=(f // t,),
        in_specs=[whole((r, d)), whole((1, d)), col, col, row, row],
        out_specs=[whole((r, d)), whole((r, d)), hid, hid],
        scratch=[pltpu.VMEM((r, d), F32)], flops=8 * r * d * f,
    )


def mlp_backward_body(dy_ref, x_ref, w_ref, h_ref, act_ref, slope_ref, im, io, tm, to,
                      dx_ref, dw_ref, gim, gio, gtm, gto, da_ref, tr_ref, dh_ref):
    step = pl.program_id(0)

    @pl.when(step == 0)
    def _():
        da_ref[...] = dy_ref[...].astype(BF)
        tr_ref[...] = h_ref[...].T
        dh_ref[...] = jnp.zeros_like(dh_ref)

    for half, (wi, wo, gi, go) in enumerate(((im, tm, gim, gtm), (io, to, gio, gto))):
        dact = nt(da_ref[...], wo[...])
        dz = (dact * slope_ref[half].astype(F32)).astype(BF)
        go[...] = tn(act_ref[half], da_ref[...]).astype(BF)
        gi[...] = nn(tr_ref[...], dz).astype(BF)
        dh_ref[...] += nt(dz, wi[...])

    @pl.when(step == pl.num_programs(0) - 1)
    def _():
        n, rr, _ = norm_forward(x_ref[...], w_ref[...])
        dv, dw = norm_backward(n, rr, w_ref[...], dh_ref[...])
        dx_ref[...] = dy_ref[...] + dv
        dw_ref[...] = dw


def mlp_backward(dy, x, gain, h, act, slope, im, io, tm, to):
    r, d = x.shape
    f = im.shape[1]
    t = tile_of(f)
    col = pl.BlockSpec((d, t), lambda i: (0, i))
    row = pl.BlockSpec((t, d), lambda i: (i, 0))
    hid = pl.BlockSpec((2, r, t), lambda i: (0, 0, i))
    return call(
        mlp_backward_body,
        [out((r, d), F32), out((1, d), F32), out((d, f), BF), out((d, f), BF), out((f, d), BF), out((f, d), BF)],
        dy, x, gain, h, act, slope, im, io, tm, to, grid=(f // t,),
        in_specs=[whole((r, d)), whole((r, d)), whole((1, d)), whole((r, d)), hid, hid, col, col, row, row],
        out_specs=[whole((r, d)), whole((1, d)), col, col, row, row],
        scratch=[pltpu.VMEM((r, d), BF), pltpu.VMEM((d, r), BF), pltpu.VMEM((r, d), F32)], flops=16 * r * d * f,
    )


def routing_body(experts, capacity, half, cols_ref, rows_ref, tc_ref, tr_ref):
    n = cols_ref.shape[0]
    slots = experts * half

    def slot(rank, expert, live):
        core = (rank >= half).astype(I32)
        kept = (rank < capacity) & (live > 0)
        return jnp.where(kept, core * slots + expert * half + rank - core * half, -1)

    r0, r1, pc, lc = (cols_ref[:, i : i + 1] for i in range(4))
    s0, s1, pr, lr = (rows_ref[i : i + 1, :] for i in range(4))
    wide = lax.broadcasted_iota(I32, (n, LANES), 1)
    hot = (((wide == r0) | (wide == r1)) & (lc > 0)).astype(F32).astype(BF)
    earlier = (pr < pc).astype(F32).astype(BF)
    rank = nn(earlier, hot)
    for k, e in enumerate((r0, r1)):
        mine = jnp.sum(jnp.where(wide == e, rank, 0.0), axis=1, keepdims=True).astype(I32)
        tc_ref[:, k : k + 1] = slot(mine, e, lc)
    tall = lax.broadcasted_iota(I32, (max(experts, 8), n), 0)
    hot = (((tall == s0) | (tall == s1)) & (lr > 0)).astype(F32).astype(BF)
    earlier = (pc < pr).astype(F32).astype(BF)
    rank = nn(hot, earlier)
    for k, e in enumerate((s0, s1)):
        mine = jnp.sum(jnp.where(tall == e, rank, 0.0), axis=0, keepdims=True).astype(I32)
        tr_ref[k : k + 1, :] = slot(mine, e, lr)


def dispatch_body(ta_ref, tb_ref, a_ref, b_ref, y_ref):
    slots = y_ref.shape[0]
    n = a_ref.shape[0]
    place = lax.broadcasted_iota(I32, (slots, n), 0)
    total = None
    for t, v in ((ta_ref, a_ref), (tb_ref, b_ref)):
        hot = ((place == t[0:1, :]) | (place == t[1:2, :])).astype(F32).astype(BF)
        part = nn(hot, v[...])
        total = part if total is None else total + part
    y_ref[...] = total.astype(BF)


def dispatch(ta, tb, a, b, slots):
    return call(dispatch_body, [out((slots, a.shape[1]), BF)], ta, tb, a, b,
                flops=4 * slots * a.shape[0] * a.shape[1])[0]


def router_probs(h, router, experts):
    logits = nn(h, router)
    lane = lax.broadcasted_iota(I32, logits.shape, 1)
    logits = jnp.where(lane < experts, logits, -1e30)
    e = jnp.exp(logits - jnp.max(logits, axis=-1, keepdims=True))
    return e / jnp.sum(e, axis=-1, keepdims=True), lane


def expert_body(experts, x_ref, dy_ref, router_ref, mine_ref, im, io, tm, to,
                eout_ref, ret_ref, act_ref, dz_ref, wd_ref, acc_ref, dx_ref):
    step = pl.program_id(0)
    d = x_ref.shape[1]

    @pl.when(step == 0)
    def _():
        probs, _ = router_probs(x_ref[...], router_ref[...], experts)
        gate = jnp.sum(probs * mine_ref[...], axis=-1, keepdims=True)
        wd_ref[...] = (gate * dy_ref[...].astype(F32)).astype(BF)
        acc_ref[...] = jnp.zeros_like(acc_ref)
        dx_ref[...] = jnp.zeros_like(dx_ref)

    for half, (wi, wo) in enumerate(((im, tm), (io, to))):
        a, s = gelu_parts(nn(x_ref[...], wi[...]))
        act = a.astype(BF)
        act_ref[half] = act
        acc_ref[...] += nn(act, wo[...])
        dz = (nt(wd_ref[...], wo[...]) * s).astype(BF)
        dz_ref[half] = dz
        dx_ref[...] += nt(dz, wi[...])

    @pl.when(step == pl.num_programs(0) - 1)
    def _():
        eout = acc_ref[...].astype(BF)
        eout_ref[...] = eout
        ret_ref[:, :d] = dx_ref[...].astype(BF)
        dgate = jnp.sum(dy_ref[...].astype(F32) * eout.astype(F32), axis=-1, keepdims=True)
        high = dgate.astype(BF).astype(F32)
        lane = lax.broadcasted_iota(I32, (x_ref.shape[0], LANES), 1)
        ret_ref[:, d:] = jnp.where(lane < LANES // 2, high, dgate - high).astype(BF)


def expert_forward_backward(x, dy, router, mine, im, io, tm, to, experts):
    r, d = x.shape
    f = im.shape[1]
    t = tile_of(f) // 2
    col = pl.BlockSpec((d, t), lambda i: (0, i))
    row = pl.BlockSpec((t, d), lambda i: (i, 0))
    hid = pl.BlockSpec((2, r, t), lambda i: (0, 0, i))
    return call(
        functools.partial(expert_body, experts),
        [out((r, d), BF), out((r, d + LANES), BF), out((2, r, f), BF), out((2, r, f), BF), out((r, d), BF)],
        x, dy, router, mine, im, io, tm, to, grid=(f // t,),
        in_specs=[whole((r, d)), whole((r, d)), whole(router.shape), whole(mine.shape), col, col, row, row],
        out_specs=[whole((r, d)), whole((r, d + LANES)), hid, hid, whole((r, d))],
        scratch=[pltpu.VMEM((r, d), F32), pltpu.VMEM((r, d), F32)], flops=16 * r * d * f,
    )


def expert_weights_body(x_ref, wd_ref, act_ref, dz_ref, gm_ref, go_ref, xt_ref, wt_ref):
    @pl.when(pl.program_id(0) == 0)
    def _():
        xt_ref[...] = x_ref[...].T
        wt_ref[...] = wd_ref[...].T

    for half, g in enumerate((gm_ref, go_ref)):
        g[0] = nn(xt_ref[...], dz_ref[half]).astype(BF)
        g[1] = nn(wt_ref[...], act_ref[half]).astype(BF)


def expert_weights(x, wd, act, dz):
    r, d = x.shape
    f = act.shape[2]
    t = tile_of(f) // 2
    hid = pl.BlockSpec((2, r, t), lambda i: (0, 0, i))
    grad = pl.BlockSpec((2, d, t), lambda i: (0, 0, i))
    return call(
        expert_weights_body, [out((2, d, f), BF), out((2, d, f), BF)], x, wd, act, dz, grid=(f // t,),
        in_specs=[whole((r, d)), whole((r, d)), hid, hid], out_specs=[grad, grad],
        scratch=[pltpu.VMEM((d, r), BF), pltpu.VMEM((d, r), BF)], flops=8 * r * d * f,
    )


def merge_hots(t_ref, k, n, slots):
    lane = lax.broadcasted_iota(I32, (n, slots), 1)
    return (lane == t_ref[:, k : k + 1]).astype(F32).astype(BF)


def mixture_backward_body(experts, x_ref, w_ref, h_ref, router_ref, dy_ref, route_ref, ta_ref, tb_ref, a_ref, b_ref,
                          dx_ref, dw_ref, dr_ref):
    n, d = x_ref.shape
    slots = a_ref.shape[0]
    probs, lane = router_probs(h_ref[...], router_ref[...], experts)
    dh = jnp.zeros((n, d), F32)
    dsoft = jnp.zeros(probs.shape, F32)
    for k in range(TOPK):
        part = nn(merge_hots(ta_ref, k, n, slots), a_ref[...]) + nn(merge_hots(tb_ref, k, n, slots), b_ref[...])
        dh = dh + part[:, :d]
        dgate = part[:, d : d + 1] + part[:, d + LANES // 2 : d + LANES // 2 + 1]
        dsoft = dsoft + jnp.where(lane == route_ref[:, k : k + 1], dgate, 0.0)
    dlog = (probs * (dsoft - jnp.sum(dsoft * probs, axis=-1, keepdims=True))).astype(BF)
    dr_ref[...] = tn(h_ref[...], dlog)
    dh = dh + nt(dlog, router_ref[...])
    nrm, rr, _ = norm_forward(x_ref[...], w_ref[...])
    dv, dw = norm_backward(nrm, rr, w_ref[...], dh)
    dx_ref[...] = dy_ref[...].astype(F32) + dv
    dw_ref[...] = dw


def mixture_output_body(experts, x_ref, h_ref, router_ref, route_ref, live_ref, ta_ref, tb_ref, a_ref, b_ref, y_ref):
    n, d = x_ref.shape
    slots = a_ref.shape[0]
    probs, lane = router_probs(h_ref[...], router_ref[...], experts)
    total = x_ref[...]
    mixed = jnp.zeros((n, d), F32)
    for k in range(TOPK):
        gate = jnp.sum(jnp.where(lane == route_ref[:, k : k + 1], probs, 0.0), axis=-1, keepdims=True)
        part = nn(merge_hots(ta_ref, k, n, slots), a_ref[...]) + nn(merge_hots(tb_ref, k, n, slots), b_ref[...])
        mixed = mixed + gate * part
    y_ref[...] = (live_ref[...] * (total + mixed)).astype(BF)


def flip(axis, bit):
    size = lax.axis_size(axis)
    return [(i, i ^ bit) for i in range(size)]


def bits_of(axis):
    size = lax.axis_size(axis)
    return [1 << b for b in range(size.bit_length() - 1)]


def other_core(v):
    return lax.ppermute(v, "mdl", flip("mdl", 1))


def add16(a, b):
    return (a.astype(F32) + b.astype(F32)).astype(BF)


def halve(v, axis, bit):
    side = (lax.axis_index(axis) // bit) % 2
    n = v.shape[0] // 2
    keep = lax.dynamic_slice_in_dim(v, side * n, n)
    send = lax.dynamic_slice_in_dim(v, (1 - side) * n, n)
    return add16(keep, lax.ppermute(send, axis, flip(axis, bit)))


def double(v, axis, bit):
    side = (lax.axis_index(axis) // bit) % 2
    got = lax.ppermute(v, axis, flip(axis, bit))
    return jnp.where(side == 0, jnp.concatenate([v, got]), jnp.concatenate([got, v]))


def sum_everywhere(v):
    n = v.shape[0] // 2
    bits = bits_of("grp")
    parts = []
    for part, order in ((v[:n], bits), (v[n:], bits[::-1])):
        for bit in order:
            part = halve(part, "grp", bit)
        parts.append(part)
    size = lax.axis_size("exp")
    joined = jnp.concatenate(parts)
    rows = joined.shape[0] // size
    spread = lax.all_to_all(joined.reshape(size, rows, -1), "exp", 0, 0, tiled=True)
    mine = jnp.sum(spread.astype(F32), axis=0).astype(BF)
    joined = lax.all_gather(mine, "exp", axis=0, tiled=True)
    h = joined.shape[0] // 2
    done = []
    for part, order in ((joined[:h], bits), (joined[h:], bits[::-1])):
        for bit in order[::-1]:
            part = double(part, "grp", bit)
        done.append(part)
    return jnp.concatenate(done)


def shard_sum(v):
    bits = bits_of("grp")
    size = lax.axis_size("grp")
    two, d, f = v.shape
    n = f // 2
    done = []
    for part, order in ((v[:, :, :n], bits[::-1]), (v[:, :, n:], bits)):
        part = part.reshape((two,) + (2,) * len(bits) + (d // size, n))
        for bit in order:
            axis = len(bits) - bits.index(bit)
            side = (lax.axis_index("grp") // bit) % 2
            keep = lax.dynamic_slice_in_dim(part, side, 1, axis)
            send = lax.dynamic_slice_in_dim(part, 1 - side, 1, axis)
            part = add16(keep, lax.ppermute(send, "grp", flip("grp", bit)))
        done.append(part.reshape(two, d // size, n))
    return jnp.concatenate(done, axis=2)


def small_sum(v):
    for axis in ("mdl", "grp", "exp"):
        for bit in bits_of(axis):
            v = v + lax.ppermute(v, axis, flip(axis, bit))
    return v


def on_device(images, counts, routes, priority, gain_one, qkv_one, out_one, gain_two, fc_in, fc_out, gain_three,
              qkv_two, out_two, gain_four, router, expert_in, expert_out, cotangent):
    n_slot, length, d = images.shape
    experts = router.shape[1]
    n_mdl = lax.axis_size("mdl")
    capacity = (25 * L * TOPK + 8 * experts - 1) // (8 * experts)
    half = -(-(-(-capacity // n_mdl)) // 16) * 16
    slots = experts * half
    own_img = n_slot // n_mdl
    rows = own_img * LP
    core = lax.axis_index("mdl")

    def own(v, axis=0):
        return lax.dynamic_slice_in_dim(v, core * rows, rows, axis)

    def oth(v, axis=0):
        return lax.dynamic_slice_in_dim(v, (1 - core) * rows, rows, axis)

    def padded(v):
        return jnp.pad(v, ((0, 0), (0, LP - length), (0, 0))).reshape(n_slot * LP, -1)

    qm1, om1, im, tm, qm2, om2, em, fm = qkv_one, out_one, fc_in, fc_out, qkv_two, out_two, expert_in[0], expert_out[0]
    qo1, oo1, io, to, qo2, oo2, eo, fo = (other_core(w) for w in (qm1, om1, im, tm, qm2, om2, em, fm))
    g1, g2, g3, g4 = (g.reshape(1, d) for g in (gain_one, gain_two, gain_three, gain_four))
    router_wide = jnp.pad(router, ((0, 0), (0, LANES - experts)))
    mine = (jnp.arange(LANES, dtype=I32) == lax.axis_index("exp")).astype(F32)[None]

    img_live = (jnp.arange(n_slot, dtype=I32) < counts[0, 0]).astype(I32)
    live = jnp.pad(jnp.broadcast_to(img_live[:, None], (n_slot, length)), ((0, 0), (0, LP - length))).reshape(-1)
    x0 = own(padded(images))
    dy = padded(cotangent * img_live[:, None, None].astype(BF))
    route = padded(routes)
    prior = padded(priority.reshape(n_slot, length, 1))
    cols = jnp.concatenate([route, prior, live[:, None]], axis=1)
    slot_cols, slot_rows = call(
        functools.partial(routing_body, experts, capacity, half),
        [out((n_slot * LP, TOPK), I32), out((TOPK, n_slot * LP), I32)], cols, cols.T,
    )
    mine_rows = slot_rows - core * slots
    own_tokens_here = own(slot_cols) - core * slots
    own_tokens_there = own(slot_cols) - (1 - core) * slots
    own_tokens_there = jnp.where(own_tokens_there < slots, own_tokens_there, -1)
    peers = lax.axis_size("exp")

    def exchange(v):
        shaped = v.reshape(peers, v.shape[0] // peers, v.shape[1])
        return lax.all_to_all(shaped, "exp", 0, 0, tiled=True).reshape(v.shape)

    dy_out = dispatch(mine_rows[:, :rows], mine_rows[:, rows:], dy[:rows], dy[rows:], slots)
    dy_in = exchange(dy_out)

    x1, *kept1 = attention_forward(x0, g1, qm1, qo1, om1, oo1)
    x2, h2, act2, slope2 = mlp_forward(x1, g2, im, io, tm, to)
    x3, *kept3, h4 = attention_forward(x2, g3, qm2, qo2, om2, oo2, g4)

    h4_out = dispatch(own(mine_rows, 1), oth(mine_rows, 1), h4, other_core(h4), slots)
    h4_in = exchange(h4_out)
    eout, ret, eact, edz, ewd = expert_forward_backward(h4_in, dy_in, router_wide, mine, em, eo, fm, fo, experts)
    ret = exchange(ret)
    ret_there = other_core(ret)
    eout = exchange(eout)
    eout_there = other_core(eout)
    ge_mine, ge_other = expert_weights(h4_in, ewd, eact, edz)

    own_route = own(route)
    dx3, dg4, dr = call(
        functools.partial(mixture_backward_body, experts),
        [out((rows, d), F32), out((1, d), F32), out((d, LANES), F32)],
        x3, g4, h4, router_wide, own(dy), own_route, own_tokens_here, own_tokens_there, ret, ret_there,
        flops=8 * rows * slots * d,
    )
    [output] = call(
        functools.partial(mixture_output_body, experts), [out((rows, d), BF)],
        x3, h4, router_wide, own_route, own(live).astype(F32)[:, None], own_tokens_here, own_tokens_there, eout, eout_there,
        flops=8 * rows * slots * d,
    )
    expert_sum = shard_sum(add16(ge_mine, other_core(ge_other)))

    dx2, dg3, a2_mine, a2_other = attention_backward(dx3, x2, g3, kept3, qm2, qo2, om2, oo2)
    a2_sum = sum_everywhere(add16(a2_mine, other_core(a2_other)))
    dx1, dg2, gim, gio, gtm, gto = mlp_backward(dx2, x1, g2, h2, act2, slope2, im, io, tm, to)
    fi_sum = sum_everywhere(add16(gim, other_core(gio)))
    fo_sum = sum_everywhere(add16(gtm, other_core(gto)))
    dx0, dg1, a1_mine, a1_other = attention_backward(dx1, x0, g1, kept1, qm1, qo1, om1, oo1)
    a1_sum = sum_everywhere(add16(a1_mine, other_core(a1_other)))

    small = small_sum(jnp.concatenate([dg1, dg2, dg3, dg4, dr.T[:experts]], axis=0))

    def unpack(total):
        c = total.shape[1]
        qkv = total[: 3 * d].reshape(3, d, c).astype(F32)
        proj = jnp.concatenate([total[3 * d + i * c : 3 * d + (i + 1) * c] for i in range(d // c)], axis=1)
        return qkv, proj.astype(F32)

    def both(v):
        there = other_core(v)
        joined = jnp.where(core == 0, jnp.concatenate([v, there]), jnp.concatenate([there, v]))
        return joined.reshape(n_slot, LP, d)[:, :length]

    grad_qkv_one, grad_out_one = unpack(a1_sum)
    grad_qkv_two, grad_out_two = unpack(a2_sum)
    return (
        both(output), both(dx0.astype(BF)),
        small[0], grad_qkv_one, grad_out_one, small[1], fi_sum.astype(F32), fo_sum.astype(F32),
        small[2], grad_qkv_two, grad_out_two, small[3], small[4:].T,
        expert_sum[0].astype(F32)[None], expert_sum[1].astype(F32).T[None],
    )


def solution(mesh):
    token = P(("grp", "exp"), None, None)
    column, line = P(None, None, "mdl"), P("mdl", None)
    return jax.shard_map(
        on_device,
        mesh=mesh,
        in_specs=(token, P("grp", "exp"), token, P(("grp", "exp"), None), P(), column, line, P(), P(None, "mdl"), line,
                  P(), column, line, P(), P(), P("exp", None, "mdl"), P("exp", "mdl", None), token),
        out_specs=(token, token, P(), column, line, P(), P(None, "mdl"), line, P(), column, line, P(), P(),
                   P("exp", "grp", "mdl"), P("exp", "mdl", "grp")),
        check_vma=False,
    )
```

```python
import functools
import math

import jax
import jax.numpy as jnp
from jax import lax
from jax.experimental import pallas as pl
from jax.experimental.pallas import tpu as pltpu
from jax.sharding import PartitionSpec as P

HDIM = 64
L = 197
TOPK = 2
LP = (L + 15) // 16 * 16
LANES = 128
BF = jnp.bfloat16
F32 = jnp.float32
I32 = jnp.int32

EPSILON = 1e-06
ROOT_HALF = 0.7071067811865476
DENSITY_FACTOR = 0.3989422804014327
VMEM_BYTES = 60 * 1024 * 1024
MESH = pl.DeviceIdType.MESH


def nn(a, b):
    return lax.dot_general(a, b, (((1,), (0,)), ((), ())), preferred_element_type=F32)


def nt(a, b):
    return lax.dot_general(a, b, (((1,), (1,)), ((), ())), preferred_element_type=F32)


def tn(a, b):
    return lax.dot_general(a, b, (((0,), (0,)), ((), ())), preferred_element_type=F32)


def norm_forward(v, w):
    c = v - jnp.mean(v, axis=-1, keepdims=True)
    r = lax.rsqrt(jnp.mean(c * c, axis=-1, keepdims=True) + EPSILON)
    n = c * r
    return n, r, (n * w).astype(BF)


def norm_backward(n, r, w, dh):
    dn = dh * w
    dw = jnp.sum(dh * n, axis=0, keepdims=True)
    dv = r * (dn - jnp.mean(dn, axis=-1, keepdims=True) - n * jnp.mean(dn * n, axis=-1, keepdims=True))
    return dv, dw


def whole(shape):
    return pl.BlockSpec(shape, lambda *i: (0,) * len(shape))


def call(body, out_shape, *args, grid=(), in_specs=None, out_specs=None, scratch=(), flops=0):
    if in_specs is None:
        in_specs = [whole(a.shape) for a in args]
    if out_specs is None:
        out_specs = [whole(o.shape) for o in out_shape]
    moved = sum(math.prod(a.shape) * a.dtype.itemsize for a in args)
    moved += sum(math.prod(o.shape) * jnp.dtype(o.dtype).itemsize for o in out_shape)
    return pl.pallas_call(
        body,
        grid=grid,
        in_specs=in_specs,
        out_specs=out_specs,
        out_shape=out_shape,
        scratch_shapes=list(scratch),
        cost_estimate=pl.CostEstimate(flops=int(flops), bytes_accessed=int(moved), transcendentals=0),
        compiler_params=pltpu.CompilerParams(vmem_limit_bytes=VMEM_BYTES),
    )(*args)


def out(shape, dtype):
    return jax.ShapeDtypeStruct(shape, dtype)


def head_mask(dtype):
    lane = lax.broadcasted_iota(I32, (LP, LANES), 1)
    return (lane < HDIM).astype(dtype)


def attention_forward_body(n_img, tail, *refs):
    if tail:
        x_ref, w_ref, qm, qo, om, oo, w4_ref, y_ref, h_ref, qkv_ref, p_ref, o_ref, h4_ref = refs
    else:
        x_ref, w_ref, qm, qo, om, oo, y_ref, h_ref, qkv_ref, p_ref, o_ref = refs
    d = x_ref.shape[1]
    c = qm.shape[2]
    pairs = d // LANES
    _, _, h = norm_forward(x_ref[...].astype(F32), w_ref[...])
    h_ref[...] = h
    for k in range(3):
        for half, w in ((0, qm), (1, qo)):
            at = (2 * k + half) * c
            qkv_ref[:, at : at + c] = nn(h_ref[...], w[k]).astype(BF)
    mask = head_mask(BF)
    key_ok = lax.broadcasted_iota(I32, (LP, LP), 1) < L

    def one(i, _):
        rows = pl.ds(pl.multiple_of((i // pairs) * LP, LP), LP)
        col = (i % pairs) * LANES
        q = qkv_ref[rows, pl.ds(pl.multiple_of(col, LANES), LANES)]
        ke = qkv_ref[rows, pl.ds(pl.multiple_of(d + col, LANES), LANES)]
        u = qkv_ref[rows, pl.ds(pl.multiple_of(2 * d + col, LANES), LANES)]
        o = jnp.zeros((LP, LANES), F32)
        for hh in range(2):
            mk = mask if hh == 0 else 1 - mask
            s = nt(q * mk, ke) * HDIM ** (-0.5)
            s = jnp.where(key_ok, s, -1e30)
            e = jnp.exp(s - jnp.max(s, axis=-1, keepdims=True))
            p = (e / jnp.sum(e, axis=-1, keepdims=True)).astype(BF)
            p_ref[2 * i + hh] = p
            o = o + nn(p, u * mk)
        o_ref[rows, pl.ds(pl.multiple_of(col, LANES), LANES)] = o.astype(BF)
        return 0

    lax.fori_loop(0, n_img * pairs, one, 0, unroll=2)
    y = x_ref[...].astype(F32) + nn(o_ref[:, :c], om[...]) + nn(o_ref[:, c:], oo[...])
    y_ref[...] = y
    if tail:
        _, _, h4 = norm_forward(y, w4_ref[...])
        h4_ref[...] = h4


def attention_forward(x, gain, qm, qo, om, oo, gain4=None):
    r, d = x.shape
    n_img = r // LP
    heads = d // HDIM
    shapes = [out((r, d), F32), out((r, d), BF), out((r, 3 * d), BF), out((n_img * heads, LP, LP), BF), out((r, d), BF)]
    args = [x, gain, qm, qo, om, oo]
    if gain4 is not None:
        shapes.append(out((r, d), BF))
        args.append(gain4)
    return call(
        functools.partial(attention_forward_body, n_img, gain4 is not None),
        shapes, *args, flops=2 * r * d * d * 4 + 4 * n_img * heads * LP * LP * LANES,
    )


def attention_backward_body(n_img, dy_ref, x_ref, w_ref, h_ref, qkv_ref, p_ref, o_ref, qm, qo, om, oo,
                            dx_ref, dw_ref, gm_ref, go_ref, do_ref, dqkv_ref, tr_ref):
    d = x_ref.shape[1]
    c = qm.shape[2]
    pairs = d // LANES
    da = dy_ref[...].astype(BF)
    tr_ref[...] = o_ref[...].T
    for half, (w, g) in enumerate(((om, gm_ref), (oo, go_ref))):
        gw = nn(tr_ref[half * c : (half + 1) * c, :], da).astype(BF)
        for part in range(d // c):
            g[3 * d + part * c : 3 * d + (part + 1) * c, :] = gw[:, part * c : (part + 1) * c]
        do_ref[:, half * c : (half + 1) * c] = nt(da, w[...]).astype(BF)
    mask = head_mask(BF)

    def one(i, _):
        rows = pl.ds(pl.multiple_of((i // pairs) * LP, LP), LP)
        col = (i % pairs) * LANES
        cq = pl.ds(pl.multiple_of(col, LANES), LANES)
        ck = pl.ds(pl.multiple_of(d + col, LANES), LANES)
        cu = pl.ds(pl.multiple_of(2 * d + col, LANES), LANES)
        q, ke, u, do = qkv_ref[rows, cq], qkv_ref[rows, ck], qkv_ref[rows, cu], do_ref[rows, cq]
        dq = jnp.zeros((LP, LANES), F32)
        dk = jnp.zeros((LP, LANES), F32)
        du = jnp.zeros((LP, LANES), F32)
        for hh in range(2):
            mk = mask if hh == 0 else 1 - mask
            p = p_ref[2 * i + hh]
            du = du + tn(p, do * mk)
            dp = nt(do * mk, u)
            pf = p.astype(F32)
            ds = (pf * (dp - jnp.sum(dp * pf, axis=-1, keepdims=True))).astype(BF)
            dq = dq + nn(ds, ke * mk)
            dk = dk + tn(ds, q * mk)
        dqkv_ref[rows, cq] = (dq * HDIM ** (-0.5)).astype(BF)
        dqkv_ref[rows, ck] = (dk * HDIM ** (-0.5)).astype(BF)
        dqkv_ref[rows, cu] = du.astype(BF)
        return 0

    lax.fori_loop(0, n_img * pairs, one, 0, unroll=2)
    tr_ref[...] = h_ref[...].T
    dh = jnp.zeros(x_ref.shape, F32)
    for k in range(3):
        for half, (w, g) in enumerate(((qm, gm_ref), (qo, go_ref))):
            at = (2 * k + half) * c
            g[k * d : (k + 1) * d, :] = nn(tr_ref[...], dqkv_ref[:, at : at + c]).astype(BF)
            dh = dh + nt(dqkv_ref[:, at : at + c], w[k])
    n, rr, _ = norm_forward(x_ref[...].astype(F32), w_ref[...])
    dv, dw = norm_backward(n, rr, w_ref[...], dh)
    dx_ref[...] = dy_ref[...] + dv
    dw_ref[...] = dw


def attention_backward(dy, x, gain, kept, qm, qo, om, oo):
    r, d = x.shape
    c = qm.shape[2]
    n_img = r // LP
    heads = d // HDIM
    return call(
        functools.partial(attention_backward_body, n_img),
        [out((r, d), F32), out((1, d), F32), out((3 * d + d, c), BF), out((3 * d + d, c), BF)],
        dy, x, gain, *kept, qm, qo, om, oo,
        scratch=[pltpu.VMEM((r, d), BF), pltpu.VMEM((r, 3 * d), BF), pltpu.VMEM((d, r), BF)],
        flops=4 * r * d * d * 4 + 8 * n_img * heads * LP * LP * LANES,
    )


def gelu_parts(z):
    phi = 0.5 * (1.0 + lax.erf(z * ROOT_HALF))
    return z * phi, phi + z * jnp.exp(-0.5 * z * z) * DENSITY_FACTOR


def tile_of(f):
    for t in (512, 256, 128):
        if f % t == 0:
            return t
    return f


def mlp_forward_body(x_ref, w_ref, im, io, tm, to, y_ref, h_ref, act_ref, slope_ref, acc_ref):
    step = pl.program_id(0)

    @pl.when(step == 0)
    def _():
        x = x_ref[...]
        _, _, h = norm_forward(x, w_ref[...])
        h_ref[...] = h
        acc_ref[...] = x

    for half, (wi, wo) in enumerate(((im, tm), (io, to))):
        a, s = gelu_parts(nn(h_ref[...], wi[...]))
        act = a.astype(BF)
        act_ref[half] = act
        slope_ref[half] = s.astype(BF)
        acc_ref[...] += nn(act, wo[...])

    @pl.when(step == pl.num_programs(0) - 1)
    def _():
        y_ref[...] = acc_ref[...]


def mlp_forward(x, gain, im, io, tm, to):
    r, d = x.shape
    f = im.shape[1]
    t = tile_of(f)
    col = pl.BlockSpec((d, t), lambda i: (0, i))
    row = pl.BlockSpec((t, d), lambda i: (i, 0))
    hid = pl.BlockSpec((2, r, t), lambda i: (0, 0, i))
    return call(
        mlp_forward_body,
        [out((r, d), F32), out((r, d), BF), out((2, r, f), BF), out((2, r, f), BF)],
        x, gain, im, io, tm, to, grid=(f // t,),
        in_specs=[whole((r, d)), whole((1, d)), col, col, row, row],
        out_specs=[whole((r, d)), whole((r, d)), hid, hid],
        scratch=[pltpu.VMEM((r, d), F32)], flops=8 * r * d * f,
    )


def mlp_backward_body(dy_ref, x_ref, w_ref, h_ref, act_ref, slope_ref, im, io, tm, to,
                      dx_ref, dw_ref, gim, gio, gtm, gto, da_ref, tr_ref, dh_ref):
    step = pl.program_id(0)

    @pl.when(step == 0)
    def _():
        da_ref[...] = dy_ref[...].astype(BF)
        tr_ref[...] = h_ref[...].T
        dh_ref[...] = jnp.zeros_like(dh_ref)

    for half, (wi, wo, gi, go) in enumerate(((im, tm, gim, gtm), (io, to, gio, gto))):
        dact = nt(da_ref[...], wo[...])
        dz = (dact * slope_ref[half].astype(F32)).astype(BF)
        gw = tn(act_ref[half], da_ref[...]).astype(BF)
        t = gw.shape[0]
        for part in range(gw.shape[1] // t):
            go[part] = gw[:, part * t : (part + 1) * t]
        gi[0] = nn(tr_ref[...], dz).astype(BF)
        dh_ref[...] += nt(dz, wi[...])

    @pl.when(step == pl.num_programs(0) - 1)
    def _():
        n, rr, _ = norm_forward(x_ref[...], w_ref[...])
        dv, dw = norm_backward(n, rr, w_ref[...], dh_ref[...])
        dx_ref[...] = dy_ref[...] + dv
        dw_ref[...] = dw


def mlp_backward(dy, x, gain, h, act, slope, im, io, tm, to, t):
    r, d = x.shape
    f = im.shape[1]
    col = pl.BlockSpec((d, t), lambda i: (0, i))
    row = pl.BlockSpec((t, d), lambda i: (i, 0))
    hid = pl.BlockSpec((2, r, t), lambda i: (0, 0, i))
    gin = pl.BlockSpec((1, d, t), lambda i: (i, 0, 0))
    gout = pl.BlockSpec((d // t, t, t), lambda i: (0, i, 0))
    return call(
        mlp_backward_body,
        [out((r, d), F32), out((1, d), F32), out((f // t, d, t), BF), out((f // t, d, t), BF),
         out((d // t, f, t), BF), out((d // t, f, t), BF)],
        dy, x, gain, h, act, slope, im, io, tm, to, grid=(f // t,),
        in_specs=[whole((r, d)), whole((r, d)), whole((1, d)), whole((r, d)), hid, hid, col, col, row, row],
        out_specs=[whole((r, d)), whole((1, d)), gin, gin, gout, gout],
        scratch=[pltpu.VMEM((r, d), BF), pltpu.VMEM((d, r), BF), pltpu.VMEM((r, d), F32)], flops=16 * r * d * f,
    )


def routing_body(experts, capacity, half, cols_ref, rows_ref, tc_ref, tr_ref):
    n = cols_ref.shape[0]
    slots = experts * half

    def slot(rank, expert, live):
        core = (rank >= half).astype(I32)
        kept = (rank < capacity) & (live > 0)
        return jnp.where(kept, core * slots + expert * half + rank - core * half, -1)

    r0, r1, pc, lc = (cols_ref[:, i : i + 1] for i in range(4))
    s0, s1, pr, lr = (rows_ref[i : i + 1, :] for i in range(4))
    wide = lax.broadcasted_iota(I32, (n, LANES), 1)
    hot = (((wide == r0) | (wide == r1)) & (lc > 0)).astype(F32).astype(BF)
    earlier = (pr < pc).astype(F32).astype(BF)
    rank = nn(earlier, hot)
    for k, e in enumerate((r0, r1)):
        mine = jnp.sum(jnp.where(wide == e, rank, 0.0), axis=1, keepdims=True).astype(I32)
        tc_ref[:, k : k + 1] = slot(mine, e, lc)
    tall = lax.broadcasted_iota(I32, (max(experts, 8), n), 0)
    hot = (((tall == s0) | (tall == s1)) & (lr > 0)).astype(F32).astype(BF)
    earlier = (pc < pr).astype(F32).astype(BF)
    rank = nn(hot, earlier)
    for k, e in enumerate((s0, s1)):
        mine = jnp.sum(jnp.where(tall == e, rank, 0.0), axis=0, keepdims=True).astype(I32)
        tr_ref[k : k + 1, :] = slot(mine, e, lr)


def dispatch_body(ta_ref, tb_ref, a_ref, b_ref, y_ref):
    slots = y_ref.shape[0]
    n = a_ref.shape[0]
    place = lax.broadcasted_iota(I32, (slots, n), 0)
    total = None
    for t, v in ((ta_ref, a_ref), (tb_ref, b_ref)):
        hot = ((place == t[0:1, :]) | (place == t[1:2, :])).astype(F32).astype(BF)
        part = nn(hot, v[...])
        total = part if total is None else total + part
    y_ref[...] = total.astype(BF)


def dispatch(ta, tb, a, b, slots):
    return call(dispatch_body, [out((slots, a.shape[1]), BF)], ta, tb, a, b,
                flops=4 * slots * a.shape[0] * a.shape[1])[0]


def router_probs(h, router, experts):
    logits = nn(h, router)
    lane = lax.broadcasted_iota(I32, logits.shape, 1)
    logits = jnp.where(lane < experts, logits, -1e30)
    e = jnp.exp(logits - jnp.max(logits, axis=-1, keepdims=True))
    return e / jnp.sum(e, axis=-1, keepdims=True), lane


def expert_body(experts, x_ref, dy_ref, router_ref, mine_ref, im, io, tm, to,
                eout_ref, ret_ref, act_ref, dz_ref, wd_ref, acc_ref, dx_ref):
    step = pl.program_id(0)
    d = x_ref.shape[1]

    @pl.when(step == 0)
    def _():
        probs, _ = router_probs(x_ref[...], router_ref[...], experts)
        gate = jnp.sum(probs * mine_ref[...], axis=-1, keepdims=True)
        wd_ref[...] = (gate * dy_ref[...].astype(F32)).astype(BF)
        acc_ref[...] = jnp.zeros_like(acc_ref)
        dx_ref[...] = jnp.zeros_like(dx_ref)

    for half, (wi, wo) in enumerate(((im, tm), (io, to))):
        a, s = gelu_parts(nn(x_ref[...], wi[...]))
        act = a.astype(BF)
        act_ref[half] = act
        acc_ref[...] += nn(act, wo[...])
        dz = (nt(wd_ref[...], wo[...]) * s).astype(BF)
        dz_ref[half] = dz
        dx_ref[...] += nt(dz, wi[...])

    @pl.when(step == pl.num_programs(0) - 1)
    def _():
        eout = acc_ref[...].astype(BF)
        eout_ref[...] = eout
        ret_ref[:, :d] = dx_ref[...].astype(BF)
        dgate = jnp.sum(dy_ref[...].astype(F32) * eout.astype(F32), axis=-1, keepdims=True)
        high = dgate.astype(BF).astype(F32)
        lane = lax.broadcasted_iota(I32, (x_ref.shape[0], LANES), 1)
        ret_ref[:, d:] = jnp.where(lane < LANES // 2, high, dgate - high).astype(BF)


def expert_forward_backward(x, dy, router, mine, im, io, tm, to, experts):
    r, d = x.shape
    f = im.shape[1]
    t = tile_of(f) // 2
    col = pl.BlockSpec((d, t), lambda i: (0, i))
    row = pl.BlockSpec((t, d), lambda i: (i, 0))
    hid = pl.BlockSpec((2, r, t), lambda i: (0, 0, i))
    return call(
        functools.partial(expert_body, experts),
        [out((r, d), BF), out((r, d + LANES), BF), out((2, r, f), BF), out((2, r, f), BF), out((r, d), BF)],
        x, dy, router, mine, im, io, tm, to, grid=(f // t,),
        in_specs=[whole((r, d)), whole((r, d)), whole(router.shape), whole(mine.shape), col, col, row, row],
        out_specs=[whole((r, d)), whole((r, d + LANES)), hid, hid, whole((r, d))],
        scratch=[pltpu.VMEM((r, d), F32), pltpu.VMEM((r, d), F32)], flops=16 * r * d * f,
    )


def expert_weights_body(x_ref, wd_ref, act_ref, dz_ref, gm_ref, go_ref, xt_ref, wt_ref):
    @pl.when(pl.program_id(0) == 0)
    def _():
        xt_ref[...] = x_ref[...].T
        wt_ref[...] = wd_ref[...].T

    for half, g in enumerate((gm_ref, go_ref)):
        g[0] = nn(xt_ref[...], dz_ref[half]).astype(BF)
        g[1] = nn(wt_ref[...], act_ref[half]).astype(BF)


def expert_weights(x, wd, act, dz):
    r, d = x.shape
    f = act.shape[2]
    t = tile_of(f) // 2
    hid = pl.BlockSpec((2, r, t), lambda i: (0, 0, i))
    grad = pl.BlockSpec((2, d, t), lambda i: (0, 0, i))
    return call(
        expert_weights_body, [out((2, d, f), BF), out((2, d, f), BF)], x, wd, act, dz, grid=(f // t,),
        in_specs=[whole((r, d)), whole((r, d)), hid, hid], out_specs=[grad, grad],
        scratch=[pltpu.VMEM((d, r), BF), pltpu.VMEM((d, r), BF)], flops=8 * r * d * f,
    )


def merge_hots(t_ref, k, n, slots):
    lane = lax.broadcasted_iota(I32, (n, slots), 1)
    return (lane == t_ref[:, k : k + 1]).astype(F32).astype(BF)


def mixture_backward_body(experts, x_ref, w_ref, h_ref, router_ref, dy_ref, route_ref, ta_ref, tb_ref, a_ref, b_ref,
                          dx_ref, dw_ref, dr_ref):
    n, d = x_ref.shape
    slots = a_ref.shape[0]
    probs, lane = router_probs(h_ref[...], router_ref[...], experts)
    dh = jnp.zeros((n, d), F32)
    dsoft = jnp.zeros(probs.shape, F32)
    for k in range(TOPK):
        part = nn(merge_hots(ta_ref, k, n, slots), a_ref[...]) + nn(merge_hots(tb_ref, k, n, slots), b_ref[...])
        dh = dh + part[:, :d]
        dgate = part[:, d : d + 1] + part[:, d + LANES // 2 : d + LANES // 2 + 1]
        dsoft = dsoft + jnp.where(lane == route_ref[:, k : k + 1], dgate, 0.0)
    dlog = (probs * (dsoft - jnp.sum(dsoft * probs, axis=-1, keepdims=True))).astype(BF)
    dr_ref[...] = tn(h_ref[...], dlog)
    dh = dh + nt(dlog, router_ref[...])
    nrm, rr, _ = norm_forward(x_ref[...], w_ref[...])
    dv, dw = norm_backward(nrm, rr, w_ref[...], dh)
    dx_ref[...] = dy_ref[...].astype(F32) + dv
    dw_ref[...] = dw


def mixture_output_body(experts, x_ref, h_ref, router_ref, route_ref, live_ref, ta_ref, tb_ref, a_ref, b_ref, y_ref):
    n, d = x_ref.shape
    slots = a_ref.shape[0]
    probs, lane = router_probs(h_ref[...], router_ref[...], experts)
    total = x_ref[...]
    mixed = jnp.zeros((n, d), F32)
    for k in range(TOPK):
        gate = jnp.sum(jnp.where(lane == route_ref[:, k : k + 1], probs, 0.0), axis=-1, keepdims=True)
        part = nn(merge_hots(ta_ref, k, n, slots), a_ref[...]) + nn(merge_hots(tb_ref, k, n, slots), b_ref[...])
        mixed = mixed + gate * part
    y_ref[...] = (live_ref[...] * (total + mixed)).astype(BF)


def flip(axis, bit):
    size = lax.axis_size(axis)
    return [(i, i ^ bit) for i in range(size)]


def bits_of(axis):
    size = lax.axis_size(axis)
    return [1 << b for b in range(size.bit_length() - 1)]


def other_core(v):
    return lax.ppermute(v, "mdl", flip("mdl", 1))


def add16(a, b):
    return (a.astype(F32) + b.astype(F32)).astype(BF)


def halve(v, axis, bit):
    side = (lax.axis_index(axis) // bit) % 2
    n = v.shape[0] // 2
    keep = lax.dynamic_slice_in_dim(v, side * n, n)
    send = lax.dynamic_slice_in_dim(v, (1 - side) * n, n)
    return add16(keep, lax.ppermute(send, axis, flip(axis, bit)))


def double(v, axis, bit):
    side = (lax.axis_index(axis) // bit) % 2
    got = lax.ppermute(v, axis, flip(axis, bit))
    return jnp.where(side == 0, jnp.concatenate([v, got]), jnp.concatenate([got, v]))


def sum_everywhere(v):
    n = v.shape[0] // 2
    bits = bits_of("grp")
    parts = []
    for part, order in ((v[:n], bits), (v[n:], bits[::-1])):
        for bit in order:
            part = halve(part, "grp", bit)
        parts.append(part)
    size = lax.axis_size("exp")
    joined = jnp.concatenate(parts)
    rows = joined.shape[0] // size
    spread = lax.all_to_all(joined.reshape(size, rows, -1), "exp", 0, 0, tiled=True)
    mine = jnp.sum(spread.astype(F32), axis=0).astype(BF)
    joined = lax.all_gather(mine, "exp", axis=0, tiled=True)
    h = joined.shape[0] // 2
    done = []
    for part, order in ((joined[:h], bits), (joined[h:], bits[::-1])):
        for bit in order[::-1]:
            part = double(part, "grp", bit)
        done.append(part)
    return jnp.concatenate(done)


def small_sum(v):
    for axis in ("mdl", "grp", "exp"):
        for bit in bits_of(axis):
            v = v + lax.ppermute(v, axis, flip(axis, bit))
    return v


def reduce_body(n_in, per, n_exp, *refs):
    mine = refs[:n_in]
    other = refs[n_in : 2 * n_in]
    small_ref = refs[2 * n_in]
    out_ref, sum_ref = refs[2 * n_in + 1 : 2 * n_in + 3]
    (acc, got, r1, r2, zr, sm, load_sem, m_send, m_recv, x_send, x_recv, z_send, z_recv, s_send, s_recv) = refs[2 * n_in + 3 :]
    n = n_in * per
    rows = acc.shape[2]
    h, q = rows // 2, rows // 4
    t = q // n_exp
    g = lax.axis_index("grp")
    z = lax.axis_index("exp")
    core = lax.axis_index("mdl")
    bx, by = g % 2, g // 2
    flat = {"x": g + 1 - 2 * bx, "y": g + 2 - 4 * by}
    order = (("x", "y"), ("y", "x"))
    bits = ((bx, by), (by, bx))

    barrier = pltpu.get_barrier_semaphore()
    others = [{"mdl": 1 - core}, {"grp": flat["x"]}, {"grp": flat["y"]}]
    others += [{"exp": (z + o) % n_exp} for o in range(1, n_exp)]
    for dev in others:
        pl.semaphore_signal(barrier, inc=1, device_id=dev, device_id_type=MESH)
    pl.semaphore_wait(barrier, len(others))

    def load(c):
        i, p = c // per, c % per
        return pltpu.make_async_copy(mine[i].at[p], acc.at[c], load_sem.at[c])

    def swap(c):
        i, p = c // per, c % per
        return pltpu.make_async_remote_copy(other[i].at[p], got.at[c], m_send.at[c], m_recv.at[c],
                                            device_id={"mdl": 1 - core}, device_id_type=MESH)

    for c in range(n):
        swap(c).start()
        load(c).start()

    def swap_at(c):
        return pltpu.make_async_remote_copy(other[0].at[0], got.at[c], m_send.at[c], m_recv.at[c],
                                            device_id={"mdl": 1 - core}, device_id_type=MESH)

    def load_at(c):
        return pltpu.make_async_copy(mine[0].at[0], acc.at[c], load_sem.at[c])

    def over(u, leg, src, dst, slot, c):
        return pltpu.make_async_remote_copy(src, dst, x_send.at[slot, u, c], x_recv.at[slot, u, c],
                                            device_id={"grp": flat[order[u][leg]]}, device_id_type=MESH)

    def first(u, c):
        return over(u, 0, acc.at[c, u, pl.ds(pl.multiple_of((1 - bits[u][0]) * h, h), h)], r1.at[c, u], 0, c)

    def second(u, c):
        return over(u, 1, r1.at[c, u, pl.ds(pl.multiple_of((1 - bits[u][1]) * q, q), q)], r2.at[c, u], 1, c)

    def along(u, c, o):
        return pltpu.make_async_remote_copy(
            r2.at[c, u, pl.ds(pl.multiple_of(((z + o) % n_exp) * t, t), t)], zr.at[c, u, o - 1],
            z_send.at[0, u, o - 1, c], z_recv.at[0, u, o - 1, c],
            device_id={"exp": (z + o) % n_exp}, device_id_type=MESH)

    def place(u):
        return bits[u][0] * h + bits[u][1] * q

    def back(u, c, o):
        here = out_ref.at[c, u, pl.ds(pl.multiple_of(place(u) + z * t, t), t)]
        return pltpu.make_async_remote_copy(here, here, z_send.at[1, u, o - 1, c], z_recv.at[1, u, o - 1, c],
                                            device_id={"exp": (z + o) % n_exp}, device_id_type=MESH)

    def third(u, c):
        here = out_ref.at[c, u, pl.ds(pl.multiple_of(place(u), q), q)]
        return over(u, 1, here, here, 2, c)

    def fourth(u, c):
        here = out_ref.at[c, u, pl.ds(pl.multiple_of(bits[u][0] * h, h), h)]
        return over(u, 0, here, here, 3, c)

    def plus(a, b):
        return (a.astype(F32) + b.astype(F32)).astype(BF)

    def s1(c):
        load_at(c).wait()
        swap_at(c).wait_recv()
        for u in range(2):
            acc[c, u] = plus(acc[c, u], got[c, u])
            first(u, c).start()

    def s2(c):
        for u in range(2):
            first(u, c).wait_recv()
            keep = acc[c, u, pl.ds(pl.multiple_of(bits[u][0] * h, h), h)]
            r1[c, u] = plus(keep, r1[c, u])
            second(u, c).start()

    def s3(c):
        for u in range(2):
            second(u, c).wait_recv()
            keep = r1[c, u, pl.ds(pl.multiple_of(bits[u][1] * q, q), q)]
            r2[c, u] = plus(keep, r2[c, u])
            for o in range(1, n_exp):
                along(u, c, o).start()

    def s4(c):
        for u in range(2):
            total = r2[c, u, pl.ds(pl.multiple_of(z * t, t), t)].astype(F32)
            for o in range(1, n_exp):
                along(u, c, o).wait_recv()
                total = total + zr[c, u, o - 1].astype(F32)
            out_ref[c, u, pl.ds(pl.multiple_of(place(u) + z * t, t), t)] = total.astype(BF)
            for o in range(1, n_exp):
                back(u, c, o).start()

    def s5(c):
        for u in range(2):
            for o in range(1, n_exp):
                back(u, c, o).wait_recv()
            third(u, c).start()

    def s6(c):
        for u in range(2):
            third(u, c).wait_recv()
            fourth(u, c).start()

    def s7(c):
        for u in range(2):
            fourth(u, c).wait_recv()
        swap_at(c).wait_send()
        for u in range(2):
            for make in (first, second, third, fourth):
                make(u, c).wait_send()
            for o in range(1, n_exp):
                along(u, c, o).wait_send()
                back(u, c, o).wait_send()

    steps = (s1, s2, s3, s4, s5, s6, s7)

    def wave(tau, _):
        for s, step in enumerate(steps):
            c = tau - s

            @pl.when((c >= 0) & (c < n))
            def _(step=step, c=c):
                step(c)

        return 0

    lax.fori_loop(0, n + len(steps) - 1, wave, 0)

    sm[0] = small_ref[...]
    legs = [({"mdl": 1 - core}), ({"grp": flat["x"]}), ({"grp": flat["y"]})]
    for i, dev in enumerate(legs):
        cp = pltpu.make_async_remote_copy(sm.at[2 * i], sm.at[2 * i + 1], s_send.at[i], s_recv.at[i], device_id=dev, device_id_type=MESH)
        cp.start()
        cp.wait()
        sm[2 * i + 2] = sm[2 * i] + sm[2 * i + 1]
    base = 2 * len(legs) + 1
    sm[pl.ds(base + z, 1)] = sm[pl.ds(base - 1, 1)]
    cps = []
    for o in range(1, n_exp):
        cps.append(pltpu.make_async_remote_copy(sm.at[base - 1], sm.at[base + z], s_send.at[len(legs) + o - 1], s_recv.at[len(legs) + o - 1],
                                                device_id={"exp": (z + o) % n_exp}, device_id_type=MESH))
        cps[-1].start()
    for cp in cps:
        cp.wait()
    total = sm[base]
    for k in range(1, n_exp):
        total = total + sm[base + k]
    sum_ref[...] = total


def reduce_all(mine, other, small, n_exp):
    per, _, rows, c = mine[0].shape
    n = len(mine) * per
    h, q = rows // 2, rows // 4
    t = q // n_exp
    D = pltpu.SemaphoreType.DMA
    any_ = pl.BlockSpec(memory_space=pl.ANY)
    vm = pl.BlockSpec(memory_space=pltpu.VMEM)
    return pl.pallas_call(
        functools.partial(reduce_body, len(mine), per, n_exp),
        in_specs=[any_] * (2 * len(mine)) + [vm],
        out_specs=[vm, vm],
        out_shape=[jax.ShapeDtypeStruct((n, 2, rows, c), BF), jax.ShapeDtypeStruct(small.shape, F32)],
        scratch_shapes=[
            pltpu.VMEM((n, 2, rows, c), BF), pltpu.VMEM((n, 2, rows, c), BF), pltpu.VMEM((n, 2, h, c), BF),
            pltpu.VMEM((n, 2, q, c), BF), pltpu.VMEM((n, 2, n_exp - 1, t, c), BF), pltpu.VMEM((7 + n_exp,) + small.shape, F32),
            D((n,)), D((n,)), D((n,)), D((4, 2, n)), D((4, 2, n)), D((2, 2, n_exp - 1, n)), D((2, 2, n_exp - 1, n)),
            D((3 + n_exp,)), D((3 + n_exp,)),
        ],
        compiler_params=pltpu.CompilerParams(collective_id=0, has_side_effects=True, vmem_limit_bytes=VMEM_BYTES),
    )(*mine, *other, small)


def on_device(images, counts, routes, priority, gain_one, qkv_one, out_one, gain_two, fc_in, fc_out, gain_three,
              qkv_two, out_two, gain_four, router, expert_in, expert_out, cotangent):
    n_slot, length, d = images.shape
    experts = router.shape[1]
    n_mdl = lax.axis_size("mdl")
    capacity = (25 * L * TOPK + 8 * experts - 1) // (8 * experts)
    half = -(-(-(-capacity // n_mdl)) // 16) * 16
    slots = experts * half
    own_img = n_slot // n_mdl
    f = fc_in.shape[1]
    rows = own_img * LP
    core = lax.axis_index("mdl")

    def own(v, axis=0):
        return lax.dynamic_slice_in_dim(v, core * rows, rows, axis)

    def oth(v, axis=0):
        return lax.dynamic_slice_in_dim(v, (1 - core) * rows, rows, axis)

    def padded(v):
        return jnp.pad(v, ((0, 0), (0, LP - length), (0, 0))).reshape(n_slot * LP, -1)

    qm1, om1, im, tm, qm2, om2, em, fm = qkv_one, out_one, fc_in, fc_out, qkv_two, out_two, expert_in[0], expert_out[0]
    qo1, oo1, io, to, qo2, oo2, eo, fo = (other_core(w) for w in (qm1, om1, im, tm, qm2, om2, em, fm))
    g1, g2, g3, g4 = (g.reshape(1, d) for g in (gain_one, gain_two, gain_three, gain_four))
    router_wide = jnp.pad(router, ((0, 0), (0, LANES - experts)))
    mine = (jnp.arange(LANES, dtype=I32) == lax.axis_index("exp")).astype(F32)[None]

    img_live = (jnp.arange(n_slot, dtype=I32) < counts[0, 0]).astype(I32)
    live = jnp.pad(jnp.broadcast_to(img_live[:, None], (n_slot, length)), ((0, 0), (0, LP - length))).reshape(-1)
    x0 = own(padded(images))
    dy = padded(cotangent * img_live[:, None, None].astype(BF))
    route = padded(routes)
    prior = padded(priority.reshape(n_slot, length, 1))
    cols = jnp.concatenate([route, prior, live[:, None]], axis=1)
    slot_cols, slot_rows = call(
        functools.partial(routing_body, experts, capacity, half),
        [out((n_slot * LP, TOPK), I32), out((TOPK, n_slot * LP), I32)], cols, cols.T,
    )
    mine_rows = slot_rows - core * slots
    own_tokens_here = own(slot_cols) - core * slots
    own_tokens_there = own(slot_cols) - (1 - core) * slots
    own_tokens_there = jnp.where(own_tokens_there < slots, own_tokens_there, -1)
    peers = lax.axis_size("exp")

    def exchange(v):
        shaped = v.reshape(peers, v.shape[0] // peers, v.shape[1])
        return lax.all_to_all(shaped, "exp", 0, 0, tiled=True).reshape(v.shape)

    dy_out = dispatch(mine_rows[:, :rows], mine_rows[:, rows:], dy[:rows], dy[rows:], slots)
    dy_in = exchange(dy_out)

    x1, *kept1 = attention_forward(x0, g1, qm1, qo1, om1, oo1)
    x2, h2, act2, slope2 = mlp_forward(x1, g2, im, io, tm, to)
    x3, *kept3, h4 = attention_forward(x2, g3, qm2, qo2, om2, oo2, g4)

    h4_out = dispatch(own(mine_rows, 1), oth(mine_rows, 1), h4, other_core(h4), slots)
    h4_in = exchange(h4_out)
    eout, ret, eact, edz, ewd = expert_forward_backward(h4_in, dy_in, router_wide, mine, em, eo, fm, fo, experts)
    ret = exchange(ret)
    ret_there = other_core(ret)
    eout = exchange(eout)
    eout_there = other_core(eout)
    ge_mine, ge_other = expert_weights(h4_in, ewd, eact, edz)

    own_route = own(route)
    dx3, dg4, dr = call(
        functools.partial(mixture_backward_body, experts),
        [out((rows, d), F32), out((1, d), F32), out((d, LANES), F32)],
        x3, g4, h4, router_wide, own(dy), own_route, own_tokens_here, own_tokens_there, ret, ret_there,
        flops=8 * rows * slots * d,
    )
    [output] = call(
        functools.partial(mixture_output_body, experts), [out((rows, d), BF)],
        x3, h4, router_wide, own_route, own(live).astype(F32)[:, None], own_tokens_here, own_tokens_there, eout, eout_there,
        flops=8 * rows * slots * d,
    )
    expert_sum = lax.psum_scatter(
        add16(ge_mine, other_core(ge_other)), "grp", scatter_dimension=1, tiled=True)

    dx2, dg3, a2_mine, a2_other = attention_backward(dx3, x2, g3, kept3, qm2, qo2, om2, oo2)
    c = qkv_one.shape[2]
    dx1, dg2, gim, gio, gtm, gto = mlp_backward(dx2, x1, g2, h2, act2, slope2, im, io, tm, to, c)
    dx0, dg1, a1_mine, a1_other = attention_backward(dx1, x0, g1, kept1, qm1, qo1, om1, oo1)
    small = jnp.concatenate([dg1, dg2, dg3, dg4, dr.T[:experts]], axis=0)
    mines, others = (a2_mine, gim, gtm, a1_mine), (a2_other, gio, gto, a1_other)

    per = 2
    unit = 4 * d // (2 * per)
    if lax.axis_size("grp") == 4 and n_mdl == 2 and unit % (64 * peers) == 0 and f * 2 == 4 * d:
        split = [[v.reshape(per, 2, unit, c) for v in side] for side in (mines, others)]
        totals, small = reduce_all(*split, small, peers)
        sums = totals.reshape(len(mines), 4 * d, c)
    else:
        flat = [[v.reshape(4 * d, c) for v in side] for side in (mines, others)]
        sums = [sum_everywhere(add16(a, other_core(b))) for a, b in zip(*flat)]
        small = small_sum(small)

    def unpack(total):
        qkv = total[: 3 * d].reshape(3, d, c).astype(F32)
        return qkv, panels(total[3 * d :].reshape(d // c, c, c))

    def panels(v):
        return jnp.concatenate([v[i] for i in range(v.shape[0])], axis=1).astype(F32)

    def both(v):
        there = other_core(v)
        joined = jnp.where(core == 0, jnp.concatenate([v, there]), jnp.concatenate([there, v]))
        return joined.reshape(n_slot, LP, d)[:, :length]

    grad_qkv_two, grad_out_two = unpack(sums[0])
    grad_fc_in = panels(sums[1].reshape(f // c, d, c))
    grad_fc_out = panels(sums[2].reshape(d // c, f, c))
    grad_qkv_one, grad_out_one = unpack(sums[3])
    return (
        both(output), both(dx0.astype(BF)),
        small[0], grad_qkv_one, grad_out_one, small[1], grad_fc_in, grad_fc_out,
        small[2], grad_qkv_two, grad_out_two, small[3], small[4:].T,
        expert_sum[0].astype(F32)[None], expert_sum[1].astype(F32).T[None],
    )


def solution(mesh):
    token = P(("grp", "exp"), None, None)
    column, line = P(None, None, "mdl"), P("mdl", None)
    return jax.shard_map(
        on_device,
        mesh=mesh,
        in_specs=(token, P("grp", "exp"), token, P(("grp", "exp"), None), P(), column, line, P(), P(None, "mdl"), line,
                  P(), column, line, P(), P(), P("exp", None, "mdl"), P("exp", "mdl", None), token),
        out_specs=(token, token, P(), column, line, P(), P(None, "mdl"), line, P(), column, line, P(), P(),
                   P("exp", "grp", "mdl"), P("exp", "mdl", "grp")),
        check_vma=False,
    )
```

```python
import functools
import math

import jax
import jax.numpy as jnp
from jax import lax
from jax.experimental import pallas as pl
from jax.experimental.pallas import tpu as pltpu
from jax.sharding import PartitionSpec as P

HDIM = 64
L = 197
TOPK = 2
LP = (L + 15) // 16 * 16
LANES = 128
BF = jnp.bfloat16
F32 = jnp.float32
I32 = jnp.int32

EPSILON = 1e-06
ROOT_HALF = 0.7071067811865476
DENSITY_FACTOR = 0.3989422804014327
VMEM_BYTES = 60 * 1024 * 1024
MESH = pl.DeviceIdType.MESH


def nn(a, b):
    return lax.dot_general(a, b, (((1,), (0,)), ((), ())), preferred_element_type=F32)


def nt(a, b):
    return lax.dot_general(a, b, (((1,), (1,)), ((), ())), preferred_element_type=F32)


def tn(a, b):
    return lax.dot_general(a, b, (((0,), (0,)), ((), ())), preferred_element_type=F32)


def norm_forward(v, w):
    c = v - jnp.mean(v, axis=-1, keepdims=True)
    r = lax.rsqrt(jnp.mean(c * c, axis=-1, keepdims=True) + EPSILON)
    n = c * r
    return n, r, (n * w).astype(BF)


def norm_backward(n, r, w, dh):
    dn = dh * w
    dw = jnp.sum(dh * n, axis=0, keepdims=True)
    dv = r * (dn - jnp.mean(dn, axis=-1, keepdims=True) - n * jnp.mean(dn * n, axis=-1, keepdims=True))
    return dv, dw


def whole(shape):
    return pl.BlockSpec(shape, lambda *i: (0,) * len(shape))


def call(body, out_shape, *args, grid=(), in_specs=None, out_specs=None, scratch=(), flops=0):
    if in_specs is None:
        in_specs = [whole(a.shape) for a in args]
    if out_specs is None:
        out_specs = [whole(o.shape) for o in out_shape]
    moved = sum(math.prod(a.shape) * a.dtype.itemsize for a in args)
    moved += sum(math.prod(o.shape) * jnp.dtype(o.dtype).itemsize for o in out_shape)
    return pl.pallas_call(
        body,
        grid=grid,
        in_specs=in_specs,
        out_specs=out_specs,
        out_shape=out_shape,
        scratch_shapes=list(scratch),
        cost_estimate=pl.CostEstimate(flops=int(flops), bytes_accessed=int(moved), transcendentals=0),
        compiler_params=pltpu.CompilerParams(vmem_limit_bytes=VMEM_BYTES),
    )(*args)


def out(shape, dtype):
    return jax.ShapeDtypeStruct(shape, dtype)


def head_mask(dtype):
    lane = lax.broadcasted_iota(I32, (LP, LANES), 1)
    return (lane < HDIM).astype(dtype)


def attention_forward_body(n_img, tail, *refs):
    if tail:
        x_ref, w_ref, qm, qo, om, oo, w4_ref, y_ref, h_ref, qkv_ref, p_ref, o_ref, h4_ref = refs
    else:
        x_ref, w_ref, qm, qo, om, oo, y_ref, h_ref, qkv_ref, p_ref, o_ref = refs
    d = x_ref.shape[1]
    c = qm.shape[2]
    pairs = d // LANES
    _, _, h = norm_forward(x_ref[...].astype(F32), w_ref[...])
    h_ref[...] = h
    for k in range(3):
        for half, w in ((0, qm), (1, qo)):
            at = (2 * k + half) * c
            qkv_ref[:, at : at + c] = nn(h_ref[...], w[k]).astype(BF)
    mask = head_mask(BF)
    key_ok = lax.broadcasted_iota(I32, (LP, LP), 1) < L

    def one(i, _):
        rows = pl.ds(pl.multiple_of((i // pairs) * LP, LP), LP)
        col = (i % pairs) * LANES
        q = qkv_ref[rows, pl.ds(pl.multiple_of(col, LANES), LANES)]
        ke = qkv_ref[rows, pl.ds(pl.multiple_of(d + col, LANES), LANES)]
        u = qkv_ref[rows, pl.ds(pl.multiple_of(2 * d + col, LANES), LANES)]
        o = jnp.zeros((LP, LANES), F32)
        for hh in range(2):
            mk = mask if hh == 0 else 1 - mask
            s = nt(q * mk, ke) * HDIM ** (-0.5)
            s = jnp.where(key_ok, s, -1e30)
            e = jnp.exp(s - jnp.max(s, axis=-1, keepdims=True))
            p = (e / jnp.sum(e, axis=-1, keepdims=True)).astype(BF)
            p_ref[2 * i + hh] = p
            o = o + nn(p, u * mk)
        o_ref[rows, pl.ds(pl.multiple_of(col, LANES), LANES)] = o.astype(BF)
        return 0

    lax.fori_loop(0, n_img * pairs, one, 0, unroll=2)
    y = x_ref[...].astype(F32) + nn(o_ref[:, :c], om[...]) + nn(o_ref[:, c:], oo[...])
    y_ref[...] = y
    if tail:
        _, _, h4 = norm_forward(y, w4_ref[...])
        h4_ref[...] = h4


def attention_forward(x, gain, qm, qo, om, oo, gain4=None):
    r, d = x.shape
    n_img = r // LP
    heads = d // HDIM
    shapes = [out((r, d), F32), out((r, d), BF), out((r, 3 * d), BF), out((n_img * heads, LP, LP), BF), out((r, d), BF)]
    args = [x, gain, qm, qo, om, oo]
    if gain4 is not None:
        shapes.append(out((r, d), BF))
        args.append(gain4)
    return call(
        functools.partial(attention_forward_body, n_img, gain4 is not None),
        shapes, *args, flops=2 * r * d * d * 4 + 4 * n_img * heads * LP * LP * LANES,
    )


def attention_backward_body(n_img, dy_ref, x_ref, w_ref, h_ref, qkv_ref, p_ref, o_ref, qm, qo, om, oo,
                            dx_ref, dw_ref, gm_ref, go_ref, do_ref, dqkv_ref, tr_ref):
    d = x_ref.shape[1]
    c = qm.shape[2]
    pairs = d // LANES
    da = dy_ref[...].astype(BF)
    tr_ref[...] = o_ref[...].T
    for half, (w, g) in enumerate(((om, gm_ref), (oo, go_ref))):
        gw = nn(tr_ref[half * c : (half + 1) * c, :], da).astype(BF)
        for part in range(d // c):
            g[3 * d + part * c : 3 * d + (part + 1) * c, :] = gw[:, part * c : (part + 1) * c]
        do_ref[:, half * c : (half + 1) * c] = nt(da, w[...]).astype(BF)
    mask = head_mask(BF)

    def one(i, _):
        rows = pl.ds(pl.multiple_of((i // pairs) * LP, LP), LP)
        col = (i % pairs) * LANES
        cq = pl.ds(pl.multiple_of(col, LANES), LANES)
        ck = pl.ds(pl.multiple_of(d + col, LANES), LANES)
        cu = pl.ds(pl.multiple_of(2 * d + col, LANES), LANES)
        q, ke, u, do = qkv_ref[rows, cq], qkv_ref[rows, ck], qkv_ref[rows, cu], do_ref[rows, cq]
        dq = jnp.zeros((LP, LANES), F32)
        dk = jnp.zeros((LP, LANES), F32)
        du = jnp.zeros((LP, LANES), F32)
        for hh in range(2):
            mk = mask if hh == 0 else 1 - mask
            p = p_ref[2 * i + hh]
            du = du + tn(p, do * mk)
            dp = nt(do * mk, u)
            pf = p.astype(F32)
            ds = (pf * (dp - jnp.sum(dp * pf, axis=-1, keepdims=True))).astype(BF)
            dq = dq + nn(ds, ke * mk)
            dk = dk + tn(ds, q * mk)
        dqkv_ref[rows, cq] = (dq * HDIM ** (-0.5)).astype(BF)
        dqkv_ref[rows, ck] = (dk * HDIM ** (-0.5)).astype(BF)
        dqkv_ref[rows, cu] = du.astype(BF)
        return 0

    lax.fori_loop(0, n_img * pairs, one, 0, unroll=2)
    tr_ref[...] = h_ref[...].T
    dh = jnp.zeros(x_ref.shape, F32)
    for k in range(3):
        for half, (w, g) in enumerate(((qm, gm_ref), (qo, go_ref))):
            at = (2 * k + half) * c
            g[k * d : (k + 1) * d, :] = nn(tr_ref[...], dqkv_ref[:, at : at + c]).astype(BF)
            dh = dh + nt(dqkv_ref[:, at : at + c], w[k])
    n, rr, _ = norm_forward(x_ref[...].astype(F32), w_ref[...])
    dv, dw = norm_backward(n, rr, w_ref[...], dh)
    dx_ref[...] = dy_ref[...] + dv
    dw_ref[...] = dw


def attention_backward(dy, x, gain, kept, qm, qo, om, oo):
    r, d = x.shape
    c = qm.shape[2]
    n_img = r // LP
    heads = d // HDIM
    return call(
        functools.partial(attention_backward_body, n_img),
        [out((r, d), F32), out((1, d), F32), out((3 * d + d, c), BF), out((3 * d + d, c), BF)],
        dy, x, gain, *kept, qm, qo, om, oo,
        scratch=[pltpu.VMEM((r, d), BF), pltpu.VMEM((r, 3 * d), BF), pltpu.VMEM((d, r), BF)],
        flops=4 * r * d * d * 4 + 8 * n_img * heads * LP * LP * LANES,
    )


def gelu_parts(z):
    phi = 0.5 * (1.0 + lax.erf(z * ROOT_HALF))
    return z * phi, phi + z * jnp.exp(-0.5 * z * z) * DENSITY_FACTOR


def tile_of(f):
    for t in (512, 256, 128):
        if f % t == 0:
            return t
    return f


def mlp_forward_body(x_ref, w_ref, im, io, tm, to, y_ref, h_ref, act_ref, slope_ref, acc_ref):
    step = pl.program_id(0)

    @pl.when(step == 0)
    def _():
        x = x_ref[...]
        _, _, h = norm_forward(x, w_ref[...])
        h_ref[...] = h
        acc_ref[...] = x

    for half, (wi, wo) in enumerate(((im, tm), (io, to))):
        a, s = gelu_parts(nn(h_ref[...], wi[...]))
        act = a.astype(BF)
        act_ref[half] = act
        slope_ref[half] = s.astype(BF)
        acc_ref[...] += nn(act, wo[...])

    @pl.when(step == pl.num_programs(0) - 1)
    def _():
        y_ref[...] = acc_ref[...]


def mlp_forward(x, gain, im, io, tm, to):
    r, d = x.shape
    f = im.shape[1]
    t = tile_of(f)
    col = pl.BlockSpec((d, t), lambda i: (0, i))
    row = pl.BlockSpec((t, d), lambda i: (i, 0))
    hid = pl.BlockSpec((2, r, t), lambda i: (0, 0, i))
    return call(
        mlp_forward_body,
        [out((r, d), F32), out((r, d), BF), out((2, r, f), BF), out((2, r, f), BF)],
        x, gain, im, io, tm, to, grid=(f // t,),
        in_specs=[whole((r, d)), whole((1, d)), col, col, row, row],
        out_specs=[whole((r, d)), whole((r, d)), hid, hid],
        scratch=[pltpu.VMEM((r, d), F32)], flops=8 * r * d * f,
    )


def mlp_backward_body(dy_ref, x_ref, w_ref, h_ref, act_ref, slope_ref, im, io, tm, to,
                      dx_ref, dw_ref, gim, gio, gtm, gto, da_ref, tr_ref, dh_ref):
    step = pl.program_id(0)

    @pl.when(step == 0)
    def _():
        da_ref[...] = dy_ref[...].astype(BF)
        tr_ref[...] = h_ref[...].T
        dh_ref[...] = jnp.zeros_like(dh_ref)

    for half, (wi, wo, gi, go) in enumerate(((im, tm, gim, gtm), (io, to, gio, gto))):
        dact = nt(da_ref[...], wo[...])
        dz = (dact * slope_ref[half].astype(F32)).astype(BF)
        gw = tn(act_ref[half], da_ref[...]).astype(BF)
        t = gw.shape[0]
        for part in range(gw.shape[1] // t):
            go[part] = gw[:, part * t : (part + 1) * t]
        gi[0] = nn(tr_ref[...], dz).astype(BF)
        dh_ref[...] += nt(dz, wi[...])

    @pl.when(step == pl.num_programs(0) - 1)
    def _():
        n, rr, _ = norm_forward(x_ref[...], w_ref[...])
        dv, dw = norm_backward(n, rr, w_ref[...], dh_ref[...])
        dx_ref[...] = dy_ref[...] + dv
        dw_ref[...] = dw


def mlp_backward(dy, x, gain, h, act, slope, im, io, tm, to, t):
    r, d = x.shape
    f = im.shape[1]
    col = pl.BlockSpec((d, t), lambda i: (0, i))
    row = pl.BlockSpec((t, d), lambda i: (i, 0))
    hid = pl.BlockSpec((2, r, t), lambda i: (0, 0, i))
    gin = pl.BlockSpec((1, d, t), lambda i: (i, 0, 0))
    gout = pl.BlockSpec((d // t, t, t), lambda i: (0, i, 0))
    return call(
        mlp_backward_body,
        [out((r, d), F32), out((1, d), F32), out((f // t, d, t), BF), out((f // t, d, t), BF),
         out((d // t, f, t), BF), out((d // t, f, t), BF)],
        dy, x, gain, h, act, slope, im, io, tm, to, grid=(f // t,),
        in_specs=[whole((r, d)), whole((r, d)), whole((1, d)), whole((r, d)), hid, hid, col, col, row, row],
        out_specs=[whole((r, d)), whole((1, d)), gin, gin, gout, gout],
        scratch=[pltpu.VMEM((r, d), BF), pltpu.VMEM((d, r), BF), pltpu.VMEM((r, d), F32)], flops=16 * r * d * f,
    )


def routing_body(experts, capacity, half, cols_ref, rows_ref, tc_ref, tr_ref):
    n = cols_ref.shape[0]
    slots = experts * half

    def slot(rank, expert, live):
        core = (rank >= half).astype(I32)
        kept = (rank < capacity) & (live > 0)
        return jnp.where(kept, core * slots + expert * half + rank - core * half, -1)

    r0, r1, pc, lc = (cols_ref[:, i : i + 1] for i in range(4))
    s0, s1, pr, lr = (rows_ref[i : i + 1, :] for i in range(4))
    wide = lax.broadcasted_iota(I32, (n, LANES), 1)
    hot = (((wide == r0) | (wide == r1)) & (lc > 0)).astype(F32).astype(BF)
    earlier = (pr < pc).astype(F32).astype(BF)
    rank = nn(earlier, hot)
    for k, e in enumerate((r0, r1)):
        mine = jnp.sum(jnp.where(wide == e, rank, 0.0), axis=1, keepdims=True).astype(I32)
        tc_ref[:, k : k + 1] = slot(mine, e, lc)
    tall = lax.broadcasted_iota(I32, (max(experts, 8), n), 0)
    hot = (((tall == s0) | (tall == s1)) & (lr > 0)).astype(F32).astype(BF)
    earlier = (pc < pr).astype(F32).astype(BF)
    rank = nn(hot, earlier)
    for k, e in enumerate((s0, s1)):
        mine = jnp.sum(jnp.where(tall == e, rank, 0.0), axis=0, keepdims=True).astype(I32)
        tr_ref[k : k + 1, :] = slot(mine, e, lr)


def dispatch_body(ta_ref, tb_ref, a_ref, b_ref, y_ref):
    slots = y_ref.shape[0]
    n = a_ref.shape[0]
    place = lax.broadcasted_iota(I32, (slots, n), 0)
    total = None
    for t, v in ((ta_ref, a_ref), (tb_ref, b_ref)):
        hot = ((place == t[0:1, :]) | (place == t[1:2, :])).astype(F32).astype(BF)
        part = nn(hot, v[...])
        total = part if total is None else total + part
    y_ref[...] = total.astype(BF)


def dispatch(ta, tb, a, b, slots):
    return call(dispatch_body, [out((slots, a.shape[1]), BF)], ta, tb, a, b,
                flops=4 * slots * a.shape[0] * a.shape[1])[0]


def router_probs(h, router, experts):
    logits = nn(h, router)
    lane = lax.broadcasted_iota(I32, logits.shape, 1)
    logits = jnp.where(lane < experts, logits, -1e30)
    e = jnp.exp(logits - jnp.max(logits, axis=-1, keepdims=True))
    return e / jnp.sum(e, axis=-1, keepdims=True), lane


def expert_body(experts, x_ref, dy_ref, router_ref, mine_ref, im, io, tm, to,
                eout_ref, ret_ref, act_ref, dz_ref, wd_ref, acc_ref, dx_ref):
    step = pl.program_id(0)
    d = x_ref.shape[1]

    @pl.when(step == 0)
    def _():
        probs, _ = router_probs(x_ref[...], router_ref[...], experts)
        gate = jnp.sum(probs * mine_ref[...], axis=-1, keepdims=True)
        wd_ref[...] = (gate * dy_ref[...].astype(F32)).astype(BF)
        acc_ref[...] = jnp.zeros_like(acc_ref)
        dx_ref[...] = jnp.zeros_like(dx_ref)

    for half, (wi, wo) in enumerate(((im, tm), (io, to))):
        a, s = gelu_parts(nn(x_ref[...], wi[...]))
        act = a.astype(BF)
        act_ref[half] = act
        acc_ref[...] += nn(act, wo[...])
        dz = (nt(wd_ref[...], wo[...]) * s).astype(BF)
        dz_ref[half] = dz
        dx_ref[...] += nt(dz, wi[...])

    @pl.when(step == pl.num_programs(0) - 1)
    def _():
        eout = acc_ref[...].astype(BF)
        eout_ref[...] = eout
        ret_ref[:, :d] = dx_ref[...].astype(BF)
        dgate = jnp.sum(dy_ref[...].astype(F32) * eout.astype(F32), axis=-1, keepdims=True)
        high = dgate.astype(BF).astype(F32)
        lane = lax.broadcasted_iota(I32, (x_ref.shape[0], LANES), 1)
        ret_ref[:, d:] = jnp.where(lane < LANES // 2, high, dgate - high).astype(BF)


def expert_forward_backward(x, dy, router, mine, im, io, tm, to, experts):
    r, d = x.shape
    f = im.shape[1]
    t = tile_of(f) // 2
    col = pl.BlockSpec((d, t), lambda i: (0, i))
    row = pl.BlockSpec((t, d), lambda i: (i, 0))
    hid = pl.BlockSpec((2, r, t), lambda i: (0, 0, i))
    return call(
        functools.partial(expert_body, experts),
        [out((r, d), BF), out((r, d + LANES), BF), out((2, r, f), BF), out((2, r, f), BF), out((r, d), BF)],
        x, dy, router, mine, im, io, tm, to, grid=(f // t,),
        in_specs=[whole((r, d)), whole((r, d)), whole(router.shape), whole(mine.shape), col, col, row, row],
        out_specs=[whole((r, d)), whole((r, d + LANES)), hid, hid, whole((r, d))],
        scratch=[pltpu.VMEM((r, d), F32), pltpu.VMEM((r, d), F32)], flops=16 * r * d * f,
    )


def expert_weights_body(x_ref, wd_ref, act_ref, dz_ref, gm_ref, go_ref, xt_ref, wt_ref):
    @pl.when(pl.program_id(0) == 0)
    def _():
        xt_ref[...] = x_ref[...].T
        wt_ref[...] = wd_ref[...].T

    for half, g in enumerate((gm_ref, go_ref)):
        g[0] = nn(xt_ref[...], dz_ref[half]).astype(BF)
        g[1] = nn(wt_ref[...], act_ref[half]).astype(BF)


def expert_weights(x, wd, act, dz):
    r, d = x.shape
    f = act.shape[2]
    t = tile_of(f) // 2
    hid = pl.BlockSpec((2, r, t), lambda i: (0, 0, i))
    grad = pl.BlockSpec((2, d, t), lambda i: (0, 0, i))
    return call(
        expert_weights_body, [out((2, d, f), BF), out((2, d, f), BF)], x, wd, act, dz, grid=(f // t,),
        in_specs=[whole((r, d)), whole((r, d)), hid, hid], out_specs=[grad, grad],
        scratch=[pltpu.VMEM((d, r), BF), pltpu.VMEM((d, r), BF)], flops=8 * r * d * f,
    )


def merge_hots(t_ref, k, n, slots):
    lane = lax.broadcasted_iota(I32, (n, slots), 1)
    return (lane == t_ref[:, k : k + 1]).astype(F32).astype(BF)


def mixture_backward_body(experts, x_ref, w_ref, h_ref, router_ref, dy_ref, route_ref, ta_ref, tb_ref, ab_ref,
                          dx_ref, dw_ref, dr_ref):
    n, d = x_ref.shape
    slots = ab_ref.shape[1]
    probs, lane = router_probs(h_ref[...], router_ref[...], experts)
    dh = jnp.zeros((n, d), F32)
    dsoft = jnp.zeros(probs.shape, F32)
    for k in range(TOPK):
        part = nn(merge_hots(ta_ref, k, n, slots), ab_ref[0]) + nn(merge_hots(tb_ref, k, n, slots), ab_ref[1])
        dh = dh + part[:, :d]
        dgate = part[:, d : d + 1] + part[:, d + LANES // 2 : d + LANES // 2 + 1]
        dsoft = dsoft + jnp.where(lane == route_ref[:, k : k + 1], dgate, 0.0)
    dlog = (probs * (dsoft - jnp.sum(dsoft * probs, axis=-1, keepdims=True))).astype(BF)
    dr_ref[...] = tn(h_ref[...], dlog)
    dh = dh + nt(dlog, router_ref[...])
    nrm, rr, _ = norm_forward(x_ref[...], w_ref[...])
    dv, dw = norm_backward(nrm, rr, w_ref[...], dh)
    dx_ref[...] = dy_ref[...].astype(F32) + dv
    dw_ref[...] = dw


def mixture_output_body(experts, x_ref, h_ref, router_ref, route_ref, live_ref, ta_ref, tb_ref, ab_ref, y_ref):
    n, d = x_ref.shape
    slots = ab_ref.shape[1]
    probs, lane = router_probs(h_ref[...], router_ref[...], experts)
    total = x_ref[...]
    mixed = jnp.zeros((n, d), F32)
    for k in range(TOPK):
        gate = jnp.sum(jnp.where(lane == route_ref[:, k : k + 1], probs, 0.0), axis=-1, keepdims=True)
        part = nn(merge_hots(ta_ref, k, n, slots), ab_ref[0]) + nn(merge_hots(tb_ref, k, n, slots), ab_ref[1])
        mixed = mixed + gate * part
    y_ref[...] = (live_ref[...] * (total + mixed)).astype(BF)


def flip(axis, bit):
    size = lax.axis_size(axis)
    return [(i, i ^ bit) for i in range(size)]


def bits_of(axis):
    size = lax.axis_size(axis)
    return [1 << b for b in range(size.bit_length() - 1)]


def other_core(v):
    return lax.ppermute(v, "mdl", flip("mdl", 1))


def add16(a, b):
    return (a.astype(F32) + b.astype(F32)).astype(BF)


def halve(v, axis, bit):
    side = (lax.axis_index(axis) // bit) % 2
    n = v.shape[0] // 2
    keep = lax.dynamic_slice_in_dim(v, side * n, n)
    send = lax.dynamic_slice_in_dim(v, (1 - side) * n, n)
    return add16(keep, lax.ppermute(send, axis, flip(axis, bit)))


def double(v, axis, bit):
    side = (lax.axis_index(axis) // bit) % 2
    got = lax.ppermute(v, axis, flip(axis, bit))
    return jnp.where(side == 0, jnp.concatenate([v, got]), jnp.concatenate([got, v]))


def sum_everywhere(v):
    n = v.shape[0] // 2
    bits = bits_of("grp")
    parts = []
    for part, order in ((v[:n], bits), (v[n:], bits[::-1])):
        for bit in order:
            part = halve(part, "grp", bit)
        parts.append(part)
    size = lax.axis_size("exp")
    joined = jnp.concatenate(parts)
    rows = joined.shape[0] // size
    spread = lax.all_to_all(joined.reshape(size, rows, -1), "exp", 0, 0, tiled=True)
    mine = jnp.sum(spread.astype(F32), axis=0).astype(BF)
    joined = lax.all_gather(mine, "exp", axis=0, tiled=True)
    h = joined.shape[0] // 2
    done = []
    for part, order in ((joined[:h], bits), (joined[h:], bits[::-1])):
        for bit in order[::-1]:
            part = double(part, "grp", bit)
        done.append(part)
    return jnp.concatenate(done)


def small_sum(v):
    for axis in ("mdl", "grp", "exp"):
        for bit in bits_of(axis):
            v = v + lax.ppermute(v, axis, flip(axis, bit))
    return v


def reduce_body(n_in, per, n_exp, *refs):
    mine = refs[:n_in]
    other = refs[n_in : 2 * n_in]
    small_ref = refs[2 * n_in]
    out_ref, sum_ref = refs[2 * n_in + 1 : 2 * n_in + 3]
    (acc, got, r1, r2, zr, sm, load_sem, m_send, m_recv, x_send, x_recv, z_send, z_recv, s_send, s_recv) = refs[2 * n_in + 3 :]
    n = n_in * per
    rows = acc.shape[2]
    h, q = rows // 2, rows // 4
    t = q // n_exp
    g = lax.axis_index("grp")
    z = lax.axis_index("exp")
    core = lax.axis_index("mdl")
    bx, by = g % 2, g // 2
    flat = {"x": g + 1 - 2 * bx, "y": g + 2 - 4 * by}
    order = (("x", "y"), ("y", "x"))
    bits = ((bx, by), (by, bx))

    barrier = pltpu.get_barrier_semaphore()
    others = [{"mdl": 1 - core}, {"grp": flat["x"]}, {"grp": flat["y"]}]
    others += [{"exp": (z + o) % n_exp} for o in range(1, n_exp)]
    for dev in others:
        pl.semaphore_signal(barrier, inc=1, device_id=dev, device_id_type=MESH)
    pl.semaphore_wait(barrier, len(others))

    def load(c):
        i, p = c // per, c % per
        return pltpu.make_async_copy(mine[i].at[p], acc.at[c], load_sem.at[c])

    def swap(c):
        i, p = c // per, c % per
        return pltpu.make_async_remote_copy(other[i].at[p], got.at[c], m_send.at[c], m_recv.at[c],
                                            device_id={"mdl": 1 - core}, device_id_type=MESH)

    for c in range(n):
        swap(c).start()
        load(c).start()

    def swap_at(c):
        return pltpu.make_async_remote_copy(other[0].at[0], got.at[c], m_send.at[c], m_recv.at[c],
                                            device_id={"mdl": 1 - core}, device_id_type=MESH)

    def load_at(c):
        return pltpu.make_async_copy(mine[0].at[0], acc.at[c], load_sem.at[c])

    def over(u, leg, src, dst, slot, c):
        return pltpu.make_async_remote_copy(src, dst, x_send.at[slot, u, c], x_recv.at[slot, u, c],
                                            device_id={"grp": flat[order[u][leg]]}, device_id_type=MESH)

    def first(u, c):
        return over(u, 0, acc.at[c, u, pl.ds(pl.multiple_of((1 - bits[u][0]) * h, h), h)], r1.at[c, u], 0, c)

    def second(u, c):
        return over(u, 1, r1.at[c, u, pl.ds(pl.multiple_of((1 - bits[u][1]) * q, q), q)], r2.at[c, u], 1, c)

    def along(u, c, o):
        return pltpu.make_async_remote_copy(
            r2.at[c, u, pl.ds(pl.multiple_of(((z + o) % n_exp) * t, t), t)], zr.at[c, u, o - 1],
            z_send.at[0, u, o - 1, c], z_recv.at[0, u, o - 1, c],
            device_id={"exp": (z + o) % n_exp}, device_id_type=MESH)

    def place(u):
        return bits[u][0] * h + bits[u][1] * q

    def back(u, c, o):
        here = out_ref.at[c, u, pl.ds(pl.multiple_of(place(u) + z * t, t), t)]
        return pltpu.make_async_remote_copy(here, here, z_send.at[1, u, o - 1, c], z_recv.at[1, u, o - 1, c],
                                            device_id={"exp": (z + o) % n_exp}, device_id_type=MESH)

    def third(u, c):
        here = out_ref.at[c, u, pl.ds(pl.multiple_of(place(u), q), q)]
        return over(u, 1, here, here, 2, c)

    def fourth(u, c):
        here = out_ref.at[c, u, pl.ds(pl.multiple_of(bits[u][0] * h, h), h)]
        return over(u, 0, here, here, 3, c)

    def plus(a, b):
        return (a.astype(F32) + b.astype(F32)).astype(BF)

    def s1(c):
        load_at(c).wait()
        swap_at(c).wait_recv()
        for u in range(2):
            acc[c, u] = plus(acc[c, u], got[c, u])
            first(u, c).start()

    def s2(c):
        for u in range(2):
            first(u, c).wait_recv()
            keep = acc[c, u, pl.ds(pl.multiple_of(bits[u][0] * h, h), h)]
            r1[c, u] = plus(keep, r1[c, u])
            second(u, c).start()

    def s3(c):
        for u in range(2):
            second(u, c).wait_recv()
            keep = r1[c, u, pl.ds(pl.multiple_of(bits[u][1] * q, q), q)]
            r2[c, u] = plus(keep, r2[c, u])
            for o in range(1, n_exp):
                along(u, c, o).start()

    def s4(c):
        for u in range(2):
            total = r2[c, u, pl.ds(pl.multiple_of(z * t, t), t)].astype(F32)
            for o in range(1, n_exp):
                along(u, c, o).wait_recv()
                total = total + zr[c, u, o - 1].astype(F32)
            out_ref[c, u, pl.ds(pl.multiple_of(place(u) + z * t, t), t)] = total.astype(BF)
            for o in range(1, n_exp):
                back(u, c, o).start()

    def s5(c):
        for u in range(2):
            for o in range(1, n_exp):
                back(u, c, o).wait_recv()
            third(u, c).start()

    def s6(c):
        for u in range(2):
            third(u, c).wait_recv()
            fourth(u, c).start()

    def s7(c):
        for u in range(2):
            fourth(u, c).wait_recv()
        swap_at(c).wait_send()
        for u in range(2):
            for make in (first, second, third, fourth):
                make(u, c).wait_send()
            for o in range(1, n_exp):
                along(u, c, o).wait_send()
                back(u, c, o).wait_send()

    steps = (s1, s2, s3, s4, s5, s6, s7)

    def wave(tau, _):
        for s, step in enumerate(steps):
            c = tau - s

            @pl.when((c >= 0) & (c < n))
            def _(step=step, c=c):
                step(c)

        return 0

    lax.fori_loop(0, n + len(steps) - 1, wave, 0)

    sm[0] = small_ref[...]
    legs = [({"mdl": 1 - core}), ({"grp": flat["x"]}), ({"grp": flat["y"]})]
    for i, dev in enumerate(legs):
        cp = pltpu.make_async_remote_copy(sm.at[2 * i], sm.at[2 * i + 1], s_send.at[i], s_recv.at[i], device_id=dev, device_id_type=MESH)
        cp.start()
        cp.wait()
        sm[2 * i + 2] = sm[2 * i] + sm[2 * i + 1]
    base = 2 * len(legs) + 1
    sm[pl.ds(base + z, 1)] = sm[pl.ds(base - 1, 1)]
    cps = []
    for o in range(1, n_exp):
        cps.append(pltpu.make_async_remote_copy(sm.at[base - 1], sm.at[base + z], s_send.at[len(legs) + o - 1], s_recv.at[len(legs) + o - 1],
                                                device_id={"exp": (z + o) % n_exp}, device_id_type=MESH))
        cps[-1].start()
    for cp in cps:
        cp.wait()
    total = sm[base]
    for k in range(1, n_exp):
        total = total + sm[base + k]
    sum_ref[...] = total


def reduce_all(mine, other, small, n_exp):
    per, _, rows, c = mine[0].shape
    n = len(mine) * per
    h, q = rows // 2, rows // 4
    t = q // n_exp
    D = pltpu.SemaphoreType.DMA
    any_ = pl.BlockSpec(memory_space=pl.ANY)
    vm = pl.BlockSpec(memory_space=pltpu.VMEM)
    return pl.pallas_call(
        functools.partial(reduce_body, len(mine), per, n_exp),
        in_specs=[any_] * (2 * len(mine)) + [vm],
        out_specs=[vm, vm],
        out_shape=[jax.ShapeDtypeStruct((n, 2, rows, c), BF), jax.ShapeDtypeStruct(small.shape, F32)],
        scratch_shapes=[
            pltpu.VMEM((n, 2, rows, c), BF), pltpu.VMEM((n, 2, rows, c), BF), pltpu.VMEM((n, 2, h, c), BF),
            pltpu.VMEM((n, 2, q, c), BF), pltpu.VMEM((n, 2, n_exp - 1, t, c), BF), pltpu.VMEM((7 + n_exp,) + small.shape, F32),
            D((n,)), D((n,)), D((n,)), D((4, 2, n)), D((4, 2, n)), D((2, 2, n_exp - 1, n)), D((2, 2, n_exp - 1, n)),
            D((3 + n_exp,)), D((3 + n_exp,)),
        ],
        compiler_params=pltpu.CompilerParams(collective_id=0, has_side_effects=True, vmem_limit_bytes=VMEM_BYTES),
    )(*mine, *other, small)


def expert_exchange_body(experts, half, h4_ref, ta_ref, tb_ref, dyin_ref, router_ref, mine_ref, im, io, tm, to,
                         ret_ref, eout_ref, gm_ref, go_ref,
                         h_oth, part, xo, x, wi, wo, act, dz, wd, acc, dxa, rsend, gscr, xt, wt,
                         w_sem, swap_sem, x_send, x_recv, r_send, r_recv, f_send, f_recv, g_sem):
    n, d = h4_ref.shape
    f = im.shape[1]
    t = 256 if f % 256 == 0 else tile_of(f)
    z = lax.axis_index("exp")
    core = lax.axis_index("mdl")
    partner = {"mdl": 1 - core}
    size = experts
    near_first = [1, 3, 2]

    def there(j):
        b0, b1 = z % 2, z // 2
        if j & 1:
            b0 = 1 - b0
        if j & 2:
            b1 = 1 - b1
        return b0 + 2 * b1

    loads = [pltpu.make_async_copy(src, dst, w_sem.at[k]) for k, (src, dst) in enumerate(
        ((im, wi.at[0]), (io, wi.at[1]), (tm, wo.at[0]), (to, wo.at[1])))]
    for cp in loads:
        cp.start()
    barrier = pltpu.get_barrier_semaphore()
    for dev in [partner] + [{"exp": there(j)} for j in range(1, size)]:
        pl.semaphore_signal(barrier, inc=1, device_id=dev, device_id_type=MESH)
    pl.semaphore_wait(barrier, size)
    swap = pltpu.make_async_remote_copy(h4_ref, h_oth, swap_sem.at[0], swap_sem.at[1], device_id=partner, device_id_type=MESH)
    swap.start()

    def hot(t_ref, e):
        slot = lax.broadcasted_iota(I32, (half, n), 0) + e * half
        return ((slot == t_ref[0:1, :]) | (slot == t_ref[1:2, :])).astype(F32).astype(BF)

    def rows(j):
        return slice(j * half, (j + 1) * half)

    def place(e):
        return pl.ds(pl.multiple_of(e * half, half), half)

    for j in near_first + [0]:
        part[rows(j), :] = nn(hot(ta_ref, there(j)), h4_ref[...])
    swap.wait_recv()
    sends = {}
    for j in near_first + [0]:
        block = (part[rows(j), :] + nn(hot(tb_ref, there(j)), h_oth[...])).astype(BF)
        if j == 0:
            x[rows(0), :] = block
        else:
            xo[rows(j), :] = block
            sends[j] = pltpu.make_async_remote_copy(xo.at[rows(j)], x.at[rows(j)], x_send.at[j], x_recv.at[j],
                                                    device_id={"exp": there(j)}, device_id_type=MESH)
            sends[j].start()

    returns, forwards = {}, {}

    def forward(j):
        here = ret_ref.at[0, place(there(j))]
        forwards[j] = pltpu.make_async_remote_copy(here, ret_ref.at[1, place(there(j))], f_send.at[j], f_recv.at[j],
                                                   device_id=partner, device_id_type=MESH)
        forwards[j].start()

    def run(blocks):
        r0, r1 = blocks[0] * half, (blocks[-1] + 1) * half
        m = r1 - r0
        for j in blocks:
            probs, _ = router_probs(x[rows(j), :], router_ref[...], experts)
            gate = jnp.sum(probs * mine_ref[...], axis=-1, keepdims=True)
            wd[rows(j), :] = (gate * dyin_ref[place(there(j)), :].astype(F32)).astype(BF)
        acc[0:m, :] = jnp.zeros((m, d), F32)
        dxa[0:m, :] = jnp.zeros((m, d), F32)

        def tile(i, _):
            at = pl.ds(pl.multiple_of(i * t, t), t)
            for side in range(2):
                a, s = gelu_parts(nn(x[r0:r1, :], wi[side, :, at]))
                a = a.astype(BF)
                act[side, r0:r1, at] = a
                acc[0:m, :] += nn(a, wo[side, at, :])
                g = (nt(wd[r0:r1, :], wo[side, at, :]) * s).astype(BF)
                dz[side, r0:r1, at] = g
                dxa[0:m, :] += nt(g, wi[side, :, at])
            return 0

        lax.fori_loop(0, f // t, tile, 0)
        for b, j in enumerate(blocks):
            here = slice(b * half, (b + 1) * half)
            e_rows = acc[here, :].astype(BF)
            eout_ref[place(there(j)), :] = e_rows
            dgate = jnp.sum(dyin_ref[place(there(j)), :].astype(F32) * e_rows.astype(F32), axis=-1, keepdims=True)
            high = dgate.astype(BF).astype(F32)
            lane = lax.broadcasted_iota(I32, (half, LANES), 1)
            extra = jnp.where(lane < LANES // 2, high, dgate - high).astype(BF)
            if j == 0:
                ret_ref[0, place(z), 0:d] = dxa[here, :].astype(BF)
                ret_ref[0, place(z), d:] = extra
                forward(0)
            else:
                rsend[rows(j), 0:d] = dxa[here, :].astype(BF)
                rsend[rows(j), d:] = extra
                returns[j] = pltpu.make_async_remote_copy(rsend.at[rows(j)], ret_ref.at[0, place(z)], r_send.at[j], r_recv.at[j],
                                                          device_id={"exp": there(j)}, device_id_type=MESH)
                returns[j].start()

    for cp in loads:
        cp.wait()
    sends[1].wait_recv()
    run([0, 1])
    for j in near_first[1:]:
        sends[j].wait_recv()
        run([j])

    xt[...] = x[...].T
    wt[...] = wd[...].T

    def stored(i, side, ref):
        at = pl.ds(pl.multiple_of(i * t, t), t)
        return pltpu.make_async_copy(gscr.at[side, :, :, at], ref.at[:, :, at], g_sem.at[side, i])

    def weight_tile(i, _):
        at = pl.ds(pl.multiple_of(i * t, t), t)
        for side, ref in enumerate((gm_ref, go_ref)):
            gscr[side, 0, :, at] = nn(xt[...], dz[side, :, at]).astype(BF)
            gscr[side, 1, :, at] = nn(wt[...], act[side, :, at]).astype(BF)
            stored(i, side, ref).start()
        return 0

    lax.fori_loop(0, f // t, weight_tile, 0)

    def recv_return(j):
        return pltpu.make_async_remote_copy(rsend.at[rows(j)], ret_ref.at[0, place(there(j))], r_send.at[j], r_recv.at[j],
                                            device_id={"exp": there(j)}, device_id_type=MESH)

    for j in near_first:
        recv_return(j).wait_recv()
        forward(j)

    def drain(i, _):
        for side, ref in enumerate((gm_ref, go_ref)):
            stored(i, side, ref).wait()
        return 0

    lax.fori_loop(0, f // t, drain, 0)
    swap.wait_send()
    for j in range(size):
        if j:
            sends[j].wait_send()
            returns[j].wait_send()
        forwards[j].wait()


def expert_exchange(h4, ta, tb, dy_in, router, mine, im, io, tm, to, experts, half):
    n, d = h4.shape
    f = im.shape[1]
    s = experts * half
    tiles = f // (256 if f % 256 == 0 else tile_of(f))
    D, V = pltpu.SemaphoreType.DMA, pltpu.VMEM
    any_ = pl.BlockSpec(memory_space=pl.ANY)
    vm = pl.BlockSpec(memory_space=pltpu.VMEM)
    return pl.pallas_call(
        functools.partial(expert_exchange_body, experts, half),
        in_specs=[vm] * 6 + [any_] * 4,
        out_specs=[vm, vm, any_, any_],
        out_shape=[out((2, s, d + LANES), BF), out((s, d), BF), out((2, d, f), BF), out((2, d, f), BF)],
        scratch_shapes=[
            V((n, d), BF), V((s, d), F32), V((s, d), BF), V((s, d), BF), V((2, d, f), BF), V((2, f, d), BF),
            V((2, s, f), BF), V((2, s, f), BF), V((s, d), BF), V((2 * half, d), F32), V((2 * half, d), F32),
            V((s, d + LANES), BF), V((2, 2, d, f), BF), V((d, s), BF), V((d, s), BF),
            D((4,)), D((2,)), D((experts,)), D((experts,)), D((experts,)), D((experts,)), D((experts,)), D((experts,)),
            D((2, tiles)),
        ],
        compiler_params=pltpu.CompilerParams(collective_id=1, has_side_effects=True, vmem_limit_bytes=VMEM_BYTES),
        cost_estimate=pl.CostEstimate(flops=24 * s * d * f, bytes_accessed=20 * d * f, transcendentals=0),
    )(h4, ta, tb, dy_in, router, mine, im, io, tm, to)


def on_device(images, counts, routes, priority, gain_one, qkv_one, out_one, gain_two, fc_in, fc_out, gain_three,
              qkv_two, out_two, gain_four, router, expert_in, expert_out, cotangent):
    n_slot, length, d = images.shape
    experts = router.shape[1]
    n_mdl = lax.axis_size("mdl")
    capacity = (25 * L * TOPK + 8 * experts - 1) // (8 * experts)
    half = -(-(-(-capacity // n_mdl)) // 16) * 16
    slots = experts * half
    own_img = n_slot // n_mdl
    f = fc_in.shape[1]
    rows = own_img * LP
    core = lax.axis_index("mdl")

    def own(v, axis=0):
        return lax.dynamic_slice_in_dim(v, core * rows, rows, axis)

    def oth(v, axis=0):
        return lax.dynamic_slice_in_dim(v, (1 - core) * rows, rows, axis)

    def padded(v):
        return jnp.pad(v, ((0, 0), (0, LP - length), (0, 0))).reshape(n_slot * LP, -1)

    qm1, om1, im, tm, qm2, om2, em, fm = qkv_one, out_one, fc_in, fc_out, qkv_two, out_two, expert_in[0], expert_out[0]
    qo1, oo1, io, to, qo2, oo2, eo, fo = (other_core(w) for w in (qm1, om1, im, tm, qm2, om2, em, fm))
    g1, g2, g3, g4 = (g.reshape(1, d) for g in (gain_one, gain_two, gain_three, gain_four))
    router_wide = jnp.pad(router, ((0, 0), (0, LANES - experts)))
    mine = (jnp.arange(LANES, dtype=I32) == lax.axis_index("exp")).astype(F32)[None]

    img_live = (jnp.arange(n_slot, dtype=I32) < counts[0, 0]).astype(I32)
    live = jnp.pad(jnp.broadcast_to(img_live[:, None], (n_slot, length)), ((0, 0), (0, LP - length))).reshape(-1)
    x0 = own(padded(images))
    dy = padded(cotangent * img_live[:, None, None].astype(BF))
    route = padded(routes)
    prior = padded(priority.reshape(n_slot, length, 1))
    cols = jnp.concatenate([route, prior, live[:, None]], axis=1)
    slot_cols, slot_rows = call(
        functools.partial(routing_body, experts, capacity, half),
        [out((n_slot * LP, TOPK), I32), out((TOPK, n_slot * LP), I32)], cols, cols.T,
    )
    mine_rows = slot_rows - core * slots
    own_tokens_here = own(slot_cols) - core * slots
    own_tokens_there = own(slot_cols) - (1 - core) * slots
    own_tokens_there = jnp.where(own_tokens_there < slots, own_tokens_there, -1)
    peers = lax.axis_size("exp")

    def exchange(v):
        shaped = v.reshape(peers, v.shape[0] // peers, v.shape[1])
        return lax.all_to_all(shaped, "exp", 0, 0, tiled=True).reshape(v.shape)

    dy_out = dispatch(mine_rows[:, :rows], mine_rows[:, rows:], dy[:rows], dy[rows:], slots)
    dy_in = exchange(dy_out)

    x1, *kept1 = attention_forward(x0, g1, qm1, qo1, om1, oo1)
    x2, h2, act2, slope2 = mlp_forward(x1, g2, im, io, tm, to)
    x3, *kept3, h4 = attention_forward(x2, g3, qm2, qo2, om2, oo2, g4)

    grouped = peers == 4 and experts == 4 and n_mdl == 2
    if grouped:
        ret, eout, ge_mine, ge_other = expert_exchange(
            h4, own(mine_rows, 1), oth(mine_rows, 1), dy_in, router_wide, mine, em, eo, fm, fo, experts, half)
    else:
        h4_out = dispatch(own(mine_rows, 1), oth(mine_rows, 1), h4, other_core(h4), slots)
        h4_in = exchange(h4_out)
        eout, ret, eact, edz, ewd = expert_forward_backward(h4_in, dy_in, router_wide, mine, em, eo, fm, fo, experts)
        ret = exchange(ret)
        ret = jnp.stack([ret, other_core(ret)])
        ge_mine, ge_other = expert_weights(h4_in, ewd, eact, edz)
    eout = exchange(eout)

    own_route = own(route)
    dx3, dg4, dr = call(
        functools.partial(mixture_backward_body, experts),
        [out((rows, d), F32), out((1, d), F32), out((d, LANES), F32)],
        x3, g4, h4, router_wide, own(dy), own_route, own_tokens_here, own_tokens_there, ret,
        flops=8 * rows * slots * d,
    )
    expert_sum = lax.psum_scatter(
        add16(ge_mine, other_core(ge_other)), "grp", scatter_dimension=1, tiled=True)

    dx2, dg3, a2_mine, a2_other = attention_backward(dx3, x2, g3, kept3, qm2, qo2, om2, oo2)
    c = qkv_one.shape[2]
    dx1, dg2, gim, gio, gtm, gto = mlp_backward(dx2, x1, g2, h2, act2, slope2, im, io, tm, to, c)
    dx0, dg1, a1_mine, a1_other = attention_backward(dx1, x0, g1, kept1, qm1, qo1, om1, oo1)
    eout, dx1 = lax.optimization_barrier((eout, dx1))
    [output] = call(
        functools.partial(mixture_output_body, experts), [out((rows, d), BF)],
        x3, h4, router_wide, own_route, own(live).astype(F32)[:, None], own_tokens_here, own_tokens_there, jnp.stack([eout, other_core(eout)]),
        flops=8 * rows * slots * d,
    )
    small = jnp.concatenate([dg1, dg2, dg3, dg4, dr.T[:experts]], axis=0)
    mines, others = (a2_mine, gim, gtm, a1_mine), (a2_other, gio, gto, a1_other)

    per = 2
    unit = 4 * d // (2 * per)
    if lax.axis_size("grp") == 4 and n_mdl == 2 and unit % (64 * peers) == 0 and f * 2 == 4 * d:
        split = [[v.reshape(per, 2, unit, c) for v in side] for side in (mines, others)]
        totals, small = reduce_all(*split, small, peers)
        sums = totals.reshape(len(mines), 4 * d, c)
    else:
        flat = [[v.reshape(4 * d, c) for v in side] for side in (mines, others)]
        sums = [sum_everywhere(add16(a, other_core(b))) for a, b in zip(*flat)]
        small = small_sum(small)

    def unpack(total):
        qkv = total[: 3 * d].reshape(3, d, c).astype(F32)
        return qkv, panels(total[3 * d :].reshape(d // c, c, c))

    def panels(v):
        return jnp.concatenate([v[i] for i in range(v.shape[0])], axis=1).astype(F32)

    def both(v):
        there = other_core(v)
        joined = jnp.where(core == 0, jnp.concatenate([v, there]), jnp.concatenate([there, v]))
        return joined.reshape(n_slot, LP, d)[:, :length]

    grad_qkv_two, grad_out_two = unpack(sums[0])
    grad_fc_in = panels(sums[1].reshape(f // c, d, c))
    grad_fc_out = panels(sums[2].reshape(d // c, f, c))
    grad_qkv_one, grad_out_one = unpack(sums[3])
    return (
        both(output), both(dx0.astype(BF)),
        small[0], grad_qkv_one, grad_out_one, small[1], grad_fc_in, grad_fc_out,
        small[2], grad_qkv_two, grad_out_two, small[3], small[4:].T,
        expert_sum[0].astype(F32)[None], expert_sum[1].astype(F32).T[None],
    )


def solution(mesh):
    token = P(("grp", "exp"), None, None)
    column, line = P(None, None, "mdl"), P("mdl", None)
    return jax.shard_map(
        on_device,
        mesh=mesh,
        in_specs=(token, P("grp", "exp"), token, P(("grp", "exp"), None), P(), column, line, P(), P(None, "mdl"), line,
                  P(), column, line, P(), P(), P("exp", None, "mdl"), P("exp", "mdl", None), token),
        out_specs=(token, token, P(), column, line, P(), P(None, "mdl"), line, P(), column, line, P(), P(),
                   P("exp", "grp", "mdl"), P("exp", "mdl", "grp")),
        check_vma=False,
    )
```

```python
import functools
import math

import jax
import jax.numpy as jnp
from jax import lax
from jax.experimental import pallas as pl
from jax.experimental.pallas import tpu as pltpu
from jax.sharding import PartitionSpec as P

HDIM = 64
L = 197
TOPK = 2
LP = (L + 15) // 16 * 16
LANES = 128
LQ = (L + LANES - 1) // LANES * LANES
BF = jnp.bfloat16
F32 = jnp.float32
I32 = jnp.int32

EPSILON = 1e-06
ROOT_HALF = 0.7071067811865476
DENSITY_FACTOR = 0.3989422804014327
VMEM_BYTES = 60 * 1024 * 1024
MESH = pl.DeviceIdType.MESH


def nn(a, b):
    return lax.dot_general(a, b, (((1,), (0,)), ((), ())), preferred_element_type=F32)


def nt(a, b):
    return lax.dot_general(a, b, (((1,), (1,)), ((), ())), preferred_element_type=F32)


def tn(a, b):
    return lax.dot_general(a, b, (((0,), (0,)), ((), ())), preferred_element_type=F32)


def norm_forward(v, w):
    c = v - jnp.mean(v, axis=-1, keepdims=True)
    r = lax.rsqrt(jnp.mean(c * c, axis=-1, keepdims=True) + EPSILON)
    n = c * r
    return n, r, (n * w).astype(BF)


def norm_backward(n, r, w, dh):
    dn = dh * w
    dw = jnp.sum(dh * n, axis=0, keepdims=True)
    dv = r * (dn - jnp.mean(dn, axis=-1, keepdims=True) - n * jnp.mean(dn * n, axis=-1, keepdims=True))
    return dv, dw


def whole(shape):
    return pl.BlockSpec(shape, lambda *i: (0,) * len(shape))


def call(body, out_shape, *args, grid=(), in_specs=None, out_specs=None, scratch=(), flops=0):
    if in_specs is None:
        in_specs = [whole(a.shape) for a in args]
    if out_specs is None:
        out_specs = [whole(o.shape) for o in out_shape]
    moved = sum(math.prod(a.shape) * a.dtype.itemsize for a in args)
    moved += sum(math.prod(o.shape) * jnp.dtype(o.dtype).itemsize for o in out_shape)
    return pl.pallas_call(
        body,
        grid=grid,
        in_specs=in_specs,
        out_specs=out_specs,
        out_shape=out_shape,
        scratch_shapes=list(scratch),
        cost_estimate=pl.CostEstimate(flops=int(flops), bytes_accessed=int(moved), transcendentals=0),
        compiler_params=pltpu.CompilerParams(vmem_limit_bytes=VMEM_BYTES),
    )(*args)


def out(shape, dtype):
    return jax.ShapeDtypeStruct(shape, dtype)


def head_mask(dtype):
    lane = lax.broadcasted_iota(I32, (LP, LANES), 1)
    return (lane < HDIM).astype(dtype)


class Exchange:
    def __init__(self, size, half, src, dst, send, recv, local):
        self.z = lax.axis_index("exp")
        self.size, self.half, self.src, self.dst = size, half, src, dst
        self.send, self.recv, self.local = send, recv, local

    def signal(self):
        barrier = pltpu.get_barrier_semaphore()
        for o in range(1, self.size):
            pl.semaphore_signal(barrier, inc=1, device_id={"exp": (self.z + o) % self.size}, device_id_type=MESH)

    def at(self, e):
        return pl.ds(pl.multiple_of(e * self.half, self.half), self.half)

    def copies(self):
        for o in range(1, self.size):
            to = (self.z + o) % self.size
            yield pltpu.make_async_remote_copy(self.src.at[self.at(to)], self.dst.at[self.at(self.z)], self.send.at[o - 1],
                                               self.recv.at[o - 1], device_id={"exp": to}, device_id_type=MESH)

    def own(self):
        return pltpu.make_async_copy(self.src.at[self.at(self.z)], self.dst.at[self.at(self.z)], self.local)

    def start(self):
        self.own().start()
        for cp in self.copies():
            cp.start()

    def arrived(self):
        self.own().wait()
        for o in range(1, self.size):
            come = (self.z + self.size - o) % self.size
            pltpu.make_async_remote_copy(self.src.at[self.at(come)], self.dst.at[self.at(come)], self.send.at[o - 1],
                                         self.recv.at[o - 1], device_id={"exp": come}, device_id_type=MESH).wait_recv()

    def left(self):
        for cp in self.copies():
            cp.wait_send()


def attention_forward_body(n_img, g_at, tail, size, half, *refs):
    refs = list(refs)
    x_ref, g_ref, qm, qo, om, oo = refs[:6]
    del refs[:6]
    src = refs.pop(0) if size else None
    y_ref, h_ref, qkv_ref, p_ref, o_ref = refs[:5]
    del refs[:5]
    h4_ref = refs.pop(0) if tail is not None else None
    if size:
        dst, send, recv, local = refs
        carried = Exchange(size, half, src, dst, send, recv, local)
        carried.signal()
    d = x_ref.shape[1]
    c = qm.shape[2]
    pairs = d // LANES
    _, _, h = norm_forward(x_ref[...].astype(F32), g_ref[g_at : g_at + 1, :])
    h_ref[...] = h
    if size:
        pl.semaphore_wait(pltpu.get_barrier_semaphore(), size - 1)
        carried.start()
    for k in range(3):
        for side, w in ((0, qm), (1, qo)):
            at = (2 * k + side) * c
            qkv_ref[:, at : at + c] = nn(h_ref[...], w[k]).astype(BF)
    mask = head_mask(BF)
    key_ok = lax.broadcasted_iota(I32, (LP, LP), 1) < L

    def one(i, _):
        rows = pl.ds(pl.multiple_of((i // pairs) * LP, LP), LP)
        col = (i % pairs) * LANES
        q = qkv_ref[rows, pl.ds(pl.multiple_of(col, LANES), LANES)]
        ke = qkv_ref[rows, pl.ds(pl.multiple_of(d + col, LANES), LANES)]
        u = qkv_ref[rows, pl.ds(pl.multiple_of(2 * d + col, LANES), LANES)]
        o = jnp.zeros((LP, LANES), F32)
        for hh in range(2):
            mk = mask if hh == 0 else 1 - mask
            s = nt(q * mk, ke) * HDIM ** (-0.5)
            s = jnp.where(key_ok, s, -1e30)
            e = jnp.exp(s - jnp.max(s, axis=-1, keepdims=True))
            p = (e / jnp.sum(e, axis=-1, keepdims=True)).astype(BF)
            p_ref[2 * i + hh] = p
            o = o + nn(p, u * mk)
        o_ref[rows, pl.ds(pl.multiple_of(col, LANES), LANES)] = o.astype(BF)
        return 0

    lax.fori_loop(0, n_img * pairs, one, 0, unroll=2)
    y = x_ref[...].astype(F32) + nn(o_ref[:, :c], om[...]) + nn(o_ref[:, c:], oo[...])
    y_ref[...] = y
    if tail is not None:
        _, _, h4 = norm_forward(y, g_ref[tail : tail + 1, :])
        h4_ref[...] = h4
    if size:
        carried.arrived()
        carried.left()


def attention_forward(x, gains, g_at, qm, qo, om, oo, tail=None, carry=None):
    r, d = x.shape
    n_img = r // LP
    heads = d // HDIM
    shapes = [out((r, d), F32), out((r, d), BF), out((r, 3 * d), BF), out((n_img * heads, LP, LP), BF), out((r, d), BF)]
    args = [x, gains, qm, qo, om, oo]
    flops = 2 * r * d * d * 4 + 4 * n_img * heads * LP * LP * LANES
    if tail is not None:
        shapes.append(out((r, d), BF))
    if carry is None:
        return call(functools.partial(attention_forward_body, n_img, g_at, tail, 0, 0), shapes, *args, flops=flops)
    src, size, half = carry
    any_ = pl.BlockSpec(memory_space=pl.ANY)
    vm = pl.BlockSpec(memory_space=pltpu.VMEM)
    D = pltpu.SemaphoreType.DMA
    return pl.pallas_call(
        functools.partial(attention_forward_body, n_img, g_at, tail, size, half),
        in_specs=[vm] * 6 + [any_], out_specs=[vm] * len(shapes) + [any_],
        out_shape=shapes + [out(src.shape, src.dtype)],
        scratch_shapes=[D((size - 1,)), D((size - 1,)), D],
        compiler_params=pltpu.CompilerParams(collective_id=2, has_side_effects=True, vmem_limit_bytes=VMEM_BYTES),
        cost_estimate=pl.CostEstimate(flops=flops, bytes_accessed=16 * r * d * 8, transcendentals=0),
    )(*args, src)


def attention_backward_core(n_img, dy, x_ref, gain, h_ref, qkv_ref, p_ref, o_ref, qm, qo, om, oo,
                            gm_ref, go_ref, do_ref, dqkv_ref, tr_ref):
    d = x_ref.shape[1]
    c = qm.shape[2]
    pairs = d // LANES
    da = dy().astype(BF)
    tr_ref[...] = o_ref[...].T
    for side, (w, g) in enumerate(((om, gm_ref), (oo, go_ref))):
        gw = nn(tr_ref[side * c : (side + 1) * c, :], da).astype(BF)
        for part in range(d // c):
            g[3 * d + part * c : 3 * d + (part + 1) * c, :] = gw[:, part * c : (part + 1) * c]
        do_ref[:, side * c : (side + 1) * c] = nt(da, w[...]).astype(BF)
    mask = head_mask(BF)

    def one(i, _):
        rows = pl.ds(pl.multiple_of((i // pairs) * LP, LP), LP)
        col = (i % pairs) * LANES
        cq = pl.ds(pl.multiple_of(col, LANES), LANES)
        ck = pl.ds(pl.multiple_of(d + col, LANES), LANES)
        cu = pl.ds(pl.multiple_of(2 * d + col, LANES), LANES)
        q, ke, u, do = qkv_ref[rows, cq], qkv_ref[rows, ck], qkv_ref[rows, cu], do_ref[rows, cq]
        dq = jnp.zeros((LP, LANES), F32)
        dk = jnp.zeros((LP, LANES), F32)
        du = jnp.zeros((LP, LANES), F32)
        for hh in range(2):
            mk = mask if hh == 0 else 1 - mask
            p = p_ref[2 * i + hh]
            du = du + tn(p, do * mk)
            dp = nt(do * mk, u)
            pf = p.astype(F32)
            ds = (pf * (dp - jnp.sum(dp * pf, axis=-1, keepdims=True))).astype(BF)
            dq = dq + nn(ds, ke * mk)
            dk = dk + tn(ds, q * mk)
        dqkv_ref[rows, cq] = (dq * HDIM ** (-0.5)).astype(BF)
        dqkv_ref[rows, ck] = (dk * HDIM ** (-0.5)).astype(BF)
        dqkv_ref[rows, cu] = du.astype(BF)
        return 0

    lax.fori_loop(0, n_img * pairs, one, 0, unroll=2)
    tr_ref[...] = h_ref[...].T
    dh = jnp.zeros(x_ref.shape, F32)
    for k in range(3):
        for side, (w, g) in enumerate(((qm, gm_ref), (qo, go_ref))):
            at = (2 * k + side) * c
            g[k * d : (k + 1) * d, :] = nn(tr_ref[...], dqkv_ref[:, at : at + c]).astype(BF)
            dh = dh + nt(dqkv_ref[:, at : at + c], w[k])
    n, rr, _ = norm_forward(x_ref[...].astype(F32), gain)
    dv, dw = norm_backward(n, rr, gain, dh)
    return dy() + dv, dw


def attention_backward_body(n_img, g_at, dy_ref, x_ref, g_ref, h_ref, qkv_ref, p_ref, o_ref, qm, qo, om, oo,
                            dx_ref, dw_ref, gm_ref, go_ref, do_ref, dqkv_ref, tr_ref):
    dx, dw = attention_backward_core(
        n_img, lambda: dy_ref[...], x_ref, g_ref[g_at : g_at + 1, :], h_ref, qkv_ref, p_ref, o_ref, qm, qo, om, oo,
        gm_ref, go_ref, do_ref, dqkv_ref, tr_ref)
    for i in range(n_img):
        dx_ref[i] = dx[i * LP : i * LP + L].astype(BF)
    dw_ref[...] = dw


def attention_backward_scratch(r, d):
    return [pltpu.VMEM((r, d), BF), pltpu.VMEM((r, 3 * d), BF), pltpu.VMEM((d, r), BF)]


def attention_backward(dy, x, gains, g_at, kept, qm, qo, om, oo):
    r, d = x.shape
    c = qm.shape[2]
    n_img = r // LP
    heads = d // HDIM
    return call(
        functools.partial(attention_backward_body, n_img, g_at),
        [out((n_img, L, d), BF), out((1, d), F32), out((3 * d + d, c), BF), out((3 * d + d, c), BF)],
        dy, x, gains, *kept, qm, qo, om, oo,
        scratch=attention_backward_scratch(r, d),
        flops=4 * r * d * d * 4 + 8 * n_img * heads * LP * LP * LANES,
    )


def gelu_parts(z):
    phi = 0.5 * (1.0 + lax.erf(z * ROOT_HALF))
    return z * phi, phi + z * jnp.exp(-0.5 * z * z) * DENSITY_FACTOR


def tile_of(f):
    for t in (512, 256, 128):
        if f % t == 0:
            return t
    return f


def mlp_forward_body(g_at, x_ref, g_ref, im, io, tm, to, y_ref, h_ref, act_ref, slope_ref, acc_ref):
    step = pl.program_id(0)

    @pl.when(step == 0)
    def _():
        x = x_ref[...]
        _, _, h = norm_forward(x, g_ref[g_at : g_at + 1, :])
        h_ref[...] = h
        acc_ref[...] = x

    for half, (wi, wo) in enumerate(((im, tm), (io, to))):
        a, s = gelu_parts(nn(h_ref[...], wi[...]))
        act = a.astype(BF)
        act_ref[half] = act
        slope_ref[half] = s.astype(BF)
        acc_ref[...] += nn(act, wo[...])

    @pl.when(step == pl.num_programs(0) - 1)
    def _():
        y_ref[...] = acc_ref[...]


def mlp_forward(x, gains, g_at, im, io, tm, to):
    r, d = x.shape
    f = im.shape[1]
    t = tile_of(f)
    col = pl.BlockSpec((d, t), lambda i: (0, i))
    row = pl.BlockSpec((t, d), lambda i: (i, 0))
    hid = pl.BlockSpec((2, r, t), lambda i: (0, 0, i))
    return call(
        functools.partial(mlp_forward_body, g_at),
        [out((r, d), F32), out((r, d), BF), out((2, r, f), BF), out((2, r, f), BF)],
        x, gains, im, io, tm, to, grid=(f // t,),
        in_specs=[whole((r, d)), whole(gains.shape), col, col, row, row],
        out_specs=[whole((r, d)), whole((r, d)), hid, hid],
        scratch=[pltpu.VMEM((r, d), F32)], flops=8 * r * d * f,
    )


def mlp_backward_body(g_at, dy_ref, x_ref, g_ref, h_ref, act_ref, slope_ref, im, io, tm, to,
                      dx_ref, dw_ref, gim, gio, gtm, gto, da_ref, tr_ref, dh_ref):
    step = pl.program_id(0)

    @pl.when(step == 0)
    def _():
        da_ref[...] = dy_ref[...].astype(BF)
        tr_ref[...] = h_ref[...].T
        dh_ref[...] = jnp.zeros_like(dh_ref)

    for half, (wi, wo, gi, go) in enumerate(((im, tm, gim, gtm), (io, to, gio, gto))):
        dact = nt(da_ref[...], wo[...])
        dz = (dact * slope_ref[half].astype(F32)).astype(BF)
        gw = tn(act_ref[half], da_ref[...]).astype(BF)
        t = gw.shape[0]
        for part in range(gw.shape[1] // t):
            go[part] = gw[:, part * t : (part + 1) * t]
        gi[0] = nn(tr_ref[...], dz).astype(BF)
        dh_ref[...] += nt(dz, wi[...])

    @pl.when(step == pl.num_programs(0) - 1)
    def _():
        gain = g_ref[g_at : g_at + 1, :]
        n, rr, _ = norm_forward(x_ref[...], gain)
        dv, dw = norm_backward(n, rr, gain, dh_ref[...])
        dx_ref[...] = dy_ref[...] + dv
        dw_ref[...] = dw


def mlp_backward(dy, x, gains, g_at, h, act, slope, im, io, tm, to, t):
    r, d = x.shape
    f = im.shape[1]
    col = pl.BlockSpec((d, t), lambda i: (0, i))
    row = pl.BlockSpec((t, d), lambda i: (i, 0))
    hid = pl.BlockSpec((2, r, t), lambda i: (0, 0, i))
    gin = pl.BlockSpec((1, d, t), lambda i: (i, 0, 0))
    gout = pl.BlockSpec((d // t, t, t), lambda i: (0, i, 0))
    return call(
        functools.partial(mlp_backward_body, g_at),
        [out((r, d), F32), out((1, d), F32), out((f // t, d, t), BF), out((f // t, d, t), BF),
         out((d // t, f, t), BF), out((d // t, f, t), BF)],
        dy, x, gains, h, act, slope, im, io, tm, to, grid=(f // t,),
        in_specs=[whole((r, d)), whole((r, d)), whole(gains.shape), whole((r, d)), hid, hid, col, col, row, row],
        out_specs=[whole((r, d)), whole((1, d)), gin, gin, gout, gout],
        scratch=[pltpu.VMEM((r, d), BF), pltpu.VMEM((d, r), BF), pltpu.VMEM((r, d), F32)], flops=16 * r * d * f,
    )


def routing_body(experts, capacity, half, rows_ref, dy_ref, tr_ref, col_ref, out_ref, tmp):
    n_img = rows_ref.shape[0]
    slots = experts * half
    core = lax.axis_index("mdl")
    own_img = n_img // 2
    tall = lax.broadcasted_iota(I32, (max(experts, 8), LQ), 0)
    hots, priors = [], []
    for i in range(n_img):
        r = rows_ref[i]
        live = r[3:4, :] > 0
        hots.append((((tall == r[0:1, :]) | (tall == r[1:2, :])) & live).astype(F32).astype(BF))
        priors.append(r.astype(F32).T[:, 2:3])
    for i in range(n_img):
        r = rows_ref[i]
        rank = None
        for k in range(n_img):
            part = nn(hots[k], (priors[k] < r[2:3, :].astype(F32)).astype(F32).astype(BF))
            rank = part if rank is None else rank + part
        for k in range(TOPK):
            e = r[k : k + 1, :]
            mine = jnp.sum(jnp.where(tall == e, rank, 0.0), axis=0, keepdims=True).astype(I32)
            side = (mine >= half).astype(I32)
            slot = side * slots + e * half + mine - side * half
            tr_ref[i, k : k + 1, :] = jnp.where((mine < capacity) & (r[3:4, :] > 0), slot, -1)
        tr_ref[i, TOPK:, :] = jnp.full((8 - TOPK, LQ), -1, I32)
    for i in range(own_img):
        at = core * own_img + i
        for k in range(TOPK):
            t = tr_ref[at, k : k + 1, :]
            there = t - (1 - core) * slots
            tmp[k : k + 1, :] = t - core * slots
            tmp[TOPK + k : TOPK + k + 1, :] = jnp.where(there < slots, there, -1)
        tmp[4:8, :] = rows_ref[at, 0:4, :]
        tmp[6:7, :] = rows_ref[at, 3:4, :]
        col_ref[i * LP : (i + 1) * LP, :] = tmp[...].astype(F32).T[:LP, :].astype(I32)
    total = None
    for i in range(n_img):
        part = nn(slot_hots(tr_ref[i], core * slots, slots), dy_ref[i * LP : (i + 1) * LP, :])
        total = part if total is None else total + part
    out_ref[...] = total.astype(BF)


def slot_hots(t, base, count):
    place = lax.broadcasted_iota(I32, (count, LP), 0) + base
    return ((place == t[0:1, :LP]) | (place == t[1:2, :LP])).astype(F32).astype(BF)


def dispatch_body(experts, half, tr_ref, own_ref, oth_ref, y_ref):
    core = lax.axis_index("mdl")
    own_img = own_ref.shape[0] // LP
    total = None
    for a, v in ((core, own_ref), (1 - core, oth_ref)):
        for i in range(own_img):
            hot = slot_hots(tr_ref[a * own_img + i], core * experts * half, experts * half)
            part = nn(hot, v[i * LP : (i + 1) * LP, :])
            total = part if total is None else total + part
    y_ref[...] = total.astype(BF)


def router_probs(h, router, experts):
    logits = nt(h, router)
    lane = lax.broadcasted_iota(I32, logits.shape, 1)
    logits = jnp.where(lane < experts, logits, -1e30)
    e = jnp.exp(logits - jnp.max(logits, axis=-1, keepdims=True))
    return e / jnp.sum(e, axis=-1, keepdims=True), lane


def expert_body(experts, x_ref, dy_ref, router_ref, im, io, tm, to,
                eout_ref, ret_ref, act_ref, dz_ref, wd_ref, acc_ref, dx_ref):
    step = pl.program_id(0)
    d = x_ref.shape[1]

    @pl.when(step == 0)
    def _():
        probs, lane = router_probs(x_ref[...], router_ref[...], experts)
        gate = jnp.sum(jnp.where(lane == lax.axis_index("exp"), probs, 0.0), axis=-1, keepdims=True)
        wd_ref[...] = (gate * dy_ref[...].astype(F32)).astype(BF)
        acc_ref[...] = jnp.zeros_like(acc_ref)
        dx_ref[...] = jnp.zeros_like(dx_ref)

    for half, (wi, wo) in enumerate(((im, tm), (io, to))):
        a, s = gelu_parts(nn(x_ref[...], wi[...]))
        act = a.astype(BF)
        act_ref[half] = act
        acc_ref[...] += nn(act, wo[...])
        dz = (nt(wd_ref[...], wo[...]) * s).astype(BF)
        dz_ref[half] = dz
        dx_ref[...] += nt(dz, wi[...])

    @pl.when(step == pl.num_programs(0) - 1)
    def _():
        eout = acc_ref[...].astype(BF)
        eout_ref[...] = eout
        ret_ref[:, :d] = dx_ref[...].astype(BF)
        dgate = jnp.sum(dy_ref[...].astype(F32) * eout.astype(F32), axis=-1, keepdims=True)
        high = dgate.astype(BF).astype(F32)
        lane = lax.broadcasted_iota(I32, (x_ref.shape[0], LANES), 1)
        ret_ref[:, d:] = jnp.where(lane < LANES // 2, high, dgate - high).astype(BF)


def expert_forward_backward(x, dy, router, im, io, tm, to, experts):
    r, d = x.shape
    f = im.shape[1]
    t = tile_of(f) // 2
    col = pl.BlockSpec((d, t), lambda i: (0, i))
    row = pl.BlockSpec((t, d), lambda i: (i, 0))
    hid = pl.BlockSpec((2, r, t), lambda i: (0, 0, i))
    return call(
        functools.partial(expert_body, experts),
        [out((r, d), BF), out((r, d + LANES), BF), out((2, r, f), BF), out((2, r, f), BF), out((r, d), BF)],
        x, dy, router, im, io, tm, to, grid=(f // t,),
        in_specs=[whole((r, d)), whole((r, d)), whole(router.shape), col, col, row, row],
        out_specs=[whole((r, d)), whole((r, d + LANES)), hid, hid, whole((r, d))],
        scratch=[pltpu.VMEM((r, d), F32), pltpu.VMEM((r, d), F32)], flops=16 * r * d * f,
    )


def expert_weights_body(x_ref, wd_ref, act_ref, dz_ref, gm_ref, go_ref, xt_ref, wt_ref):
    @pl.when(pl.program_id(0) == 0)
    def _():
        xt_ref[...] = x_ref[...].T
        wt_ref[...] = wd_ref[...].T

    for half, g in enumerate((gm_ref, go_ref)):
        g[0] = nn(xt_ref[...], dz_ref[half]).astype(BF)
        g[1] = nn(wt_ref[...], act_ref[half]).astype(BF)


def expert_weights(x, wd, act, dz):
    r, d = x.shape
    f = act.shape[2]
    t = tile_of(f) // 2
    hid = pl.BlockSpec((2, r, t), lambda i: (0, 0, i))
    grad = pl.BlockSpec((2, d, t), lambda i: (0, 0, i))
    return call(
        expert_weights_body, [out((2, d, f), BF), out((2, d, f), BF)], x, wd, act, dz, grid=(f // t,),
        in_specs=[whole((r, d)), whole((r, d)), hid, hid], out_specs=[grad, grad],
        scratch=[pltpu.VMEM((d, r), BF), pltpu.VMEM((d, r), BF)], flops=8 * r * d * f,
    )


def merge(col_ref, k, ab_ref, n):
    slots = ab_ref.shape[1]
    lane = lax.broadcasted_iota(I32, (n, slots), 1)
    rows = None
    for side in range(2):
        hot = (lane == col_ref[:, 2 * side + k : 2 * side + k + 1]).astype(F32).astype(BF)
        part = nn(hot, ab_ref[side])
        rows = part if rows is None else rows + part
    return rows


def mixture_backward_core(experts, x_ref, gain, h_ref, router_ref, dy_ref, col_ref, ab_ref, dr_ref):
    n, d = x_ref.shape
    probs, lane = router_probs(h_ref[...], router_ref[...], experts)
    dh = jnp.zeros((n, d), F32)
    dsoft = jnp.zeros(probs.shape, F32)
    for k in range(TOPK):
        part = merge(col_ref, k, ab_ref, n)
        dh = dh + part[:, :d]
        dgate = part[:, d : d + 1] + part[:, d + LANES // 2 : d + LANES // 2 + 1]
        dsoft = dsoft + jnp.where(lane == col_ref[:, 4 + k : 5 + k], dgate, 0.0)
    dlog = (probs * (dsoft - jnp.sum(dsoft * probs, axis=-1, keepdims=True))).astype(BF)
    dr_ref[...] = tn(dlog, h_ref[...])
    dh = dh + nn(dlog, router_ref[...])
    nrm, rr, _ = norm_forward(x_ref[...], gain)
    dv, dw = norm_backward(nrm, rr, gain, dh)
    return dy_ref[...].astype(F32) * col_ref[:, 6:7].astype(F32) + dv, dw


def mixture_attention_backward_body(n_img, experts, size, half, *refs):
    refs = list(refs)
    x3_ref, h4_ref, router_ref, dy_ref, col_ref, ret_ref, x_ref, g_ref, h_ref, qkv_ref, p_ref, o_ref, qm, qo, om, oo = refs[:16]
    del refs[:16]
    src = refs.pop(0) if size else None
    dx_ref, dw3_ref, dw4_ref, dr_ref, gm_ref, go_ref = refs[:6]
    del refs[:6]
    dst = refs.pop(0) if size else None
    dx3, do_ref, dqkv_ref, tr_ref = refs[:4]
    if size:
        send, recv, local, f_send, f_recv = refs[4:]
        core = lax.axis_index("mdl")
        carried = Exchange(size, half, src, dst.at[0], send, recv, local)
        carried.signal()
        barrier = pltpu.get_barrier_semaphore()
        pl.semaphore_signal(barrier, inc=1, device_id={"mdl": 1 - core}, device_id_type=MESH)
        pl.semaphore_wait(barrier, size)
        carried.start()
    grad, dw4 = mixture_backward_core(experts, x3_ref, g_ref[3:4, :], h4_ref, router_ref, dy_ref, col_ref, ret_ref, dr_ref)
    dx3[...] = grad
    dw4_ref[...] = dw4
    dx, dw3 = attention_backward_core(
        n_img, lambda: dx3[...], x_ref, g_ref[2:3, :], h_ref, qkv_ref, p_ref, o_ref, qm, qo, om, oo,
        gm_ref, go_ref, do_ref, dqkv_ref, tr_ref)
    dx_ref[...] = dx
    dw3_ref[...] = dw3
    if size:
        carried.arrived()
        pass_on = pltpu.make_async_remote_copy(dst.at[0], dst.at[1], f_send, f_recv, device_id={"mdl": 1 - core},
                                               device_id_type=MESH)
        pass_on.start()
        carried.left()
        pass_on.wait()


def mixture_attention_backward(experts, x3, h4, router, dy, col, ret, x, gains, kept, qm, qo, om, oo, carry=None):
    r, d = x.shape
    c = qm.shape[2]
    n_img = r // LP
    heads = d // HDIM
    args = [x3, h4, router, dy, col, ret, x, gains, *kept, qm, qo, om, oo]
    shapes = [out((r, d), F32), out((1, d), F32), out((1, d), F32), out(router.shape, F32),
              out((3 * d + d, c), BF), out((3 * d + d, c), BF)]
    scratch = [pltpu.VMEM((r, d), F32)] + attention_backward_scratch(r, d)
    flops = 4 * r * d * d * 4 + 8 * n_img * heads * LP * LP * LANES + 8 * r * ret.shape[1] * d
    if carry is None:
        return call(functools.partial(mixture_attention_backward_body, n_img, experts, 0, 0), shapes, *args,
                    scratch=scratch, flops=flops)
    src, size, half = carry
    any_ = pl.BlockSpec(memory_space=pl.ANY)
    vm = pl.BlockSpec(memory_space=pltpu.VMEM)
    D = pltpu.SemaphoreType.DMA
    return pl.pallas_call(
        functools.partial(mixture_attention_backward_body, n_img, experts, size, half),
        in_specs=[vm] * len(args) + [any_], out_specs=[vm] * len(shapes) + [any_],
        out_shape=shapes + [out((2,) + src.shape, src.dtype)],
        scratch_shapes=scratch + [D((size - 1,)), D((size - 1,)), D, D, D],
        compiler_params=pltpu.CompilerParams(collective_id=3, has_side_effects=True, vmem_limit_bytes=VMEM_BYTES),
        cost_estimate=pl.CostEstimate(flops=flops, bytes_accessed=24 * r * d * 8, transcendentals=0),
    )(*args, src)


def mixture_output(experts, x_ref, h_ref, router_ref, col_ref, ab_ref):
    n, d = x_ref.shape
    probs, lane = router_probs(h_ref[...], router_ref[...], experts)
    mixed = jnp.zeros((n, d), F32)
    for k in range(TOPK):
        gate = jnp.sum(jnp.where(lane == col_ref[:, 4 + k : 5 + k], probs, 0.0), axis=-1, keepdims=True)
        mixed = mixed + gate * merge(col_ref, k, ab_ref, n)
    return (col_ref[:, 6:7].astype(F32) * (x_ref[...] + mixed)).astype(BF)


def mixture_output_body(experts, x_ref, h_ref, router_ref, col_ref, ab_ref, y_ref):
    y = mixture_output(experts, x_ref, h_ref, router_ref, col_ref, ab_ref)
    for i in range(y_ref.shape[0]):
        y_ref[i] = y[i * LP : i * LP + L]


def flip(axis, bit):
    size = lax.axis_size(axis)
    return [(i, i ^ bit) for i in range(size)]


def bits_of(axis):
    size = lax.axis_size(axis)
    return [1 << b for b in range(size.bit_length() - 1)]


def other_core(v):
    return lax.ppermute(v, "mdl", flip("mdl", 1))


def add16(a, b):
    return (a.astype(F32) + b.astype(F32)).astype(BF)


def halve(v, axis, bit):
    side = (lax.axis_index(axis) // bit) % 2
    n = v.shape[0] // 2
    keep = lax.dynamic_slice_in_dim(v, side * n, n)
    send = lax.dynamic_slice_in_dim(v, (1 - side) * n, n)
    return add16(keep, lax.ppermute(send, axis, flip(axis, bit)))


def double(v, axis, bit):
    side = (lax.axis_index(axis) // bit) % 2
    got = lax.ppermute(v, axis, flip(axis, bit))
    return jnp.where(side == 0, jnp.concatenate([v, got]), jnp.concatenate([got, v]))


def sum_everywhere(v):
    n = v.shape[0] // 2
    bits = bits_of("grp")
    parts = []
    for part, order in ((v[:n], bits), (v[n:], bits[::-1])):
        for bit in order:
            part = halve(part, "grp", bit)
        parts.append(part)
    size = lax.axis_size("exp")
    joined = jnp.concatenate(parts)
    rows = joined.shape[0] // size
    spread = lax.all_to_all(joined.reshape(size, rows, -1), "exp", 0, 0, tiled=True)
    mine = jnp.sum(spread.astype(F32), axis=0).astype(BF)
    joined = lax.all_gather(mine, "exp", axis=0, tiled=True)
    h = joined.shape[0] // 2
    done = []
    for part, order in ((joined[:h], bits), (joined[h:], bits[::-1])):
        for bit in order[::-1]:
            part = double(part, "grp", bit)
        done.append(part)
    return jnp.concatenate(done)


def small_sum(v):
    for axis in ("mdl", "grp", "exp"):
        for bit in bits_of(axis):
            v = v + lax.ppermute(v, axis, flip(axis, bit))
    return v


def reduce_body(n_in, per, n_exp, experts, *refs):
    mine = refs[:n_in]
    other = refs[n_in : 2 * n_in]
    dg = refs[2 * n_in : 2 * n_in + 4]
    dr_ref, x3_ref, h4_ref, router_ref, col_ref, ab_ref, image_ref = refs[2 * n_in + 4 : 2 * n_in + 11]
    outs = refs[2 * n_in + 11 :]
    qkv2, proj2, fc_in, fc_out, qkv1, proj1, sum_ref, y_ref, gx_ref = outs[:9]
    (acc, got, r1, r2, zr, sm, y_own, load_sem, m_send, m_recv, x_send, x_recv, z_send, z_recv, s_send, s_recv,
     i_local, i_send, i_recv) = outs[9:]
    out_ref = got
    n = n_in * per
    rows = acc.shape[2]
    h, q = rows // 2, rows // 4
    t = q // n_exp
    g = lax.axis_index("grp")
    z = lax.axis_index("exp")
    core = lax.axis_index("mdl")
    bx, by = g % 2, g // 2
    flat = {"x": g + 1 - 2 * bx, "y": g + 2 - 4 * by}
    order = (("x", "y"), ("y", "x"))
    bits = ((bx, by), (by, bx))

    barrier = pltpu.get_barrier_semaphore()
    others = [{"mdl": 1 - core}, {"grp": flat["x"]}, {"grp": flat["y"]}]
    others += [{"exp": (z + o) % n_exp} for o in range(1, n_exp)]
    for dev in others:
        pl.semaphore_signal(barrier, inc=1, device_id=dev, device_id_type=MESH)
    pl.semaphore_wait(barrier, len(others))

    def load(c):
        i, p = c // per, c % per
        return pltpu.make_async_copy(mine[i].at[p], acc.at[c], load_sem.at[c])

    def swap(c):
        i, p = c // per, c % per
        return pltpu.make_async_remote_copy(other[i].at[p], got.at[c], m_send.at[c], m_recv.at[c],
                                            device_id={"mdl": 1 - core}, device_id_type=MESH)

    for c in range(n):
        swap(c).start()
        load(c).start()

    own_img = image_ref.shape[0]
    places = pl.ds(core * own_img, own_img)

    def image_copies(k, src, dst):
        return (pltpu.make_async_copy(src, dst.at[places], i_local.at[k]),
                pltpu.make_async_remote_copy(src, dst.at[places], i_send.at[k], i_recv.at[k], device_id={"mdl": 1 - core},
                                             device_id_type=MESH))

    def image_come(k, src, dst):
        there = pl.ds((1 - core) * own_img, own_img)
        return pltpu.make_async_remote_copy(src, dst.at[there], i_send.at[k], i_recv.at[k], device_id={"mdl": 1 - core},
                                            device_id_type=MESH)

    for cp in image_copies(0, image_ref, gx_ref):
        cp.start()

    def swap_at(c):
        return pltpu.make_async_remote_copy(other[0].at[0], got.at[c], m_send.at[c], m_recv.at[c],
                                            device_id={"mdl": 1 - core}, device_id_type=MESH)

    def load_at(c):
        return pltpu.make_async_copy(mine[0].at[0], acc.at[c], load_sem.at[c])

    def over(u, leg, src, dst, slot, c):
        return pltpu.make_async_remote_copy(src, dst, x_send.at[slot, u, c], x_recv.at[slot, u, c],
                                            device_id={"grp": flat[order[u][leg]]}, device_id_type=MESH)

    def first(u, c):
        return over(u, 0, acc.at[c, u, pl.ds(pl.multiple_of((1 - bits[u][0]) * h, h), h)], r1.at[c, u], 0, c)

    def second(u, c):
        return over(u, 1, r1.at[c, u, pl.ds(pl.multiple_of((1 - bits[u][1]) * q, q), q)], r2.at[c, u], 1, c)

    def along(u, c, o):
        return pltpu.make_async_remote_copy(
            r2.at[c, u, pl.ds(pl.multiple_of(((z + o) % n_exp) * t, t), t)], zr.at[c, u, o - 1],
            z_send.at[0, u, o - 1, c], z_recv.at[0, u, o - 1, c],
            device_id={"exp": (z + o) % n_exp}, device_id_type=MESH)

    def place(u):
        return bits[u][0] * h + bits[u][1] * q

    def back(u, c, o):
        here = out_ref.at[c, u, pl.ds(pl.multiple_of(place(u) + z * t, t), t)]
        return pltpu.make_async_remote_copy(here, here, z_send.at[1, u, o - 1, c], z_recv.at[1, u, o - 1, c],
                                            device_id={"exp": (z + o) % n_exp}, device_id_type=MESH)

    def third(u, c):
        here = out_ref.at[c, u, pl.ds(pl.multiple_of(place(u), q), q)]
        return over(u, 1, here, here, 2, c)

    def fourth(u, c):
        here = out_ref.at[c, u, pl.ds(pl.multiple_of(bits[u][0] * h, h), h)]
        return over(u, 0, here, here, 3, c)

    def plus(a, b):
        return (a.astype(F32) + b.astype(F32)).astype(BF)

    def s1(c):
        load_at(c).wait()
        swap_at(c).wait_recv()
        for u in range(2):
            acc[c, u] = plus(acc[c, u], got[c, u])
            first(u, c).start()

    def s2(c):
        for u in range(2):
            first(u, c).wait_recv()
            keep = acc[c, u, pl.ds(pl.multiple_of(bits[u][0] * h, h), h)]
            r1[c, u] = plus(keep, r1[c, u])
            second(u, c).start()

    def s3(c):
        for u in range(2):
            second(u, c).wait_recv()
            keep = r1[c, u, pl.ds(pl.multiple_of(bits[u][1] * q, q), q)]
            r2[c, u] = plus(keep, r2[c, u])
            for o in range(1, n_exp):
                along(u, c, o).start()

    def s4(c):
        for u in range(2):
            total = r2[c, u, pl.ds(pl.multiple_of(z * t, t), t)].astype(F32)
            for o in range(1, n_exp):
                along(u, c, o).wait_recv()
                total = total + zr[c, u, o - 1].astype(F32)
            out_ref[c, u, pl.ds(pl.multiple_of(place(u) + z * t, t), t)] = total.astype(BF)
            for o in range(1, n_exp):
                back(u, c, o).start()

    def s5(c):
        for u in range(2):
            for o in range(1, n_exp):
                back(u, c, o).wait_recv()
            third(u, c).start()

    def s6(c):
        for u in range(2):
            third(u, c).wait_recv()
            fourth(u, c).start()

    def s7(c):
        for u in range(2):
            fourth(u, c).wait_recv()
        swap_at(c).wait_send()
        for u in range(2):
            for make in (first, second, third, fourth):
                make(u, c).wait_send()
            for o in range(1, n_exp):
                along(u, c, o).wait_send()
                back(u, c, o).wait_send()

    def natural(c):
        i, p = c // per, c % per
        side = rows // 2
        for u in range(2):
            v = 2 * p + u
            if i in (0, 3):
                qkv, proj = (qkv2, proj2) if i == 0 else (qkv1, proj1)
                if v < 3:
                    qkv[v] = out_ref[c, u]
                else:
                    for k in range(2):
                        proj[:, k * side : (k + 1) * side] = out_ref[c, u, k * side : (k + 1) * side]
            elif i == 1:
                fc_in[:, v * side : (v + 1) * side] = out_ref[c, u]
            else:
                fc_out[v % 2 * rows : (v % 2 + 1) * rows, v // 2 * side : (v // 2 + 1) * side] = out_ref[c, u]

    steps = (s1, s2, s3, s4, s5, s6, s7)

    def wave(tau, _):
        for s, step in enumerate(steps):
            c = tau - s

            @pl.when((c >= 0) & (c < n))
            def _(step=step, c=c):
                step(c)

        return 0

    first_waves = 3
    lax.fori_loop(0, first_waves, wave, 0)
    y = mixture_output(experts, x3_ref, h4_ref, router_ref, col_ref, ab_ref)
    for i in range(own_img):
        y_own[i] = y[i * LP : i * LP + L]
    for cp in image_copies(1, y_own, y_ref):
        cp.start()
    lax.fori_loop(first_waves, n + len(steps) - 1, wave, 0)
    for c in range(n):
        natural(c)
    for k, (src, dst) in enumerate(((image_ref, gx_ref), (y_own, y_ref))):
        local, sent = image_copies(k, src, dst)
        local.wait()
        sent.wait_send()
        image_come(k, src, dst).wait_recv()

    sm[0] = jnp.zeros(sm.shape[1:], F32)
    for k in range(4):
        sm[0, k : k + 1, :] = dg[k][...]
    sm[0, 4 : 4 + experts, :] = dr_ref[:experts, :]
    legs = [({"mdl": 1 - core}), ({"grp": flat["x"]}), ({"grp": flat["y"]})]
    for i, dev in enumerate(legs):
        cp = pltpu.make_async_remote_copy(sm.at[2 * i], sm.at[2 * i + 1], s_send.at[i], s_recv.at[i], device_id=dev, device_id_type=MESH)
        cp.start()
        cp.wait()
        sm[2 * i + 2] = sm[2 * i] + sm[2 * i + 1]
    base = 2 * len(legs) + 1
    sm[pl.ds(base + z, 1)] = sm[pl.ds(base - 1, 1)]
    cps = []
    for o in range(1, n_exp):
        cps.append(pltpu.make_async_remote_copy(sm.at[base - 1], sm.at[base + z], s_send.at[len(legs) + o - 1], s_recv.at[len(legs) + o - 1],
                                                device_id={"exp": (z + o) % n_exp}, device_id_type=MESH))
        cps[-1].start()
    for cp in cps:
        cp.wait()
    total = sm[base]
    for k in range(1, n_exp):
        total = total + sm[base + k]
    sum_ref[...] = total


def reduce_all(mine, other, dgs, dr, x3, h4, router, col, ab, image, n_exp, experts):
    per, _, rows, c = mine[0].shape
    n = len(mine) * per
    d, f = 2 * c, 4 * c
    h, q = rows // 2, rows // 4
    t = q // n_exp
    small = (-(-(4 + experts) // 8) * 8, d)
    n_img, length, _ = image.shape
    D, V = pltpu.SemaphoreType.DMA, pltpu.VMEM
    any_ = pl.BlockSpec(memory_space=pl.ANY)
    vm = pl.BlockSpec(memory_space=pltpu.VMEM)
    return pl.pallas_call(
        functools.partial(reduce_body, len(mine), per, n_exp, experts),
        in_specs=[any_] * (2 * len(mine)) + [vm] * 10 + [any_],
        out_specs=[vm] * 7 + [any_] * 2,
        out_shape=[out((3, d, c), BF), out((c, d), BF), out((d, f), BF), out((f, d), BF), out((3, d, c), BF), out((c, d), BF),
                   out(small, F32), out((2 * n_img, length, d), BF), out((2 * n_img, length, d), BF)],
        scratch_shapes=[
            V((n, 2, rows, c), BF), V((n, 2, rows, c), BF), V((n, 2, h, c), BF), V((n, 2, q, c), BF),
            V((n, 2, n_exp - 1, t, c), BF), V((7 + n_exp,) + small, F32), V((n_img, length, d), BF),
            D((n,)), D((n,)), D((n,)), D((4, 2, n)), D((4, 2, n)), D((2, 2, n_exp - 1, n)), D((2, 2, n_exp - 1, n)),
            D((3 + n_exp,)), D((3 + n_exp,)), D((2,)), D((2,)), D((2,)),
        ],
        compiler_params=pltpu.CompilerParams(collective_id=0, has_side_effects=True, vmem_limit_bytes=VMEM_BYTES),
        cost_estimate=pl.CostEstimate(flops=8 * x3.shape[0] * ab.shape[1] * d, bytes_accessed=n * 8 * rows * c, transcendentals=0),
    )(*mine, *other, *dgs, dr, x3, h4, router, col, ab, image)


def expert_exchange_body(experts, half, h4_ref, tr_ref, dyin_ref, router_ref, im, io, tm, to,
                         ret_ref, eout_ref, gw_ref,
                         h_oth, part, xo, x, wi, wo, act, dz, wd, acc, dxa, rsend, gscr, ggot, xt, wt,
                         w_sem, swap_sem, x_send, x_recv, r_send, r_recv, f_send, f_recv, g_send, g_recv, g_sem):
    n, d = h4_ref.shape
    f = im.shape[1]
    t = 256 if f % 256 == 0 else tile_of(f)
    z = lax.axis_index("exp")
    core = lax.axis_index("mdl")
    partner = {"mdl": 1 - core}
    size = experts
    near_first = [1, 3, 2]

    def there(j):
        b0, b1 = z % 2, z // 2
        if j & 1:
            b0 = 1 - b0
        if j & 2:
            b1 = 1 - b1
        return b0 + 2 * b1

    loads = [pltpu.make_async_copy(src, dst, w_sem.at[k]) for k, (src, dst) in enumerate(
        ((im, wi.at[0]), (io, wi.at[1]), (tm, wo.at[0]), (to, wo.at[1])))]
    for cp in loads:
        cp.start()
    barrier = pltpu.get_barrier_semaphore()
    for dev in [partner] + [{"exp": there(j)} for j in range(1, size)]:
        pl.semaphore_signal(barrier, inc=1, device_id=dev, device_id_type=MESH)
    pl.semaphore_wait(barrier, size)
    swap = pltpu.make_async_remote_copy(h4_ref, h_oth, swap_sem.at[0], swap_sem.at[1], device_id=partner, device_id_type=MESH)
    swap.start()

    own_img = n // LP
    base = core * size * half

    def spread(side, v, j):
        total = None
        for i in range(own_img):
            p = nn(slot_hots(tr_ref[side * own_img + i], base + there(j) * half, half), v[i * LP : (i + 1) * LP, :])
            total = p if total is None else total + p
        return total

    def rows(j):
        return slice(j * half, (j + 1) * half)

    def place(e):
        return pl.ds(pl.multiple_of(e * half, half), half)

    for j in near_first + [0]:
        part[rows(j), :] = spread(core, h4_ref, j)
    swap.wait_recv()
    sends = {}
    for j in near_first + [0]:
        block = (part[rows(j), :] + spread(1 - core, h_oth, j)).astype(BF)
        if j == 0:
            x[rows(0), :] = block
        else:
            xo[rows(j), :] = block
            sends[j] = pltpu.make_async_remote_copy(xo.at[rows(j)], x.at[rows(j)], x_send.at[j], x_recv.at[j],
                                                    device_id={"exp": there(j)}, device_id_type=MESH)
            sends[j].start()

    returns, forwards = {}, {}

    def forward(j):
        here = ret_ref.at[0, place(there(j))]
        forwards[j] = pltpu.make_async_remote_copy(here, ret_ref.at[1, place(there(j))], f_send.at[j], f_recv.at[j],
                                                   device_id=partner, device_id_type=MESH)
        forwards[j].start()

    def run(blocks):
        r0, r1 = blocks[0] * half, (blocks[-1] + 1) * half
        m = r1 - r0
        for j in blocks:
            probs, lane = router_probs(x[rows(j), :], router_ref[...], experts)
            gate = jnp.sum(jnp.where(lane == z, probs, 0.0), axis=-1, keepdims=True)
            wd[rows(j), :] = (gate * dyin_ref[place(there(j)), :].astype(F32)).astype(BF)
        acc[0:m, :] = jnp.zeros((m, d), F32)
        dxa[0:m, :] = jnp.zeros((m, d), F32)

        def tile(i, _):
            at = pl.ds(pl.multiple_of(i * t, t), t)
            for side in range(2):
                a, s = gelu_parts(nn(x[r0:r1, :], wi[side, :, at]))
                a = a.astype(BF)
                act[side, r0:r1, at] = a
                acc[0:m, :] += nn(a, wo[side, at, :])
                g = (nt(wd[r0:r1, :], wo[side, at, :]) * s).astype(BF)
                dz[side, r0:r1, at] = g
                dxa[0:m, :] += nt(g, wi[side, :, at])
            return 0

        lax.fori_loop(0, f // t, tile, 0)
        for b, j in enumerate(blocks):
            here = slice(b * half, (b + 1) * half)
            e_rows = acc[here, :].astype(BF)
            eout_ref[place(there(j)), :] = e_rows
            dgate = jnp.sum(dyin_ref[place(there(j)), :].astype(F32) * e_rows.astype(F32), axis=-1, keepdims=True)
            high = dgate.astype(BF).astype(F32)
            lane = lax.broadcasted_iota(I32, (half, LANES), 1)
            extra = jnp.where(lane < LANES // 2, high, dgate - high).astype(BF)
            if j == 0:
                ret_ref[0, place(z), 0:d] = dxa[here, :].astype(BF)
                ret_ref[0, place(z), d:] = extra
                forward(0)
            else:
                rsend[rows(j), 0:d] = dxa[here, :].astype(BF)
                rsend[rows(j), d:] = extra
                returns[j] = pltpu.make_async_remote_copy(rsend.at[rows(j)], ret_ref.at[0, place(z)], r_send.at[j], r_recv.at[j],
                                                          device_id={"exp": there(j)}, device_id_type=MESH)
                returns[j].start()

    for cp in loads:
        cp.wait()
    sends[1].wait_recv()
    run([0, 1])
    for j in near_first[1:]:
        sends[j].wait_recv()
        run([j])

    xt[...] = x[...].T
    wt[...] = wd[...].T

    tiles = f // t

    def cols(i):
        return pl.ds(pl.multiple_of(i * t, t), t)

    def swapped(i):
        return pltpu.make_async_remote_copy(gscr.at[1, :, :, cols(i)], ggot.at[:, :, cols(i)], g_send.at[i], g_recv.at[i],
                                            device_id=partner, device_id_type=MESH)

    def stored(i):
        return pltpu.make_async_copy(gscr.at[0, :, :, cols(i)], gw_ref.at[:, :, cols(i)], g_sem.at[i])

    def weight_tile(i, _):
        for side in (1, 0):
            gscr[side, 0, :, cols(i)] = nn(xt[...], dz[side, :, cols(i)]).astype(BF)
            gscr[side, 1, :, cols(i)] = nn(wt[...], act[side, :, cols(i)]).astype(BF)
            if side == 1:
                swapped(i).start()
        return 0

    lax.fori_loop(0, tiles, weight_tile, 0)

    def sum_tile(i, _):
        swapped(i).wait_recv()
        for k in range(2):
            gscr[0, k, :, cols(i)] = (gscr[0, k, :, cols(i)].astype(F32) + ggot[k, :, cols(i)].astype(F32)).astype(BF)
        stored(i).start()
        return 0

    lax.fori_loop(0, tiles, sum_tile, 0)

    def recv_return(j):
        return pltpu.make_async_remote_copy(rsend.at[rows(j)], ret_ref.at[0, place(there(j))], r_send.at[j], r_recv.at[j],
                                            device_id={"exp": there(j)}, device_id_type=MESH)

    for j in near_first:
        recv_return(j).wait_recv()
        forward(j)

    def drain(i, _):
        stored(i).wait()
        swapped(i).wait_send()
        return 0

    lax.fori_loop(0, tiles, drain, 0)
    swap.wait_send()
    for j in range(size):
        if j:
            sends[j].wait_send()
            returns[j].wait_send()
        forwards[j].wait()


def expert_exchange(h4, tr, dy_in, router, im, io, tm, to, experts, half):
    n, d = h4.shape
    f = im.shape[1]
    s = experts * half
    tiles = f // (256 if f % 256 == 0 else tile_of(f))
    D, V = pltpu.SemaphoreType.DMA, pltpu.VMEM
    any_ = pl.BlockSpec(memory_space=pl.ANY)
    vm = pl.BlockSpec(memory_space=pltpu.VMEM)
    return pl.pallas_call(
        functools.partial(expert_exchange_body, experts, half),
        in_specs=[vm] * 4 + [any_] * 4,
        out_specs=[vm, vm, any_],
        out_shape=[out((2, s, d + LANES), BF), out((s, d), BF), out((2, d, f), BF)],
        scratch_shapes=[
            V((n, d), BF), V((s, d), F32), V((s, d), BF), V((s, d), BF), V((2, d, f), BF), V((2, f, d), BF),
            V((2, s, f), BF), V((2, s, f), BF), V((s, d), BF), V((2 * half, d), F32), V((2 * half, d), F32),
            V((s, d + LANES), BF), V((2, 2, d, f), BF), V((2, d, f), BF), V((d, s), BF), V((d, s), BF),
            D((4,)), D((2,)), D((experts,)), D((experts,)), D((experts,)), D((experts,)), D((experts,)), D((experts,)),
            D((tiles,)), D((tiles,)), D((tiles,)),
        ],
        compiler_params=pltpu.CompilerParams(collective_id=1, has_side_effects=True, vmem_limit_bytes=VMEM_BYTES),
        cost_estimate=pl.CostEstimate(flops=24 * s * d * f, bytes_accessed=20 * d * f, transcendentals=0),
    )(h4, tr, dy_in, router, im, io, tm, to)


FUSED = True


def on_device(images, counts, routes, priority, gain_one, qkv_one, out_one, gain_two, fc_in, fc_out, gain_three,
              qkv_two, out_two, gain_four, router, expert_in, expert_out, cotangent):
    n_slot, length, d = images.shape
    experts = router.shape[1]
    n_mdl = lax.axis_size("mdl")
    peers = lax.axis_size("exp")
    capacity = (25 * L * TOPK + 8 * experts - 1) // (8 * experts)
    half = -(-(-(-capacity // n_mdl)) // 16) * 16
    slots = experts * half
    own_img = n_slot // n_mdl
    f = fc_in.shape[1]
    c = qkv_one.shape[2]
    rows = own_img * LP
    core = lax.axis_index("mdl")
    per = 2
    unit = 4 * d // (2 * per)
    fused = FUSED and (lax.axis_size("grp"), peers, n_mdl) == (4, experts, 2) and peers == 4
    fused = fused and d == 2 * c and f == 4 * c and unit % (64 * peers) == 0

    def own(v):
        return lax.dynamic_slice_in_dim(v, core * rows, rows)

    def padded(v):
        return jnp.pad(v, ((0, 0), (0, LP - length), (0, 0))).reshape(n_slot * LP, -1)

    qm1, om1, im, tm, qm2, om2, em, fm = qkv_one, out_one, fc_in, fc_out, qkv_two, out_two, expert_in[0], expert_out[0]
    qo1, oo1, io, to, qo2, oo2, eo, fo = (other_core(w) for w in (qm1, om1, im, tm, qm2, om2, em, fm))
    gains = jnp.stack([gain_one, gain_two, gain_three, gain_four])
    router_rows = jnp.pad(router.T, ((0, LANES - experts), (0, 0)))

    live = jnp.broadcast_to((jnp.arange(n_slot, dtype=I32) < counts[0, 0]).astype(I32)[:, None, None], (n_slot, 1, length))
    lines = jnp.concatenate([jnp.transpose(routes, (0, 2, 1)), priority.reshape(n_slot, 1, length), live], axis=1)
    lines = jnp.pad(lines, ((0, 0), (0, 4), (0, LQ - length)))
    dy = padded(cotangent)
    slot_rows, col, dy_out = call(
        functools.partial(routing_body, experts, capacity, half),
        [out((n_slot, 8, LQ), I32), out((rows, 8), I32), out((slots, d), BF)], lines, dy,
        scratch=[pltpu.VMEM((8, LQ), I32)], flops=4 * slots * n_slot * LP * d,
    )

    def exchange(v):
        shaped = v.reshape(peers, v.shape[0] // peers, v.shape[1])
        return lax.all_to_all(shaped, "exp", 0, 0, tiled=True).reshape(v.shape)

    x0 = own(padded(images))
    if fused:
        x1, *kept1, dy_in = attention_forward(x0, gains, 0, qm1, qo1, om1, oo1, carry=(dy_out, peers, half))
    else:
        x1, *kept1 = attention_forward(x0, gains, 0, qm1, qo1, om1, oo1)
        dy_in = exchange(dy_out)
    x2, h2, act2, slope2 = mlp_forward(x1, gains, 1, im, io, tm, to)
    x3, *kept3, h4 = attention_forward(x2, gains, 2, qm2, qo2, om2, oo2, tail=3)

    own_dy = own(dy)
    second = (x2, gains, kept3, qm2, qo2, om2, oo2)
    if fused:
        ret, eout, ge = expert_exchange(h4, slot_rows, dy_in, router_rows, em, eo, fm, fo, experts, half)
        dx2, dg3, dg4, dr, a2_mine, a2_other, eback = mixture_attention_backward(
            experts, x3, h4, router_rows, own_dy, col, ret, *second, carry=(eout, peers, half))
    else:
        [h4_out] = call(functools.partial(dispatch_body, experts, half), [out((slots, d), BF)], slot_rows, h4, other_core(h4))
        h4_in = exchange(h4_out)
        eout, ret, eact, edz, ewd = expert_forward_backward(h4_in, dy_in, router_rows, em, eo, fm, fo, experts)
        ret, eout = exchange(ret), exchange(eout)
        ret, eback = jnp.stack([ret, other_core(ret)]), jnp.stack([eout, other_core(eout)])
        ge_mine, ge_other = expert_weights(h4_in, ewd, eact, edz)
        ge = add16(ge_mine, other_core(ge_other))
        dx2, dg3, dg4, dr, a2_mine, a2_other = mixture_attention_backward(
            experts, x3, h4, router_rows, own_dy, col, ret, *second)
    expert_sum = lax.psum_scatter(ge, "grp", scatter_dimension=1, tiled=True)

    dx1, dg2, gim, gio, gtm, gto = mlp_backward(dx2, x1, gains, 1, h2, act2, slope2, im, io, tm, to, c)
    image, dg1, a1_mine, a1_other = attention_backward(dx1, x0, gains, 0, kept1, qm1, qo1, om1, oo1)
    mines, others = (a2_mine, gim, gtm, a1_mine), (a2_other, gio, gto, a1_other)

    if fused:
        split = [[v.reshape(per, 2, unit, c) for v in side] for side in (mines, others)]
        qkv2, proj2, fi, fo_, qkv1, proj1, small, output, grad_images = reduce_all(
            *split, (dg1, dg2, dg3, dg4), dr, x3, h4, router_rows, col, eback, image, peers, experts)
    else:
        sums = [sum_everywhere(add16(a.reshape(4 * d, c), other_core(b.reshape(4 * d, c)))) for a, b in zip(mines, others)]
        small = small_sum(jnp.concatenate([dg1, dg2, dg3, dg4, dr[:experts]], axis=0))

        def panels(v):
            return jnp.concatenate([v[i] for i in range(v.shape[0])], axis=1)

        (qkv2, proj2), (qkv1, proj1) = (
            (v[: 3 * d].reshape(3, d, c), panels(v[3 * d :].reshape(d // c, c, c))) for v in (sums[0], sums[3]))
        fi, fo_ = panels(sums[1].reshape(f // c, d, c)), panels(sums[2].reshape(d // c, f, c))
        [own_out] = call(
            functools.partial(mixture_output_body, experts), [out((own_img, L, d), BF)], x3, h4, router_rows, col, eback,
            flops=8 * rows * slots * d)

        def both(v):
            there = other_core(v)
            return jnp.where(core == 0, jnp.concatenate([v, there]), jnp.concatenate([there, v]))

        output, grad_images = both(own_out), both(image)
    return (
        output, grad_images,
        small[0], qkv1.astype(F32), proj1.astype(F32), small[1], fi.astype(F32), fo_.astype(F32),
        small[2], qkv2.astype(F32), proj2.astype(F32), small[3], small[4 : 4 + experts].T,
        expert_sum[0].astype(F32)[None], expert_sum[1].astype(F32).T[None],
    )


def solution(mesh):
    token = P(("grp", "exp"), None, None)
    column, line = P(None, None, "mdl"), P("mdl", None)
    return jax.shard_map(
        on_device,
        mesh=mesh,
        in_specs=(token, P("grp", "exp"), token, P(("grp", "exp"), None), P(), column, line, P(), P(None, "mdl"), line,
                  P(), column, line, P(), P(), P("exp", None, "mdl"), P("exp", "mdl", None), token),
        out_specs=(token, token, P(), column, line, P(), P(None, "mdl"), line, P(), column, line, P(), P(),
                   P("exp", "grp", "mdl"), P("exp", "mdl", "grp")),
        check_vma=False,
    )
```

```python
import functools
import math

import jax
import jax.numpy as jnp
from jax import lax
from jax.experimental import pallas as pl
from jax.experimental.pallas import tpu as pltpu
from jax.sharding import PartitionSpec as P

HDIM = 64
L = 197
TOPK = 2
LP = (L + 15) // 16 * 16
LANES = 128
LQ = (L + LANES - 1) // LANES * LANES
BF = jnp.bfloat16
F32 = jnp.float32
I32 = jnp.int32

EPSILON = 1e-06
ROOT_HALF = 0.7071067811865476
DENSITY_FACTOR = 0.3989422804014327
VMEM_BYTES = 60 * 1024 * 1024
MESH = pl.DeviceIdType.MESH


def nn(a, b):
    return lax.dot_general(a, b, (((1,), (0,)), ((), ())), preferred_element_type=F32)


def nt(a, b):
    return lax.dot_general(a, b, (((1,), (1,)), ((), ())), preferred_element_type=F32)


def tn(a, b):
    return lax.dot_general(a, b, (((0,), (0,)), ((), ())), preferred_element_type=F32)


def norm_forward(v, w):
    c = v - jnp.mean(v, axis=-1, keepdims=True)
    r = lax.rsqrt(jnp.mean(c * c, axis=-1, keepdims=True) + EPSILON)
    n = c * r
    return n, r, (n * w).astype(BF)


def norm_backward(n, r, w, dh):
    dn = dh * w
    dw = jnp.sum(dh * n, axis=0, keepdims=True)
    dv = r * (dn - jnp.mean(dn, axis=-1, keepdims=True) - n * jnp.mean(dn * n, axis=-1, keepdims=True))
    return dv, dw


def whole(shape):
    return pl.BlockSpec(shape, lambda *i: (0,) * len(shape))


def call(body, out_shape, *args, grid=(), in_specs=None, out_specs=None, scratch=(), flops=0):
    if in_specs is None:
        in_specs = [whole(a.shape) for a in args]
    if out_specs is None:
        out_specs = [whole(o.shape) for o in out_shape]
    moved = sum(math.prod(a.shape) * a.dtype.itemsize for a in args)
    moved += sum(math.prod(o.shape) * jnp.dtype(o.dtype).itemsize for o in out_shape)
    return pl.pallas_call(
        body,
        grid=grid,
        in_specs=in_specs,
        out_specs=out_specs,
        out_shape=out_shape,
        scratch_shapes=list(scratch),
        cost_estimate=pl.CostEstimate(flops=int(flops), bytes_accessed=int(moved), transcendentals=0),
        compiler_params=pltpu.CompilerParams(vmem_limit_bytes=VMEM_BYTES),
    )(*args)


def out(shape, dtype):
    return jax.ShapeDtypeStruct(shape, dtype)


def head_mask(dtype):
    lane = lax.broadcasted_iota(I32, (LP, LANES), 1)
    return (lane < HDIM).astype(dtype)


def beside(z, j):
    b0, b1 = z % 2, z // 2
    if j & 1:
        b0 = 1 - b0
    if j & 2:
        b1 = 1 - b1
    return b0 + 2 * b1


def own_rows(ref, n):
    if ref.shape[0] == n:
        return ref[...]
    return ref[pl.ds(pl.multiple_of(lax.axis_index("mdl") * n, 16), n), :]


def attend(img, pair, d, qkv_ref, p_ref, o_ref):
    mask = head_mask(BF)
    key_ok = lax.broadcasted_iota(I32, (LP, LP), 1) < L
    rows = pl.ds(pl.multiple_of(img * LP, LP), LP)
    col = pair * LANES
    q = qkv_ref[rows, pl.ds(pl.multiple_of(col, LANES), LANES)]
    ke = qkv_ref[rows, pl.ds(pl.multiple_of(d + col, LANES), LANES)]
    u = qkv_ref[rows, pl.ds(pl.multiple_of(2 * d + col, LANES), LANES)]
    o = jnp.zeros((LP, LANES), F32)
    for hh in range(2):
        mk = mask if hh == 0 else 1 - mask
        s = nt(q * mk, ke) * HDIM ** (-0.5)
        s = jnp.where(key_ok, s, -1e30)
        e = jnp.exp(s - jnp.max(s, axis=-1, keepdims=True))
        p = (e / jnp.sum(e, axis=-1, keepdims=True)).astype(BF)
        p_ref[2 * (img * (d // LANES) + pair) + hh] = p
        o = o + nn(p, u * mk)
    o_ref[rows, pl.ds(pl.multiple_of(col, LANES), LANES)] = o.astype(BF)
    return 0


def attention_forward_body(n_img, g_at, tail, *refs):
    refs = list(refs)
    x_ref, g_ref, qm, qo, om, oo = refs[:6]
    del refs[:6]
    y_ref, h_ref, qkv_ref, p_ref, o_ref = refs[:5]
    del refs[:5]
    h4_ref = refs.pop(0) if tail is not None else None
    rows_all = n_img * LP
    d = x_ref.shape[1]
    c = qm.shape[2]
    pairs = d // LANES
    _, _, h = norm_forward(own_rows(x_ref, rows_all).astype(F32), g_ref[g_at : g_at + 1, :])
    h_ref[...] = h
    for k in range(3):
        for side, w in ((0, qm), (1, qo)):
            at = (2 * k + side) * c
            qkv_ref[:, at : at + c] = nn(h_ref[...], w[k]).astype(BF)
    lax.fori_loop(0, n_img * pairs, lambda i, _: attend(i // pairs, i % pairs, d, qkv_ref, p_ref, o_ref), 0, unroll=2)
    y = own_rows(x_ref, rows_all).astype(F32) + nn(o_ref[:, :c], om[...]) + nn(o_ref[:, c:], oo[...])
    y_ref[...] = y
    if tail is not None:
        _, _, h4 = norm_forward(y, g_ref[tail : tail + 1, :])
        h4_ref[...] = h4


def attention_forward(x, r, gains, g_at, qm, qo, om, oo, tail=None):
    d = x.shape[1]
    n_img = r // LP
    heads = d // HDIM
    shapes = [out((r, d), F32), out((r, d), BF), out((r, 3 * d), BF), out((n_img * heads, LP, LP), BF), out((r, d), BF)]
    if tail is not None:
        shapes.append(out((r, d), BF))
    return call(functools.partial(attention_forward_body, n_img, g_at, tail), shapes, x, gains, qm, qo, om, oo,
                flops=2 * r * d * d * 4 + 4 * n_img * heads * LP * LP * LANES)


def attention_backward_core(n_img, dy, x_ref, gain, h_ref, qkv_ref, p_ref, o_ref, qm, qo, om, oo,
                            gm_ref, go_ref, do_ref, dqkv_ref, tr_ref):
    d = x_ref.shape[1]
    c = qm.shape[2]
    pairs = d // LANES
    da = dy().astype(BF)
    tr_ref[...] = o_ref[...].T
    for side, (w, g) in enumerate(((om, gm_ref), (oo, go_ref))):
        gw = nn(tr_ref[side * c : (side + 1) * c, :], da).astype(BF)
        for part in range(d // c):
            g[3 * d + part * c : 3 * d + (part + 1) * c, :] = gw[:, part * c : (part + 1) * c]
        do_ref[:, side * c : (side + 1) * c] = nt(da, w[...]).astype(BF)
    mask = head_mask(BF)

    def one(i, _):
        rows = pl.ds(pl.multiple_of((i // pairs) * LP, LP), LP)
        col = (i % pairs) * LANES
        cq = pl.ds(pl.multiple_of(col, LANES), LANES)
        ck = pl.ds(pl.multiple_of(d + col, LANES), LANES)
        cu = pl.ds(pl.multiple_of(2 * d + col, LANES), LANES)
        q, ke, u, do = qkv_ref[rows, cq], qkv_ref[rows, ck], qkv_ref[rows, cu], do_ref[rows, cq]
        dq = jnp.zeros((LP, LANES), F32)
        dk = jnp.zeros((LP, LANES), F32)
        du = jnp.zeros((LP, LANES), F32)
        for hh in range(2):
            mk = mask if hh == 0 else 1 - mask
            p = p_ref[2 * i + hh]
            du = du + tn(p, do * mk)
            dp = nt(do * mk, u)
            pf = p.astype(F32)
            ds = (pf * (dp - jnp.sum(dp * pf, axis=-1, keepdims=True))).astype(BF)
            dq = dq + nn(ds, ke * mk)
            dk = dk + tn(ds, q * mk)
        dqkv_ref[rows, cq] = (dq * HDIM ** (-0.5)).astype(BF)
        dqkv_ref[rows, ck] = (dk * HDIM ** (-0.5)).astype(BF)
        dqkv_ref[rows, cu] = du.astype(BF)
        return 0

    lax.fori_loop(0, n_img * pairs, one, 0, unroll=2)
    tr_ref[...] = h_ref[...].T
    dh = jnp.zeros((n_img * LP, d), F32)
    for k in range(3):
        for side, (w, g) in enumerate(((qm, gm_ref), (qo, go_ref))):
            at = (2 * k + side) * c
            g[k * d : (k + 1) * d, :] = nn(tr_ref[...], dqkv_ref[:, at : at + c]).astype(BF)
            dh = dh + nt(dqkv_ref[:, at : at + c], w[k])
    n, rr, _ = norm_forward(own_rows(x_ref, n_img * LP).astype(F32), gain)
    dv, dw = norm_backward(n, rr, gain, dh)
    return dy() + dv, dw


def attention_backward_body(n_img, g_at, dy_ref, x_ref, g_ref, h_ref, qkv_ref, p_ref, o_ref, qm, qo, om, oo,
                            dx_ref, dw_ref, gm_ref, go_ref, do_ref, dqkv_ref, tr_ref):
    dx, dw = attention_backward_core(
        n_img, lambda: dy_ref[...], x_ref, g_ref[g_at : g_at + 1, :], h_ref, qkv_ref, p_ref, o_ref, qm, qo, om, oo,
        gm_ref, go_ref, do_ref, dqkv_ref, tr_ref)
    for i in range(n_img):
        dx_ref[i] = dx[i * LP : i * LP + L].astype(BF)
    dw_ref[...] = dw


def attention_backward_scratch(r, d):
    return [pltpu.VMEM((r, d), BF), pltpu.VMEM((r, 3 * d), BF), pltpu.VMEM((d, r), BF)]


def attention_backward(dy, x, gains, g_at, kept, qm, qo, om, oo):
    r, d = dy.shape
    c = qm.shape[2]
    n_img = r // LP
    heads = d // HDIM
    return call(
        functools.partial(attention_backward_body, n_img, g_at),
        [out((n_img, L, d), BF), out((1, d), F32), out((3 * d + d, c), BF), out((3 * d + d, c), BF)],
        dy, x, gains, *kept, qm, qo, om, oo,
        scratch=attention_backward_scratch(r, d),
        flops=4 * r * d * d * 4 + 8 * n_img * heads * LP * LP * LANES,
    )


def gelu_parts(z):
    phi = 0.5 * (1.0 + lax.erf(z * ROOT_HALF))
    return z * phi, phi + z * jnp.exp(-0.5 * z * z) * DENSITY_FACTOR


def tile_of(f):
    for t in (512, 256, 128):
        if f % t == 0:
            return t
    return f


def mlp_forward_body(g_at, x_ref, g_ref, im, io, tm, to, y_ref, h_ref, act_ref, slope_ref, acc_ref):
    step = pl.program_id(0)

    @pl.when(step == 0)
    def _():
        x = x_ref[...]
        _, _, h = norm_forward(x, g_ref[g_at : g_at + 1, :])
        h_ref[...] = h
        acc_ref[...] = x

    for half, (wi, wo) in enumerate(((im, tm), (io, to))):
        a, s = gelu_parts(nn(h_ref[...], wi[...]))
        act = a.astype(BF)
        act_ref[half] = act
        slope_ref[half] = s.astype(BF)
        acc_ref[...] += nn(act, wo[...])

    @pl.when(step == pl.num_programs(0) - 1)
    def _():
        y_ref[...] = acc_ref[...]


def mlp_forward(x, gains, g_at, im, io, tm, to):
    r, d = x.shape
    f = im.shape[1]
    t = tile_of(f)
    col = pl.BlockSpec((d, t), lambda i: (0, i))
    row = pl.BlockSpec((t, d), lambda i: (i, 0))
    hid = pl.BlockSpec((2, r, t), lambda i: (0, 0, i))
    return call(
        functools.partial(mlp_forward_body, g_at),
        [out((r, d), F32), out((r, d), BF), out((2, r, f), BF), out((2, r, f), BF)],
        x, gains, im, io, tm, to, grid=(f // t,),
        in_specs=[whole((r, d)), whole(gains.shape), col, col, row, row],
        out_specs=[whole((r, d)), whole((r, d)), hid, hid],
        scratch=[pltpu.VMEM((r, d), F32)], flops=8 * r * d * f,
    )


def mlp_backward_body(g_at, dy_ref, x_ref, g_ref, h_ref, act_ref, slope_ref, im, io, tm, to,
                      dx_ref, dw_ref, gim, gio, gtm, gto, da_ref, tr_ref, dh_ref):
    step = pl.program_id(0)

    @pl.when(step == 0)
    def _():
        da_ref[...] = dy_ref[...].astype(BF)
        tr_ref[...] = h_ref[...].T
        dh_ref[...] = jnp.zeros_like(dh_ref)

    for half, (wi, wo, gi, go) in enumerate(((im, tm, gim, gtm), (io, to, gio, gto))):
        dact = nt(da_ref[...], wo[...])
        dz = (dact * slope_ref[half].astype(F32)).astype(BF)
        gw = tn(act_ref[half], da_ref[...]).astype(BF)
        t = gw.shape[0]
        for part in range(gw.shape[1] // t):
            go[part] = gw[:, part * t : (part + 1) * t]
        gi[0] = nn(tr_ref[...], dz).astype(BF)
        dh_ref[...] += nt(dz, wi[...])

    @pl.when(step == pl.num_programs(0) - 1)
    def _():
        gain = g_ref[g_at : g_at + 1, :]
        n, rr, _ = norm_forward(x_ref[...], gain)
        dv, dw = norm_backward(n, rr, gain, dh_ref[...])
        dx_ref[...] = dy_ref[...] + dv
        dw_ref[...] = dw


def mlp_backward(dy, x, gains, g_at, h, act, slope, im, io, tm, to, t):
    r, d = x.shape
    f = im.shape[1]
    col = pl.BlockSpec((d, t), lambda i: (0, i))
    row = pl.BlockSpec((t, d), lambda i: (i, 0))
    hid = pl.BlockSpec((2, r, t), lambda i: (0, 0, i))
    gin = pl.BlockSpec((1, d, t), lambda i: (i, 0, 0))
    gout = pl.BlockSpec((d // t, t, t), lambda i: (0, i, 0))
    return call(
        functools.partial(mlp_backward_body, g_at),
        [out((r, d), F32), out((1, d), F32), out((f // t, d, t), BF), out((f // t, d, t), BF),
         out((d // t, f, t), BF), out((d // t, f, t), BF)],
        dy, x, gains, h, act, slope, im, io, tm, to, grid=(f // t,),
        in_specs=[whole((r, d)), whole((r, d)), whole(gains.shape), whole((r, d)), hid, hid, col, col, row, row],
        out_specs=[whole((r, d)), whole((1, d)), gin, gin, gout, gout],
        scratch=[pltpu.VMEM((r, d), BF), pltpu.VMEM((d, r), BF), pltpu.VMEM((r, d), F32)], flops=16 * r * d * f,
    )


def forward_body(n_img, size, *refs):
    refs = list(refs)

    def take(n):
        r = refs[:n]
        del refs[:n]
        return r

    x_ref, g_ref = take(2)
    own_w = take(8)
    dy_out = take(size - 1)
    results = take(15)
    other_w = take(8)
    dy_in = take(size - 1)
    weights = take(6)
    held = take(15)
    load_sem, w_send, w_recv, o_sem, r_sem, d_send, d_recv = refs
    x1, h1, qkv1, p1, o1, x2, h2, act, slope, x3, h3, qkv3, p3, o3, h4 = held
    q1, w1, fi, fo, q3, w3 = weights
    r = n_img * LP
    d = x_ref.shape[1]
    c = q1.shape[3]
    f = fi.shape[2]
    z = lax.axis_index("exp")
    partner = {"mdl": 1 - lax.axis_index("mdl")}

    loads = [pltpu.make_async_copy(own_w[k], weights[k].at[0], load_sem.at[k]) for k in range(6)]
    for cp in loads:
        cp.start()
    barrier = pltpu.get_barrier_semaphore()
    for dev in [partner] + [{"exp": beside(z, j)} for j in range(1, size)]:
        pl.semaphore_signal(barrier, inc=1, device_id=dev, device_id_type=MESH)
    pl.semaphore_wait(barrier, size)
    swaps = [pltpu.make_async_remote_copy(own_w[k], weights[k].at[1] if k < 6 else other_w[k], w_send.at[k], w_recv.at[k],
                                          device_id=partner, device_id_type=MESH) for k in range(8)]
    for cp in swaps:
        cp.start()
    blocks = [pltpu.make_async_remote_copy(dy_out[j - 1], dy_in[j - 1], d_send.at[j - 1], d_recv.at[j - 1],
                                           device_id={"exp": beside(z, j)}, device_id_type=MESH) for j in range(1, size)]
    for cp in blocks:
        cp.start()
    keeps = [pltpu.make_async_copy(weights[k].at[1], other_w[k], o_sem.at[k]) for k in range(6)]
    stores = [pltpu.make_async_copy(held[k], results[k], r_sem.at[k]) for k in range(15)]

    def store(*at):
        for k in at:
            stores[k].start()

    def attention(x, gain, wq, wo, kq, ko, h, qkv, p, o, y):
        _, _, n = norm_forward(x(), gain)
        h[...] = n
        per_half = c // LANES
        for side in range(2):
            if side == 0:
                loads[kq].wait()
            else:
                swaps[kq].wait_recv()
                keeps[kq].start()
            for k in range(3):
                at = (2 * k + side) * c
                qkv[:, at : at + c] = nn(h[...], wq[side, k]).astype(BF)
            lax.fori_loop(
                0, n_img * per_half,
                lambda i, _, side=side: attend(i // per_half, side * per_half + i % per_half, d, qkv, p, o), 0, unroll=2)
        loads[ko].wait()
        swaps[ko].wait_recv()
        keeps[ko].start()
        y[...] = x() + nn(o[:, :c], wo[0]) + nn(o[:, c:], wo[1])

    attention(lambda: own_rows(x_ref, r).astype(F32), g_ref[0:1, :], q1, w1, 0, 1, h1, qkv1, p1, o1, x1)
    store(0, 1, 2, 3, 4)

    _, _, n = norm_forward(x1[...], g_ref[1:2, :])
    h2[...] = n
    x2[...] = x1[...]
    t = tile_of(f)
    for side in range(2):
        for k in (2, 3):
            if side == 0:
                loads[k].wait()
            else:
                swaps[k].wait_recv()
                keeps[k].start()

        def tile(i, _, side=side):
            at = pl.ds(pl.multiple_of(i * t, t), t)
            a, sl = gelu_parts(nn(h2[...], fi[side, :, at]))
            a = a.astype(BF)
            act[side, :, at] = a
            slope[side, :, at] = sl.astype(BF)
            x2[...] += nn(a, fo[side, at, :])
            return 0

        lax.fori_loop(0, f // t, tile, 0)
    store(5, 6, 7, 8)

    attention(lambda: x2[...], g_ref[2:3, :], q3, w3, 4, 5, h3, qkv3, p3, o3, x3)
    store(9, 10, 11, 12, 13)
    _, _, n = norm_forward(x3[...], g_ref[3:4, :])
    h4[...] = n
    store(14)
    for cp in blocks:
        cp.wait()
    for cp in keeps + stores:
        cp.wait()
    for cp in swaps[6:]:
        cp.wait_recv()
    for cp in swaps:
        cp.wait_send()


def forward(x, gains, own_w, dy_out, r):
    d = x.shape[1]
    c, f = own_w[0].shape[2], own_w[2].shape[1]
    n_img = r // LP
    heads = d // HDIM
    size = len(dy_out) + 1
    half = dy_out[0].shape[0]
    kept = [out((r, d), F32), out((r, d), BF), out((r, 3 * d), BF), out((n_img * heads, LP, LP), BF), out((r, d), BF)]
    results = kept + [out((r, d), F32), out((r, d), BF), out((2, r, f), BF), out((2, r, f), BF)] + kept + [out((r, d), BF)]
    shapes = results + [out(w.shape, BF) for w in own_w] + [out((half, d), BF)] * (size - 1)
    D, V = pltpu.SemaphoreType.DMA, pltpu.VMEM
    any_ = pl.BlockSpec(memory_space=pl.ANY)
    vm = pl.BlockSpec(memory_space=pltpu.VMEM)
    got = pl.pallas_call(
        functools.partial(forward_body, n_img, size),
        in_specs=[vm] * 2 + [any_] * (len(own_w) + size - 1), out_specs=[any_] * len(shapes), out_shape=shapes,
        scratch_shapes=[V((2,) + w.shape, BF) for w in own_w[:6]] + [V(o.shape, o.dtype) for o in results]
        + [D((6,)), D((8,)), D((8,)), D((6,)), D((len(results),)), D((size - 1,)), D((size - 1,))],
        compiler_params=pltpu.CompilerParams(collective_id=2, has_side_effects=True, vmem_limit_bytes=VMEM_BYTES),
        cost_estimate=pl.CostEstimate(flops=16 * r * d * d + 8 * r * d * f, bytes_accessed=80 * r * d, transcendentals=0),
    )(x, gains, *own_w, *dy_out)
    n = len(results)
    return got[:n], got[n : n + 8], got[n + 8 :]


def routing_body(experts, capacity, half, rows_ref, dy_ref, tr_ref, col_ref, *refs):
    out_refs, tmp = refs[:-1], refs[-1]
    n_img = rows_ref.shape[0]
    slots = experts * half
    core = lax.axis_index("mdl")
    own_img = n_img // 2
    tall = lax.broadcasted_iota(I32, (max(experts, 8), LQ), 0)
    hots, priors = [], []
    for i in range(n_img):
        r = rows_ref[i]
        live = r[3:4, :] > 0
        hots.append((((tall == r[0:1, :]) | (tall == r[1:2, :])) & live).astype(F32).astype(BF))
        priors.append(r.astype(F32).T[:, 2:3])
    for i in range(n_img):
        r = rows_ref[i]
        rank = None
        for k in range(n_img):
            part = nn(hots[k], (priors[k] < r[2:3, :].astype(F32)).astype(F32).astype(BF))
            rank = part if rank is None else rank + part
        for k in range(TOPK):
            e = r[k : k + 1, :]
            mine = jnp.sum(jnp.where(tall == e, rank, 0.0), axis=0, keepdims=True).astype(I32)
            side = (mine >= half).astype(I32)
            slot = side * slots + e * half + mine - side * half
            tr_ref[i, k : k + 1, :] = jnp.where((mine < capacity) & (r[3:4, :] > 0), slot, -1)
        tr_ref[i, TOPK:, :] = jnp.full((8 - TOPK, LQ), -1, I32)
    for i in range(own_img):
        at = core * own_img + i
        for k in range(TOPK):
            t = tr_ref[at, k : k + 1, :]
            there = t - (1 - core) * slots
            tmp[k : k + 1, :] = t - core * slots
            tmp[TOPK + k : TOPK + k + 1, :] = jnp.where(there < slots, there, -1)
        tmp[4:8, :] = rows_ref[at, 0:4, :]
        tmp[6:7, :] = rows_ref[at, 3:4, :]
        col_ref[i * LP : (i + 1) * LP, :] = tmp[...].astype(F32).T[:LP, :].astype(I32)
    z = lax.axis_index("exp")
    for j, o_ref in enumerate(out_refs):
        at = core * slots + (beside(z, j) * half if len(out_refs) > 1 else 0)
        total = None
        for i in range(n_img):
            part = nn(slot_hots(tr_ref[i], at, o_ref.shape[0]), dy_ref[i * LP : (i + 1) * LP, :])
            total = part if total is None else total + part
        o_ref[...] = total.astype(BF)


def slot_hots(t, base, count):
    place = lax.broadcasted_iota(I32, (count, LP), 0) + base
    return ((place == t[0:1, :LP]) | (place == t[1:2, :LP])).astype(F32).astype(BF)


def dispatch_body(experts, half, tr_ref, own_ref, oth_ref, y_ref):
    core = lax.axis_index("mdl")
    own_img = own_ref.shape[0] // LP
    total = None
    for a, v in ((core, own_ref), (1 - core, oth_ref)):
        for i in range(own_img):
            hot = slot_hots(tr_ref[a * own_img + i], core * experts * half, experts * half)
            part = nn(hot, v[i * LP : (i + 1) * LP, :])
            total = part if total is None else total + part
    y_ref[...] = total.astype(BF)


def router_probs(h, router, experts):
    logits = nt(h, router)
    lane = lax.broadcasted_iota(I32, logits.shape, 1)
    logits = jnp.where(lane < experts, logits, -1e30)
    e = jnp.exp(logits - jnp.max(logits, axis=-1, keepdims=True))
    return e / jnp.sum(e, axis=-1, keepdims=True), lane


def expert_body(experts, x_ref, dy_ref, router_ref, im, io, tm, to,
                eout_ref, ret_ref, act_ref, dz_ref, wd_ref, acc_ref, dx_ref):
    step = pl.program_id(0)
    d = x_ref.shape[1]

    @pl.when(step == 0)
    def _():
        probs, lane = router_probs(x_ref[...], router_ref[...], experts)
        gate = jnp.sum(jnp.where(lane == lax.axis_index("exp"), probs, 0.0), axis=-1, keepdims=True)
        wd_ref[...] = (gate * dy_ref[...].astype(F32)).astype(BF)
        acc_ref[...] = jnp.zeros_like(acc_ref)
        dx_ref[...] = jnp.zeros_like(dx_ref)

    for half, (wi, wo) in enumerate(((im, tm), (io, to))):
        a, s = gelu_parts(nn(x_ref[...], wi[...]))
        act = a.astype(BF)
        act_ref[half] = act
        acc_ref[...] += nn(act, wo[...])
        dz = (nt(wd_ref[...], wo[...]) * s).astype(BF)
        dz_ref[half] = dz
        dx_ref[...] += nt(dz, wi[...])

    @pl.when(step == pl.num_programs(0) - 1)
    def _():
        eout = acc_ref[...].astype(BF)
        eout_ref[...] = eout
        ret_ref[:, :d] = dx_ref[...].astype(BF)
        dgate = jnp.sum(dy_ref[...].astype(F32) * eout.astype(F32), axis=-1, keepdims=True)
        high = dgate.astype(BF).astype(F32)
        lane = lax.broadcasted_iota(I32, (x_ref.shape[0], LANES), 1)
        ret_ref[:, d:] = jnp.where(lane < LANES // 2, high, dgate - high).astype(BF)


def expert_forward_backward(x, dy, router, im, io, tm, to, experts):
    r, d = x.shape
    f = im.shape[1]
    t = tile_of(f) // 2
    col = pl.BlockSpec((d, t), lambda i: (0, i))
    row = pl.BlockSpec((t, d), lambda i: (i, 0))
    hid = pl.BlockSpec((2, r, t), lambda i: (0, 0, i))
    return call(
        functools.partial(expert_body, experts),
        [out((r, d), BF), out((r, d + LANES), BF), out((2, r, f), BF), out((2, r, f), BF), out((r, d), BF)],
        x, dy, router, im, io, tm, to, grid=(f // t,),
        in_specs=[whole((r, d)), whole((r, d)), whole(router.shape), col, col, row, row],
        out_specs=[whole((r, d)), whole((r, d + LANES)), hid, hid, whole((r, d))],
        scratch=[pltpu.VMEM((r, d), F32), pltpu.VMEM((r, d), F32)], flops=16 * r * d * f,
    )


def expert_weights_body(x_ref, wd_ref, act_ref, dz_ref, gm_ref, go_ref, xt_ref, wt_ref):
    @pl.when(pl.program_id(0) == 0)
    def _():
        xt_ref[...] = x_ref[...].T
        wt_ref[...] = wd_ref[...].T

    for half, g in enumerate((gm_ref, go_ref)):
        g[0] = nn(xt_ref[...], dz_ref[half]).astype(BF)
        g[1] = nn(wt_ref[...], act_ref[half]).astype(BF)


def expert_weights(x, wd, act, dz):
    r, d = x.shape
    f = act.shape[2]
    t = tile_of(f) // 2
    hid = pl.BlockSpec((2, r, t), lambda i: (0, 0, i))
    grad = pl.BlockSpec((2, d, t), lambda i: (0, 0, i))
    return call(
        expert_weights_body, [out((2, d, f), BF), out((2, d, f), BF)], x, wd, act, dz, grid=(f // t,),
        in_specs=[whole((r, d)), whole((r, d)), hid, hid], out_specs=[grad, grad],
        scratch=[pltpu.VMEM((d, r), BF), pltpu.VMEM((d, r), BF)], flops=8 * r * d * f,
    )


def merge(col_ref, k, ab_ref, n):
    slots = ab_ref.shape[1]
    lane = lax.broadcasted_iota(I32, (n, slots), 1)
    rows = None
    for side in range(2):
        hot = (lane == col_ref[:, 2 * side + k : 2 * side + k + 1]).astype(F32).astype(BF)
        part = nn(hot, ab_ref[side])
        rows = part if rows is None else rows + part
    return rows


def merge_blocks(col_ref, k, blocks, n):
    rows = None
    for side in range(2):
        for e, ref in blocks[side]:
            half = ref.shape[0]
            lane = lax.broadcasted_iota(I32, (n, half), 1) + e * half
            hot = (lane == col_ref[:, 2 * side + k : 2 * side + k + 1]).astype(F32).astype(BF)
            part = nn(hot, ref[...])
            rows = part if rows is None else rows + part
    return rows


def mixture_backward_core(experts, x_ref, gain, h_ref, router_ref, dy_ref, col_ref, ab_ref, dr_ref):
    n, d = x_ref.shape
    probs, lane = router_probs(h_ref[...], router_ref[...], experts)
    dh = jnp.zeros((n, d), F32)
    dsoft = jnp.zeros(probs.shape, F32)
    for k in range(TOPK):
        part = merge(col_ref, k, ab_ref, n)
        dh = dh + part[:, :d]
        dgate = part[:, d : d + 1] + part[:, d + LANES // 2 : d + LANES // 2 + 1]
        dsoft = dsoft + jnp.where(lane == col_ref[:, 4 + k : 5 + k], dgate, 0.0)
    dlog = (probs * (dsoft - jnp.sum(dsoft * probs, axis=-1, keepdims=True))).astype(BF)
    dr_ref[...] = tn(dlog, h_ref[...])
    dh = dh + nn(dlog, router_ref[...])
    nrm, rr, _ = norm_forward(x_ref[...], gain)
    dv, dw = norm_backward(nrm, rr, gain, dh)
    return own_rows(dy_ref, n).astype(F32) * col_ref[:, 6:7].astype(F32) + dv, dw


def mixture_attention_backward_body(n_img, experts, x3_ref, h4_ref, router_ref, dy_ref, col_ref, ret_ref, x_ref, g_ref, h_ref,
                                    qkv_ref, p_ref, o_ref, qm, qo, om, oo, dx_ref, dw3_ref, dw4_ref, dr_ref, gm_ref, go_ref,
                                    dx3, do_ref, dqkv_ref, tr_ref):
    grad, dw4 = mixture_backward_core(experts, x3_ref, g_ref[3:4, :], h4_ref, router_ref, dy_ref, col_ref, ret_ref, dr_ref)
    dx3[...] = grad
    dw4_ref[...] = dw4
    dx, dw3 = attention_backward_core(
        n_img, lambda: dx3[...], x_ref, g_ref[2:3, :], h_ref, qkv_ref, p_ref, o_ref, qm, qo, om, oo,
        gm_ref, go_ref, do_ref, dqkv_ref, tr_ref)
    dx_ref[...] = dx
    dw3_ref[...] = dw3


def mixture_attention_backward(experts, x3, h4, router, dy, col, ret, x, gains, kept, qm, qo, om, oo):
    r, d = x.shape
    c = qm.shape[2]
    n_img = r // LP
    heads = d // HDIM
    shapes = [out((r, d), F32), out((1, d), F32), out((1, d), F32), out(router.shape, F32),
              out((3 * d + d, c), BF), out((3 * d + d, c), BF)]
    return call(functools.partial(mixture_attention_backward_body, n_img, experts), shapes,
                x3, h4, router, dy, col, ret, x, gains, *kept, qm, qo, om, oo,
                scratch=[pltpu.VMEM((r, d), F32)] + attention_backward_scratch(r, d),
                flops=4 * r * d * d * 4 + 8 * n_img * heads * LP * LP * LANES + 8 * r * ret.shape[1] * d)


def mixture_output(experts, x_ref, h_ref, router_ref, col_ref, rows_of):
    n, d = x_ref.shape
    probs, lane = router_probs(h_ref[...], router_ref[...], experts)
    mixed = jnp.zeros((n, d), F32)
    for k in range(TOPK):
        gate = jnp.sum(jnp.where(lane == col_ref[:, 4 + k : 5 + k], probs, 0.0), axis=-1, keepdims=True)
        mixed = mixed + gate * rows_of(k)
    return (col_ref[:, 6:7].astype(F32) * (x_ref[...] + mixed)).astype(BF)


def mixture_output_body(experts, x_ref, h_ref, router_ref, col_ref, ab_ref, y_ref):
    y = mixture_output(experts, x_ref, h_ref, router_ref, col_ref, lambda k: merge(col_ref, k, ab_ref, x_ref.shape[0]))
    for i in range(y_ref.shape[0]):
        y_ref[i] = y[i * LP : i * LP + L]


def flip(axis, bit):
    size = lax.axis_size(axis)
    return [(i, i ^ bit) for i in range(size)]


def bits_of(axis):
    size = lax.axis_size(axis)
    return [1 << b for b in range(size.bit_length() - 1)]


def other_core(v):
    return lax.ppermute(v, "mdl", flip("mdl", 1))


def add16(a, b):
    return (a.astype(F32) + b.astype(F32)).astype(BF)


def halve(v, axis, bit):
    side = (lax.axis_index(axis) // bit) % 2
    n = v.shape[0] // 2
    keep = lax.dynamic_slice_in_dim(v, side * n, n)
    send = lax.dynamic_slice_in_dim(v, (1 - side) * n, n)
    return add16(keep, lax.ppermute(send, axis, flip(axis, bit)))


def double(v, axis, bit):
    side = (lax.axis_index(axis) // bit) % 2
    got = lax.ppermute(v, axis, flip(axis, bit))
    return jnp.where(side == 0, jnp.concatenate([v, got]), jnp.concatenate([got, v]))


def sum_everywhere(v):
    n = v.shape[0] // 2
    bits = bits_of("grp")
    parts = []
    for part, order in ((v[:n], bits), (v[n:], bits[::-1])):
        for bit in order:
            part = halve(part, "grp", bit)
        parts.append(part)
    size = lax.axis_size("exp")
    joined = jnp.concatenate(parts)
    rows = joined.shape[0] // size
    spread = lax.all_to_all(joined.reshape(size, rows, -1), "exp", 0, 0, tiled=True)
    mine = jnp.sum(spread.astype(F32), axis=0).astype(BF)
    joined = lax.all_gather(mine, "exp", axis=0, tiled=True)
    h = joined.shape[0] // 2
    done = []
    for part, order in ((joined[:h], bits), (joined[h:], bits[::-1])):
        for bit in order[::-1]:
            part = double(part, "grp", bit)
        done.append(part)
    return jnp.concatenate(done)


def small_sum(v):
    for axis in ("mdl", "grp", "exp"):
        for bit in bits_of(axis):
            v = v + lax.ppermute(v, axis, flip(axis, bit))
    return v


def reduce_body(n_in, per, n_exp, experts, *refs):
    mine = refs[:n_in]
    other = refs[n_in : 2 * n_in]
    dg = refs[2 * n_in : 2 * n_in + 4]
    dr_ref, x3_ref, h4_ref, router_ref, col_ref = refs[2 * n_in + 4 : 2 * n_in + 9]
    eouts = refs[2 * n_in + 9 : 2 * n_in + 13]
    image_ref = refs[2 * n_in + 13]
    outs = refs[2 * n_in + 14 :]
    qkv2, proj2, fc_in, fc_out, qkv1, proj1, sum_ref, y_ref, gx_ref = outs[:9]
    (acc, got, r1, r2, zr, zz, zs, sm, y_own, load_sem, m_send, m_recv, x_send, x_recv, z_send, z_recv, s_send, s_recv,
     i_local, i_send, i_recv, e_oth, e_send, e_recv) = outs[9:]
    out_ref = got
    n = n_in * per
    rows = acc.shape[2]
    h, q = rows // 2, rows // 4
    t = q // n_exp
    g = lax.axis_index("grp")
    z = lax.axis_index("exp")
    core = lax.axis_index("mdl")
    bx, by = g % 2, g // 2
    flat = {"x": g + 1 - 2 * bx, "y": g + 2 - 4 * by}
    order = (("x", "y"), ("y", "x"))
    bits = ((bx, by), (by, bx))

    barrier = pltpu.get_barrier_semaphore()
    others = [{"mdl": 1 - core}, {"grp": flat["x"]}, {"grp": flat["y"]}]
    others += [{"exp": (z + o) % n_exp} for o in range(1, n_exp)]
    for dev in others:
        pl.semaphore_signal(barrier, inc=1, device_id=dev, device_id_type=MESH)
    pl.semaphore_wait(barrier, len(others))

    def load(c):
        i, p = c // per, c % per
        return pltpu.make_async_copy(mine[i].at[p], acc.at[c], load_sem.at[c])

    def swap(c):
        i, p = c // per, c % per
        return pltpu.make_async_remote_copy(other[i].at[p], got.at[c], m_send.at[c], m_recv.at[c],
                                            device_id={"mdl": 1 - core}, device_id_type=MESH)

    for c in range(n):
        swap(c).start()
        load(c).start()

    own_img = image_ref.shape[0]
    places = pl.ds(core * own_img, own_img)

    def image_copies(k, src, dst):
        return (pltpu.make_async_copy(src, dst.at[places], i_local.at[k]),
                pltpu.make_async_remote_copy(src, dst.at[places], i_send.at[k], i_recv.at[k], device_id={"mdl": 1 - core},
                                             device_id_type=MESH))

    def image_come(k, src, dst):
        there = pl.ds((1 - core) * own_img, own_img)
        return pltpu.make_async_remote_copy(src, dst.at[there], i_send.at[k], i_recv.at[k], device_id={"mdl": 1 - core},
                                            device_id_type=MESH)

    for cp in image_copies(0, image_ref, gx_ref):
        cp.start()

    e_copies = [pltpu.make_async_remote_copy(eouts[j], e_oth.at[j], e_send.at[j], e_recv.at[j], device_id={"mdl": 1 - core},
                                             device_id_type=MESH) for j in range(n_exp)]
    for cp in e_copies:
        cp.start()

    def swap_at(c):
        return pltpu.make_async_remote_copy(other[0].at[0], got.at[c], m_send.at[c], m_recv.at[c],
                                            device_id={"mdl": 1 - core}, device_id_type=MESH)

    def load_at(c):
        return pltpu.make_async_copy(mine[0].at[0], acc.at[c], load_sem.at[c])

    def over(u, leg, src, dst, slot, c):
        return pltpu.make_async_remote_copy(src, dst, x_send.at[slot, u, c], x_recv.at[slot, u, c],
                                            device_id={"grp": flat[order[u][leg]]}, device_id_type=MESH)

    def first(u, c):
        return over(u, 0, acc.at[c, u, pl.ds(pl.multiple_of((1 - bits[u][0]) * h, h), h)], r1.at[c, u], 0, c)

    def second(u, c):
        return over(u, 1, r1.at[c, u, pl.ds(pl.multiple_of((1 - bits[u][1]) * q, q), q)], r2.at[c, u], 1, c)

    def along(u, c, o):
        return pltpu.make_async_remote_copy(
            r2.at[c, u, pl.ds(pl.multiple_of(((z + o) % n_exp) * t, t), t)], zr.at[c, u, o - 1],
            z_send.at[0, u, o - 1, c], z_recv.at[0, u, o - 1, c],
            device_id={"exp": (z + o) % n_exp}, device_id_type=MESH)

    def place(u):
        return bits[u][0] * h + bits[u][1] * q

    def back(u, c, o):
        here = out_ref.at[c, u, pl.ds(pl.multiple_of(place(u) + z * t, t), t)]
        return pltpu.make_async_remote_copy(here, here, z_send.at[1, u, o - 1, c], z_recv.at[1, u, o - 1, c],
                                            device_id={"exp": (z + o) % n_exp}, device_id_type=MESH)

    def third(u, c):
        here = out_ref.at[c, u, pl.ds(pl.multiple_of(place(u), q), q)]
        return over(u, 1, here, here, 2, c)

    def fourth(u, c):
        here = out_ref.at[c, u, pl.ds(pl.multiple_of(bits[u][0] * h, h), h)]
        return over(u, 0, here, here, 3, c)

    def plus(a, b):
        return (a.astype(F32) + b.astype(F32)).astype(BF)

    def s1(c):
        load_at(c).wait()
        swap_at(c).wait_recv()
        for u in range(2):
            acc[c, u] = plus(acc[c, u], got[c, u])
            first(u, c).start()

    def s2(c):
        for u in range(2):
            first(u, c).wait_recv()
            keep = acc[c, u, pl.ds(pl.multiple_of(bits[u][0] * h, h), h)]
            r1[c, u] = plus(keep, r1[c, u])
            second(u, c).start()

    def s3(c):
        for u in range(2):
            second(u, c).wait_recv()
            keep = r1[c, u, pl.ds(pl.multiple_of(bits[u][1] * q, q), q)]
            r2[c, u] = plus(keep, r2[c, u])
            for o in range(1, n_exp):
                along(u, c, o).start()

    def s4(c):
        for u in range(2):
            total = r2[c, u, pl.ds(pl.multiple_of(z * t, t), t)].astype(F32)
            for o in range(1, n_exp):
                along(u, c, o).wait_recv()
                total = total + zr[c, u, o - 1].astype(F32)
            out_ref[c, u, pl.ds(pl.multiple_of(place(u) + z * t, t), t)] = total.astype(BF)
            for o in range(1, n_exp):
                back(u, c, o).start()

    def s5(c):
        for u in range(2):
            for o in range(1, n_exp):
                back(u, c, o).wait_recv()
            third(u, c).start()

    def s6(c):
        for u in range(2):
            third(u, c).wait_recv()
            fourth(u, c).start()

    def s7(c):
        for u in range(2):
            fourth(u, c).wait_recv()
        for k in range(n):

            @pl.when(c == k)
            def _(k=k):
                natural(k)

    zc = 0
    e, e2, e4 = rows // n_exp, rows // n_exp // 2, rows // n_exp // 4

    def z_out(u, o):
        return pltpu.make_async_remote_copy(
            acc.at[zc, u, pl.ds(pl.multiple_of(((z + o) % n_exp) * e, e), e)], zz.at[u, o - 1],
            z_send.at[0, u, o - 1, zc], z_recv.at[0, u, o - 1, zc], device_id={"exp": (z + o) % n_exp}, device_id_type=MESH)

    def z_first(u):
        return over(u, 0, zs.at[u, pl.ds(pl.multiple_of((1 - bits[u][0]) * e2, e2), e2)], r1.at[zc, u, 0:e2], 0, zc)

    def z_second(u):
        return over(u, 1, r1.at[zc, u, pl.ds(pl.multiple_of((1 - bits[u][1]) * e4, e4), e4)], r2.at[zc, u, 0:e4], 1, zc)

    def z_third(u):
        here = out_ref.at[zc, u, pl.ds(pl.multiple_of(z * e + bits[u][0] * e2 + bits[u][1] * e4, e4), e4)]
        return over(u, 1, here, here, 2, zc)

    def z_fourth(u):
        here = out_ref.at[zc, u, pl.ds(pl.multiple_of(z * e + bits[u][0] * e2, e2), e2)]
        return over(u, 0, here, here, 3, zc)

    def z_back(u, o):
        here = out_ref.at[zc, u, pl.ds(pl.multiple_of(z * e, e), e)]
        return pltpu.make_async_remote_copy(here, here, z_send.at[1, u, o - 1, zc], z_recv.at[1, u, o - 1, zc],
                                            device_id={"exp": (z + o) % n_exp}, device_id_type=MESH)

    def z1():
        load_at(zc).wait()
        swap_at(zc).wait_recv()
        for u in range(2):
            acc[zc, u] = plus(acc[zc, u], got[zc, u])
            for o in range(1, n_exp):
                z_out(u, o).start()

    def z2():
        for u in range(2):
            total = acc[zc, u, pl.ds(pl.multiple_of(z * e, e), e)].astype(F32)
            for o in range(1, n_exp):
                z_out(u, o).wait_recv()
                total = total + zz[u, o - 1].astype(F32)
            zs[u] = total.astype(BF)
            z_first(u).start()

    def z3():
        for u in range(2):
            z_first(u).wait_recv()
            r1[zc, u, 0:e2] = plus(zs[u, pl.ds(pl.multiple_of(bits[u][0] * e2, e2), e2)], r1[zc, u, 0:e2])
            z_second(u).start()

    def z4():
        for u in range(2):
            z_second(u).wait_recv()
            mine_rows = pl.ds(pl.multiple_of(z * e + bits[u][0] * e2 + bits[u][1] * e4, e4), e4)
            out_ref[zc, u, mine_rows] = plus(r1[zc, u, pl.ds(pl.multiple_of(bits[u][1] * e4, e4), e4)], r2[zc, u, 0:e4])
            z_third(u).start()

    def z5():
        for u in range(2):
            z_third(u).wait_recv()
            z_fourth(u).start()

    def z6():
        for u in range(2):
            z_fourth(u).wait_recv()
            for o in range(1, n_exp):
                z_back(u, o).start()

    def z7():
        for u in range(2):
            for o in range(1, n_exp):
                z_back(u, o).wait_recv()
        natural(zc)

    def drain(c, _):
        swap_at(c).wait_send()
        for u in range(2):
            for make in (first, second, third, fourth):
                make(u, c).wait_send()
            for o in range(1, n_exp):
                along(u, c, o).wait_send()
                back(u, c, o).wait_send()
        return 0

    legs = [({"mdl": 1 - core}), ({"grp": flat["x"]}), ({"grp": flat["y"]})]
    base = 2 * len(legs) + 1

    def small_leg(i):
        return pltpu.make_async_remote_copy(sm.at[2 * i], sm.at[2 * i + 1], s_send.at[i], s_recv.at[i], device_id=legs[i],
                                            device_id_type=MESH)

    def small_along(o):
        return pltpu.make_async_remote_copy(sm.at[base - 1], sm.at[base + z], s_send.at[len(legs) + o - 1],
                                            s_recv.at[len(legs) + o - 1], device_id={"exp": (z + o) % n_exp},
                                            device_id_type=MESH)

    def small_step(i):
        if i == 0:
            sm[0] = jnp.zeros(sm.shape[1:], F32)
            for k in range(4):
                sm[0, k : k + 1, :] = dg[k][...]
            sm[0, 4 : 4 + experts, :] = dr_ref[:experts, :]
        else:
            small_leg(i - 1).wait()
            sm[2 * i] = sm[2 * i - 2] + sm[2 * i - 1]
        if i < len(legs):
            small_leg(i).start()
        else:
            sm[pl.ds(base + z, 1)] = sm[pl.ds(base - 1, 1)]
            for o in range(1, n_exp):
                small_along(o).start()

    def natural(c):
        i, p = c // per, c % per
        side = rows // 2
        for u in range(2):
            v = 2 * p + u
            if i in (0, 3):
                qkv, proj = (qkv2, proj2) if i == 0 else (qkv1, proj1)
                if v < 3:
                    qkv[v] = out_ref[c, u]
                else:
                    for k in range(2):
                        proj[:, k * side : (k + 1) * side] = out_ref[c, u, k * side : (k + 1) * side]
            elif i == 1:
                fc_in[:, v * side : (v + 1) * side] = out_ref[c, u]
            else:
                fc_out[v % 2 * rows : (v % 2 + 1) * rows, v // 2 * side : (v // 2 + 1) * side] = out_ref[c, u]

    steps = (s1, s2, s3, s4, s5, s6, s7)
    waves = n - 1 + len(steps) - 1
    late = waves - 2
    z_steps = ((0, z1), (2, z2), (3, z3), (4, z4), (5, z5), (6, z6), (late, z7))
    small_steps = {1: 0, 3: 1, 5: 2, 7: 3}

    def wave(tau, _):
        for s, step in enumerate(steps):
            c = tau - s + 1

            @pl.when((c >= 1) & (c < n))
            def _(step=step, c=c):
                step(c)

        for at, step in z_steps:
            pl.when(tau == at)(step)
        for at, i in small_steps.items():
            pl.when(tau == at)(functools.partial(small_step, i))
        return 0

    first_waves = 2
    lax.fori_loop(0, first_waves, wave, 0)
    for cp in e_copies:
        cp.wait_recv()
    blocks = [[(beside(z, j), eouts[j]) for j in range(n_exp)], [(beside(z, j), e_oth.at[j]) for j in range(n_exp)]]
    y = mixture_output(experts, x3_ref, h4_ref, router_ref, col_ref, lambda k: merge_blocks(col_ref, k, blocks, x3_ref.shape[0]))
    for i in range(own_img):
        y_own[i] = y[i * LP : i * LP + L]
    for cp in image_copies(1, y_own, y_ref):
        cp.start()
    lax.fori_loop(first_waves, waves, wave, 0)
    for cp in e_copies:
        cp.wait_send()
    for k, (src, dst) in enumerate(((image_ref, gx_ref), (y_own, y_ref))):
        local, sent = image_copies(k, src, dst)
        local.wait()
        sent.wait_send()
        image_come(k, src, dst).wait_recv()
    lax.fori_loop(1, n, drain, 0)
    swap_at(zc).wait_send()
    for u in range(2):
        for make in (z_first, z_second, z_third, z_fourth):
            make(u).wait_send()
        for o in range(1, n_exp):
            z_out(u, o).wait_send()
            z_back(u, o).wait_send()
    for o in range(1, n_exp):
        small_along(o).wait()
    total = sm[base]
    for k in range(1, n_exp):
        total = total + sm[base + k]
    sum_ref[...] = total


def reduce_all(mine, other, dgs, dr, x3, h4, router, col, eouts, image, n_exp, experts):
    per, _, rows, c = mine[0].shape
    n = len(mine) * per
    d, f = 2 * c, 4 * c
    h, q = rows // 2, rows // 4
    t = q // n_exp
    small = (-(-(4 + experts) // 8) * 8, d)
    n_img, length, _ = image.shape
    D, V = pltpu.SemaphoreType.DMA, pltpu.VMEM
    any_ = pl.BlockSpec(memory_space=pl.ANY)
    vm = pl.BlockSpec(memory_space=pltpu.VMEM)
    return pl.pallas_call(
        functools.partial(reduce_body, len(mine), per, n_exp, experts),
        in_specs=[any_] * (2 * len(mine)) + [vm] * 13 + [any_],
        out_specs=[vm] * 7 + [any_] * 2,
        out_shape=[out((3, d, c), BF), out((c, d), BF), out((d, f), BF), out((f, d), BF), out((3, d, c), BF), out((c, d), BF),
                   out(small, F32), out((2 * n_img, length, d), BF), out((2 * n_img, length, d), BF)],
        scratch_shapes=[
            V((n, 2, rows, c), BF), V((n, 2, rows, c), BF), V((n, 2, h, c), BF), V((n, 2, q, c), BF),
            V((n, 2, n_exp - 1, t, c), BF), V((2, n_exp - 1, rows // n_exp, c), BF), V((2, rows // n_exp, c), BF),
            V((7 + n_exp,) + small, F32), V((n_img, length, d), BF),
            D((n,)), D((n,)), D((n,)), D((4, 2, n)), D((4, 2, n)), D((2, 2, n_exp - 1, n)), D((2, 2, n_exp - 1, n)),
            D((3 + n_exp,)), D((3 + n_exp,)), D((2,)), D((2,)), D((2,)), V((n_exp,) + eouts[0].shape, BF), D((n_exp,)), D((n_exp,)),
        ],
        compiler_params=pltpu.CompilerParams(collective_id=0, has_side_effects=True, vmem_limit_bytes=VMEM_BYTES),
        cost_estimate=pl.CostEstimate(flops=8 * x3.shape[0] * x3.shape[0] * d, bytes_accessed=n * 8 * rows * c, transcendentals=0),
    )(*mine, *other, *dgs, dr, x3, h4, router, col, *eouts, image)


def expert_exchange_body(experts, half, h4_ref, tr_ref, dy0, dy1, dy2, dy3, router_ref, im, io, tm, to,
                         ret_ref, e0, e1, e2, e3, gw_ref,
                         h_oth, part, xo, x, wi, wo, act, dz, wd, acc, dxa, rsend, gscr, ggot, xt, wt,
                         w_sem, swap_sem, x_send, x_recv, r_send, r_recv, f_send, f_recv, g_send, g_recv, g_sem):
    n, d = h4_ref.shape
    f = im.shape[1]
    t = 256 if f % 256 == 0 else tile_of(f)
    z = lax.axis_index("exp")
    core = lax.axis_index("mdl")
    partner = {"mdl": 1 - core}
    size = experts
    near_first = [1, 3, 2]

    out_grad, eouts = (dy0, dy1, dy2, dy3), (e0, e1, e2, e3)

    def there(j):
        return beside(z, j)

    loads = [pltpu.make_async_copy(src, dst, w_sem.at[k]) for k, (src, dst) in enumerate(
        ((im, wi.at[0]), (io, wi.at[1]), (tm, wo.at[0]), (to, wo.at[1])))]
    for cp in loads:
        cp.start()
    barrier = pltpu.get_barrier_semaphore()
    for dev in [partner] + [{"exp": there(j)} for j in range(1, size)]:
        pl.semaphore_signal(barrier, inc=1, device_id=dev, device_id_type=MESH)
    pl.semaphore_wait(barrier, size)
    swap = pltpu.make_async_remote_copy(h4_ref, h_oth, swap_sem.at[0], swap_sem.at[1], device_id=partner, device_id_type=MESH)
    swap.start()

    own_img = n // LP
    base = core * size * half

    def spread(side, v, j):
        total = None
        for i in range(own_img):
            p = nn(slot_hots(tr_ref[side * own_img + i], base + there(j) * half, half), v[i * LP : (i + 1) * LP, :])
            total = p if total is None else total + p
        return total

    def rows(j):
        return slice(j * half, (j + 1) * half)

    def place(e):
        return pl.ds(pl.multiple_of(e * half, half), half)

    for j in near_first + [0]:
        part[rows(j), :] = spread(core, h4_ref, j)
    swap.wait_recv()
    sends = {}
    for j in near_first + [0]:
        block = (part[rows(j), :] + spread(1 - core, h_oth, j)).astype(BF)
        if j == 0:
            x[rows(0), :] = block
        else:
            xo[rows(j), :] = block
            sends[j] = pltpu.make_async_remote_copy(xo.at[rows(j)], x.at[rows(j)], x_send.at[j], x_recv.at[j],
                                                    device_id={"exp": there(j)}, device_id_type=MESH)
            sends[j].start()

    returns, forwards = {}, {}

    def forward(j):
        here = ret_ref.at[0, place(there(j))]
        forwards[j] = pltpu.make_async_remote_copy(here, ret_ref.at[1, place(there(j))], f_send.at[j], f_recv.at[j],
                                                   device_id=partner, device_id_type=MESH)
        forwards[j].start()

    def run(blocks):
        r0, r1 = blocks[0] * half, (blocks[-1] + 1) * half
        m = r1 - r0
        for j in blocks:
            probs, lane = router_probs(x[rows(j), :], router_ref[...], experts)
            gate = jnp.sum(jnp.where(lane == z, probs, 0.0), axis=-1, keepdims=True)
            wd[rows(j), :] = (gate * out_grad[j][...].astype(F32)).astype(BF)
        acc[0:m, :] = jnp.zeros((m, d), F32)
        dxa[0:m, :] = jnp.zeros((m, d), F32)

        def tile(i, _):
            at = pl.ds(pl.multiple_of(i * t, t), t)
            for side in range(2):
                a, s = gelu_parts(nn(x[r0:r1, :], wi[side, :, at]))
                a = a.astype(BF)
                act[side, r0:r1, at] = a
                acc[0:m, :] += nn(a, wo[side, at, :])
                g = (nt(wd[r0:r1, :], wo[side, at, :]) * s).astype(BF)
                dz[side, r0:r1, at] = g
                dxa[0:m, :] += nt(g, wi[side, :, at])
            return 0

        lax.fori_loop(0, f // t, tile, 0)
        for b, j in enumerate(blocks):
            here = slice(b * half, (b + 1) * half)
            e_rows = acc[here, :].astype(BF)
            eouts[j][...] = e_rows
            dgate = jnp.sum(out_grad[j][...].astype(F32) * e_rows.astype(F32), axis=-1, keepdims=True)
            high = dgate.astype(BF).astype(F32)
            lane = lax.broadcasted_iota(I32, (half, LANES), 1)
            extra = jnp.where(lane < LANES // 2, high, dgate - high).astype(BF)
            if j == 0:
                ret_ref[0, place(z), 0:d] = dxa[here, :].astype(BF)
                ret_ref[0, place(z), d:] = extra
                forward(0)
            else:
                rsend[rows(j), 0:d] = dxa[here, :].astype(BF)
                rsend[rows(j), d:] = extra
                returns[j] = pltpu.make_async_remote_copy(rsend.at[rows(j)], ret_ref.at[0, place(z)], r_send.at[j], r_recv.at[j],
                                                          device_id={"exp": there(j)}, device_id_type=MESH)
                returns[j].start()

    for cp in loads:
        cp.wait()
    sends[1].wait_recv()
    run([0, 1])
    for j in near_first[1:]:
        sends[j].wait_recv()
        run([j])

    xt[...] = x[...].T
    wt[...] = wd[...].T

    tiles = f // t

    def cols(i):
        return pl.ds(pl.multiple_of(i * t, t), t)

    def swapped(i):
        return pltpu.make_async_remote_copy(gscr.at[1, :, :, cols(i)], ggot.at[:, :, cols(i)], g_send.at[i], g_recv.at[i],
                                            device_id=partner, device_id_type=MESH)

    def stored(i):
        return pltpu.make_async_copy(gscr.at[0, :, :, cols(i)], gw_ref.at[:, :, cols(i)], g_sem.at[i])

    def weight_tile(i, _):
        for side in (1, 0):
            gscr[side, 0, :, cols(i)] = nn(xt[...], dz[side, :, cols(i)]).astype(BF)
            gscr[side, 1, :, cols(i)] = nn(wt[...], act[side, :, cols(i)]).astype(BF)
            if side == 1:
                swapped(i).start()
        return 0

    lax.fori_loop(0, tiles, weight_tile, 0)

    def sum_tile(i, _):
        swapped(i).wait_recv()
        for k in range(2):
            gscr[0, k, :, cols(i)] = (gscr[0, k, :, cols(i)].astype(F32) + ggot[k, :, cols(i)].astype(F32)).astype(BF)
        stored(i).start()
        return 0

    lax.fori_loop(0, tiles, sum_tile, 0)

    def recv_return(j):
        return pltpu.make_async_remote_copy(rsend.at[rows(j)], ret_ref.at[0, place(there(j))], r_send.at[j], r_recv.at[j],
                                            device_id={"exp": there(j)}, device_id_type=MESH)

    for j in near_first:
        recv_return(j).wait_recv()
        forward(j)

    def drain(i, _):
        stored(i).wait()
        swapped(i).wait_send()
        return 0

    lax.fori_loop(0, tiles, drain, 0)
    swap.wait_send()
    for j in range(size):
        if j:
            sends[j].wait_send()
            returns[j].wait_send()
        forwards[j].wait()


def expert_exchange(h4, tr, dys, router, im, io, tm, to, experts, half):
    n, d = h4.shape
    f = im.shape[1]
    s = experts * half
    tiles = f // (256 if f % 256 == 0 else tile_of(f))
    D, V = pltpu.SemaphoreType.DMA, pltpu.VMEM
    any_ = pl.BlockSpec(memory_space=pl.ANY)
    vm = pl.BlockSpec(memory_space=pltpu.VMEM)
    return pl.pallas_call(
        functools.partial(expert_exchange_body, experts, half),
        in_specs=[vm] * 7 + [any_] * 4,
        out_specs=[vm] * 5 + [any_],
        out_shape=[out((2, s, d + LANES), BF)] + [out((half, d), BF)] * 4 + [out((2, d, f), BF)],
        scratch_shapes=[
            V((n, d), BF), V((s, d), F32), V((s, d), BF), V((s, d), BF), V((2, d, f), BF), V((2, f, d), BF),
            V((2, s, f), BF), V((2, s, f), BF), V((s, d), BF), V((2 * half, d), F32), V((2 * half, d), F32),
            V((s, d + LANES), BF), V((2, 2, d, f), BF), V((2, d, f), BF), V((d, s), BF), V((d, s), BF),
            D((4,)), D((2,)), D((experts,)), D((experts,)), D((experts,)), D((experts,)), D((experts,)), D((experts,)),
            D((tiles,)), D((tiles,)), D((tiles,)),
        ],
        compiler_params=pltpu.CompilerParams(collective_id=1, has_side_effects=True, vmem_limit_bytes=VMEM_BYTES),
        cost_estimate=pl.CostEstimate(flops=24 * s * d * f, bytes_accessed=20 * d * f, transcendentals=0),
    )(h4, tr, *dys, router, im, io, tm, to)


FUSED = True


def on_device(images, counts, routes, priority, gain_one, qkv_one, out_one, gain_two, fc_in, fc_out, gain_three,
              qkv_two, out_two, gain_four, router, expert_in, expert_out, cotangent):
    n_slot, length, d = images.shape
    experts = router.shape[1]
    n_mdl = lax.axis_size("mdl")
    peers = lax.axis_size("exp")
    capacity = (25 * L * TOPK + 8 * experts - 1) // (8 * experts)
    half = -(-(-(-capacity // n_mdl)) // 16) * 16
    slots = experts * half
    own_img = n_slot // n_mdl
    f = fc_in.shape[1]
    c = qkv_one.shape[2]
    rows = own_img * LP
    core = lax.axis_index("mdl")
    per = 2
    unit = 4 * d // (2 * per)
    fused = FUSED and (lax.axis_size("grp"), peers, n_mdl) == (4, experts, 2) and peers == 4
    fused = fused and d == 2 * c and f == 4 * c and unit % (64 * peers) == 0

    def padded(v):
        return jnp.pad(v, ((0, 0), (0, LP - length), (0, 0))).reshape(n_slot * LP, -1)

    qm1, om1, im, tm, qm2, om2, em, fm = halves = (
        qkv_one, out_one, fc_in, fc_out, qkv_two, out_two, expert_in[0], expert_out[0])
    gains = jnp.stack([gain_one, gain_two, gain_three, gain_four])
    router_rows = jnp.pad(router.T, ((0, LANES - experts), (0, 0)))

    live = jnp.broadcast_to((jnp.arange(n_slot, dtype=I32) < counts[0, 0]).astype(I32)[:, None, None], (n_slot, 1, length))
    lines = jnp.concatenate([jnp.transpose(routes, (0, 2, 1)), priority.reshape(n_slot, 1, length), live], axis=1)
    lines = jnp.pad(lines, ((0, 0), (0, 4), (0, LQ - length)))
    dy = padded(cotangent)
    blocks = [(half, d)] * peers if fused else [(slots, d)]
    slot_rows, col, *dy_out = call(
        functools.partial(routing_body, experts, capacity, half),
        [out((n_slot, 8, LQ), I32), out((rows, 8), I32)] + [out(b, BF) for b in blocks], lines, dy,
        scratch=[pltpu.VMEM((8, LQ), I32)], flops=4 * slots * n_slot * LP * d,
    )
    def along_z(v):
        return [v[0]] + [lax.ppermute(v[j], "exp", [(i, i ^ j) for i in range(peers)]) for j in range(1, peers)]

    def exchange(v):
        shaped = v.reshape(peers, v.shape[0] // peers, v.shape[1])
        return lax.all_to_all(shaped, "exp", 0, 0, tiled=True).reshape(v.shape)

    x0 = padded(images)
    if fused:
        got, (qo1, oo1, io, to, qo2, oo2, eo, fo), dy_in = forward(x0, gains, halves, dy_out[1:], rows)
        x1, *kept1, x2, h2, act2, slope2, x3 = got[:10]
        kept3, h4 = got[10:14], got[14]
        dy_in = [dy_out[0], *dy_in]
    else:
        qo1, oo1, io, to, qo2, oo2, eo, fo = (other_core(w) for w in halves)
        dy_in = exchange(dy_out[0])
        x1, *kept1 = attention_forward(x0, rows, gains, 0, qm1, qo1, om1, oo1)
        x2, h2, act2, slope2 = mlp_forward(x1, gains, 1, im, io, tm, to)
        x3, *kept3, h4 = attention_forward(x2, rows, gains, 2, qm2, qo2, om2, oo2, tail=3)

    second = (x2, gains, kept3, qm2, qo2, om2, oo2)
    if fused:
        ret, *eout, ge = expert_exchange(h4, slot_rows, dy_in, router_rows, em, eo, fm, fo, experts, half)
        eback = along_z(eout)
    else:
        [h4_out] = call(functools.partial(dispatch_body, experts, half), [out((slots, d), BF)], slot_rows, h4, other_core(h4))
        h4_in = exchange(h4_out)
        eout, ret, eact, edz, ewd = expert_forward_backward(h4_in, dy_in, router_rows, em, eo, fm, fo, experts)
        ret, eout = exchange(ret), exchange(eout)
        ret, eback = jnp.stack([ret, other_core(ret)]), jnp.stack([eout, other_core(eout)])
        ge_mine, ge_other = expert_weights(h4_in, ewd, eact, edz)
        ge = add16(ge_mine, other_core(ge_other))
    dx2, dg3, dg4, dr, a2_mine, a2_other = mixture_attention_backward(experts, x3, h4, router_rows, dy, col, ret, *second)
    expert_sum = lax.psum_scatter(ge, "grp", scatter_dimension=1, tiled=True)

    dx1, dg2, gim, gio, gtm, gto = mlp_backward(dx2, x1, gains, 1, h2, act2, slope2, im, io, tm, to, c)
    image, dg1, a1_mine, a1_other = attention_backward(dx1, x0, gains, 0, kept1, qm1, qo1, om1, oo1)
    mines, others = (a2_mine, gim, gtm, a1_mine), (a2_other, gio, gto, a1_other)

    if fused:
        split = [[v.reshape(per, 2, unit, c) for v in side] for side in (mines, others)]
        qkv2, proj2, fi, fo_, qkv1, proj1, small, output, grad_images = reduce_all(
            *split, (dg1, dg2, dg3, dg4), dr, x3, h4, router_rows, col, eback, image, peers, experts)
    else:
        sums = [sum_everywhere(add16(a.reshape(4 * d, c), other_core(b.reshape(4 * d, c)))) for a, b in zip(mines, others)]
        small = small_sum(jnp.concatenate([dg1, dg2, dg3, dg4, dr[:experts]], axis=0))

        def panels(v):
            return jnp.concatenate([v[i] for i in range(v.shape[0])], axis=1)

        (qkv2, proj2), (qkv1, proj1) = (
            (v[: 3 * d].reshape(3, d, c), panels(v[3 * d :].reshape(d // c, c, c))) for v in (sums[0], sums[3]))
        fi, fo_ = panels(sums[1].reshape(f // c, d, c)), panels(sums[2].reshape(d // c, f, c))
        [own_out] = call(
            functools.partial(mixture_output_body, experts), [out((own_img, L, d), BF)], x3, h4, router_rows, col, eback,
            flops=8 * rows * slots * d)

        def both(v):
            there = other_core(v)
            return jnp.where(core == 0, jnp.concatenate([v, there]), jnp.concatenate([there, v]))

        output, grad_images = both(own_out), both(image)
    return (
        output, grad_images,
        small[0], qkv1.astype(F32), proj1.astype(F32), small[1], fi.astype(F32), fo_.astype(F32),
        small[2], qkv2.astype(F32), proj2.astype(F32), small[3], small[4 : 4 + experts].T,
        expert_sum[0].astype(F32)[None], expert_sum[1].astype(F32).T[None],
    )


def solution(mesh):
    token = P(("grp", "exp"), None, None)
    column, line = P(None, None, "mdl"), P("mdl", None)
    return jax.shard_map(
        on_device,
        mesh=mesh,
        in_specs=(token, P("grp", "exp"), token, P(("grp", "exp"), None), P(), column, line, P(), P(None, "mdl"), line,
                  P(), column, line, P(), P(), P("exp", None, "mdl"), P("exp", "mdl", None), token),
        out_specs=(token, token, P(), column, line, P(), P(None, "mdl"), line, P(), column, line, P(), P(),
                   P("exp", "grp", "mdl"), P("exp", "mdl", "grp")),
        check_vma=False,
    )
```

```python
import functools
import math

import jax
import jax.numpy as jnp
from jax import lax
from jax.experimental import pallas as pl
from jax.experimental.pallas import tpu as pltpu
from jax.sharding import PartitionSpec as P

HDIM = 64
L = 197
TOPK = 2
LP = (L + 15) // 16 * 16
LANES = 128
LQ = (L + LANES - 1) // LANES * LANES
BF = jnp.bfloat16
F32 = jnp.float32
I32 = jnp.int32

EPSILON = 1e-06
ROOT_HALF = 0.7071067811865476
DENSITY_FACTOR = 0.3989422804014327
VMEM_BYTES = 60 * 1024 * 1024
MESH = pl.DeviceIdType.MESH


def nn(a, b):
    return lax.dot_general(a, b, (((1,), (0,)), ((), ())), preferred_element_type=F32)


def nt(a, b):
    return lax.dot_general(a, b, (((1,), (1,)), ((), ())), preferred_element_type=F32)


def tn(a, b):
    return lax.dot_general(a, b, (((0,), (0,)), ((), ())), preferred_element_type=F32)


def norm_forward(v, w):
    c = v - jnp.mean(v, axis=-1, keepdims=True)
    r = lax.rsqrt(jnp.mean(c * c, axis=-1, keepdims=True) + EPSILON)
    n = c * r
    return n, r, (n * w).astype(BF)


def norm_backward(n, r, w, dh):
    dn = dh * w
    dw = jnp.sum(dh * n, axis=0, keepdims=True)
    dv = r * (dn - jnp.mean(dn, axis=-1, keepdims=True) - n * jnp.mean(dn * n, axis=-1, keepdims=True))
    return dv, dw


def whole(shape):
    return pl.BlockSpec(shape, lambda *i: (0,) * len(shape))


def call(body, out_shape, *args, grid=(), in_specs=None, out_specs=None, scratch=(), flops=0):
    if in_specs is None:
        in_specs = [whole(a.shape) for a in args]
    if out_specs is None:
        out_specs = [whole(o.shape) for o in out_shape]
    moved = sum(math.prod(a.shape) * a.dtype.itemsize for a in args)
    moved += sum(math.prod(o.shape) * jnp.dtype(o.dtype).itemsize for o in out_shape)
    return pl.pallas_call(
        body,
        grid=grid,
        in_specs=in_specs,
        out_specs=out_specs,
        out_shape=out_shape,
        scratch_shapes=list(scratch),
        cost_estimate=pl.CostEstimate(flops=int(flops), bytes_accessed=int(moved), transcendentals=0),
        compiler_params=pltpu.CompilerParams(vmem_limit_bytes=VMEM_BYTES),
    )(*args)


def out(shape, dtype):
    return jax.ShapeDtypeStruct(shape, dtype)


def head_mask(dtype):
    lane = lax.broadcasted_iota(I32, (LP, LANES), 1)
    return (lane < HDIM).astype(dtype)


def beside(z, j):
    b0, b1 = z % 2, z // 2
    if j & 1:
        b0 = 1 - b0
    if j & 2:
        b1 = 1 - b1
    return b0 + 2 * b1


def fill_rows(ref, at, images, first, count):
    for i in range(count):
        ref[at + i * LP : at + i * LP + L, :] = images[first + i].astype(ref.dtype)
        ref[at + i * LP + L : at + (i + 1) * LP, :] = jnp.zeros((LP - L, ref.shape[1]), ref.dtype)


def own_rows(ref, n):
    if ref.shape[0] == n:
        return ref[...]
    return ref[pl.ds(pl.multiple_of(lax.axis_index("mdl") * n, 16), n), :]


def attend(img, pair, d, qkv_ref, p_ref, o_ref):
    mask = head_mask(BF)
    key_ok = lax.broadcasted_iota(I32, (LP, LP), 1) < L
    rows = pl.ds(pl.multiple_of(img * LP, LP), LP)
    col = pair * LANES
    q = qkv_ref[rows, pl.ds(pl.multiple_of(col, LANES), LANES)]
    ke = qkv_ref[rows, pl.ds(pl.multiple_of(d + col, LANES), LANES)]
    u = qkv_ref[rows, pl.ds(pl.multiple_of(2 * d + col, LANES), LANES)]
    o = jnp.zeros((LP, LANES), F32)
    for hh in range(2):
        mk = mask if hh == 0 else 1 - mask
        s = nt(q * mk, ke) * HDIM ** (-0.5)
        s = jnp.where(key_ok, s, -1e30)
        e = jnp.exp(s - jnp.max(s, axis=-1, keepdims=True))
        p = (e / jnp.sum(e, axis=-1, keepdims=True)).astype(BF)
        p_ref[2 * (img * (d // LANES) + pair) + hh] = p
        o = o + nn(p, u * mk)
    o_ref[rows, pl.ds(pl.multiple_of(col, LANES), LANES)] = o.astype(BF)
    return 0


def attention_forward_body(n_img, g_at, tail, *refs):
    refs = list(refs)
    x_ref, g_ref, qm, qo, om, oo = refs[:6]
    del refs[:6]
    y_ref, h_ref, qkv_ref, p_ref, o_ref = refs[:5]
    del refs[:5]
    h4_ref = refs.pop(0) if tail is not None else None
    rows_all = n_img * LP
    d = x_ref.shape[1]
    c = qm.shape[2]
    pairs = d // LANES
    _, _, h = norm_forward(own_rows(x_ref, rows_all).astype(F32), g_ref[g_at : g_at + 1, :])
    h_ref[...] = h
    for k in range(3):
        for side, w in ((0, qm), (1, qo)):
            at = (2 * k + side) * c
            qkv_ref[:, at : at + c] = nn(h_ref[...], w[k]).astype(BF)
    lax.fori_loop(0, n_img * pairs, lambda i, _: attend(i // pairs, i % pairs, d, qkv_ref, p_ref, o_ref), 0, unroll=2)
    y = own_rows(x_ref, rows_all).astype(F32) + nn(o_ref[:, :c], om[...]) + nn(o_ref[:, c:], oo[...])
    y_ref[...] = y
    if tail is not None:
        _, _, h4 = norm_forward(y, g_ref[tail : tail + 1, :])
        h4_ref[...] = h4


def attention_forward(x, r, gains, g_at, qm, qo, om, oo, tail=None):
    d = x.shape[1]
    n_img = r // LP
    heads = d // HDIM
    shapes = [out((r, d), F32), out((r, d), BF), out((r, 3 * d), BF), out((n_img * heads, LP, LP), BF), out((r, d), BF)]
    if tail is not None:
        shapes.append(out((r, d), BF))
    return call(functools.partial(attention_forward_body, n_img, g_at, tail), shapes, x, gains, qm, qo, om, oo,
                flops=2 * r * d * d * 4 + 4 * n_img * heads * LP * LP * LANES)


def attention_backward_core(n_img, dy, x_ref, gain, h_ref, qkv_ref, p_ref, o_ref, qm, qo, om, oo,
                            gm_ref, go_ref, do_ref, dqkv_ref, tr_ref):
    d = x_ref.shape[1]
    c = qm.shape[2]
    pairs = d // LANES
    da = dy().astype(BF)
    tr_ref[...] = o_ref[...].T
    for side, (w, g) in enumerate(((om, gm_ref), (oo, go_ref))):
        gw = nn(tr_ref[side * c : (side + 1) * c, :], da).astype(BF)
        for part in range(d // c):
            g[3 * d + part * c : 3 * d + (part + 1) * c, :] = gw[:, part * c : (part + 1) * c]
        do_ref[:, side * c : (side + 1) * c] = nt(da, w[...]).astype(BF)
    mask = head_mask(BF)

    def one(i, _):
        rows = pl.ds(pl.multiple_of((i // pairs) * LP, LP), LP)
        col = (i % pairs) * LANES
        cq = pl.ds(pl.multiple_of(col, LANES), LANES)
        ck = pl.ds(pl.multiple_of(d + col, LANES), LANES)
        cu = pl.ds(pl.multiple_of(2 * d + col, LANES), LANES)
        q, ke, u, do = qkv_ref[rows, cq], qkv_ref[rows, ck], qkv_ref[rows, cu], do_ref[rows, cq]
        dq = jnp.zeros((LP, LANES), F32)
        dk = jnp.zeros((LP, LANES), F32)
        du = jnp.zeros((LP, LANES), F32)
        for hh in range(2):
            mk = mask if hh == 0 else 1 - mask
            p = p_ref[2 * i + hh]
            du = du + tn(p, do * mk)
            dp = nt(do * mk, u)
            pf = p.astype(F32)
            ds = (pf * (dp - jnp.sum(dp * pf, axis=-1, keepdims=True))).astype(BF)
            dq = dq + nn(ds, ke * mk)
            dk = dk + tn(ds, q * mk)
        dqkv_ref[rows, cq] = (dq * HDIM ** (-0.5)).astype(BF)
        dqkv_ref[rows, ck] = (dk * HDIM ** (-0.5)).astype(BF)
        dqkv_ref[rows, cu] = du.astype(BF)
        return 0

    lax.fori_loop(0, n_img * pairs, one, 0, unroll=2)
    tr_ref[...] = h_ref[...].T
    dh = jnp.zeros((n_img * LP, d), F32)
    for k in range(3):
        for side, (w, g) in enumerate(((qm, gm_ref), (qo, go_ref))):
            at = (2 * k + side) * c
            g[k * d : (k + 1) * d, :] = nn(tr_ref[...], dqkv_ref[:, at : at + c]).astype(BF)
            dh = dh + nt(dqkv_ref[:, at : at + c], w[k])
    n, rr, _ = norm_forward(own_rows(x_ref, n_img * LP).astype(F32), gain)
    dv, dw = norm_backward(n, rr, gain, dh)
    return dy() + dv, dw


def attention_backward_body(n_img, g_at, dy_ref, x_ref, g_ref, h_ref, qkv_ref, p_ref, o_ref, qm, qo, om, oo,
                            dx_ref, dw_ref, gm_ref, go_ref, do_ref, dqkv_ref, tr_ref):
    dx, dw = attention_backward_core(
        n_img, lambda: dy_ref[...], x_ref, g_ref[g_at : g_at + 1, :], h_ref, qkv_ref, p_ref, o_ref, qm, qo, om, oo,
        gm_ref, go_ref, do_ref, dqkv_ref, tr_ref)
    for i in range(n_img):
        dx_ref[i] = dx[i * LP : i * LP + L].astype(BF)
    dw_ref[...] = dw


def attention_backward_scratch(r, d):
    return [pltpu.VMEM((r, d), BF), pltpu.VMEM((r, 3 * d), BF), pltpu.VMEM((d, r), BF)]


def attention_backward(dy, x, gains, g_at, kept, qm, qo, om, oo):
    r, d = dy.shape
    c = qm.shape[2]
    n_img = r // LP
    heads = d // HDIM
    return call(
        functools.partial(attention_backward_body, n_img, g_at),
        [out((n_img, L, d), BF), out((1, d), F32), out((3 * d + d, c), BF), out((3 * d + d, c), BF)],
        dy, x, gains, *kept, qm, qo, om, oo,
        scratch=attention_backward_scratch(r, d),
        flops=4 * r * d * d * 4 + 8 * n_img * heads * LP * LP * LANES,
    )


def gelu_parts(z):
    phi = 0.5 * (1.0 + lax.erf(z * ROOT_HALF))
    return z * phi, phi + z * jnp.exp(-0.5 * z * z) * DENSITY_FACTOR


def tile_of(f):
    for t in (512, 256, 128):
        if f % t == 0:
            return t
    return f


def mlp_forward_body(g_at, x_ref, g_ref, im, io, tm, to, y_ref, h_ref, act_ref, slope_ref, acc_ref):
    step = pl.program_id(0)

    @pl.when(step == 0)
    def _():
        x = x_ref[...]
        _, _, h = norm_forward(x, g_ref[g_at : g_at + 1, :])
        h_ref[...] = h
        acc_ref[...] = x

    for half, (wi, wo) in enumerate(((im, tm), (io, to))):
        a, s = gelu_parts(nn(h_ref[...], wi[...]))
        act = a.astype(BF)
        act_ref[half] = act
        slope_ref[half] = s.astype(BF)
        acc_ref[...] += nn(act, wo[...])

    @pl.when(step == pl.num_programs(0) - 1)
    def _():
        y_ref[...] = acc_ref[...]


def mlp_forward(x, gains, g_at, im, io, tm, to):
    r, d = x.shape
    f = im.shape[1]
    t = tile_of(f)
    col = pl.BlockSpec((d, t), lambda i: (0, i))
    row = pl.BlockSpec((t, d), lambda i: (i, 0))
    hid = pl.BlockSpec((2, r, t), lambda i: (0, 0, i))
    return call(
        functools.partial(mlp_forward_body, g_at),
        [out((r, d), F32), out((r, d), BF), out((2, r, f), BF), out((2, r, f), BF)],
        x, gains, im, io, tm, to, grid=(f // t,),
        in_specs=[whole((r, d)), whole(gains.shape), col, col, row, row],
        out_specs=[whole((r, d)), whole((r, d)), hid, hid],
        scratch=[pltpu.VMEM((r, d), F32)], flops=8 * r * d * f,
    )


def mlp_backward_body(g_at, dy_ref, x_ref, g_ref, h_ref, act_ref, slope_ref, im, io, tm, to,
                      dx_ref, dw_ref, gim, gio, gtm, gto, da_ref, tr_ref, dh_ref):
    step = pl.program_id(0)

    @pl.when(step == 0)
    def _():
        da_ref[...] = dy_ref[...].astype(BF)
        tr_ref[...] = h_ref[...].T
        dh_ref[...] = jnp.zeros_like(dh_ref)

    for half, (wi, wo, gi, go) in enumerate(((im, tm, gim, gtm), (io, to, gio, gto))):
        dact = nt(da_ref[...], wo[...])
        dz = (dact * slope_ref[half].astype(F32)).astype(BF)
        gw = tn(act_ref[half], da_ref[...]).astype(BF)
        t = gw.shape[0]
        for part in range(gw.shape[1] // t):
            go[part] = gw[:, part * t : (part + 1) * t]
        gi[0] = nn(tr_ref[...], dz).astype(BF)
        dh_ref[...] += nt(dz, wi[...])

    @pl.when(step == pl.num_programs(0) - 1)
    def _():
        gain = g_ref[g_at : g_at + 1, :]
        n, rr, _ = norm_forward(x_ref[...], gain)
        dv, dw = norm_backward(n, rr, gain, dh_ref[...])
        dx_ref[...] = dy_ref[...] + dv
        dw_ref[...] = dw


def mlp_backward(dy, x, gains, g_at, h, act, slope, im, io, tm, to, t):
    r, d = x.shape
    f = im.shape[1]
    col = pl.BlockSpec((d, t), lambda i: (0, i))
    row = pl.BlockSpec((t, d), lambda i: (i, 0))
    hid = pl.BlockSpec((2, r, t), lambda i: (0, 0, i))
    gin = pl.BlockSpec((1, d, t), lambda i: (i, 0, 0))
    gout = pl.BlockSpec((d // t, t, t), lambda i: (0, i, 0))
    return call(
        functools.partial(mlp_backward_body, g_at),
        [out((r, d), F32), out((1, d), F32), out((f // t, d, t), BF), out((f // t, d, t), BF),
         out((d // t, f, t), BF), out((d // t, f, t), BF)],
        dy, x, gains, h, act, slope, im, io, tm, to, grid=(f // t,),
        in_specs=[whole((r, d)), whole((r, d)), whole(gains.shape), whole((r, d)), hid, hid, col, col, row, row],
        out_specs=[whole((r, d)), whole((1, d)), gin, gin, gout, gout],
        scratch=[pltpu.VMEM((r, d), BF), pltpu.VMEM((d, r), BF), pltpu.VMEM((r, d), F32)], flops=16 * r * d * f,
    )


def forward_body(n_img, size, *refs):
    refs = list(refs)

    def take(n):
        r = refs[:n]
        del refs[:n]
        return r

    images, g_ref = take(2)
    own_w = take(8)
    dy_out = take(size - 1)
    results = take(16)
    other_w = take(8)
    dy_in = take(size - 1)
    weights = take(6)
    held = take(16)
    load_sem, w_send, w_recv, o_sem, r_sem, d_send, d_recv = refs
    x1, h1, qkv1, p1, o1, x2, h2, act, slope, x3, h3, qkv3, p3, o3, h4, x0 = held
    q1, w1, fi, fo, q3, w3 = weights
    r = n_img * LP
    d = x0.shape[1]
    c = q1.shape[3]
    f = fi.shape[2]
    z = lax.axis_index("exp")
    partner = {"mdl": 1 - lax.axis_index("mdl")}

    loads = [pltpu.make_async_copy(own_w[k], weights[k].at[0], load_sem.at[k]) for k in range(6)]
    for cp in loads:
        cp.start()
    barrier = pltpu.get_barrier_semaphore()
    for dev in [partner] + [{"exp": beside(z, j)} for j in range(1, size)]:
        pl.semaphore_signal(barrier, inc=1, device_id=dev, device_id_type=MESH)
    pl.semaphore_wait(barrier, size)
    swaps = [pltpu.make_async_remote_copy(own_w[k], weights[k].at[1] if k < 6 else other_w[k], w_send.at[k], w_recv.at[k],
                                          device_id=partner, device_id_type=MESH) for k in range(8)]
    for cp in swaps[0:2]:
        cp.start()
    blocks = [pltpu.make_async_remote_copy(dy_out[j - 1], dy_in[j - 1], d_send.at[j - 1], d_recv.at[j - 1],
                                           device_id={"exp": beside(z, j)}, device_id_type=MESH) for j in range(1, size)]
    for cp in blocks:
        cp.start()
    keeps = [pltpu.make_async_copy(weights[k].at[1], other_w[k], o_sem.at[k]) for k in range(6)]
    stores = [pltpu.make_async_copy(held[k], results[k], r_sem.at[k]) for k in range(16)]

    def store(*at):
        for k in at:
            stores[k].start()

    def attention(x, gain, wq, wo, kq, ko, h, qkv, p, o, y, then):
        _, _, n = norm_forward(x(), gain)
        h[...] = n
        per_half = c // LANES
        for side in range(2):
            if side == 0:
                loads[kq].wait()
            else:
                swaps[kq].wait_recv()
                keeps[kq].start()
                for cp in swaps[then : then + 2]:
                    cp.start()
            for k in range(3):
                at = (2 * k + side) * c
                qkv[:, at : at + c] = nn(h[...], wq[side, k]).astype(BF)
            lax.fori_loop(
                0, n_img * per_half,
                lambda i, _, side=side: attend(i // per_half, side * per_half + i % per_half, d, qkv, p, o), 0, unroll=2)
        loads[ko].wait()
        swaps[ko].wait_recv()
        keeps[ko].start()
        y[...] = x() + nn(o[:, :c], wo[0]) + nn(o[:, c:], wo[1])

    fill_rows(x0, 0, images, lax.axis_index("mdl") * n_img, n_img)
    store(15)
    attention(lambda: x0[...].astype(F32), g_ref[0:1, :], q1, w1, 0, 1, h1, qkv1, p1, o1, x1, 2)
    store(0, 1, 2, 3, 4)

    _, _, n = norm_forward(x1[...], g_ref[1:2, :])
    h2[...] = n
    x2[...] = x1[...]
    t = tile_of(f)
    for side in range(2):
        for k in (2, 3):
            if side == 0:
                loads[k].wait()
            else:
                swaps[k].wait_recv()
                keeps[k].start()

        def tile(i, _, side=side):
            at = pl.ds(pl.multiple_of(i * t, t), t)
            a, sl = gelu_parts(nn(h2[...], fi[side, :, at]))
            a = a.astype(BF)
            act[side, :, at] = a
            slope[side, :, at] = sl.astype(BF)
            x2[...] += nn(a, fo[side, at, :])
            return 0

        if side == 0:
            for cp in swaps[4:6]:
                cp.start()
        lax.fori_loop(0, f // t, tile, 0)
    store(5, 6, 7, 8)

    attention(lambda: x2[...], g_ref[2:3, :], q3, w3, 4, 5, h3, qkv3, p3, o3, x3, 6)
    store(9, 10, 11, 12, 13)
    _, _, n = norm_forward(x3[...], g_ref[3:4, :])
    h4[...] = n
    store(14)
    for cp in blocks:
        cp.wait()
    for cp in keeps + stores:
        cp.wait()
    for cp in swaps[6:]:
        cp.wait_recv()
    for cp in swaps:
        cp.wait_send()


def forward(x, gains, own_w, dy_out, r):
    d = x.shape[2]
    c, f = own_w[0].shape[2], own_w[2].shape[1]
    n_img = r // LP
    heads = d // HDIM
    size = len(dy_out) + 1
    half = dy_out[0].shape[0]
    kept = [out((r, d), F32), out((r, d), BF), out((r, 3 * d), BF), out((n_img * heads, LP, LP), BF), out((r, d), BF)]
    results = kept + [out((r, d), F32), out((r, d), BF), out((2, r, f), BF), out((2, r, f), BF)] + kept + [out((r, d), BF), out((r, d), BF)]
    shapes = results + [out(w.shape, BF) for w in own_w] + [out((half, d), BF)] * (size - 1)
    D, V = pltpu.SemaphoreType.DMA, pltpu.VMEM
    any_ = pl.BlockSpec(memory_space=pl.ANY)
    vm = pl.BlockSpec(memory_space=pltpu.VMEM)
    got = pl.pallas_call(
        functools.partial(forward_body, n_img, size),
        in_specs=[vm] * 2 + [any_] * (len(own_w) + size - 1), out_specs=[any_] * len(shapes), out_shape=shapes,
        scratch_shapes=[V((2,) + w.shape, BF) for w in own_w[:6]] + [V(o.shape, o.dtype) for o in results]
        + [D((6,)), D((8,)), D((8,)), D((6,)), D((len(results),)), D((size - 1,)), D((size - 1,))],
        compiler_params=pltpu.CompilerParams(collective_id=2, has_side_effects=True, vmem_limit_bytes=VMEM_BYTES),
        cost_estimate=pl.CostEstimate(flops=16 * r * d * d + 8 * r * d * f, bytes_accessed=80 * r * d, transcendentals=0),
    )(x, gains, *own_w, *dy_out)
    n = len(results)
    return got[:n], got[n : n + 8], got[n + 8 :]


def routing_body(experts, capacity, half, rows_ref, dy_ref, tr_ref, col_ref, *refs):
    out_refs, (dy_rows, tmp) = refs[:-2], refs[-2:]
    fill_rows(dy_rows, 0, dy_ref, 0, rows_ref.shape[0])
    n_img = rows_ref.shape[0]
    slots = experts * half
    core = lax.axis_index("mdl")
    own_img = n_img // 2
    tall = lax.broadcasted_iota(I32, (max(experts, 8), LQ), 0)
    hots, priors = [], []
    for i in range(n_img):
        r = rows_ref[i]
        live = r[3:4, :] > 0
        hots.append((((tall == r[0:1, :]) | (tall == r[1:2, :])) & live).astype(F32).astype(BF))
        priors.append(r.astype(F32).T[:, 2:3])
    for i in range(n_img):
        r = rows_ref[i]
        rank = None
        for k in range(n_img):
            part = nn(hots[k], (priors[k] < r[2:3, :].astype(F32)).astype(F32).astype(BF))
            rank = part if rank is None else rank + part
        for k in range(TOPK):
            e = r[k : k + 1, :]
            mine = jnp.sum(jnp.where(tall == e, rank, 0.0), axis=0, keepdims=True).astype(I32)
            side = (mine >= half).astype(I32)
            slot = side * slots + e * half + mine - side * half
            tr_ref[i, k : k + 1, :] = jnp.where((mine < capacity) & (r[3:4, :] > 0), slot, -1)
        tr_ref[i, TOPK:, :] = jnp.full((8 - TOPK, LQ), -1, I32)
    for i in range(own_img):
        at = core * own_img + i
        for k in range(TOPK):
            t = tr_ref[at, k : k + 1, :]
            there = t - (1 - core) * slots
            tmp[k : k + 1, :] = t - core * slots
            tmp[TOPK + k : TOPK + k + 1, :] = jnp.where(there < slots, there, -1)
        tmp[4:8, :] = rows_ref[at, 0:4, :]
        tmp[6:7, :] = rows_ref[at, 3:4, :]
        col_ref[i * LP : (i + 1) * LP, :] = tmp[...].astype(F32).T[:LP, :].astype(I32)
    z = lax.axis_index("exp")
    for j, o_ref in enumerate(out_refs):
        at = core * slots + (beside(z, j) * half if len(out_refs) > 1 else 0)
        total = None
        for i in range(n_img):
            part = nn(slot_hots(tr_ref[i], at, o_ref.shape[0]), dy_rows[i * LP : (i + 1) * LP, :])
            total = part if total is None else total + part
        o_ref[...] = total.astype(BF)


def slot_hots(t, base, count):
    place = lax.broadcasted_iota(I32, (count, LP), 0) + base
    return ((place == t[0:1, :LP]) | (place == t[1:2, :LP])).astype(F32).astype(BF)


def dispatch_body(experts, half, tr_ref, own_ref, oth_ref, y_ref):
    core = lax.axis_index("mdl")
    own_img = own_ref.shape[0] // LP
    total = None
    for a, v in ((core, own_ref), (1 - core, oth_ref)):
        for i in range(own_img):
            hot = slot_hots(tr_ref[a * own_img + i], core * experts * half, experts * half)
            part = nn(hot, v[i * LP : (i + 1) * LP, :])
            total = part if total is None else total + part
    y_ref[...] = total.astype(BF)


def router_probs(h, router, experts):
    logits = nt(h, router)
    lane = lax.broadcasted_iota(I32, logits.shape, 1)
    logits = jnp.where(lane < experts, logits, -1e30)
    e = jnp.exp(logits - jnp.max(logits, axis=-1, keepdims=True))
    return e / jnp.sum(e, axis=-1, keepdims=True), lane


def expert_body(experts, x_ref, dy_ref, router_ref, im, io, tm, to,
                eout_ref, ret_ref, act_ref, dz_ref, wd_ref, acc_ref, dx_ref):
    step = pl.program_id(0)
    d = x_ref.shape[1]

    @pl.when(step == 0)
    def _():
        probs, lane = router_probs(x_ref[...], router_ref[...], experts)
        gate = jnp.sum(jnp.where(lane == lax.axis_index("exp"), probs, 0.0), axis=-1, keepdims=True)
        wd_ref[...] = (gate * dy_ref[...].astype(F32)).astype(BF)
        acc_ref[...] = jnp.zeros_like(acc_ref)
        dx_ref[...] = jnp.zeros_like(dx_ref)

    for half, (wi, wo) in enumerate(((im, tm), (io, to))):
        a, s = gelu_parts(nn(x_ref[...], wi[...]))
        act = a.astype(BF)
        act_ref[half] = act
        acc_ref[...] += nn(act, wo[...])
        dz = (nt(wd_ref[...], wo[...]) * s).astype(BF)
        dz_ref[half] = dz
        dx_ref[...] += nt(dz, wi[...])

    @pl.when(step == pl.num_programs(0) - 1)
    def _():
        eout = acc_ref[...].astype(BF)
        eout_ref[...] = eout
        ret_ref[:, :d] = dx_ref[...].astype(BF)
        dgate = jnp.sum(dy_ref[...].astype(F32) * eout.astype(F32), axis=-1, keepdims=True)
        high = dgate.astype(BF).astype(F32)
        lane = lax.broadcasted_iota(I32, (x_ref.shape[0], LANES), 1)
        ret_ref[:, d:] = jnp.where(lane < LANES // 2, high, dgate - high).astype(BF)


def expert_forward_backward(x, dy, router, im, io, tm, to, experts):
    r, d = x.shape
    f = im.shape[1]
    t = tile_of(f) // 2
    col = pl.BlockSpec((d, t), lambda i: (0, i))
    row = pl.BlockSpec((t, d), lambda i: (i, 0))
    hid = pl.BlockSpec((2, r, t), lambda i: (0, 0, i))
    return call(
        functools.partial(expert_body, experts),
        [out((r, d), BF), out((r, d + LANES), BF), out((2, r, f), BF), out((2, r, f), BF), out((r, d), BF)],
        x, dy, router, im, io, tm, to, grid=(f // t,),
        in_specs=[whole((r, d)), whole((r, d)), whole(router.shape), col, col, row, row],
        out_specs=[whole((r, d)), whole((r, d + LANES)), hid, hid, whole((r, d))],
        scratch=[pltpu.VMEM((r, d), F32), pltpu.VMEM((r, d), F32)], flops=16 * r * d * f,
    )


def expert_weights_body(x_ref, wd_ref, act_ref, dz_ref, gm_ref, go_ref, xt_ref, wt_ref):
    @pl.when(pl.program_id(0) == 0)
    def _():
        xt_ref[...] = x_ref[...].T
        wt_ref[...] = wd_ref[...].T

    for half, g in enumerate((gm_ref, go_ref)):
        g[0] = nn(xt_ref[...], dz_ref[half]).astype(BF)
        g[1] = nn(wt_ref[...], act_ref[half]).astype(BF)


def expert_weights(x, wd, act, dz):
    r, d = x.shape
    f = act.shape[2]
    t = tile_of(f) // 2
    hid = pl.BlockSpec((2, r, t), lambda i: (0, 0, i))
    grad = pl.BlockSpec((2, d, t), lambda i: (0, 0, i))
    return call(
        expert_weights_body, [out((2, d, f), BF), out((2, d, f), BF)], x, wd, act, dz, grid=(f // t,),
        in_specs=[whole((r, d)), whole((r, d)), hid, hid], out_specs=[grad, grad],
        scratch=[pltpu.VMEM((d, r), BF), pltpu.VMEM((d, r), BF)], flops=8 * r * d * f,
    )


def merge(col_ref, k, ab_ref, n):
    slots = ab_ref.shape[1]
    lane = lax.broadcasted_iota(I32, (n, slots), 1)
    rows = None
    for side in range(2):
        hot = (lane == col_ref[:, 2 * side + k : 2 * side + k + 1]).astype(F32).astype(BF)
        part = nn(hot, ab_ref[side])
        rows = part if rows is None else rows + part
    return rows


def merge_blocks(col_ref, k, blocks, n):
    rows = None
    for side in range(2):
        for e, ref in blocks[side]:
            half = ref.shape[0]
            lane = lax.broadcasted_iota(I32, (n, half), 1) + e * half
            hot = (lane == col_ref[:, 2 * side + k : 2 * side + k + 1]).astype(F32).astype(BF)
            part = nn(hot, ref[...])
            rows = part if rows is None else rows + part
    return rows


def mixture_backward_core(experts, half, x_ref, gain, h_ref, router_ref, dy_ref, col_ref, ab_ref, dgate_ref, dr_ref, dy_rows):
    n, d = x_ref.shape
    n_img = n // LP
    fill_rows(dy_rows, 0, dy_ref, lax.axis_index("mdl") * n_img, n_img)
    probs, lane = router_probs(h_ref[...], router_ref[...], experts)
    dsoft = jnp.zeros(probs.shape, F32)
    dh = jnp.zeros((n, d), F32)
    for k in range(TOPK):
        dh = dh + merge(col_ref, k, ab_ref, n)
        dgate = jnp.zeros((n, 1), F32)
        for side in range(2):
            t = col_ref[:, 2 * side + k : 2 * side + k + 1]
            for e in range(experts):
                line = dgate_ref[side, e, 0:1, :]
                place = lax.broadcasted_iota(I32, (n, line.shape[1]), 1)
                hit = (place + e * half == t) & (place < half)
                dgate = dgate + jnp.sum(jnp.where(hit, line, 0.0), axis=-1, keepdims=True)
        dsoft = dsoft + jnp.where(lane == col_ref[:, 4 + k : 5 + k], dgate, 0.0)
    dlog = (probs * (dsoft - jnp.sum(dsoft * probs, axis=-1, keepdims=True))).astype(BF)
    dr_ref[...] = tn(dlog, h_ref[...])
    dh = dh + nn(dlog, router_ref[...])
    nrm, rr, _ = norm_forward(x_ref[...], gain)
    dv, dw = norm_backward(nrm, rr, gain, dh)
    return dy_rows[...].astype(F32) * col_ref[:, 6:7].astype(F32) + dv, dw


def gate_lines(dgate):
    half = dgate.shape[0]
    wide = -(-half // LANES) * LANES
    tall = jnp.concatenate([dgate, jnp.zeros((wide - half, 1), F32)], axis=0) if wide > half else dgate
    return jnp.broadcast_to(tall, (wide, LANES)).T[0:8, :]


def mixture_attention_backward_body(n_img, experts, half, x3_ref, h4_ref, router_ref, dy_ref, col_ref, ret_ref, dgate_ref, x_ref, g_ref, h_ref,
                                    qkv_ref, p_ref, o_ref, qm, qo, om, oo, dx_ref, dw3_ref, dw4_ref, dr_ref, gm_ref, go_ref,
                                    dx3, dy_rows, do_ref, dqkv_ref, tr_ref):
    grad, dw4 = mixture_backward_core(experts, half, x3_ref, g_ref[3:4, :], h4_ref, router_ref, dy_ref, col_ref, ret_ref, dgate_ref,
                                      dr_ref, dy_rows)
    dx3[...] = grad
    dw4_ref[...] = dw4
    dx, dw3 = attention_backward_core(
        n_img, lambda: dx3[...], x_ref, g_ref[2:3, :], h_ref, qkv_ref, p_ref, o_ref, qm, qo, om, oo,
        gm_ref, go_ref, do_ref, dqkv_ref, tr_ref)
    dx_ref[...] = dx
    dw3_ref[...] = dw3


def mixture_attention_backward(experts, half, x3, h4, router, dy, col, ret, dgate, x, gains, kept, qm, qo, om, oo):
    r, d = x.shape
    c = qm.shape[2]
    n_img = r // LP
    heads = d // HDIM
    shapes = [out((r, d), F32), out((1, d), F32), out((1, d), F32), out(router.shape, F32),
              out((3 * d + d, c), BF), out((3 * d + d, c), BF)]
    return call(functools.partial(mixture_attention_backward_body, n_img, experts, half), shapes,
                x3, h4, router, dy, col, ret, dgate, x, gains, *kept, qm, qo, om, oo,
                scratch=[pltpu.VMEM((r, d), F32), pltpu.VMEM((r, d), BF)] + attention_backward_scratch(r, d),
                flops=4 * r * d * d * 4 + 8 * n_img * heads * LP * LP * LANES + 8 * r * ret.shape[1] * d)


def backward_body(n_img, experts, half, size, *refs):
    refs = list(refs)

    def take(n):
        r = refs[:n]
        del refs[:n]
        return r

    x3, h4, router, cotangent, col, ret, dgate, g_ref = take(8)
    src_two, src_mlp, src_one = take(9), take(8), take(9)
    eouts = take(size - 1)
    dg1, dg2, dg3, dg4, dr, image = take(6)
    out_two, out_mlp, out_one = take(2), take(4), take(2)
    ebacks = take(size - 1)
    attn = take(9)
    x0, x1, h2, act, slope, fi, fo, ga, gi, go, dxs, dy_rows, do, dqkv, tr, da, dh = take(17)
    a_sem, m_sem, b_sem, ga_sem, gi_sem, e_send, e_recv = refs
    d = x3.shape[1]
    f = fi.shape[2]
    t = gi.shape[4]
    z = lax.axis_index("exp")

    def fetch(srcs, dsts, sem):
        return [pltpu.make_async_copy(a, b, sem.at[k]) for k, (a, b) in enumerate(zip(srcs, dsts))]

    two = fetch(src_two, attn, a_sem)
    mlp = fetch(src_mlp, [x1, h2, act, slope, fi.at[0], fi.at[1], fo.at[0], fo.at[1]], m_sem)
    one = fetch(src_one, [x0] + attn[1:], b_sem)
    for cp in two + mlp:
        cp.start()
    barrier = pltpu.get_barrier_semaphore()
    for j in range(1, size):
        pl.semaphore_signal(barrier, inc=1, device_id={"exp": beside(z, j)}, device_id_type=MESH)
    pl.semaphore_wait(barrier, size - 1)
    blocks = [pltpu.make_async_remote_copy(eouts[j - 1], ebacks[j - 1], e_send.at[j - 1], e_recv.at[j - 1],
                                           device_id={"exp": beside(z, j)}, device_id_type=MESH) for j in range(1, size)]
    for cp in blocks:
        cp.start()

    def attention(x, gain, dst):
        dx, dw = attention_backward_core(n_img, lambda: dxs[...], x, gain, *attn[1:], ga.at[0], ga.at[1], do, dqkv, tr)
        leave = [pltpu.make_async_copy(ga.at[k], dst[k], ga_sem.at[k]) for k in range(2)]
        for cp in leave:
            cp.start()
        return dx, dw, leave

    grad, dw4 = mixture_backward_core(experts, half, x3, g_ref[3:4, :], h4, router, cotangent, col, ret, dgate, dr, dy_rows)
    dxs[...] = grad
    dg4[...] = dw4
    for cp in two:
        cp.wait()
    dx, dw, leave = attention(attn[0], g_ref[2:3, :], out_two)
    dxs[...] = dx
    dg3[...] = dw
    for cp in one:
        cp.start()

    da[...] = dxs[...].astype(BF)
    for cp in mlp:
        cp.wait()
    tr[...] = h2[...].T
    dh[...] = jnp.zeros(dh.shape, F32)
    gone = {}
    for i in range(f // t):
        at = slice(i * t, (i + 1) * t)
        slot = i % 2
        for cp in gone.pop(slot, ()):
            cp.wait()
        gone[slot] = []
        for side in range(2):
            dz = (nt(da[...], fo[side, at, :]) * slope[side, :, at].astype(F32)).astype(BF)
            gw = tn(act[side, :, at], da[...]).astype(BF)
            for part in range(d // t):
                go[slot, side, part] = gw[:, part * t : (part + 1) * t]
            gi[slot, side, 0] = nn(tr[...], dz).astype(BF)
            dh[...] += nt(dz, fi[side, :, at])
            gone[slot] += [
                pltpu.make_async_copy(gi.at[slot, side], out_mlp[side].at[i : i + 1], gi_sem.at[slot, side, 0]),
                pltpu.make_async_copy(go.at[slot, side], out_mlp[2 + side].at[:, at], gi_sem.at[slot, side, 1])]
            for cp in gone[slot][-2:]:
                cp.start()
    gain = g_ref[1:2, :]
    n, rr, _ = norm_forward(x1[...], gain)
    dv, dw = norm_backward(n, rr, gain, dh[...])
    dxs[...] += dv
    dg2[...] = dw

    for cp in one + leave:
        cp.wait()
    dx, dw, leave = attention(x0, g_ref[0:1, :], out_one)
    for i in range(n_img):
        image[i] = dx[i * LP : i * LP + L].astype(BF)
    dg1[...] = dw
    for cp in leave + gone[0] + gone[1] + blocks:
        cp.wait()


def backward(experts, half, x3, h4, router, cotangent, col, ret, dgate, gains, x2, kept3, w2, x1, h2, act, slope, mlp_w, x0, kept1,
             w1, eouts):
    r, d = x3.shape
    c, f = w1[0].shape[2], mlp_w[0].shape[1]
    n_img = r // LP
    heads = d // HDIM
    size = len(eouts) + 1
    t = c
    flat = [x2, *kept3, *w2, x1, h2, act, slope, *mlp_w, x0, *kept1, *w1, *eouts]
    near = [x3, h4, router, cotangent, col, ret, dgate, gains]
    D, V = pltpu.SemaphoreType.DMA, pltpu.VMEM
    any_ = pl.BlockSpec(memory_space=pl.ANY)
    vm = pl.BlockSpec(memory_space=pltpu.VMEM)
    shapes = [out((1, d), F32)] * 4 + [out(router.shape, F32), out((n_img, L, d), BF)]
    shapes += [out((4 * d, c), BF)] * 2 + [out((f // t, d, t), BF)] * 2 + [out((d // t, f, t), BF)] * 2 + [out((4 * d, c), BF)] * 2
    shapes += [out(e.shape, BF) for e in eouts]
    like = [V(v.shape, v.dtype) for v in (x2, *kept3, *w2)]
    got = pl.pallas_call(
        functools.partial(backward_body, n_img, experts, half, size),
        in_specs=[vm] * len(near) + [any_] * len(flat), out_specs=[vm] * 6 + [any_] * (len(shapes) - 6), out_shape=shapes,
        scratch_shapes=like + [
            V(x0.shape, x0.dtype), V((r, d), F32), V((r, d), BF), V(act.shape, BF), V(slope.shape, BF), V((2, d, f), BF),
            V((2, f, d), BF), V((2, 4 * d, c), BF), V((2, 2, 1, d, t), BF), V((2, 2, d // t, t, t), BF), V((r, d), F32),
            V((r, d), BF), V((r, d), BF), V((r, 3 * d), BF), V((d, r), BF), V((r, d), BF), V((r, d), F32),
            D((9,)), D((8,)), D((9,)), D((2,)), D((2, 2, 2)), D((size - 1,)), D((size - 1,))],
        compiler_params=pltpu.CompilerParams(collective_id=3, has_side_effects=True, vmem_limit_bytes=VMEM_BYTES),
        cost_estimate=pl.CostEstimate(flops=32 * r * d * d + 16 * r * d * f, bytes_accessed=160 * r * d, transcendentals=0),
    )(*near, *flat)
    return got[:6], got[6:14], got[14:]


def mixture_output(experts, x_ref, h_ref, router_ref, col_ref, rows_of):
    n, d = x_ref.shape
    probs, lane = router_probs(h_ref[...], router_ref[...], experts)
    mixed = jnp.zeros((n, d), F32)
    for k in range(TOPK):
        gate = jnp.sum(jnp.where(lane == col_ref[:, 4 + k : 5 + k], probs, 0.0), axis=-1, keepdims=True)
        mixed = mixed + gate * rows_of(k)
    return (col_ref[:, 6:7].astype(F32) * (x_ref[...] + mixed)).astype(BF)


def mixture_output_body(experts, x_ref, h_ref, router_ref, col_ref, ab_ref, y_ref):
    y = mixture_output(experts, x_ref, h_ref, router_ref, col_ref, lambda k: merge(col_ref, k, ab_ref, x_ref.shape[0]))
    for i in range(y_ref.shape[0]):
        y_ref[i] = y[i * LP : i * LP + L]


def flip(axis, bit):
    size = lax.axis_size(axis)
    return [(i, i ^ bit) for i in range(size)]


def bits_of(axis):
    size = lax.axis_size(axis)
    return [1 << b for b in range(size.bit_length() - 1)]


def other_core(v):
    return lax.ppermute(v, "mdl", flip("mdl", 1))


def add16(a, b):
    return (a.astype(F32) + b.astype(F32)).astype(BF)


def halve(v, axis, bit):
    side = (lax.axis_index(axis) // bit) % 2
    n = v.shape[0] // 2
    keep = lax.dynamic_slice_in_dim(v, side * n, n)
    send = lax.dynamic_slice_in_dim(v, (1 - side) * n, n)
    return add16(keep, lax.ppermute(send, axis, flip(axis, bit)))


def double(v, axis, bit):
    side = (lax.axis_index(axis) // bit) % 2
    got = lax.ppermute(v, axis, flip(axis, bit))
    return jnp.where(side == 0, jnp.concatenate([v, got]), jnp.concatenate([got, v]))


def sum_everywhere(v):
    n = v.shape[0] // 2
    bits = bits_of("grp")
    parts = []
    for part, order in ((v[:n], bits), (v[n:], bits[::-1])):
        for bit in order:
            part = halve(part, "grp", bit)
        parts.append(part)
    size = lax.axis_size("exp")
    joined = jnp.concatenate(parts)
    rows = joined.shape[0] // size
    spread = lax.all_to_all(joined.reshape(size, rows, -1), "exp", 0, 0, tiled=True)
    mine = jnp.sum(spread.astype(F32), axis=0).astype(BF)
    joined = lax.all_gather(mine, "exp", axis=0, tiled=True)
    h = joined.shape[0] // 2
    done = []
    for part, order in ((joined[:h], bits), (joined[h:], bits[::-1])):
        for bit in order[::-1]:
            part = double(part, "grp", bit)
        done.append(part)
    return jnp.concatenate(done)


def small_sum(v):
    for axis in ("mdl", "grp", "exp"):
        for bit in bits_of(axis):
            v = v + lax.ppermute(v, axis, flip(axis, bit))
    return v


def reduce_body(n_in, per, n_exp, experts, *refs):
    mine = refs[:n_in]
    other = refs[n_in : 2 * n_in]
    dg = refs[2 * n_in : 2 * n_in + 4]
    dr_ref, x3_ref, h4_ref, router_ref, col_ref = refs[2 * n_in + 4 : 2 * n_in + 9]
    eouts = refs[2 * n_in + 9 : 2 * n_in + 13]
    image_ref = refs[2 * n_in + 13]
    outs = refs[2 * n_in + 14 :]
    qkv2, proj2, fc_in, fc_out, qkv1, proj1, sum_ref, y_ref, gx_ref = outs[:9]
    (acc, got, r1, r2, zr, zz, zs, sm, y_own, load_sem, m_send, m_recv, x_send, x_recv, z_send, z_recv, s_send, s_recv,
     i_local, i_send, i_recv, e_oth, e_send, e_recv) = outs[9:]
    out_ref = got
    n = n_in * per
    rows = acc.shape[2]
    h, q = rows // 2, rows // 4
    t = q // n_exp
    g = lax.axis_index("grp")
    z = lax.axis_index("exp")
    core = lax.axis_index("mdl")
    bx, by = g % 2, g // 2
    flat = {"x": g + 1 - 2 * bx, "y": g + 2 - 4 * by}
    order = (("x", "y"), ("y", "x"))
    bits = ((bx, by), (by, bx))

    barrier = pltpu.get_barrier_semaphore()
    others = [{"mdl": 1 - core}, {"grp": flat["x"]}, {"grp": flat["y"]}]
    others += [{"exp": (z + o) % n_exp} for o in range(1, n_exp)]
    for dev in others:
        pl.semaphore_signal(barrier, inc=1, device_id=dev, device_id_type=MESH)
    pl.semaphore_wait(barrier, len(others))

    def load(c):
        i, p = c // per, c % per
        return pltpu.make_async_copy(mine[i].at[p], acc.at[c], load_sem.at[c])

    def swap(c):
        i, p = c // per, c % per
        return pltpu.make_async_remote_copy(other[i].at[p], got.at[c], m_send.at[c], m_recv.at[c],
                                            device_id={"mdl": 1 - core}, device_id_type=MESH)

    for c in range(n):
        swap(c).start()
        load(c).start()

    own_img = image_ref.shape[0]
    places = pl.ds(core * own_img, own_img)

    def image_copies(k, src, dst):
        return (pltpu.make_async_copy(src, dst.at[places], i_local.at[k]),
                pltpu.make_async_remote_copy(src, dst.at[places], i_send.at[k], i_recv.at[k], device_id={"mdl": 1 - core},
                                             device_id_type=MESH))

    def image_come(k, src, dst):
        there = pl.ds((1 - core) * own_img, own_img)
        return pltpu.make_async_remote_copy(src, dst.at[there], i_send.at[k], i_recv.at[k], device_id={"mdl": 1 - core},
                                            device_id_type=MESH)

    for cp in image_copies(0, image_ref, gx_ref):
        cp.start()

    e_copies = [pltpu.make_async_remote_copy(eouts[j], e_oth.at[j], e_send.at[j], e_recv.at[j], device_id={"mdl": 1 - core},
                                             device_id_type=MESH) for j in range(n_exp)]
    for cp in e_copies:
        cp.start()

    def swap_at(c):
        return pltpu.make_async_remote_copy(other[0].at[0], got.at[c], m_send.at[c], m_recv.at[c],
                                            device_id={"mdl": 1 - core}, device_id_type=MESH)

    def load_at(c):
        return pltpu.make_async_copy(mine[0].at[0], acc.at[c], load_sem.at[c])

    def over(u, leg, src, dst, slot, c):
        return pltpu.make_async_remote_copy(src, dst, x_send.at[slot, u, c], x_recv.at[slot, u, c],
                                            device_id={"grp": flat[order[u][leg]]}, device_id_type=MESH)

    def first(u, c):
        return over(u, 0, acc.at[c, u, pl.ds(pl.multiple_of((1 - bits[u][0]) * h, h), h)], r1.at[c, u], 0, c)

    def second(u, c):
        return over(u, 1, r1.at[c, u, pl.ds(pl.multiple_of((1 - bits[u][1]) * q, q), q)], r2.at[c, u], 1, c)

    def along(u, c, o):
        return pltpu.make_async_remote_copy(
            r2.at[c, u, pl.ds(pl.multiple_of(((z + o) % n_exp) * t, t), t)], zr.at[c, u, o - 1],
            z_send.at[0, u, o - 1, c], z_recv.at[0, u, o - 1, c],
            device_id={"exp": (z + o) % n_exp}, device_id_type=MESH)

    def place(u):
        return bits[u][0] * h + bits[u][1] * q

    def back(u, c, o):
        here = out_ref.at[c, u, pl.ds(pl.multiple_of(place(u) + z * t, t), t)]
        return pltpu.make_async_remote_copy(here, here, z_send.at[1, u, o - 1, c], z_recv.at[1, u, o - 1, c],
                                            device_id={"exp": (z + o) % n_exp}, device_id_type=MESH)

    def third(u, c):
        here = out_ref.at[c, u, pl.ds(pl.multiple_of(place(u), q), q)]
        return over(u, 1, here, here, 2, c)

    def fourth(u, c):
        here = out_ref.at[c, u, pl.ds(pl.multiple_of(bits[u][0] * h, h), h)]
        return over(u, 0, here, here, 3, c)

    def plus(a, b):
        return (a.astype(F32) + b.astype(F32)).astype(BF)

    def s1(c):
        load_at(c).wait()
        swap_at(c).wait_recv()
        for u in range(2):
            acc[c, u] = plus(acc[c, u], got[c, u])
            first(u, c).start()

    def s2(c):
        for u in range(2):
            first(u, c).wait_recv()
            keep = acc[c, u, pl.ds(pl.multiple_of(bits[u][0] * h, h), h)]
            r1[c, u] = plus(keep, r1[c, u])
            second(u, c).start()

    def s3(c):
        for u in range(2):
            second(u, c).wait_recv()
            keep = r1[c, u, pl.ds(pl.multiple_of(bits[u][1] * q, q), q)]
            r2[c, u] = plus(keep, r2[c, u])
            for o in range(1, n_exp):
                along(u, c, o).start()

    def s4(c):
        for u in range(2):
            total = r2[c, u, pl.ds(pl.multiple_of(z * t, t), t)].astype(F32)
            for o in range(1, n_exp):
                along(u, c, o).wait_recv()
                total = total + zr[c, u, o - 1].astype(F32)
            out_ref[c, u, pl.ds(pl.multiple_of(place(u) + z * t, t), t)] = total.astype(BF)
            for o in range(1, n_exp):
                back(u, c, o).start()

    def s5(c):
        for u in range(2):
            for o in range(1, n_exp):
                back(u, c, o).wait_recv()
            third(u, c).start()

    def s6(c):
        for u in range(2):
            third(u, c).wait_recv()
            fourth(u, c).start()

    def s7(c):
        for u in range(2):
            fourth(u, c).wait_recv()
        for k in range(n):

            @pl.when(c == k)
            def _(k=k):
                natural(k)

    zc = 0
    e, e2, e4 = rows // n_exp, rows // n_exp // 2, rows // n_exp // 4

    def z_out(u, o):
        return pltpu.make_async_remote_copy(
            acc.at[zc, u, pl.ds(pl.multiple_of(((z + o) % n_exp) * e, e), e)], zz.at[u, o - 1],
            z_send.at[0, u, o - 1, zc], z_recv.at[0, u, o - 1, zc], device_id={"exp": (z + o) % n_exp}, device_id_type=MESH)

    def z_first(u):
        return over(u, 0, zs.at[u, pl.ds(pl.multiple_of((1 - bits[u][0]) * e2, e2), e2)], r1.at[zc, u, 0:e2], 0, zc)

    def z_second(u):
        return over(u, 1, r1.at[zc, u, pl.ds(pl.multiple_of((1 - bits[u][1]) * e4, e4), e4)], r2.at[zc, u, 0:e4], 1, zc)

    def z_third(u):
        here = out_ref.at[zc, u, pl.ds(pl.multiple_of(z * e + bits[u][0] * e2 + bits[u][1] * e4, e4), e4)]
        return over(u, 1, here, here, 2, zc)

    def z_fourth(u):
        here = out_ref.at[zc, u, pl.ds(pl.multiple_of(z * e + bits[u][0] * e2, e2), e2)]
        return over(u, 0, here, here, 3, zc)

    def z_back(u, o):
        here = out_ref.at[zc, u, pl.ds(pl.multiple_of(z * e, e), e)]
        return pltpu.make_async_remote_copy(here, here, z_send.at[1, u, o - 1, zc], z_recv.at[1, u, o - 1, zc],
                                            device_id={"exp": (z + o) % n_exp}, device_id_type=MESH)

    def z1():
        load_at(zc).wait()
        swap_at(zc).wait_recv()
        for u in range(2):
            acc[zc, u] = plus(acc[zc, u], got[zc, u])
            for o in range(1, n_exp):
                z_out(u, o).start()

    def z2():
        for u in range(2):
            total = acc[zc, u, pl.ds(pl.multiple_of(z * e, e), e)].astype(F32)
            for o in range(1, n_exp):
                z_out(u, o).wait_recv()
                total = total + zz[u, o - 1].astype(F32)
            zs[u] = total.astype(BF)
            z_first(u).start()

    def z3():
        for u in range(2):
            z_first(u).wait_recv()
            r1[zc, u, 0:e2] = plus(zs[u, pl.ds(pl.multiple_of(bits[u][0] * e2, e2), e2)], r1[zc, u, 0:e2])
            z_second(u).start()

    def z4():
        for u in range(2):
            z_second(u).wait_recv()
            mine_rows = pl.ds(pl.multiple_of(z * e + bits[u][0] * e2 + bits[u][1] * e4, e4), e4)
            out_ref[zc, u, mine_rows] = plus(r1[zc, u, pl.ds(pl.multiple_of(bits[u][1] * e4, e4), e4)], r2[zc, u, 0:e4])
            z_third(u).start()

    def z5():
        for u in range(2):
            z_third(u).wait_recv()
            z_fourth(u).start()

    def z6():
        for u in range(2):
            z_fourth(u).wait_recv()
            for o in range(1, n_exp):
                z_back(u, o).start()

    def z7():
        for u in range(2):
            for o in range(1, n_exp):
                z_back(u, o).wait_recv()
        natural(zc)

    def drain(c, _):
        swap_at(c).wait_send()
        for u in range(2):
            for make in (first, second, third, fourth):
                make(u, c).wait_send()
            for o in range(1, n_exp):
                along(u, c, o).wait_send()
                back(u, c, o).wait_send()
        return 0

    legs = [({"mdl": 1 - core}), ({"grp": flat["x"]}), ({"grp": flat["y"]})]
    base = 2 * len(legs) + 1

    def small_leg(i):
        return pltpu.make_async_remote_copy(sm.at[2 * i], sm.at[2 * i + 1], s_send.at[i], s_recv.at[i], device_id=legs[i],
                                            device_id_type=MESH)

    def small_along(o):
        return pltpu.make_async_remote_copy(sm.at[base - 1], sm.at[base + z], s_send.at[len(legs) + o - 1],
                                            s_recv.at[len(legs) + o - 1], device_id={"exp": (z + o) % n_exp},
                                            device_id_type=MESH)

    def small_step(i):
        if i == 0:
            sm[0] = jnp.zeros(sm.shape[1:], F32)
            for k in range(4):
                sm[0, k : k + 1, :] = dg[k][...]
            sm[0, 4 : 4 + experts, :] = dr_ref[:experts, :]
        else:
            small_leg(i - 1).wait()
            sm[2 * i] = sm[2 * i - 2] + sm[2 * i - 1]
        if i < len(legs):
            small_leg(i).start()
        else:
            sm[pl.ds(base + z, 1)] = sm[pl.ds(base - 1, 1)]
            for o in range(1, n_exp):
                small_along(o).start()

    def natural(c):
        i, p = c // per, c % per
        side = rows // 2
        for u in range(2):
            v = 2 * p + u
            if i in (0, 3):
                qkv, proj = (qkv2, proj2) if i == 0 else (qkv1, proj1)
                if v < 3:
                    qkv[v] = out_ref[c, u]
                else:
                    for k in range(2):
                        proj[:, k * side : (k + 1) * side] = out_ref[c, u, k * side : (k + 1) * side]
            elif i == 1:
                fc_in[:, v * side : (v + 1) * side] = out_ref[c, u]
            else:
                fc_out[v % 2 * rows : (v % 2 + 1) * rows, v // 2 * side : (v // 2 + 1) * side] = out_ref[c, u]

    steps = (s1, s2, s3, s4, s5, s6, s7)
    waves = n - 1 + len(steps) - 1
    late = waves - 2
    z_steps = ((0, z1), (2, z2), (3, z3), (4, z4), (5, z5), (6, z6), (late, z7))
    small_steps = {1: 0, 3: 1, 5: 2, 7: 3}

    def wave(tau, _):
        for s, step in enumerate(steps):
            c = tau - s + 1

            @pl.when((c >= 1) & (c < n))
            def _(step=step, c=c):
                step(c)

        for at, step in z_steps:
            pl.when(tau == at)(step)
        for at, i in small_steps.items():
            pl.when(tau == at)(functools.partial(small_step, i))
        return 0

    first_waves = 2
    lax.fori_loop(0, first_waves, wave, 0)
    for cp in e_copies:
        cp.wait_recv()
    blocks = [[(beside(z, j), eouts[j]) for j in range(n_exp)], [(beside(z, j), e_oth.at[j]) for j in range(n_exp)]]
    y = mixture_output(experts, x3_ref, h4_ref, router_ref, col_ref, lambda k: merge_blocks(col_ref, k, blocks, x3_ref.shape[0]))
    for i in range(own_img):
        y_own[i] = y[i * LP : i * LP + L]
    for cp in image_copies(1, y_own, y_ref):
        cp.start()
    lax.fori_loop(first_waves, waves, wave, 0)
    for cp in e_copies:
        cp.wait_send()
    for k, (src, dst) in enumerate(((image_ref, gx_ref), (y_own, y_ref))):
        local, sent = image_copies(k, src, dst)
        local.wait()
        sent.wait_send()
        image_come(k, src, dst).wait_recv()
    lax.fori_loop(1, n, drain, 0)
    swap_at(zc).wait_send()
    for u in range(2):
        for make in (z_first, z_second, z_third, z_fourth):
            make(u).wait_send()
        for o in range(1, n_exp):
            z_out(u, o).wait_send()
            z_back(u, o).wait_send()
    for o in range(1, n_exp):
        small_along(o).wait()
    total = sm[base]
    for k in range(1, n_exp):
        total = total + sm[base + k]
    sum_ref[...] = total


def reduce_all(mine, other, dgs, dr, x3, h4, router, col, eouts, image, n_exp, experts):
    per, _, rows, c = mine[0].shape
    n = len(mine) * per
    d, f = 2 * c, 4 * c
    h, q = rows // 2, rows // 4
    t = q // n_exp
    small = (-(-(4 + experts) // 8) * 8, d)
    n_img, length, _ = image.shape
    D, V = pltpu.SemaphoreType.DMA, pltpu.VMEM
    any_ = pl.BlockSpec(memory_space=pl.ANY)
    vm = pl.BlockSpec(memory_space=pltpu.VMEM)
    return pl.pallas_call(
        functools.partial(reduce_body, len(mine), per, n_exp, experts),
        in_specs=[any_] * (2 * len(mine)) + [vm] * 13 + [any_],
        out_specs=[vm] * 9,
        out_shape=[out((3, d, c), BF), out((c, d), BF), out((d, f), BF), out((f, d), BF), out((3, d, c), BF), out((c, d), BF),
                   out(small, F32), out((2 * n_img, length, d), BF), out((2 * n_img, length, d), BF)],
        scratch_shapes=[
            V((n, 2, rows, c), BF), V((n, 2, rows, c), BF), V((n, 2, h, c), BF), V((n, 2, q, c), BF),
            V((n, 2, n_exp - 1, t, c), BF), V((2, n_exp - 1, rows // n_exp, c), BF), V((2, rows // n_exp, c), BF),
            V((7 + n_exp,) + small, F32), V((n_img, length, d), BF),
            D((n,)), D((n,)), D((n,)), D((4, 2, n)), D((4, 2, n)), D((2, 2, n_exp - 1, n)), D((2, 2, n_exp - 1, n)),
            D((3 + n_exp,)), D((3 + n_exp,)), D((2,)), D((2,)), D((2,)), V((n_exp,) + eouts[0].shape, BF), D((n_exp,)), D((n_exp,)),
        ],
        compiler_params=pltpu.CompilerParams(collective_id=0, has_side_effects=True, vmem_limit_bytes=VMEM_BYTES),
        cost_estimate=pl.CostEstimate(flops=8 * x3.shape[0] * x3.shape[0] * d, bytes_accessed=n * 8 * rows * c, transcendentals=0),
    )(*mine, *other, *dgs, dr, x3, h4, router, col, *eouts, image)


def expert_exchange_body(experts, half, h4_ref, tr_ref, dy0, dy1, dy2, dy3, router_ref, im, io, tm, to,
                         ret_ref, dg_ref, e0, e1, e2, e3, gw_ref,
                         h_oth, part, xo, x, wi, wo, act, dz, wd, acc, dxa, rsend, gscr, ggot, xt, wt,
                         w_sem, swap_sem, x_send, x_recv, r_send, r_recv, f_send, f_recv, g_send, g_recv, g_sem,
                         dgs, l_send, l_recv, k_send, k_recv):
    n, d = h4_ref.shape
    f = im.shape[1]
    t = 256 if f % 256 == 0 else tile_of(f)
    z = lax.axis_index("exp")
    core = lax.axis_index("mdl")
    partner = {"mdl": 1 - core}
    size = experts
    near_first = [1, 3, 2]

    out_grad, eouts = (dy0, dy1, dy2, dy3), (e0, e1, e2, e3)

    def there(j):
        return beside(z, j)

    loads = [pltpu.make_async_copy(src, dst, w_sem.at[k]) for k, (src, dst) in enumerate(
        ((im, wi.at[0]), (io, wi.at[1]), (tm, wo.at[0]), (to, wo.at[1])))]
    for cp in loads:
        cp.start()
    barrier = pltpu.get_barrier_semaphore()
    for dev in [partner] + [{"exp": there(j)} for j in range(1, size)]:
        pl.semaphore_signal(barrier, inc=1, device_id=dev, device_id_type=MESH)
    pl.semaphore_wait(barrier, size)
    swap = pltpu.make_async_remote_copy(h4_ref, h_oth, swap_sem.at[0], swap_sem.at[1], device_id=partner, device_id_type=MESH)
    swap.start()

    own_img = n // LP
    base = core * size * half

    def spread(side, v, j):
        total = None
        for i in range(own_img):
            p = nn(slot_hots(tr_ref[side * own_img + i], base + there(j) * half, half), v[i * LP : (i + 1) * LP, :])
            total = p if total is None else total + p
        return total

    def rows(j):
        return slice(j * half, (j + 1) * half)

    def place(e):
        return pl.ds(pl.multiple_of(e * half, half), half)

    for j in near_first + [0]:
        part[rows(j), :] = spread(core, h4_ref, j)
    swap.wait_recv()
    sends = {}
    for j in near_first + [0]:
        block = (part[rows(j), :] + spread(1 - core, h_oth, j)).astype(BF)
        if j == 0:
            x[rows(0), :] = block
        else:
            xo[rows(j), :] = block
            sends[j] = pltpu.make_async_remote_copy(xo.at[rows(j)], x.at[rows(j)], x_send.at[j], x_recv.at[j],
                                                    device_id={"exp": there(j)}, device_id_type=MESH)
            sends[j].start()

    returns, forwards = {}, {}

    def forward(j):
        here = ret_ref.at[0, place(there(j))]
        forwards[j] = (
            pltpu.make_async_remote_copy(here, ret_ref.at[1, place(there(j))], f_send.at[j], f_recv.at[j],
                                         device_id=partner, device_id_type=MESH),
            pltpu.make_async_remote_copy(dg_ref.at[0, there(j)], dg_ref.at[1, there(j)], k_send.at[j], k_recv.at[j],
                                         device_id=partner, device_id_type=MESH))
        for cp in forwards[j]:
            cp.start()

    def run(blocks):
        r0, r1 = blocks[0] * half, (blocks[-1] + 1) * half
        m = r1 - r0
        for j in blocks:
            probs, lane = router_probs(x[rows(j), :], router_ref[...], experts)
            gate = jnp.sum(jnp.where(lane == z, probs, 0.0), axis=-1, keepdims=True)
            wd[rows(j), :] = (gate * out_grad[j][...].astype(F32)).astype(BF)
        acc[0:m, :] = jnp.zeros((m, d), F32)
        dxa[0:m, :] = jnp.zeros((m, d), F32)

        def tile(i, _):
            at = pl.ds(pl.multiple_of(i * t, t), t)
            for side in range(2):
                a, s = gelu_parts(nn(x[r0:r1, :], wi[side, :, at]))
                a = a.astype(BF)
                act[side, r0:r1, at] = a
                acc[0:m, :] += nn(a, wo[side, at, :])
                g = (nt(wd[r0:r1, :], wo[side, at, :]) * s).astype(BF)
                dz[side, r0:r1, at] = g
                dxa[0:m, :] += nt(g, wi[side, :, at])
            return 0

        lax.fori_loop(0, f // t, tile, 0)
        for b, j in enumerate(blocks):
            here = slice(b * half, (b + 1) * half)
            e_rows = acc[here, :].astype(BF)
            eouts[j][...] = e_rows
            dgate = jnp.sum(out_grad[j][...].astype(F32) * e_rows.astype(F32), axis=-1, keepdims=True)
            lines = gate_lines(dgate)
            if j == 0:
                ret_ref[0, place(z), :] = dxa[here, :].astype(BF)
                dg_ref[0, pl.ds(z, 1)] = lines[None]
                forward(0)
            else:
                rsend[rows(j), :] = dxa[here, :].astype(BF)
                dgs[j] = lines
                returns[j] = (
                    pltpu.make_async_remote_copy(rsend.at[rows(j)], ret_ref.at[0, place(z)], r_send.at[j], r_recv.at[j],
                                                 device_id={"exp": there(j)}, device_id_type=MESH),
                    pltpu.make_async_remote_copy(dgs.at[j], dg_ref.at[0, z], l_send.at[j], l_recv.at[j],
                                                 device_id={"exp": there(j)}, device_id_type=MESH))
                for cp in returns[j]:
                    cp.start()

    for cp in loads:
        cp.wait()
    sends[1].wait_recv()
    run([0, 1])
    for j in near_first[1:]:
        sends[j].wait_recv()
        run([j])

    xt[...] = x[...].T
    wt[...] = wd[...].T

    tiles = f // t

    def cols(i):
        return pl.ds(pl.multiple_of(i * t, t), t)

    def swapped(i):
        return pltpu.make_async_remote_copy(gscr.at[1, :, :, cols(i)], ggot.at[:, :, cols(i)], g_send.at[i], g_recv.at[i],
                                            device_id=partner, device_id_type=MESH)

    def stored(i):
        return pltpu.make_async_copy(gscr.at[0, :, :, cols(i)], gw_ref.at[:, :, cols(i)], g_sem.at[i])

    def weight_tile(i, _):
        for side in (1, 0):
            gscr[side, 0, :, cols(i)] = nn(xt[...], dz[side, :, cols(i)]).astype(BF)
            gscr[side, 1, :, cols(i)] = nn(wt[...], act[side, :, cols(i)]).astype(BF)
            if side == 1:
                swapped(i).start()
        return 0

    lax.fori_loop(0, tiles, weight_tile, 0)

    def sum_tile(i, _):
        swapped(i).wait_recv()
        for k in range(2):
            gscr[0, k, :, cols(i)] = (gscr[0, k, :, cols(i)].astype(F32) + ggot[k, :, cols(i)].astype(F32)).astype(BF)
        stored(i).start()
        return 0

    lax.fori_loop(0, tiles, sum_tile, 0)

    for j in near_first:
        pltpu.make_async_remote_copy(rsend.at[rows(j)], ret_ref.at[0, place(there(j))], r_send.at[j], r_recv.at[j],
                                     device_id={"exp": there(j)}, device_id_type=MESH).wait_recv()
        pltpu.make_async_remote_copy(dgs.at[j], dg_ref.at[0, there(j)], l_send.at[j], l_recv.at[j],
                                     device_id={"exp": there(j)}, device_id_type=MESH).wait_recv()
        forward(j)

    def drain(i, _):
        stored(i).wait()
        swapped(i).wait_send()
        return 0

    lax.fori_loop(0, tiles, drain, 0)
    swap.wait_send()
    for j in range(size):
        if j:
            sends[j].wait_send()
            for cp in returns[j]:
                cp.wait_send()
        for cp in forwards[j]:
            cp.wait()


def expert_exchange(h4, tr, dys, router, im, io, tm, to, experts, half):
    n, d = h4.shape
    f = im.shape[1]
    s = experts * half
    wide = -(-half // LANES) * LANES
    tiles = f // (256 if f % 256 == 0 else tile_of(f))
    D, V = pltpu.SemaphoreType.DMA, pltpu.VMEM
    any_ = pl.BlockSpec(memory_space=pl.ANY)
    vm = pl.BlockSpec(memory_space=pltpu.VMEM)
    return pl.pallas_call(
        functools.partial(expert_exchange_body, experts, half),
        in_specs=[vm] * 7 + [any_] * 4,
        out_specs=[vm] * 6 + [any_],
        out_shape=[out((2, s, d), BF), out((2, experts, 8, wide), F32)] + [out((half, d), BF)] * 4 + [out((2, d, f), BF)],
        scratch_shapes=[
            V((n, d), BF), V((s, d), F32), V((s, d), BF), V((s, d), BF), V((2, d, f), BF), V((2, f, d), BF),
            V((2, s, f), BF), V((2, s, f), BF), V((s, d), BF), V((2 * half, d), F32), V((2 * half, d), F32),
            V((s, d), BF), V((2, 2, d, f), BF), V((2, d, f), BF), V((d, s), BF), V((d, s), BF),
            D((4,)), D((2,)), D((experts,)), D((experts,)), D((experts,)), D((experts,)), D((experts,)), D((experts,)),
            D((tiles,)), D((tiles,)), D((tiles,)),
            V((experts, 8, wide), F32), D((experts,)), D((experts,)), D((experts,)), D((experts,)),
        ],
        compiler_params=pltpu.CompilerParams(collective_id=1, has_side_effects=True, vmem_limit_bytes=VMEM_BYTES),
        cost_estimate=pl.CostEstimate(flops=24 * s * d * f, bytes_accessed=20 * d * f, transcendentals=0),
    )(h4, tr, *dys, router, im, io, tm, to)


FUSED = True


def on_device(images, counts, routes, priority, gain_one, qkv_one, out_one, gain_two, fc_in, fc_out, gain_three,
              qkv_two, out_two, gain_four, router, expert_in, expert_out, cotangent):
    n_slot, length, d = images.shape
    experts = router.shape[1]
    n_mdl = lax.axis_size("mdl")
    peers = lax.axis_size("exp")
    capacity = (25 * L * TOPK + 8 * experts - 1) // (8 * experts)
    half = -(-(-(-capacity // n_mdl)) // 16) * 16
    slots = experts * half
    own_img = n_slot // n_mdl
    f = fc_in.shape[1]
    c = qkv_one.shape[2]
    rows = own_img * LP
    core = lax.axis_index("mdl")
    per = 2
    unit = 4 * d // (2 * per)
    fused = FUSED and (lax.axis_size("grp"), peers, n_mdl) == (4, experts, 2) and peers == 4
    fused = fused and d == 2 * c and f == 4 * c and unit % (64 * peers) == 0

    def padded(v):
        return jnp.pad(v, ((0, 0), (0, LP - length), (0, 0))).reshape(n_slot * LP, -1)

    qm1, om1, im, tm, qm2, om2, em, fm = halves = (
        qkv_one, out_one, fc_in, fc_out, qkv_two, out_two, expert_in[0], expert_out[0])
    gains = jnp.stack([gain_one, gain_two, gain_three, gain_four])
    router_rows = jnp.pad(router.T, ((0, LANES - experts), (0, 0)))

    live = jnp.broadcast_to((jnp.arange(n_slot, dtype=I32) < counts[0, 0]).astype(I32)[:, None, None], (n_slot, 1, length))
    lines = jnp.concatenate([jnp.transpose(routes, (0, 2, 1)), priority.reshape(n_slot, 1, length), live], axis=1)
    lines = jnp.pad(lines, ((0, 0), (0, 4), (0, LQ - length)))
    blocks = [(half, d)] * peers if fused else [(slots, d)]
    slot_rows, col, *dy_out = call(
        functools.partial(routing_body, experts, capacity, half),
        [out((n_slot, 8, LQ), I32), out((rows, 8), I32)] + [out(b, BF) for b in blocks], lines, cotangent,
        scratch=[pltpu.VMEM((n_slot * LP, d), BF), pltpu.VMEM((8, LQ), I32)], flops=4 * slots * n_slot * LP * d,
    )
    def exchange(v):
        shaped = v.reshape(peers, v.shape[0] // peers, v.shape[1])
        return lax.all_to_all(shaped, "exp", 0, 0, tiled=True).reshape(v.shape)

    if fused:
        got, (qo1, oo1, io, to, qo2, oo2, eo, fo), dy_in = forward(images, gains, halves, dy_out[1:], rows)
        x1, *kept1, x2, h2, act2, slope2, x3 = got[:10]
        kept3, h4, x0 = got[10:14], got[14], got[15]
        dy_in = [dy_out[0], *dy_in]
    else:
        x0 = padded(images)
        qo1, oo1, io, to, qo2, oo2, eo, fo = (other_core(w) for w in halves)
        dy_in = exchange(dy_out[0])
        x1, *kept1 = attention_forward(x0, rows, gains, 0, qm1, qo1, om1, oo1)
        x2, h2, act2, slope2 = mlp_forward(x1, gains, 1, im, io, tm, to)
        x3, *kept3, h4 = attention_forward(x2, rows, gains, 2, qm2, qo2, om2, oo2, tail=3)

    if fused:
        ret, dgate, *eout, ge = expert_exchange(h4, slot_rows, dy_in, router_rows, em, eo, fm, fo, experts, half)
        (dg1, dg2, dg3, dg4, dr, image), grads, eback = backward(
            experts, half, x3, h4, router_rows, cotangent, col, ret, dgate, gains, x2, kept3, (qm2, qo2, om2, oo2),
            x1, h2, act2, slope2, (im, io, tm, to), x0, kept1, (qm1, qo1, om1, oo1), eout[1:])
        a2_mine, a2_other, gim, gio, gtm, gto, a1_mine, a1_other = grads
        eback = [eout[0], *eback]
    else:
        [h4_out] = call(functools.partial(dispatch_body, experts, half), [out((slots, d), BF)], slot_rows, h4, other_core(h4))
        h4_in = exchange(h4_out)
        eout, ret, eact, edz, ewd = expert_forward_backward(h4_in, dy_in, router_rows, em, eo, fm, fo, experts)
        ret, eout = exchange(ret), exchange(eout)
        ret, eback = jnp.stack([ret, other_core(ret)]), jnp.stack([eout, other_core(eout)])
        dgate = ret[:, :, d].astype(F32) + ret[:, :, d + LANES // 2].astype(F32)
        wide = -(-half // LANES) * LANES
        dgate = jnp.pad(dgate.reshape(2, experts, 1, half), ((0, 0), (0, 0), (0, 7), (0, wide - half)))
        ret = ret[:, :, :d]
        ge_mine, ge_other = expert_weights(h4_in, ewd, eact, edz)
        ge = add16(ge_mine, other_core(ge_other))
        dx2, dg3, dg4, dr, a2_mine, a2_other = mixture_attention_backward(
            experts, half, x3, h4, router_rows, cotangent, col, ret, dgate, x2, gains, kept3, qm2, qo2, om2, oo2)
        dx1, dg2, gim, gio, gtm, gto = mlp_backward(dx2, x1, gains, 1, h2, act2, slope2, im, io, tm, to, c)
        image, dg1, a1_mine, a1_other = attention_backward(dx1, x0, gains, 0, kept1, qm1, qo1, om1, oo1)
    expert_sum = lax.psum_scatter(ge, "grp", scatter_dimension=1, tiled=True)

    mines, others = (a2_mine, gim, gtm, a1_mine), (a2_other, gio, gto, a1_other)

    if fused:
        split = [[v.reshape(per, 2, unit, c) for v in side] for side in (mines, others)]
        qkv2, proj2, fi, fo_, qkv1, proj1, small, output, grad_images = reduce_all(
            *split, (dg1, dg2, dg3, dg4), dr, x3, h4, router_rows, col, eback, image, peers, experts)
    else:
        sums = [sum_everywhere(add16(a.reshape(4 * d, c), other_core(b.reshape(4 * d, c)))) for a, b in zip(mines, others)]
        small = small_sum(jnp.concatenate([dg1, dg2, dg3, dg4, dr[:experts]], axis=0))

        def panels(v):
            return jnp.concatenate([v[i] for i in range(v.shape[0])], axis=1)

        (qkv2, proj2), (qkv1, proj1) = (
            (v[: 3 * d].reshape(3, d, c), panels(v[3 * d :].reshape(d // c, c, c))) for v in (sums[0], sums[3]))
        fi, fo_ = panels(sums[1].reshape(f // c, d, c)), panels(sums[2].reshape(d // c, f, c))
        [own_out] = call(
            functools.partial(mixture_output_body, experts), [out((own_img, L, d), BF)], x3, h4, router_rows, col, eback,
            flops=8 * rows * slots * d)

        def both(v):
            there = other_core(v)
            return jnp.where(core == 0, jnp.concatenate([v, there]), jnp.concatenate([there, v]))

        output, grad_images = both(own_out), both(image)
    return (
        output, grad_images,
        small[0], qkv1.astype(F32), proj1.astype(F32), small[1], fi.astype(F32), fo_.astype(F32),
        small[2], qkv2.astype(F32), proj2.astype(F32), small[3], small[4 : 4 + experts].T,
        expert_sum[0].astype(F32)[None], expert_sum[1].astype(F32).T[None],
    )


def solution(mesh):
    token = P(("grp", "exp"), None, None)
    column, line = P(None, None, "mdl"), P("mdl", None)
    return jax.shard_map(
        on_device,
        mesh=mesh,
        in_specs=(token, P("grp", "exp"), token, P(("grp", "exp"), None), P(), column, line, P(), P(None, "mdl"), line,
                  P(), column, line, P(), P(), P("exp", None, "mdl"), P("exp", "mdl", None), token),
        out_specs=(token, token, P(), column, line, P(), P(None, "mdl"), line, P(), column, line, P(), P(),
                   P("exp", "grp", "mdl"), P("exp", "mdl", "grp")),
        check_vma=False,
    )
```

```python
import functools
import math

import jax
import jax.numpy as jnp
from jax import lax
from jax.experimental import pallas as pl
from jax.experimental.pallas import tpu as pltpu
from jax.sharding import PartitionSpec as P

HDIM = 64
L = 197
TOPK = 2
LP = (L + 15) // 16 * 16
LANES = 128
LQ = (L + LANES - 1) // LANES * LANES
BF = jnp.bfloat16
F32 = jnp.float32
I32 = jnp.int32

EPSILON = 1e-06
ROOT_HALF = 0.7071067811865476
DENSITY_FACTOR = 0.3989422804014327
VMEM_BYTES = 60 * 1024 * 1024
MESH = pl.DeviceIdType.MESH


def nn(a, b):
    return lax.dot_general(a, b, (((1,), (0,)), ((), ())), preferred_element_type=F32)


def nt(a, b):
    return lax.dot_general(a, b, (((1,), (1,)), ((), ())), preferred_element_type=F32)


def tn(a, b):
    return lax.dot_general(a, b, (((0,), (0,)), ((), ())), preferred_element_type=F32)


def norm_forward(v, w):
    c = v - jnp.mean(v, axis=-1, keepdims=True)
    r = lax.rsqrt(jnp.mean(c * c, axis=-1, keepdims=True) + EPSILON)
    n = c * r
    return n, r, (n * w).astype(BF)


def norm_backward(n, r, w, dh):
    dn = dh * w
    dw = jnp.sum(dh * n, axis=0, keepdims=True)
    dv = r * (dn - jnp.mean(dn, axis=-1, keepdims=True) - n * jnp.mean(dn * n, axis=-1, keepdims=True))
    return dv, dw


def whole(shape):
    return pl.BlockSpec(shape, lambda *i: (0,) * len(shape))


def call(body, out_shape, *args, grid=(), in_specs=None, out_specs=None, scratch=(), flops=0):
    if in_specs is None:
        in_specs = [whole(a.shape) for a in args]
    if out_specs is None:
        out_specs = [whole(o.shape) for o in out_shape]
    moved = sum(math.prod(a.shape) * a.dtype.itemsize for a in args)
    moved += sum(math.prod(o.shape) * jnp.dtype(o.dtype).itemsize for o in out_shape)
    return pl.pallas_call(
        body,
        grid=grid,
        in_specs=in_specs,
        out_specs=out_specs,
        out_shape=out_shape,
        scratch_shapes=list(scratch),
        cost_estimate=pl.CostEstimate(flops=int(flops), bytes_accessed=int(moved), transcendentals=0),
        compiler_params=pltpu.CompilerParams(vmem_limit_bytes=VMEM_BYTES),
    )(*args)


def out(shape, dtype):
    return jax.ShapeDtypeStruct(shape, dtype)


def head_mask(dtype):
    lane = lax.broadcasted_iota(I32, (LP, LANES), 1)
    return (lane < HDIM).astype(dtype)


def beside(z, j):
    b0, b1 = z % 2, z // 2
    if j & 1:
        b0 = 1 - b0
    if j & 2:
        b1 = 1 - b1
    return b0 + 2 * b1


def fill_rows(ref, at, images, first, count):
    for i in range(count):
        ref[at + i * LP : at + i * LP + L, :] = images[first + i].astype(ref.dtype)
        ref[at + i * LP + L : at + (i + 1) * LP, :] = jnp.zeros((LP - L, ref.shape[1]), ref.dtype)


def own_rows(ref, n):
    if ref.shape[0] == n:
        return ref[...]
    return ref[pl.ds(pl.multiple_of(lax.axis_index("mdl") * n, 16), n), :]


def attend(img, pair, d, qkv_ref, p_ref, o_ref):
    mask = head_mask(BF)
    key_ok = lax.broadcasted_iota(I32, (LP, LP), 1) < L
    rows = pl.ds(pl.multiple_of(img * LP, LP), LP)
    col = pair * LANES
    q = qkv_ref[rows, pl.ds(pl.multiple_of(col, LANES), LANES)]
    ke = qkv_ref[rows, pl.ds(pl.multiple_of(d + col, LANES), LANES)]
    u = qkv_ref[rows, pl.ds(pl.multiple_of(2 * d + col, LANES), LANES)]
    o = jnp.zeros((LP, LANES), F32)
    for hh in range(2):
        mk = mask if hh == 0 else 1 - mask
        s = nt(q * mk, ke) * HDIM ** (-0.5)
        s = jnp.where(key_ok, s, -1e30)
        e = jnp.exp(s - jnp.max(s, axis=-1, keepdims=True))
        p = (e / jnp.sum(e, axis=-1, keepdims=True)).astype(BF)
        p_ref[2 * (img * (d // LANES) + pair) + hh] = p
        o = o + nn(p, u * mk)
    o_ref[rows, pl.ds(pl.multiple_of(col, LANES), LANES)] = o.astype(BF)
    return 0


def attention_forward_body(n_img, g_at, tail, *refs):
    refs = list(refs)
    x_ref, g_ref, qm, qo, om, oo = refs[:6]
    del refs[:6]
    y_ref, h_ref, qkv_ref, p_ref, o_ref = refs[:5]
    del refs[:5]
    h4_ref = refs.pop(0) if tail is not None else None
    rows_all = n_img * LP
    d = x_ref.shape[1]
    c = qm.shape[2]
    pairs = d // LANES
    _, _, h = norm_forward(own_rows(x_ref, rows_all).astype(F32), g_ref[g_at : g_at + 1, :])
    h_ref[...] = h
    for k in range(3):
        for side, w in ((0, qm), (1, qo)):
            at = (2 * k + side) * c
            qkv_ref[:, at : at + c] = nn(h_ref[...], w[k]).astype(BF)
    lax.fori_loop(0, n_img * pairs, lambda i, _: attend(i // pairs, i % pairs, d, qkv_ref, p_ref, o_ref), 0, unroll=2)
    y = own_rows(x_ref, rows_all).astype(F32) + nn(o_ref[:, :c], om[...]) + nn(o_ref[:, c:], oo[...])
    y_ref[...] = y
    if tail is not None:
        _, _, h4 = norm_forward(y, g_ref[tail : tail + 1, :])
        h4_ref[...] = h4


def attention_forward(x, r, gains, g_at, qm, qo, om, oo, tail=None):
    d = x.shape[1]
    n_img = r // LP
    heads = d // HDIM
    shapes = [out((r, d), F32), out((r, d), BF), out((r, 3 * d), BF), out((n_img * heads, LP, LP), BF), out((r, d), BF)]
    if tail is not None:
        shapes.append(out((r, d), BF))
    return call(functools.partial(attention_forward_body, n_img, g_at, tail), shapes, x, gains, qm, qo, om, oo,
                flops=2 * r * d * d * 4 + 4 * n_img * heads * LP * LP * LANES)


def attention_backward_core(n_img, dy, x_ref, gain, h_ref, qkv_ref, p_ref, o_ref, qm, qo, om, oo,
                            gm_ref, go_ref, do_ref, dqkv_ref, tr_ref):
    d = x_ref.shape[1]
    c = qm.shape[2]
    pairs = d // LANES
    da = dy().astype(BF)
    tr_ref[...] = o_ref[...].T
    for side, (w, g) in enumerate(((om, gm_ref), (oo, go_ref))):
        gw = nn(tr_ref[side * c : (side + 1) * c, :], da).astype(BF)
        for part in range(d // c):
            g[3 * d + part * c : 3 * d + (part + 1) * c, :] = gw[:, part * c : (part + 1) * c]
        do_ref[:, side * c : (side + 1) * c] = nt(da, w[...]).astype(BF)
    mask = head_mask(BF)

    def one(i, _):
        rows = pl.ds(pl.multiple_of((i // pairs) * LP, LP), LP)
        col = (i % pairs) * LANES
        cq = pl.ds(pl.multiple_of(col, LANES), LANES)
        ck = pl.ds(pl.multiple_of(d + col, LANES), LANES)
        cu = pl.ds(pl.multiple_of(2 * d + col, LANES), LANES)
        q, ke, u, do = qkv_ref[rows, cq], qkv_ref[rows, ck], qkv_ref[rows, cu], do_ref[rows, cq]
        dq = jnp.zeros((LP, LANES), F32)
        dk = jnp.zeros((LP, LANES), F32)
        du = jnp.zeros((LP, LANES), F32)
        for hh in range(2):
            mk = mask if hh == 0 else 1 - mask
            p = p_ref[2 * i + hh]
            du = du + tn(p, do * mk)
            dp = nt(do * mk, u)
            pf = p.astype(F32)
            ds = (pf * (dp - jnp.sum(dp * pf, axis=-1, keepdims=True))).astype(BF)
            dq = dq + nn(ds, ke * mk)
            dk = dk + tn(ds, q * mk)
        dqkv_ref[rows, cq] = (dq * HDIM ** (-0.5)).astype(BF)
        dqkv_ref[rows, ck] = (dk * HDIM ** (-0.5)).astype(BF)
        dqkv_ref[rows, cu] = du.astype(BF)
        return 0

    lax.fori_loop(0, n_img * pairs, one, 0, unroll=2)
    tr_ref[...] = h_ref[...].T
    dh = jnp.zeros((n_img * LP, d), F32)
    for k in range(3):
        for side, (w, g) in enumerate(((qm, gm_ref), (qo, go_ref))):
            at = (2 * k + side) * c
            g[k * d : (k + 1) * d, :] = nn(tr_ref[...], dqkv_ref[:, at : at + c]).astype(BF)
            dh = dh + nt(dqkv_ref[:, at : at + c], w[k])
    n, rr, _ = norm_forward(own_rows(x_ref, n_img * LP).astype(F32), gain)
    dv, dw = norm_backward(n, rr, gain, dh)
    return dy() + dv, dw


def attention_backward_body(n_img, g_at, dy_ref, x_ref, g_ref, h_ref, qkv_ref, p_ref, o_ref, qm, qo, om, oo,
                            dx_ref, dw_ref, gm_ref, go_ref, do_ref, dqkv_ref, tr_ref):
    dx, dw = attention_backward_core(
        n_img, lambda: dy_ref[...], x_ref, g_ref[g_at : g_at + 1, :], h_ref, qkv_ref, p_ref, o_ref, qm, qo, om, oo,
        gm_ref, go_ref, do_ref, dqkv_ref, tr_ref)
    for i in range(n_img):
        dx_ref[i] = dx[i * LP : i * LP + L].astype(BF)
    dw_ref[...] = dw


def attention_backward_scratch(r, d):
    return [pltpu.VMEM((r, d), BF), pltpu.VMEM((r, 3 * d), BF), pltpu.VMEM((d, r), BF)]


def attention_backward(dy, x, gains, g_at, kept, qm, qo, om, oo):
    r, d = dy.shape
    c = qm.shape[2]
    n_img = r // LP
    heads = d // HDIM
    return call(
        functools.partial(attention_backward_body, n_img, g_at),
        [out((n_img, L, d), BF), out((1, d), F32), out((3 * d + d, c), BF), out((3 * d + d, c), BF)],
        dy, x, gains, *kept, qm, qo, om, oo,
        scratch=attention_backward_scratch(r, d),
        flops=4 * r * d * d * 4 + 8 * n_img * heads * LP * LP * LANES,
    )


def gelu_parts(z):
    phi = 0.5 * (1.0 + lax.erf(z * ROOT_HALF))
    return z * phi, phi + z * jnp.exp(-0.5 * z * z) * DENSITY_FACTOR


def tile_of(f):
    for t in (512, 256, 128):
        if f % t == 0:
            return t
    return f


def mlp_forward_body(g_at, x_ref, g_ref, im, io, tm, to, y_ref, h_ref, act_ref, slope_ref, acc_ref):
    step = pl.program_id(0)

    @pl.when(step == 0)
    def _():
        x = x_ref[...]
        _, _, h = norm_forward(x, g_ref[g_at : g_at + 1, :])
        h_ref[...] = h
        acc_ref[...] = x

    for half, (wi, wo) in enumerate(((im, tm), (io, to))):
        a, s = gelu_parts(nn(h_ref[...], wi[...]))
        act = a.astype(BF)
        act_ref[half] = act
        slope_ref[half] = s.astype(BF)
        acc_ref[...] += nn(act, wo[...])

    @pl.when(step == pl.num_programs(0) - 1)
    def _():
        y_ref[...] = acc_ref[...]


def mlp_forward(x, gains, g_at, im, io, tm, to):
    r, d = x.shape
    f = im.shape[1]
    t = tile_of(f)
    col = pl.BlockSpec((d, t), lambda i: (0, i))
    row = pl.BlockSpec((t, d), lambda i: (i, 0))
    hid = pl.BlockSpec((2, r, t), lambda i: (0, 0, i))
    return call(
        functools.partial(mlp_forward_body, g_at),
        [out((r, d), F32), out((r, d), BF), out((2, r, f), BF), out((2, r, f), BF)],
        x, gains, im, io, tm, to, grid=(f // t,),
        in_specs=[whole((r, d)), whole(gains.shape), col, col, row, row],
        out_specs=[whole((r, d)), whole((r, d)), hid, hid],
        scratch=[pltpu.VMEM((r, d), F32)], flops=8 * r * d * f,
    )


def mlp_backward_body(g_at, dy_ref, x_ref, g_ref, h_ref, act_ref, slope_ref, im, io, tm, to,
                      dx_ref, dw_ref, gim, gio, gtm, gto, da_ref, tr_ref, dh_ref):
    step = pl.program_id(0)

    @pl.when(step == 0)
    def _():
        da_ref[...] = dy_ref[...].astype(BF)
        tr_ref[...] = h_ref[...].T
        dh_ref[...] = jnp.zeros_like(dh_ref)

    for half, (wi, wo, gi, go) in enumerate(((im, tm, gim, gtm), (io, to, gio, gto))):
        dact = nt(da_ref[...], wo[...])
        dz = (dact * slope_ref[half].astype(F32)).astype(BF)
        gw = tn(act_ref[half], da_ref[...]).astype(BF)
        t = gw.shape[0]
        for part in range(gw.shape[1] // t):
            go[part] = gw[:, part * t : (part + 1) * t]
        gi[0] = nn(tr_ref[...], dz).astype(BF)
        dh_ref[...] += nt(dz, wi[...])

    @pl.when(step == pl.num_programs(0) - 1)
    def _():
        gain = g_ref[g_at : g_at + 1, :]
        n, rr, _ = norm_forward(x_ref[...], gain)
        dv, dw = norm_backward(n, rr, gain, dh_ref[...])
        dx_ref[...] = dy_ref[...] + dv
        dw_ref[...] = dw


def mlp_backward(dy, x, gains, g_at, h, act, slope, im, io, tm, to, t):
    r, d = x.shape
    f = im.shape[1]
    col = pl.BlockSpec((d, t), lambda i: (0, i))
    row = pl.BlockSpec((t, d), lambda i: (i, 0))
    hid = pl.BlockSpec((2, r, t), lambda i: (0, 0, i))
    gin = pl.BlockSpec((1, d, t), lambda i: (i, 0, 0))
    gout = pl.BlockSpec((d // t, t, t), lambda i: (0, i, 0))
    return call(
        functools.partial(mlp_backward_body, g_at),
        [out((r, d), F32), out((1, d), F32), out((f // t, d, t), BF), out((f // t, d, t), BF),
         out((d // t, f, t), BF), out((d // t, f, t), BF)],
        dy, x, gains, h, act, slope, im, io, tm, to, grid=(f // t,),
        in_specs=[whole((r, d)), whole((r, d)), whole(gains.shape), whole((r, d)), hid, hid, col, col, row, row],
        out_specs=[whole((r, d)), whole((1, d)), gin, gin, gout, gout],
        scratch=[pltpu.VMEM((r, d), BF), pltpu.VMEM((d, r), BF), pltpu.VMEM((r, d), F32)], flops=16 * r * d * f,
    )


def forward_body(n_img, size, *refs):
    refs = list(refs)

    def take(n):
        r = refs[:n]
        del refs[:n]
        return r

    images, g_ref = take(2)
    own_w = take(8)
    dy_out = take(size - 1)
    results = take(16)
    other_w = take(8)
    dy_in = take(size - 1)
    weights = take(6)
    held = take(16)
    load_sem, w_send, w_recv, o_sem, r_sem, d_send, d_recv = refs
    x1, h1, qkv1, p1, o1, x2, h2, act, slope, x3, h3, qkv3, p3, o3, h4, x0 = held
    q1, w1, fi, fo, q3, w3 = weights
    r = n_img * LP
    d = x0.shape[1]
    c = q1.shape[3]
    f = fi.shape[2]
    z = lax.axis_index("exp")
    partner = {"mdl": 1 - lax.axis_index("mdl")}

    loads = [pltpu.make_async_copy(own_w[k], weights[k].at[0], load_sem.at[k]) for k in range(6)]
    for cp in loads:
        cp.start()
    barrier = pltpu.get_barrier_semaphore()
    for dev in [partner] + [{"exp": beside(z, j)} for j in range(1, size)]:
        pl.semaphore_signal(barrier, inc=1, device_id=dev, device_id_type=MESH)
    pl.semaphore_wait(barrier, size)
    swaps = [pltpu.make_async_remote_copy(own_w[k], weights[k].at[1] if k < 6 else other_w[k], w_send.at[k], w_recv.at[k],
                                          device_id=partner, device_id_type=MESH) for k in range(8)]
    for cp in swaps[0:2]:
        cp.start()
    blocks = [pltpu.make_async_remote_copy(dy_out[j - 1], dy_in[j - 1], d_send.at[j - 1], d_recv.at[j - 1],
                                           device_id={"exp": beside(z, j)}, device_id_type=MESH) for j in range(1, size)]
    for cp in blocks:
        cp.start()
    keeps = [pltpu.make_async_copy(weights[k].at[1], other_w[k], o_sem.at[k]) for k in range(6)]
    stores = [pltpu.make_async_copy(held[k], results[k], r_sem.at[k]) for k in range(16)]

    def store(*at):
        for k in at:
            stores[k].start()

    def attention(x, gain, wq, wo, kq, ko, h, qkv, p, o, y, then):
        _, _, n = norm_forward(x(), gain)
        h[...] = n
        per_half = c // LANES
        for side in range(2):
            if side == 0:
                loads[kq].wait()
            else:
                swaps[kq].wait_recv()
                keeps[kq].start()
                for cp in swaps[then : then + 2]:
                    cp.start()
            for k in range(3):
                at = (2 * k + side) * c
                qkv[:, at : at + c] = nn(h[...], wq[side, k]).astype(BF)
            lax.fori_loop(
                0, n_img * per_half,
                lambda i, _, side=side: attend(i // per_half, side * per_half + i % per_half, d, qkv, p, o), 0, unroll=2)
        loads[ko].wait()
        swaps[ko].wait_recv()
        keeps[ko].start()
        y[...] = x() + nn(o[:, :c], wo[0]) + nn(o[:, c:], wo[1])

    fill_rows(x0, 0, images, lax.axis_index("mdl") * n_img, n_img)
    store(15)
    attention(lambda: x0[...].astype(F32), g_ref[0:1, :], q1, w1, 0, 1, h1, qkv1, p1, o1, x1, 2)
    store(0, 1, 2, 3, 4)

    _, _, n = norm_forward(x1[...], g_ref[1:2, :])
    h2[...] = n
    x2[...] = x1[...]
    t = tile_of(f)
    for side in range(2):
        for k in (2, 3):
            if side == 0:
                loads[k].wait()
            else:
                swaps[k].wait_recv()
                keeps[k].start()

        def tile(i, _, side=side):
            at = pl.ds(pl.multiple_of(i * t, t), t)
            a, sl = gelu_parts(nn(h2[...], fi[side, :, at]))
            a = a.astype(BF)
            act[side, :, at] = a
            slope[side, :, at] = sl.astype(BF)
            x2[...] += nn(a, fo[side, at, :])
            return 0

        if side == 0:
            for cp in swaps[4:6]:
                cp.start()
        lax.fori_loop(0, f // t, tile, 0)
    store(5, 6, 7, 8)

    attention(lambda: x2[...], g_ref[2:3, :], q3, w3, 4, 5, h3, qkv3, p3, o3, x3, 6)
    store(9, 10, 11, 12, 13)
    _, _, n = norm_forward(x3[...], g_ref[3:4, :])
    h4[...] = n
    store(14)
    for cp in blocks:
        cp.wait()
    for cp in keeps + stores:
        cp.wait()
    for cp in swaps[6:]:
        cp.wait_recv()
    for cp in swaps:
        cp.wait_send()


def forward(x, gains, own_w, dy_out, r):
    d = x.shape[2]
    c, f = own_w[0].shape[2], own_w[2].shape[1]
    n_img = r // LP
    heads = d // HDIM
    size = len(dy_out) + 1
    half = dy_out[0].shape[0]
    kept = [out((r, d), F32), out((r, d), BF), out((r, 3 * d), BF), out((n_img * heads, LP, LP), BF), out((r, d), BF)]
    results = kept + [out((r, d), F32), out((r, d), BF), out((2, r, f), BF), out((2, r, f), BF)] + kept + [out((r, d), BF), out((r, d), BF)]
    shapes = results + [out(w.shape, BF) for w in own_w] + [out((half, d), BF)] * (size - 1)
    D, V = pltpu.SemaphoreType.DMA, pltpu.VMEM
    any_ = pl.BlockSpec(memory_space=pl.ANY)
    vm = pl.BlockSpec(memory_space=pltpu.VMEM)
    got = pl.pallas_call(
        functools.partial(forward_body, n_img, size),
        in_specs=[vm] * 2 + [any_] * (len(own_w) + size - 1), out_specs=[any_] * len(shapes), out_shape=shapes,
        scratch_shapes=[V((2,) + w.shape, BF) for w in own_w[:6]] + [V(o.shape, o.dtype) for o in results]
        + [D((6,)), D((8,)), D((8,)), D((6,)), D((len(results),)), D((size - 1,)), D((size - 1,))],
        compiler_params=pltpu.CompilerParams(collective_id=2, has_side_effects=True, vmem_limit_bytes=VMEM_BYTES),
        cost_estimate=pl.CostEstimate(flops=16 * r * d * d + 8 * r * d * f, bytes_accessed=80 * r * d, transcendentals=0),
    )(x, gains, *own_w, *dy_out)
    n = len(results)
    return got[:n], got[n : n + 8], got[n + 8 :]


def routing_body(experts, capacity, half, rows_ref, dy_ref, tr_ref, col_ref, *refs):
    out_refs, (dy_rows, tmp) = refs[:-2], refs[-2:]
    fill_rows(dy_rows, 0, dy_ref, 0, rows_ref.shape[0])
    n_img = rows_ref.shape[0]
    slots = experts * half
    core = lax.axis_index("mdl")
    own_img = n_img // 2
    tall = lax.broadcasted_iota(I32, (max(experts, 8), LQ), 0)
    hots, priors = [], []
    for i in range(n_img):
        r = rows_ref[i]
        live = r[3:4, :] > 0
        hots.append((((tall == r[0:1, :]) | (tall == r[1:2, :])) & live).astype(F32).astype(BF))
        priors.append(r.astype(F32).T[:, 2:3])
    for i in range(n_img):
        r = rows_ref[i]
        rank = None
        for k in range(n_img):
            part = nn(hots[k], (priors[k] < r[2:3, :].astype(F32)).astype(F32).astype(BF))
            rank = part if rank is None else rank + part
        for k in range(TOPK):
            e = r[k : k + 1, :]
            mine = jnp.sum(jnp.where(tall == e, rank, 0.0), axis=0, keepdims=True).astype(I32)
            side = (mine >= half).astype(I32)
            slot = side * slots + e * half + mine - side * half
            tr_ref[i, k : k + 1, :] = jnp.where((mine < capacity) & (r[3:4, :] > 0), slot, -1)
        tr_ref[i, TOPK:, :] = jnp.full((8 - TOPK, LQ), -1, I32)
    for i in range(own_img):
        at = core * own_img + i
        for k in range(TOPK):
            t = tr_ref[at, k : k + 1, :]
            there = t - (1 - core) * slots
            tmp[k : k + 1, :] = t - core * slots
            tmp[TOPK + k : TOPK + k + 1, :] = jnp.where(there < slots, there, -1)
        tmp[4:8, :] = rows_ref[at, 0:4, :]
        tmp[6:7, :] = rows_ref[at, 3:4, :]
        col_ref[i * LP : (i + 1) * LP, :] = tmp[...].astype(F32).T[:LP, :].astype(I32)
    z = lax.axis_index("exp")
    for j, o_ref in enumerate(out_refs):
        at = core * slots + (beside(z, j) * half if len(out_refs) > 1 else 0)
        total = None
        for i in range(n_img):
            part = nn(slot_hots(tr_ref[i], at, o_ref.shape[0]), dy_rows[i * LP : (i + 1) * LP, :])
            total = part if total is None else total + part
        o_ref[...] = total.astype(BF)


def slot_hots(t, base, count):
    place = lax.broadcasted_iota(I32, (count, LP), 0) + base
    return ((place == t[0:1, :LP]) | (place == t[1:2, :LP])).astype(F32).astype(BF)


def dispatch_body(experts, half, tr_ref, own_ref, oth_ref, y_ref):
    core = lax.axis_index("mdl")
    own_img = own_ref.shape[0] // LP
    total = None
    for a, v in ((core, own_ref), (1 - core, oth_ref)):
        for i in range(own_img):
            hot = slot_hots(tr_ref[a * own_img + i], core * experts * half, experts * half)
            part = nn(hot, v[i * LP : (i + 1) * LP, :])
            total = part if total is None else total + part
    y_ref[...] = total.astype(BF)


def router_probs(h, router, experts):
    logits = nt(h, router)
    lane = lax.broadcasted_iota(I32, logits.shape, 1)
    logits = jnp.where(lane < experts, logits, -1e30)
    e = jnp.exp(logits - jnp.max(logits, axis=-1, keepdims=True))
    return e / jnp.sum(e, axis=-1, keepdims=True), lane


def expert_body(experts, x_ref, dy_ref, router_ref, im, io, tm, to,
                eout_ref, ret_ref, act_ref, dz_ref, wd_ref, acc_ref, dx_ref):
    step = pl.program_id(0)
    d = x_ref.shape[1]

    @pl.when(step == 0)
    def _():
        probs, lane = router_probs(x_ref[...], router_ref[...], experts)
        gate = jnp.sum(jnp.where(lane == lax.axis_index("exp"), probs, 0.0), axis=-1, keepdims=True)
        wd_ref[...] = (gate * dy_ref[...].astype(F32)).astype(BF)
        acc_ref[...] = jnp.zeros_like(acc_ref)
        dx_ref[...] = jnp.zeros_like(dx_ref)

    for half, (wi, wo) in enumerate(((im, tm), (io, to))):
        a, s = gelu_parts(nn(x_ref[...], wi[...]))
        act = a.astype(BF)
        act_ref[half] = act
        acc_ref[...] += nn(act, wo[...])
        dz = (nt(wd_ref[...], wo[...]) * s).astype(BF)
        dz_ref[half] = dz
        dx_ref[...] += nt(dz, wi[...])

    @pl.when(step == pl.num_programs(0) - 1)
    def _():
        eout = acc_ref[...].astype(BF)
        eout_ref[...] = eout
        ret_ref[:, :d] = dx_ref[...].astype(BF)
        dgate = jnp.sum(dy_ref[...].astype(F32) * eout.astype(F32), axis=-1, keepdims=True)
        high = dgate.astype(BF).astype(F32)
        lane = lax.broadcasted_iota(I32, (x_ref.shape[0], LANES), 1)
        ret_ref[:, d:] = jnp.where(lane < LANES // 2, high, dgate - high).astype(BF)


def expert_forward_backward(x, dy, router, im, io, tm, to, experts):
    r, d = x.shape
    f = im.shape[1]
    t = tile_of(f) // 2
    col = pl.BlockSpec((d, t), lambda i: (0, i))
    row = pl.BlockSpec((t, d), lambda i: (i, 0))
    hid = pl.BlockSpec((2, r, t), lambda i: (0, 0, i))
    return call(
        functools.partial(expert_body, experts),
        [out((r, d), BF), out((r, d + LANES), BF), out((2, r, f), BF), out((2, r, f), BF), out((r, d), BF)],
        x, dy, router, im, io, tm, to, grid=(f // t,),
        in_specs=[whole((r, d)), whole((r, d)), whole(router.shape), col, col, row, row],
        out_specs=[whole((r, d)), whole((r, d + LANES)), hid, hid, whole((r, d))],
        scratch=[pltpu.VMEM((r, d), F32), pltpu.VMEM((r, d), F32)], flops=16 * r * d * f,
    )


def expert_weights_body(x_ref, wd_ref, act_ref, dz_ref, gm_ref, go_ref, xt_ref, wt_ref):
    @pl.when(pl.program_id(0) == 0)
    def _():
        xt_ref[...] = x_ref[...].T
        wt_ref[...] = wd_ref[...].T

    for half, g in enumerate((gm_ref, go_ref)):
        g[0] = nn(xt_ref[...], dz_ref[half]).astype(BF)
        g[1] = nn(wt_ref[...], act_ref[half]).astype(BF)


def expert_weights(x, wd, act, dz):
    r, d = x.shape
    f = act.shape[2]
    t = tile_of(f) // 2
    hid = pl.BlockSpec((2, r, t), lambda i: (0, 0, i))
    grad = pl.BlockSpec((2, d, t), lambda i: (0, 0, i))
    return call(
        expert_weights_body, [out((2, d, f), BF), out((2, d, f), BF)], x, wd, act, dz, grid=(f // t,),
        in_specs=[whole((r, d)), whole((r, d)), hid, hid], out_specs=[grad, grad],
        scratch=[pltpu.VMEM((d, r), BF), pltpu.VMEM((d, r), BF)], flops=8 * r * d * f,
    )


def merge(col_ref, k, ab_ref, n):
    slots = ab_ref.shape[1]
    lane = lax.broadcasted_iota(I32, (n, slots), 1)
    rows = None
    for side in range(2):
        hot = (lane == col_ref[:, 2 * side + k : 2 * side + k + 1]).astype(F32).astype(BF)
        part = nn(hot, ab_ref[side])
        rows = part if rows is None else rows + part
    return rows


def merge_blocks(col_ref, k, blocks, n):
    rows = None
    for side in range(2):
        for e, ref in blocks[side]:
            half = ref.shape[0]
            lane = lax.broadcasted_iota(I32, (n, half), 1) + e * half
            hot = (lane == col_ref[:, 2 * side + k : 2 * side + k + 1]).astype(F32).astype(BF)
            part = nn(hot, ref[...])
            rows = part if rows is None else rows + part
    return rows


def mixture_backward_core(experts, half, x_ref, gain, h_ref, router_ref, dy_ref, col_ref, ab_ref, dgate_ref, dr_ref, dy_rows):
    n, d = x_ref.shape
    n_img = n // LP
    fill_rows(dy_rows, 0, dy_ref, lax.axis_index("mdl") * n_img, n_img)
    probs, lane = router_probs(h_ref[...], router_ref[...], experts)
    dsoft = jnp.zeros(probs.shape, F32)
    dh = jnp.zeros((n, d), F32)
    for k in range(TOPK):
        dh = dh + merge(col_ref, k, ab_ref, n)
        dgate = jnp.zeros((n, 1), F32)
        for side in range(2):
            t = col_ref[:, 2 * side + k : 2 * side + k + 1]
            for e in range(experts):
                line = dgate_ref[side, e, 0:1, :]
                place = lax.broadcasted_iota(I32, (n, line.shape[1]), 1)
                hit = (place + e * half == t) & (place < half)
                dgate = dgate + jnp.sum(jnp.where(hit, line, 0.0), axis=-1, keepdims=True)
        dsoft = dsoft + jnp.where(lane == col_ref[:, 4 + k : 5 + k], dgate, 0.0)
    dlog = (probs * (dsoft - jnp.sum(dsoft * probs, axis=-1, keepdims=True))).astype(BF)
    dr_ref[...] = tn(dlog, h_ref[...])
    dh = dh + nn(dlog, router_ref[...])
    nrm, rr, _ = norm_forward(x_ref[...], gain)
    dv, dw = norm_backward(nrm, rr, gain, dh)
    return dy_rows[...].astype(F32) * col_ref[:, 6:7].astype(F32) + dv, dw


def gate_lines(dgate):
    half = dgate.shape[0]
    wide = -(-half // LANES) * LANES
    tall = jnp.concatenate([dgate, jnp.zeros((wide - half, 1), F32)], axis=0) if wide > half else dgate
    return jnp.broadcast_to(tall, (wide, LANES)).T[0:8, :]


def mixture_attention_backward_body(n_img, experts, half, x3_ref, h4_ref, router_ref, dy_ref, col_ref, ret_ref, dgate_ref, x_ref, g_ref, h_ref,
                                    qkv_ref, p_ref, o_ref, qm, qo, om, oo, dx_ref, dw3_ref, dw4_ref, dr_ref, gm_ref, go_ref,
                                    dx3, dy_rows, do_ref, dqkv_ref, tr_ref):
    grad, dw4 = mixture_backward_core(experts, half, x3_ref, g_ref[3:4, :], h4_ref, router_ref, dy_ref, col_ref, ret_ref, dgate_ref,
                                      dr_ref, dy_rows)
    dx3[...] = grad
    dw4_ref[...] = dw4
    dx, dw3 = attention_backward_core(
        n_img, lambda: dx3[...], x_ref, g_ref[2:3, :], h_ref, qkv_ref, p_ref, o_ref, qm, qo, om, oo,
        gm_ref, go_ref, do_ref, dqkv_ref, tr_ref)
    dx_ref[...] = dx
    dw3_ref[...] = dw3


def mixture_attention_backward(experts, half, x3, h4, router, dy, col, ret, dgate, x, gains, kept, qm, qo, om, oo):
    r, d = x.shape
    c = qm.shape[2]
    n_img = r // LP
    heads = d // HDIM
    shapes = [out((r, d), F32), out((1, d), F32), out((1, d), F32), out(router.shape, F32),
              out((3 * d + d, c), BF), out((3 * d + d, c), BF)]
    return call(functools.partial(mixture_attention_backward_body, n_img, experts, half), shapes,
                x3, h4, router, dy, col, ret, dgate, x, gains, *kept, qm, qo, om, oo,
                scratch=[pltpu.VMEM((r, d), F32), pltpu.VMEM((r, d), BF)] + attention_backward_scratch(r, d),
                flops=4 * r * d * d * 4 + 8 * n_img * heads * LP * LP * LANES + 8 * r * ret.shape[1] * d)


def backward_body(n_img, experts, half, size, *refs):
    refs = list(refs)

    def take(n):
        r = refs[:n]
        del refs[:n]
        return r

    x3, h4, router, cotangent, col, ret, dgate, g_ref = take(8)
    src_two, src_mlp, src_one = take(9), take(8), take(9)
    eouts = take(size - 1)
    dg1, dg2, dg3, dg4, dr, image = take(6)
    out_two, out_mlp, out_one = take(2), take(4), take(2)
    ebacks = take(size - 1)
    attn = take(9)
    x0, x1, h2, act, slope, fi, fo, ga, gi, go, dxs, dy_rows, do, dqkv, tr, da, dh = take(17)
    a_sem, m_sem, b_sem, ga_sem, gi_sem, e_send, e_recv = refs
    d = x3.shape[1]
    f = fi.shape[2]
    t = gi.shape[4]
    z = lax.axis_index("exp")

    def fetch(srcs, dsts, sem):
        return [pltpu.make_async_copy(a, b, sem.at[k]) for k, (a, b) in enumerate(zip(srcs, dsts))]

    two = fetch(src_two, attn, a_sem)
    mlp = fetch(src_mlp, [x1, h2, act, slope, fi.at[0], fi.at[1], fo.at[0], fo.at[1]], m_sem)
    one = fetch(src_one, [x0] + attn[1:], b_sem)
    for cp in two + mlp:
        cp.start()
    barrier = pltpu.get_barrier_semaphore()
    for j in range(1, size):
        pl.semaphore_signal(barrier, inc=1, device_id={"exp": beside(z, j)}, device_id_type=MESH)
    pl.semaphore_wait(barrier, size - 1)
    blocks = [pltpu.make_async_remote_copy(eouts[j - 1], ebacks[j - 1], e_send.at[j - 1], e_recv.at[j - 1],
                                           device_id={"exp": beside(z, j)}, device_id_type=MESH) for j in range(1, size)]
    for cp in blocks:
        cp.start()

    def attention(x, gain, dst):
        dx, dw = attention_backward_core(n_img, lambda: dxs[...], x, gain, *attn[1:], ga.at[0], ga.at[1], do, dqkv, tr)
        leave = [pltpu.make_async_copy(ga.at[k], dst[k], ga_sem.at[k]) for k in range(2)]
        for cp in leave:
            cp.start()
        return dx, dw, leave

    grad, dw4 = mixture_backward_core(experts, half, x3, g_ref[3:4, :], h4, router, cotangent, col, ret, dgate, dr, dy_rows)
    dxs[...] = grad
    dg4[...] = dw4
    for cp in two:
        cp.wait()
    dx, dw, leave = attention(attn[0], g_ref[2:3, :], out_two)
    dxs[...] = dx
    dg3[...] = dw
    for cp in one:
        cp.start()

    da[...] = dxs[...].astype(BF)
    for cp in mlp:
        cp.wait()
    tr[...] = h2[...].T
    dh[...] = jnp.zeros(dh.shape, F32)
    gone = {}
    for i in range(f // t):
        at = slice(i * t, (i + 1) * t)
        slot = i % 2
        for cp in gone.pop(slot, ()):
            cp.wait()
        gone[slot] = []
        for side in range(2):
            dz = (nt(da[...], fo[side, at, :]) * slope[side, :, at].astype(F32)).astype(BF)
            gw = tn(act[side, :, at], da[...]).astype(BF)
            for part in range(d // t):
                go[slot, side, part] = gw[:, part * t : (part + 1) * t]
            gi[slot, side, 0] = nn(tr[...], dz).astype(BF)
            dh[...] += nt(dz, fi[side, :, at])
            gone[slot] += [
                pltpu.make_async_copy(gi.at[slot, side], out_mlp[side].at[i : i + 1], gi_sem.at[slot, side, 0]),
                pltpu.make_async_copy(go.at[slot, side], out_mlp[2 + side].at[:, at], gi_sem.at[slot, side, 1])]
            for cp in gone[slot][-2:]:
                cp.start()
    gain = g_ref[1:2, :]
    n, rr, _ = norm_forward(x1[...], gain)
    dv, dw = norm_backward(n, rr, gain, dh[...])
    dxs[...] += dv
    dg2[...] = dw

    for cp in one + leave:
        cp.wait()
    dx, dw, leave = attention(x0, g_ref[0:1, :], out_one)
    for i in range(n_img):
        image[i] = dx[i * LP : i * LP + L].astype(BF)
    dg1[...] = dw
    for cp in leave + gone[0] + gone[1] + blocks:
        cp.wait()


def backward(experts, half, x3, h4, router, cotangent, col, ret, dgate, gains, x2, kept3, w2, x1, h2, act, slope, mlp_w, x0, kept1,
             w1, eouts):
    r, d = x3.shape
    c, f = w1[0].shape[2], mlp_w[0].shape[1]
    n_img = r // LP
    heads = d // HDIM
    size = len(eouts) + 1
    t = c
    flat = [x2, *kept3, *w2, x1, h2, act, slope, *mlp_w, x0, *kept1, *w1, *eouts]
    near = [x3, h4, router, cotangent, col, ret, dgate, gains]
    D, V = pltpu.SemaphoreType.DMA, pltpu.VMEM
    any_ = pl.BlockSpec(memory_space=pl.ANY)
    vm = pl.BlockSpec(memory_space=pltpu.VMEM)
    shapes = [out((1, d), F32)] * 4 + [out(router.shape, F32), out((n_img, L, d), BF)]
    shapes += [out((4 * d, c), BF)] * 2 + [out((f // t, d, t), BF)] * 2 + [out((d // t, f, t), BF)] * 2 + [out((4 * d, c), BF)] * 2
    shapes += [out(e.shape, BF) for e in eouts]
    like = [V(v.shape, v.dtype) for v in (x2, *kept3, *w2)]
    got = pl.pallas_call(
        functools.partial(backward_body, n_img, experts, half, size),
        in_specs=[vm] * len(near) + [any_] * len(flat), out_specs=[vm] * 6 + [any_] * (len(shapes) - 6), out_shape=shapes,
        scratch_shapes=like + [
            V(x0.shape, x0.dtype), V((r, d), F32), V((r, d), BF), V(act.shape, BF), V(slope.shape, BF), V((2, d, f), BF),
            V((2, f, d), BF), V((2, 4 * d, c), BF), V((2, 2, 1, d, t), BF), V((2, 2, d // t, t, t), BF), V((r, d), F32),
            V((r, d), BF), V((r, d), BF), V((r, 3 * d), BF), V((d, r), BF), V((r, d), BF), V((r, d), F32),
            D((9,)), D((8,)), D((9,)), D((2,)), D((2, 2, 2)), D((size - 1,)), D((size - 1,))],
        compiler_params=pltpu.CompilerParams(collective_id=3, has_side_effects=True, vmem_limit_bytes=VMEM_BYTES),
        cost_estimate=pl.CostEstimate(flops=32 * r * d * d + 16 * r * d * f, bytes_accessed=160 * r * d, transcendentals=0),
    )(*near, *flat)
    return got[:6], got[6:14], got[14:]


def mixture_output(experts, x_ref, h_ref, router_ref, col_ref, rows_of):
    n, d = x_ref.shape
    probs, lane = router_probs(h_ref[...], router_ref[...], experts)
    mixed = jnp.zeros((n, d), F32)
    for k in range(TOPK):
        gate = jnp.sum(jnp.where(lane == col_ref[:, 4 + k : 5 + k], probs, 0.0), axis=-1, keepdims=True)
        mixed = mixed + gate * rows_of(k)
    return (col_ref[:, 6:7].astype(F32) * (x_ref[...] + mixed)).astype(BF)


def mixture_output_body(experts, x_ref, h_ref, router_ref, col_ref, ab_ref, y_ref):
    y = mixture_output(experts, x_ref, h_ref, router_ref, col_ref, lambda k: merge(col_ref, k, ab_ref, x_ref.shape[0]))
    for i in range(y_ref.shape[0]):
        y_ref[i] = y[i * LP : i * LP + L]


def flip(axis, bit):
    size = lax.axis_size(axis)
    return [(i, i ^ bit) for i in range(size)]


def bits_of(axis):
    size = lax.axis_size(axis)
    return [1 << b for b in range(size.bit_length() - 1)]


def other_core(v):
    return lax.ppermute(v, "mdl", flip("mdl", 1))


def add16(a, b):
    return (a.astype(F32) + b.astype(F32)).astype(BF)


def halve(v, axis, bit):
    side = (lax.axis_index(axis) // bit) % 2
    n = v.shape[0] // 2
    keep = lax.dynamic_slice_in_dim(v, side * n, n)
    send = lax.dynamic_slice_in_dim(v, (1 - side) * n, n)
    return add16(keep, lax.ppermute(send, axis, flip(axis, bit)))


def double(v, axis, bit):
    side = (lax.axis_index(axis) // bit) % 2
    got = lax.ppermute(v, axis, flip(axis, bit))
    return jnp.where(side == 0, jnp.concatenate([v, got]), jnp.concatenate([got, v]))


def sum_everywhere(v):
    n = v.shape[0] // 2
    bits = bits_of("grp")
    parts = []
    for part, order in ((v[:n], bits), (v[n:], bits[::-1])):
        for bit in order:
            part = halve(part, "grp", bit)
        parts.append(part)
    size = lax.axis_size("exp")
    joined = jnp.concatenate(parts)
    rows = joined.shape[0] // size
    spread = lax.all_to_all(joined.reshape(size, rows, -1), "exp", 0, 0, tiled=True)
    mine = jnp.sum(spread.astype(F32), axis=0).astype(BF)
    joined = lax.all_gather(mine, "exp", axis=0, tiled=True)
    h = joined.shape[0] // 2
    done = []
    for part, order in ((joined[:h], bits), (joined[h:], bits[::-1])):
        for bit in order[::-1]:
            part = double(part, "grp", bit)
        done.append(part)
    return jnp.concatenate(done)


def small_sum(v):
    for axis in ("mdl", "grp", "exp"):
        for bit in bits_of(axis):
            v = v + lax.ppermute(v, axis, flip(axis, bit))
    return v


def reduce_body(n_in, per, n_exp, experts, *refs):
    mine = refs[:n_in]
    other = refs[n_in : 2 * n_in]
    dg = refs[2 * n_in : 2 * n_in + 4]
    dr_ref, x3_ref, h4_ref, router_ref, col_ref = refs[2 * n_in + 4 : 2 * n_in + 9]
    eouts = refs[2 * n_in + 9 : 2 * n_in + 13]
    image_ref = refs[2 * n_in + 13]
    outs = refs[2 * n_in + 14 :]
    qkv2, proj2, fc_in, fc_out, qkv1, proj1, sum_ref, y_ref, gx_ref = outs[:9]
    (acc, got, r1, r2, zr, zz, zs, sm, y_own, load_sem, m_send, m_recv, x_send, x_recv, z_send, z_recv, s_send, s_recv,
     i_local, i_send, i_recv, e_oth, e_send, e_recv) = outs[9:]
    out_ref = got
    n = n_in * per
    rows = acc.shape[2]
    h, q = rows // 2, rows // 4
    t = q // n_exp
    g = lax.axis_index("grp")
    z = lax.axis_index("exp")
    core = lax.axis_index("mdl")
    bx, by = g % 2, g // 2
    flat = {"x": g + 1 - 2 * bx, "y": g + 2 - 4 * by}
    order = (("x", "y"), ("y", "x"))
    bits = ((bx, by), (by, bx))

    barrier = pltpu.get_barrier_semaphore()
    others = [{"mdl": 1 - core}, {"grp": flat["x"]}, {"grp": flat["y"]}]
    others += [{"exp": (z + o) % n_exp} for o in range(1, n_exp)]
    for dev in others:
        pl.semaphore_signal(barrier, inc=1, device_id=dev, device_id_type=MESH)
    pl.semaphore_wait(barrier, len(others))

    def load(c):
        i, p = c // per, c % per
        return pltpu.make_async_copy(mine[i].at[p], acc.at[c], load_sem.at[c])

    def swap(c):
        i, p = c // per, c % per
        return pltpu.make_async_remote_copy(other[i].at[p], got.at[c], m_send.at[c], m_recv.at[c],
                                            device_id={"mdl": 1 - core}, device_id_type=MESH)

    for c in range(n):
        swap(c).start()
        load(c).start()

    own_img = image_ref.shape[0]
    places = pl.ds(core * own_img, own_img)

    def image_copies(k, src, dst):
        return (pltpu.make_async_copy(src, dst.at[places], i_local.at[k]),
                pltpu.make_async_remote_copy(src, dst.at[places], i_send.at[k], i_recv.at[k], device_id={"mdl": 1 - core},
                                             device_id_type=MESH))

    def image_come(k, src, dst):
        there = pl.ds((1 - core) * own_img, own_img)
        return pltpu.make_async_remote_copy(src, dst.at[there], i_send.at[k], i_recv.at[k], device_id={"mdl": 1 - core},
                                            device_id_type=MESH)

    for cp in image_copies(0, image_ref, gx_ref):
        cp.start()

    e_copies = [pltpu.make_async_remote_copy(eouts[j], e_oth.at[j], e_send.at[j], e_recv.at[j], device_id={"mdl": 1 - core},
                                             device_id_type=MESH) for j in range(n_exp)]
    for cp in e_copies:
        cp.start()

    def swap_at(c):
        return pltpu.make_async_remote_copy(other[0].at[0], got.at[c], m_send.at[c], m_recv.at[c],
                                            device_id={"mdl": 1 - core}, device_id_type=MESH)

    def load_at(c):
        return pltpu.make_async_copy(mine[0].at[0], acc.at[c], load_sem.at[c])

    def over(u, leg, src, dst, slot, c):
        return pltpu.make_async_remote_copy(src, dst, x_send.at[slot, u, c], x_recv.at[slot, u, c],
                                            device_id={"grp": flat[order[u][leg]]}, device_id_type=MESH)

    def first(u, c):
        return over(u, 0, acc.at[c, u, pl.ds(pl.multiple_of((1 - bits[u][0]) * h, h), h)], r1.at[c, u], 0, c)

    def second(u, c):
        return over(u, 1, r1.at[c, u, pl.ds(pl.multiple_of((1 - bits[u][1]) * q, q), q)], r2.at[c, u], 1, c)

    def along(u, c, o):
        return pltpu.make_async_remote_copy(
            r2.at[c, u, pl.ds(pl.multiple_of(((z + o) % n_exp) * t, t), t)], zr.at[c, u, o - 1],
            z_send.at[0, u, o - 1, c], z_recv.at[0, u, o - 1, c],
            device_id={"exp": (z + o) % n_exp}, device_id_type=MESH)

    def place(u):
        return bits[u][0] * h + bits[u][1] * q

    def back(u, c, o):
        here = out_ref.at[c, u, pl.ds(pl.multiple_of(place(u) + z * t, t), t)]
        return pltpu.make_async_remote_copy(here, here, z_send.at[1, u, o - 1, c], z_recv.at[1, u, o - 1, c],
                                            device_id={"exp": (z + o) % n_exp}, device_id_type=MESH)

    def third(u, c):
        here = out_ref.at[c, u, pl.ds(pl.multiple_of(place(u), q), q)]
        return over(u, 1, here, here, 2, c)

    def fourth(u, c):
        here = out_ref.at[c, u, pl.ds(pl.multiple_of(bits[u][0] * h, h), h)]
        return over(u, 0, here, here, 3, c)

    def plus(a, b):
        return (a.astype(F32) + b.astype(F32)).astype(BF)

    def s1(c):
        load_at(c).wait()
        swap_at(c).wait_recv()
        for u in range(2):
            acc[c, u] = plus(acc[c, u], got[c, u])
            first(u, c).start()

    def s2(c):
        for u in range(2):
            first(u, c).wait_recv()
            keep = acc[c, u, pl.ds(pl.multiple_of(bits[u][0] * h, h), h)]
            r1[c, u] = plus(keep, r1[c, u])
            second(u, c).start()

    def s3(c):
        for u in range(2):
            second(u, c).wait_recv()
            keep = r1[c, u, pl.ds(pl.multiple_of(bits[u][1] * q, q), q)]
            r2[c, u] = plus(keep, r2[c, u])
            for o in range(1, n_exp):
                along(u, c, o).start()

    def s4(c):
        for u in range(2):
            total = r2[c, u, pl.ds(pl.multiple_of(z * t, t), t)].astype(F32)
            for o in range(1, n_exp):
                along(u, c, o).wait_recv()
                total = total + zr[c, u, o - 1].astype(F32)
            out_ref[c, u, pl.ds(pl.multiple_of(place(u) + z * t, t), t)] = total.astype(BF)
            for o in range(1, n_exp):
                back(u, c, o).start()

    def s5(c):
        for u in range(2):
            for o in range(1, n_exp):
                back(u, c, o).wait_recv()
            third(u, c).start()

    def s6(c):
        for u in range(2):
            third(u, c).wait_recv()
            fourth(u, c).start()

    def s7(c):
        for u in range(2):
            fourth(u, c).wait_recv()
        for k in range(n):

            @pl.when(c == k)
            def _(k=k):
                natural(k)

    zc = 0
    e, e2, e4 = rows // n_exp, rows // n_exp // 2, rows // n_exp // 4

    def z_out(u, o):
        return pltpu.make_async_remote_copy(
            acc.at[zc, u, pl.ds(pl.multiple_of(((z + o) % n_exp) * e, e), e)], zz.at[u, o - 1],
            z_send.at[0, u, o - 1, zc], z_recv.at[0, u, o - 1, zc], device_id={"exp": (z + o) % n_exp}, device_id_type=MESH)

    def z_first(u):
        return over(u, 0, zs.at[u, pl.ds(pl.multiple_of((1 - bits[u][0]) * e2, e2), e2)], r1.at[zc, u, 0:e2], 0, zc)

    def z_second(u):
        return over(u, 1, r1.at[zc, u, pl.ds(pl.multiple_of((1 - bits[u][1]) * e4, e4), e4)], r2.at[zc, u, 0:e4], 1, zc)

    def z_third(u):
        here = out_ref.at[zc, u, pl.ds(pl.multiple_of(z * e + bits[u][0] * e2 + bits[u][1] * e4, e4), e4)]
        return over(u, 1, here, here, 2, zc)

    def z_fourth(u):
        here = out_ref.at[zc, u, pl.ds(pl.multiple_of(z * e + bits[u][0] * e2, e2), e2)]
        return over(u, 0, here, here, 3, zc)

    def z_back(u, o):
        here = out_ref.at[zc, u, pl.ds(pl.multiple_of(z * e, e), e)]
        return pltpu.make_async_remote_copy(here, here, z_send.at[1, u, o - 1, zc], z_recv.at[1, u, o - 1, zc],
                                            device_id={"exp": (z + o) % n_exp}, device_id_type=MESH)

    def z1():
        load_at(zc).wait()
        swap_at(zc).wait_recv()
        for u in range(2):
            acc[zc, u] = plus(acc[zc, u], got[zc, u])
            for o in range(1, n_exp):
                z_out(u, o).start()

    def z2():
        for u in range(2):
            total = acc[zc, u, pl.ds(pl.multiple_of(z * e, e), e)].astype(F32)
            for o in range(1, n_exp):
                z_out(u, o).wait_recv()
                total = total + zz[u, o - 1].astype(F32)
            zs[u] = total.astype(BF)
            z_first(u).start()

    def z3():
        for u in range(2):
            z_first(u).wait_recv()
            r1[zc, u, 0:e2] = plus(zs[u, pl.ds(pl.multiple_of(bits[u][0] * e2, e2), e2)], r1[zc, u, 0:e2])
            z_second(u).start()

    def z4():
        for u in range(2):
            z_second(u).wait_recv()
            mine_rows = pl.ds(pl.multiple_of(z * e + bits[u][0] * e2 + bits[u][1] * e4, e4), e4)
            out_ref[zc, u, mine_rows] = plus(r1[zc, u, pl.ds(pl.multiple_of(bits[u][1] * e4, e4), e4)], r2[zc, u, 0:e4])
            z_third(u).start()

    def z5():
        for u in range(2):
            z_third(u).wait_recv()
            z_fourth(u).start()

    def z6():
        for u in range(2):
            z_fourth(u).wait_recv()
            for o in range(1, n_exp):
                z_back(u, o).start()

    def z7():
        for u in range(2):
            for o in range(1, n_exp):
                z_back(u, o).wait_recv()
        natural(zc)

    def drain(c, _):
        swap_at(c).wait_send()
        for u in range(2):
            for make in (first, second, third, fourth):
                make(u, c).wait_send()
            for o in range(1, n_exp):
                along(u, c, o).wait_send()
                back(u, c, o).wait_send()
        return 0

    legs = [({"mdl": 1 - core}), ({"grp": flat["x"]}), ({"grp": flat["y"]})]
    base = 2 * len(legs) + 1

    def small_leg(i):
        return pltpu.make_async_remote_copy(sm.at[2 * i], sm.at[2 * i + 1], s_send.at[i], s_recv.at[i], device_id=legs[i],
                                            device_id_type=MESH)

    def small_along(o):
        return pltpu.make_async_remote_copy(sm.at[base - 1], sm.at[base + z], s_send.at[len(legs) + o - 1],
                                            s_recv.at[len(legs) + o - 1], device_id={"exp": (z + o) % n_exp},
                                            device_id_type=MESH)

    def small_step(i):
        if i == 0:
            sm[0] = jnp.zeros(sm.shape[1:], F32)
            for k in range(4):
                sm[0, k : k + 1, :] = dg[k][...]
            sm[0, 4 : 4 + experts, :] = dr_ref[:experts, :]
        else:
            small_leg(i - 1).wait()
            sm[2 * i] = sm[2 * i - 2] + sm[2 * i - 1]
        if i < len(legs):
            small_leg(i).start()
        else:
            sm[pl.ds(base + z, 1)] = sm[pl.ds(base - 1, 1)]
            for o in range(1, n_exp):
                small_along(o).start()

    def natural(c):
        i, p = c // per, c % per
        wide = out_ref.shape[3]
        piece = wide // 3
        for u in range(2):
            for r0 in range(0, rows, piece):
                at = (2 * p + u) * rows + r0
                value = out_ref[c, u, r0 : r0 + piece]
                if i in (0, 3):
                    qkv, proj = (qkv2, proj2) if i == 0 else (qkv1, proj1)
                    if at < 6 * wide:
                        k, at = divmod(at, 2 * wide)
                        qkv[k, at : at + piece] = value
                    else:
                        k, at = divmod(at - 6 * wide, wide)
                        proj[at : at + piece, k * wide : (k + 1) * wide] = value
                else:
                    to, tall = (fc_in, 2 * wide) if i == 1 else (fc_out, 4 * wide)
                    k, at = divmod(at, tall)
                    to[at : at + piece, k * wide : (k + 1) * wide] = value

    steps = (s1, s2, s3, s4, s5, s6, s7)
    waves = n - 1 + len(steps) - 1
    late = waves - 2
    z_steps = ((0, z1), (2, z2), (3, z3), (4, z4), (5, z5), (6, z6), (late, z7))
    small_steps = {1: 0, 3: 1, 5: 2, 7: 3}

    def wave(tau, _):
        for s, step in enumerate(steps):
            c = tau - s + 1

            @pl.when((c >= 1) & (c < n))
            def _(step=step, c=c):
                step(c)

        for at, step in z_steps:
            pl.when(tau == at)(step)
        for at, i in small_steps.items():
            pl.when(tau == at)(functools.partial(small_step, i))
        return 0

    first_waves = 2
    lax.fori_loop(0, first_waves, wave, 0)
    for cp in e_copies:
        cp.wait_recv()
    blocks = [[(beside(z, j), eouts[j]) for j in range(n_exp)], [(beside(z, j), e_oth.at[j]) for j in range(n_exp)]]
    y = mixture_output(experts, x3_ref, h4_ref, router_ref, col_ref, lambda k: merge_blocks(col_ref, k, blocks, x3_ref.shape[0]))
    for i in range(own_img):
        y_own[i] = y[i * LP : i * LP + L]
    for cp in image_copies(1, y_own, y_ref):
        cp.start()
    lax.fori_loop(first_waves, waves, wave, 0)
    for cp in e_copies:
        cp.wait_send()
    for k, (src, dst) in enumerate(((image_ref, gx_ref), (y_own, y_ref))):
        local, sent = image_copies(k, src, dst)
        local.wait()
        sent.wait_send()
        image_come(k, src, dst).wait_recv()
    lax.fori_loop(1, n, drain, 0)
    swap_at(zc).wait_send()
    for u in range(2):
        for make in (z_first, z_second, z_third, z_fourth):
            make(u).wait_send()
        for o in range(1, n_exp):
            z_out(u, o).wait_send()
            z_back(u, o).wait_send()
    for o in range(1, n_exp):
        small_along(o).wait()
    total = sm[base]
    for k in range(1, n_exp):
        total = total + sm[base + k]
    sum_ref[...] = total


def reduce_all(mine, other, dgs, dr, x3, h4, router, col, eouts, image, n_exp, experts):
    per, _, rows, c = mine[0].shape
    n = len(mine) * per
    d, f = 2 * c, 4 * c
    h, q = rows // 2, rows // 4
    t = q // n_exp
    small = (-(-(4 + experts) // 8) * 8, d)
    n_img, length, _ = image.shape
    D, V = pltpu.SemaphoreType.DMA, pltpu.VMEM
    any_ = pl.BlockSpec(memory_space=pl.ANY)
    vm = pl.BlockSpec(memory_space=pltpu.VMEM)
    return pl.pallas_call(
        functools.partial(reduce_body, len(mine), per, n_exp, experts),
        in_specs=[any_] * (2 * len(mine)) + [vm] * 13 + [any_],
        out_specs=[vm] * 9,
        out_shape=[out((3, d, c), BF), out((c, d), BF), out((d, f), BF), out((f, d), BF), out((3, d, c), BF), out((c, d), BF),
                   out(small, F32), out((2 * n_img, length, d), BF), out((2 * n_img, length, d), BF)],
        scratch_shapes=[
            V((n, 2, rows, c), BF), V((n, 2, rows, c), BF), V((n, 2, h, c), BF), V((n, 2, q, c), BF),
            V((n, 2, n_exp - 1, t, c), BF), V((2, n_exp - 1, rows // n_exp, c), BF), V((2, rows // n_exp, c), BF),
            V((7 + n_exp,) + small, F32), V((n_img, length, d), BF),
            D((n,)), D((n,)), D((n,)), D((4, 2, n)), D((4, 2, n)), D((2, 2, n_exp - 1, n)), D((2, 2, n_exp - 1, n)),
            D((3 + n_exp,)), D((3 + n_exp,)), D((2,)), D((2,)), D((2,)), V((n_exp,) + eouts[0].shape, BF), D((n_exp,)), D((n_exp,)),
        ],
        compiler_params=pltpu.CompilerParams(collective_id=0, has_side_effects=True, vmem_limit_bytes=VMEM_BYTES),
        cost_estimate=pl.CostEstimate(flops=8 * x3.shape[0] * x3.shape[0] * d, bytes_accessed=n * 8 * rows * c, transcendentals=0),
    )(*mine, *other, *dgs, dr, x3, h4, router, col, *eouts, image)


def expert_exchange_body(experts, half, h4_ref, tr_ref, dy0, dy1, dy2, dy3, router_ref, im, io, tm, to,
                         ret_ref, dg_ref, e0, e1, e2, e3, gw_ref,
                         h_oth, part, xo, x, wi, wo, act, dz, wd, acc, dxa, rsend, gscr, ggot, xt, wt,
                         w_sem, swap_sem, x_send, x_recv, r_send, r_recv, f_send, f_recv, g_send, g_recv, g_sem,
                         dgs, l_send, l_recv, k_send, k_recv):
    n, d = h4_ref.shape
    f = im.shape[1]
    t = 256 if f % 256 == 0 else tile_of(f)
    z = lax.axis_index("exp")
    core = lax.axis_index("mdl")
    partner = {"mdl": 1 - core}
    size = experts
    near_first = [1, 3, 2]

    out_grad, eouts = (dy0, dy1, dy2, dy3), (e0, e1, e2, e3)

    def there(j):
        return beside(z, j)

    loads = [pltpu.make_async_copy(src, dst, w_sem.at[k]) for k, (src, dst) in enumerate(
        ((im, wi.at[0]), (io, wi.at[1]), (tm, wo.at[0]), (to, wo.at[1])))]
    for cp in loads:
        cp.start()
    barrier = pltpu.get_barrier_semaphore()
    for dev in [partner] + [{"exp": there(j)} for j in range(1, size)]:
        pl.semaphore_signal(barrier, inc=1, device_id=dev, device_id_type=MESH)
    pl.semaphore_wait(barrier, size)
    swap = pltpu.make_async_remote_copy(h4_ref, h_oth, swap_sem.at[0], swap_sem.at[1], device_id=partner, device_id_type=MESH)
    swap.start()

    own_img = n // LP
    base = core * size * half

    def spread(side, v, j):
        total = None
        for i in range(own_img):
            p = nn(slot_hots(tr_ref[side * own_img + i], base + there(j) * half, half), v[i * LP : (i + 1) * LP, :])
            total = p if total is None else total + p
        return total

    def rows(j):
        return slice(j * half, (j + 1) * half)

    def place(e):
        return pl.ds(pl.multiple_of(e * half, half), half)

    for j in near_first + [0]:
        part[rows(j), :] = spread(core, h4_ref, j)
    swap.wait_recv()
    sends = {}
    for j in near_first + [0]:
        block = (part[rows(j), :] + spread(1 - core, h_oth, j)).astype(BF)
        if j == 0:
            x[rows(0), :] = block
        else:
            xo[rows(j), :] = block
            sends[j] = pltpu.make_async_remote_copy(xo.at[rows(j)], x.at[rows(j)], x_send.at[j], x_recv.at[j],
                                                    device_id={"exp": there(j)}, device_id_type=MESH)
            sends[j].start()

    returns, forwards = {}, {}

    def forward(j):
        here = ret_ref.at[0, place(there(j))]
        forwards[j] = (
            pltpu.make_async_remote_copy(here, ret_ref.at[1, place(there(j))], f_send.at[j], f_recv.at[j],
                                         device_id=partner, device_id_type=MESH),
            pltpu.make_async_remote_copy(dg_ref.at[0, there(j)], dg_ref.at[1, there(j)], k_send.at[j], k_recv.at[j],
                                         device_id=partner, device_id_type=MESH))
        for cp in forwards[j]:
            cp.start()

    def run(blocks):
        r0, r1 = blocks[0] * half, (blocks[-1] + 1) * half
        m = r1 - r0
        for j in blocks:
            probs, lane = router_probs(x[rows(j), :], router_ref[...], experts)
            gate = jnp.sum(jnp.where(lane == z, probs, 0.0), axis=-1, keepdims=True)
            wd[rows(j), :] = (gate * out_grad[j][...].astype(F32)).astype(BF)
        acc[0:m, :] = jnp.zeros((m, d), F32)
        dxa[0:m, :] = jnp.zeros((m, d), F32)

        def tile(i, _):
            at = pl.ds(pl.multiple_of(i * t, t), t)
            for side in range(2):
                a, s = gelu_parts(nn(x[r0:r1, :], wi[side, :, at]))
                a = a.astype(BF)
                act[side, r0:r1, at] = a
                acc[0:m, :] += nn(a, wo[side, at, :])
                g = (nt(wd[r0:r1, :], wo[side, at, :]) * s).astype(BF)
                dz[side, r0:r1, at] = g
                dxa[0:m, :] += nt(g, wi[side, :, at])
            return 0

        lax.fori_loop(0, f // t, tile, 0)
        for b, j in enumerate(blocks):
            here = slice(b * half, (b + 1) * half)
            e_rows = acc[here, :].astype(BF)
            eouts[j][...] = e_rows
            dgate = jnp.sum(out_grad[j][...].astype(F32) * e_rows.astype(F32), axis=-1, keepdims=True)
            lines = gate_lines(dgate)
            if j == 0:
                ret_ref[0, place(z), :] = dxa[here, :].astype(BF)
                dg_ref[0, pl.ds(z, 1)] = lines[None]
                forward(0)
            else:
                rsend[rows(j), :] = dxa[here, :].astype(BF)
                dgs[j] = lines
                returns[j] = (
                    pltpu.make_async_remote_copy(rsend.at[rows(j)], ret_ref.at[0, place(z)], r_send.at[j], r_recv.at[j],
                                                 device_id={"exp": there(j)}, device_id_type=MESH),
                    pltpu.make_async_remote_copy(dgs.at[j], dg_ref.at[0, z], l_send.at[j], l_recv.at[j],
                                                 device_id={"exp": there(j)}, device_id_type=MESH))
                for cp in returns[j]:
                    cp.start()

    for cp in loads:
        cp.wait()
    sends[1].wait_recv()
    run([0, 1])
    for j in near_first[1:]:
        sends[j].wait_recv()
        run([j])

    xt[...] = x[...].T
    wt[...] = wd[...].T

    tiles = f // t

    def cols(i):
        return pl.ds(pl.multiple_of(i * t, t), t)

    def swapped(i):
        return pltpu.make_async_remote_copy(gscr.at[1, :, :, cols(i)], ggot.at[:, :, cols(i)], g_send.at[i], g_recv.at[i],
                                            device_id=partner, device_id_type=MESH)

    def stored(i):
        return pltpu.make_async_copy(gscr.at[0, :, :, cols(i)], gw_ref.at[:, :, cols(i)], g_sem.at[i])

    def weight_tile(i, _):
        for side in (1, 0):
            gscr[side, 0, :, cols(i)] = nn(xt[...], dz[side, :, cols(i)]).astype(BF)
            gscr[side, 1, :, cols(i)] = nn(wt[...], act[side, :, cols(i)]).astype(BF)
            if side == 1:
                swapped(i).start()
        return 0

    lax.fori_loop(0, tiles, weight_tile, 0)

    def sum_tile(i, _):
        swapped(i).wait_recv()
        for k in range(2):
            gscr[0, k, :, cols(i)] = (gscr[0, k, :, cols(i)].astype(F32) + ggot[k, :, cols(i)].astype(F32)).astype(BF)
        stored(i).start()
        return 0

    lax.fori_loop(0, tiles, sum_tile, 0)

    for j in near_first:
        pltpu.make_async_remote_copy(rsend.at[rows(j)], ret_ref.at[0, place(there(j))], r_send.at[j], r_recv.at[j],
                                     device_id={"exp": there(j)}, device_id_type=MESH).wait_recv()
        pltpu.make_async_remote_copy(dgs.at[j], dg_ref.at[0, there(j)], l_send.at[j], l_recv.at[j],
                                     device_id={"exp": there(j)}, device_id_type=MESH).wait_recv()
        forward(j)

    def drain(i, _):
        stored(i).wait()
        swapped(i).wait_send()
        return 0

    lax.fori_loop(0, tiles, drain, 0)
    swap.wait_send()
    for j in range(size):
        if j:
            sends[j].wait_send()
            for cp in returns[j]:
                cp.wait_send()
        for cp in forwards[j]:
            cp.wait()


def expert_exchange(h4, tr, dys, router, im, io, tm, to, experts, half):
    n, d = h4.shape
    f = im.shape[1]
    s = experts * half
    wide = -(-half // LANES) * LANES
    tiles = f // (256 if f % 256 == 0 else tile_of(f))
    D, V = pltpu.SemaphoreType.DMA, pltpu.VMEM
    any_ = pl.BlockSpec(memory_space=pl.ANY)
    vm = pl.BlockSpec(memory_space=pltpu.VMEM)
    return pl.pallas_call(
        functools.partial(expert_exchange_body, experts, half),
        in_specs=[vm] * 7 + [any_] * 4,
        out_specs=[vm] * 6 + [any_],
        out_shape=[out((2, s, d), BF), out((2, experts, 8, wide), F32)] + [out((half, d), BF)] * 4 + [out((2, d, f), BF)],
        scratch_shapes=[
            V((n, d), BF), V((s, d), F32), V((s, d), BF), V((s, d), BF), V((2, d, f), BF), V((2, f, d), BF),
            V((2, s, f), BF), V((2, s, f), BF), V((s, d), BF), V((2 * half, d), F32), V((2 * half, d), F32),
            V((s, d), BF), V((2, 2, d, f), BF), V((2, d, f), BF), V((d, s), BF), V((d, s), BF),
            D((4,)), D((2,)), D((experts,)), D((experts,)), D((experts,)), D((experts,)), D((experts,)), D((experts,)),
            D((tiles,)), D((tiles,)), D((tiles,)),
            V((experts, 8, wide), F32), D((experts,)), D((experts,)), D((experts,)), D((experts,)),
        ],
        compiler_params=pltpu.CompilerParams(collective_id=1, has_side_effects=True, vmem_limit_bytes=VMEM_BYTES),
        cost_estimate=pl.CostEstimate(flops=24 * s * d * f, bytes_accessed=20 * d * f, transcendentals=0),
    )(h4, tr, *dys, router, im, io, tm, to)


FUSED = True
PER = 3


def on_device(images, counts, routes, priority, gain_one, qkv_one, out_one, gain_two, fc_in, fc_out, gain_three,
              qkv_two, out_two, gain_four, router, expert_in, expert_out, cotangent):
    n_slot, length, d = images.shape
    experts = router.shape[1]
    n_mdl = lax.axis_size("mdl")
    peers = lax.axis_size("exp")
    capacity = (25 * L * TOPK + 8 * experts - 1) // (8 * experts)
    half = -(-(-(-capacity // n_mdl)) // 16) * 16
    slots = experts * half
    own_img = n_slot // n_mdl
    f = fc_in.shape[1]
    c = qkv_one.shape[2]
    rows = own_img * LP
    core = lax.axis_index("mdl")
    per = PER
    unit = 4 * d // (2 * per)
    fused = FUSED and (lax.axis_size("grp"), peers, n_mdl) == (4, experts, 2) and peers == 4
    fused = fused and d == 2 * c and f == 4 * c and unit % (64 * peers) == 0 and c % 48 == 0

    def padded(v):
        return jnp.pad(v, ((0, 0), (0, LP - length), (0, 0))).reshape(n_slot * LP, -1)

    qm1, om1, im, tm, qm2, om2, em, fm = halves = (
        qkv_one, out_one, fc_in, fc_out, qkv_two, out_two, expert_in[0], expert_out[0])
    gains = jnp.stack([gain_one, gain_two, gain_three, gain_four])
    router_rows = jnp.pad(router.T, ((0, LANES - experts), (0, 0)))

    live = jnp.broadcast_to((jnp.arange(n_slot, dtype=I32) < counts[0, 0]).astype(I32)[:, None, None], (n_slot, 1, length))
    lines = jnp.concatenate([jnp.transpose(routes, (0, 2, 1)), priority.reshape(n_slot, 1, length), live], axis=1)
    lines = jnp.pad(lines, ((0, 0), (0, 4), (0, LQ - length)))
    blocks = [(half, d)] * peers if fused else [(slots, d)]
    slot_rows, col, *dy_out = call(
        functools.partial(routing_body, experts, capacity, half),
        [out((n_slot, 8, LQ), I32), out((rows, 8), I32)] + [out(b, BF) for b in blocks], lines, cotangent,
        scratch=[pltpu.VMEM((n_slot * LP, d), BF), pltpu.VMEM((8, LQ), I32)], flops=4 * slots * n_slot * LP * d,
    )
    def exchange(v):
        shaped = v.reshape(peers, v.shape[0] // peers, v.shape[1])
        return lax.all_to_all(shaped, "exp", 0, 0, tiled=True).reshape(v.shape)

    if fused:
        got, (qo1, oo1, io, to, qo2, oo2, eo, fo), dy_in = forward(images, gains, halves, dy_out[1:], rows)
        x1, *kept1, x2, h2, act2, slope2, x3 = got[:10]
        kept3, h4, x0 = got[10:14], got[14], got[15]
        dy_in = [dy_out[0], *dy_in]
    else:
        x0 = padded(images)
        qo1, oo1, io, to, qo2, oo2, eo, fo = (other_core(w) for w in halves)
        dy_in = exchange(dy_out[0])
        x1, *kept1 = attention_forward(x0, rows, gains, 0, qm1, qo1, om1, oo1)
        x2, h2, act2, slope2 = mlp_forward(x1, gains, 1, im, io, tm, to)
        x3, *kept3, h4 = attention_forward(x2, rows, gains, 2, qm2, qo2, om2, oo2, tail=3)

    if fused:
        ret, dgate, *eout, ge = expert_exchange(h4, slot_rows, dy_in, router_rows, em, eo, fm, fo, experts, half)
        (dg1, dg2, dg3, dg4, dr, image), grads, eback = backward(
            experts, half, x3, h4, router_rows, cotangent, col, ret, dgate, gains, x2, kept3, (qm2, qo2, om2, oo2),
            x1, h2, act2, slope2, (im, io, tm, to), x0, kept1, (qm1, qo1, om1, oo1), eout[1:])
        a2_mine, a2_other, gim, gio, gtm, gto, a1_mine, a1_other = grads
        eback = [eout[0], *eback]
    else:
        [h4_out] = call(functools.partial(dispatch_body, experts, half), [out((slots, d), BF)], slot_rows, h4, other_core(h4))
        h4_in = exchange(h4_out)
        eout, ret, eact, edz, ewd = expert_forward_backward(h4_in, dy_in, router_rows, em, eo, fm, fo, experts)
        ret, eout = exchange(ret), exchange(eout)
        ret, eback = jnp.stack([ret, other_core(ret)]), jnp.stack([eout, other_core(eout)])
        dgate = ret[:, :, d].astype(F32) + ret[:, :, d + LANES // 2].astype(F32)
        wide = -(-half // LANES) * LANES
        dgate = jnp.pad(dgate.reshape(2, experts, 1, half), ((0, 0), (0, 0), (0, 7), (0, wide - half)))
        ret = ret[:, :, :d]
        ge_mine, ge_other = expert_weights(h4_in, ewd, eact, edz)
        ge = add16(ge_mine, other_core(ge_other))
        dx2, dg3, dg4, dr, a2_mine, a2_other = mixture_attention_backward(
            experts, half, x3, h4, router_rows, cotangent, col, ret, dgate, x2, gains, kept3, qm2, qo2, om2, oo2)
        dx1, dg2, gim, gio, gtm, gto = mlp_backward(dx2, x1, gains, 1, h2, act2, slope2, im, io, tm, to, c)
        image, dg1, a1_mine, a1_other = attention_backward(dx1, x0, gains, 0, kept1, qm1, qo1, om1, oo1)
    expert_sum = lax.psum_scatter(ge, "grp", scatter_dimension=1, tiled=True)

    mines, others = (a2_mine, gim, gtm, a1_mine), (a2_other, gio, gto, a1_other)

    if fused:
        split = [[v.reshape(per, 2, unit, c) for v in side] for side in (mines, others)]
        qkv2, proj2, fi, fo_, qkv1, proj1, small, output, grad_images = reduce_all(
            *split, (dg1, dg2, dg3, dg4), dr, x3, h4, router_rows, col, eback, image, peers, experts)
    else:
        sums = [sum_everywhere(add16(a.reshape(4 * d, c), other_core(b.reshape(4 * d, c)))) for a, b in zip(mines, others)]
        small = small_sum(jnp.concatenate([dg1, dg2, dg3, dg4, dr[:experts]], axis=0))

        def panels(v):
            return jnp.concatenate([v[i] for i in range(v.shape[0])], axis=1)

        (qkv2, proj2), (qkv1, proj1) = (
            (v[: 3 * d].reshape(3, d, c), panels(v[3 * d :].reshape(d // c, c, c))) for v in (sums[0], sums[3]))
        fi, fo_ = panels(sums[1].reshape(f // c, d, c)), panels(sums[2].reshape(d // c, f, c))
        [own_out] = call(
            functools.partial(mixture_output_body, experts), [out((own_img, L, d), BF)], x3, h4, router_rows, col, eback,
            flops=8 * rows * slots * d)

        def both(v):
            there = other_core(v)
            return jnp.where(core == 0, jnp.concatenate([v, there]), jnp.concatenate([there, v]))

        output, grad_images = both(own_out), both(image)
    return (
        output, grad_images,
        small[0], qkv1.astype(F32), proj1.astype(F32), small[1], fi.astype(F32), fo_.astype(F32),
        small[2], qkv2.astype(F32), proj2.astype(F32), small[3], small[4 : 4 + experts].T,
        expert_sum[0].astype(F32)[None], expert_sum[1].astype(F32).T[None],
    )


def solution(mesh):
    token = P(("grp", "exp"), None, None)
    column, line = P(None, None, "mdl"), P("mdl", None)
    return jax.shard_map(
        on_device,
        mesh=mesh,
        in_specs=(token, P("grp", "exp"), token, P(("grp", "exp"), None), P(), column, line, P(), P(None, "mdl"), line,
                  P(), column, line, P(), P(), P("exp", None, "mdl"), P("exp", "mdl", None), token),
        out_specs=(token, token, P(), column, line, P(), P(None, "mdl"), line, P(), column, line, P(), P(),
                   P("exp", "grp", "mdl"), P("exp", "mdl", "grp")),
        check_vma=False,
    )
```

```python
import functools
import math

import jax
import jax.numpy as jnp
from jax import lax
from jax.experimental import pallas as pl
from jax.experimental.pallas import tpu as pltpu
from jax.sharding import PartitionSpec as P

HDIM = 64
L = 197
TOPK = 2
LP = (L + 15) // 16 * 16
LANES = 128
LQ = (L + LANES - 1) // LANES * LANES
BF = jnp.bfloat16
F32 = jnp.float32
I32 = jnp.int32

EPSILON = 1e-06
ROOT_HALF = 0.7071067811865476
DENSITY_FACTOR = 0.3989422804014327
VMEM_BYTES = 60 * 1024 * 1024
MESH = pl.DeviceIdType.MESH


def nn(a, b):
    return lax.dot_general(a, b, (((1,), (0,)), ((), ())), preferred_element_type=F32)


def nt(a, b):
    return lax.dot_general(a, b, (((1,), (1,)), ((), ())), preferred_element_type=F32)


def tn(a, b):
    return lax.dot_general(a, b, (((0,), (0,)), ((), ())), preferred_element_type=F32)


def norm_forward(v, w):
    c = v - jnp.mean(v, axis=-1, keepdims=True)
    r = lax.rsqrt(jnp.mean(c * c, axis=-1, keepdims=True) + EPSILON)
    n = c * r
    return n, r, (n * w).astype(BF)


def norm_backward(n, r, w, dh):
    dn = dh * w
    dw = jnp.sum(dh * n, axis=0, keepdims=True)
    dv = r * (dn - jnp.mean(dn, axis=-1, keepdims=True) - n * jnp.mean(dn * n, axis=-1, keepdims=True))
    return dv, dw


def whole(shape):
    return pl.BlockSpec(shape, lambda *i: (0,) * len(shape))


def call(body, out_shape, *args, grid=(), in_specs=None, out_specs=None, scratch=(), flops=0):
    if in_specs is None:
        in_specs = [whole(a.shape) for a in args]
    if out_specs is None:
        out_specs = [whole(o.shape) for o in out_shape]
    moved = sum(math.prod(a.shape) * a.dtype.itemsize for a in args)
    moved += sum(math.prod(o.shape) * jnp.dtype(o.dtype).itemsize for o in out_shape)
    return pl.pallas_call(
        body,
        grid=grid,
        in_specs=in_specs,
        out_specs=out_specs,
        out_shape=out_shape,
        scratch_shapes=list(scratch),
        cost_estimate=pl.CostEstimate(flops=int(flops), bytes_accessed=int(moved), transcendentals=0),
        compiler_params=pltpu.CompilerParams(vmem_limit_bytes=VMEM_BYTES),
    )(*args)


def out(shape, dtype):
    return jax.ShapeDtypeStruct(shape, dtype)


def head_mask(dtype):
    lane = lax.broadcasted_iota(I32, (LP, LANES), 1)
    return (lane < HDIM).astype(dtype)


def beside(z, j):
    b0, b1 = z % 2, z // 2
    if j & 1:
        b0 = 1 - b0
    if j & 2:
        b1 = 1 - b1
    return b0 + 2 * b1


def fill_rows(ref, at, images, first, count):
    for i in range(count):
        ref[at + i * LP : at + i * LP + L, :] = images[first + i].astype(ref.dtype)
        ref[at + i * LP + L : at + (i + 1) * LP, :] = jnp.zeros((LP - L, ref.shape[1]), ref.dtype)


def own_rows(ref, n):
    if ref.shape[0] == n:
        return ref[...]
    return ref[pl.ds(pl.multiple_of(lax.axis_index("mdl") * n, 16), n), :]


def attend(img, pair, d, qkv_ref, p_ref, o_ref):
    mask = head_mask(BF)
    key_ok = lax.broadcasted_iota(I32, (LP, LP), 1) < L
    rows = pl.ds(pl.multiple_of(img * LP, LP), LP)
    col = pair * LANES
    q = qkv_ref[rows, pl.ds(pl.multiple_of(col, LANES), LANES)]
    ke = qkv_ref[rows, pl.ds(pl.multiple_of(d + col, LANES), LANES)]
    u = qkv_ref[rows, pl.ds(pl.multiple_of(2 * d + col, LANES), LANES)]
    o = jnp.zeros((LP, LANES), F32)
    for hh in range(2):
        mk = mask if hh == 0 else 1 - mask
        s = nt(q * mk, ke) * HDIM ** (-0.5)
        s = jnp.where(key_ok, s, -1e30)
        e = jnp.exp(s - jnp.max(s, axis=-1, keepdims=True))
        p = (e / jnp.sum(e, axis=-1, keepdims=True)).astype(BF)
        p_ref[2 * (img * (d // LANES) + pair) + hh] = p
        o = o + nn(p, u * mk)
    o_ref[rows, pl.ds(pl.multiple_of(col, LANES), LANES)] = o.astype(BF)
    return 0


def attention_forward_body(n_img, g_at, tail, *refs):
    refs = list(refs)
    x_ref, g_ref, qm, qo, om, oo = refs[:6]
    del refs[:6]
    y_ref, h_ref, qkv_ref, p_ref, o_ref = refs[:5]
    del refs[:5]
    h4_ref = refs.pop(0) if tail is not None else None
    rows_all = n_img * LP
    d = x_ref.shape[1]
    c = qm.shape[2]
    pairs = d // LANES
    _, _, h = norm_forward(own_rows(x_ref, rows_all).astype(F32), g_ref[g_at : g_at + 1, :])
    h_ref[...] = h
    for k in range(3):
        for side, w in ((0, qm), (1, qo)):
            at = (2 * k + side) * c
            qkv_ref[:, at : at + c] = nn(h_ref[...], w[k]).astype(BF)
    lax.fori_loop(0, n_img * pairs, lambda i, _: attend(i // pairs, i % pairs, d, qkv_ref, p_ref, o_ref), 0, unroll=2)
    y = own_rows(x_ref, rows_all).astype(F32) + nn(o_ref[:, :c], om[...]) + nn(o_ref[:, c:], oo[...])
    y_ref[...] = y
    if tail is not None:
        _, _, h4 = norm_forward(y, g_ref[tail : tail + 1, :])
        h4_ref[...] = h4


def attention_forward(x, r, gains, g_at, qm, qo, om, oo, tail=None):
    d = x.shape[1]
    n_img = r // LP
    heads = d // HDIM
    shapes = [out((r, d), F32), out((r, d), BF), out((r, 3 * d), BF), out((n_img * heads, LP, LP), BF), out((r, d), BF)]
    if tail is not None:
        shapes.append(out((r, d), BF))
    return call(functools.partial(attention_forward_body, n_img, g_at, tail), shapes, x, gains, qm, qo, om, oo,
                flops=2 * r * d * d * 4 + 4 * n_img * heads * LP * LP * LANES)


def attention_backward_core(n_img, dy, x_ref, gain, h_ref, qkv_ref, p_ref, o_ref, qm, qo, om, oo,
                            gm_ref, go_ref, do_ref, dqkv_ref, tr_ref, done=lambda part: None):
    d = x_ref.shape[1]
    c = qm.shape[2]
    pairs = d // LANES
    da = dy().astype(BF)
    tr_ref[...] = o_ref[...].T
    for side, (w, g) in enumerate(((om, gm_ref), (oo, go_ref))):
        gw = nn(tr_ref[side * c : (side + 1) * c, :], da).astype(BF)
        for part in range(d // c):
            g[3 * d + part * c : 3 * d + (part + 1) * c, :] = gw[:, part * c : (part + 1) * c]
        do_ref[:, side * c : (side + 1) * c] = nt(da, w[...]).astype(BF)
    done(3)
    mask = head_mask(BF)

    def one(i, _):
        rows = pl.ds(pl.multiple_of((i // pairs) * LP, LP), LP)
        col = (i % pairs) * LANES
        cq = pl.ds(pl.multiple_of(col, LANES), LANES)
        ck = pl.ds(pl.multiple_of(d + col, LANES), LANES)
        cu = pl.ds(pl.multiple_of(2 * d + col, LANES), LANES)
        q, ke, u, do = qkv_ref[rows, cq], qkv_ref[rows, ck], qkv_ref[rows, cu], do_ref[rows, cq]
        dq = jnp.zeros((LP, LANES), F32)
        dk = jnp.zeros((LP, LANES), F32)
        du = jnp.zeros((LP, LANES), F32)
        for hh in range(2):
            mk = mask if hh == 0 else 1 - mask
            p = p_ref[2 * i + hh]
            du = du + tn(p, do * mk)
            dp = nt(do * mk, u)
            pf = p.astype(F32)
            ds = (pf * (dp - jnp.sum(dp * pf, axis=-1, keepdims=True))).astype(BF)
            dq = dq + nn(ds, ke * mk)
            dk = dk + tn(ds, q * mk)
        dqkv_ref[rows, cq] = (dq * HDIM ** (-0.5)).astype(BF)
        dqkv_ref[rows, ck] = (dk * HDIM ** (-0.5)).astype(BF)
        dqkv_ref[rows, cu] = du.astype(BF)
        return 0

    lax.fori_loop(0, n_img * pairs, one, 0, unroll=2)
    tr_ref[...] = h_ref[...].T
    dh = jnp.zeros((n_img * LP, d), F32)
    for k in range(3):
        for side, (w, g) in enumerate(((qm, gm_ref), (qo, go_ref))):
            at = (2 * k + side) * c
            g[k * d : (k + 1) * d, :] = nn(tr_ref[...], dqkv_ref[:, at : at + c]).astype(BF)
            dh = dh + nt(dqkv_ref[:, at : at + c], w[k])
        done(k)
    n, rr, _ = norm_forward(own_rows(x_ref, n_img * LP).astype(F32), gain)
    dv, dw = norm_backward(n, rr, gain, dh)
    return dy() + dv, dw


def attention_backward_body(n_img, g_at, dy_ref, x_ref, g_ref, h_ref, qkv_ref, p_ref, o_ref, qm, qo, om, oo,
                            dx_ref, dw_ref, gm_ref, go_ref, do_ref, dqkv_ref, tr_ref):
    dx, dw = attention_backward_core(
        n_img, lambda: dy_ref[...], x_ref, g_ref[g_at : g_at + 1, :], h_ref, qkv_ref, p_ref, o_ref, qm, qo, om, oo,
        gm_ref, go_ref, do_ref, dqkv_ref, tr_ref)
    for i in range(n_img):
        dx_ref[i] = dx[i * LP : i * LP + L].astype(BF)
    dw_ref[...] = dw


def attention_backward_scratch(r, d):
    return [pltpu.VMEM((r, d), BF), pltpu.VMEM((r, 3 * d), BF), pltpu.VMEM((d, r), BF)]


def attention_backward(dy, x, gains, g_at, kept, qm, qo, om, oo):
    r, d = dy.shape
    c = qm.shape[2]
    n_img = r // LP
    heads = d // HDIM
    return call(
        functools.partial(attention_backward_body, n_img, g_at),
        [out((n_img, L, d), BF), out((1, d), F32), out((3 * d + d, c), BF), out((3 * d + d, c), BF)],
        dy, x, gains, *kept, qm, qo, om, oo,
        scratch=attention_backward_scratch(r, d),
        flops=4 * r * d * d * 4 + 8 * n_img * heads * LP * LP * LANES,
    )


def gelu_parts(z):
    phi = 0.5 * (1.0 + lax.erf(z * ROOT_HALF))
    return z * phi, phi + z * jnp.exp(-0.5 * z * z) * DENSITY_FACTOR


def tile_of(f):
    for t in (512, 256, 128):
        if f % t == 0:
            return t
    return f


def mlp_forward_body(g_at, x_ref, g_ref, im, io, tm, to, y_ref, h_ref, act_ref, slope_ref, acc_ref):
    step = pl.program_id(0)

    @pl.when(step == 0)
    def _():
        x = x_ref[...]
        _, _, h = norm_forward(x, g_ref[g_at : g_at + 1, :])
        h_ref[...] = h
        acc_ref[...] = x

    for half, (wi, wo) in enumerate(((im, tm), (io, to))):
        a, s = gelu_parts(nn(h_ref[...], wi[...]))
        act = a.astype(BF)
        act_ref[half] = act
        slope_ref[half] = s.astype(BF)
        acc_ref[...] += nn(act, wo[...])

    @pl.when(step == pl.num_programs(0) - 1)
    def _():
        y_ref[...] = acc_ref[...]


def mlp_forward(x, gains, g_at, im, io, tm, to):
    r, d = x.shape
    f = im.shape[1]
    t = tile_of(f)
    col = pl.BlockSpec((d, t), lambda i: (0, i))
    row = pl.BlockSpec((t, d), lambda i: (i, 0))
    hid = pl.BlockSpec((2, r, t), lambda i: (0, 0, i))
    return call(
        functools.partial(mlp_forward_body, g_at),
        [out((r, d), F32), out((r, d), BF), out((2, r, f), BF), out((2, r, f), BF)],
        x, gains, im, io, tm, to, grid=(f // t,),
        in_specs=[whole((r, d)), whole(gains.shape), col, col, row, row],
        out_specs=[whole((r, d)), whole((r, d)), hid, hid],
        scratch=[pltpu.VMEM((r, d), F32)], flops=8 * r * d * f,
    )


def mlp_backward_body(g_at, dy_ref, x_ref, g_ref, h_ref, act_ref, slope_ref, im, io, tm, to,
                      dx_ref, dw_ref, gim, gio, gtm, gto, da_ref, tr_ref, dh_ref):
    step = pl.program_id(0)

    @pl.when(step == 0)
    def _():
        da_ref[...] = dy_ref[...].astype(BF)
        tr_ref[...] = h_ref[...].T
        dh_ref[...] = jnp.zeros_like(dh_ref)

    for half, (wi, wo, gi, go) in enumerate(((im, tm, gim, gtm), (io, to, gio, gto))):
        dact = nt(da_ref[...], wo[...])
        dz = (dact * slope_ref[half].astype(F32)).astype(BF)
        gw = tn(act_ref[half], da_ref[...]).astype(BF)
        t = gw.shape[0]
        for part in range(gw.shape[1] // t):
            go[part] = gw[:, part * t : (part + 1) * t]
        gi[0] = nn(tr_ref[...], dz).astype(BF)
        dh_ref[...] += nt(dz, wi[...])

    @pl.when(step == pl.num_programs(0) - 1)
    def _():
        gain = g_ref[g_at : g_at + 1, :]
        n, rr, _ = norm_forward(x_ref[...], gain)
        dv, dw = norm_backward(n, rr, gain, dh_ref[...])
        dx_ref[...] = dy_ref[...] + dv
        dw_ref[...] = dw


def mlp_backward(dy, x, gains, g_at, h, act, slope, im, io, tm, to, t):
    r, d = x.shape
    f = im.shape[1]
    col = pl.BlockSpec((d, t), lambda i: (0, i))
    row = pl.BlockSpec((t, d), lambda i: (i, 0))
    hid = pl.BlockSpec((2, r, t), lambda i: (0, 0, i))
    gin = pl.BlockSpec((1, d, t), lambda i: (i, 0, 0))
    gout = pl.BlockSpec((d // t, t, t), lambda i: (0, i, 0))
    return call(
        functools.partial(mlp_backward_body, g_at),
        [out((r, d), F32), out((1, d), F32), out((f // t, d, t), BF), out((f // t, d, t), BF),
         out((d // t, f, t), BF), out((d // t, f, t), BF)],
        dy, x, gains, h, act, slope, im, io, tm, to, grid=(f // t,),
        in_specs=[whole((r, d)), whole((r, d)), whole(gains.shape), whole((r, d)), hid, hid, col, col, row, row],
        out_specs=[whole((r, d)), whole((1, d)), gin, gin, gout, gout],
        scratch=[pltpu.VMEM((r, d), BF), pltpu.VMEM((d, r), BF), pltpu.VMEM((r, d), F32)], flops=16 * r * d * f,
    )


def forward_body(n_img, size, *refs):
    refs = list(refs)

    def take(n):
        r = refs[:n]
        del refs[:n]
        return r

    images, g_ref = take(2)
    own_w = take(8)
    dy_out = take(size - 1)
    results = take(16)
    other_w = take(8)
    dy_in = take(size - 1)
    weights = take(6)
    held = take(16)
    load_sem, w_send, w_recv, o_sem, r_sem, d_send, d_recv = refs
    x1, h1, qkv1, p1, o1, x2, h2, act, slope, x3, h3, qkv3, p3, o3, h4, x0 = held
    q1, w1, fi, fo, q3, w3 = weights
    r = n_img * LP
    d = x0.shape[1]
    c = q1.shape[3]
    f = fi.shape[2]
    z = lax.axis_index("exp")
    partner = {"mdl": 1 - lax.axis_index("mdl")}

    loads = [pltpu.make_async_copy(own_w[k], weights[k].at[0], load_sem.at[k]) for k in range(6)]
    for cp in loads:
        cp.start()
    barrier = pltpu.get_barrier_semaphore()
    for dev in [partner] + [{"exp": beside(z, j)} for j in range(1, size)]:
        pl.semaphore_signal(barrier, inc=1, device_id=dev, device_id_type=MESH)
    pl.semaphore_wait(barrier, size)
    swaps = [pltpu.make_async_remote_copy(own_w[k], weights[k].at[1] if k < 6 else other_w[k], w_send.at[k], w_recv.at[k],
                                          device_id=partner, device_id_type=MESH) for k in range(8)]
    for cp in swaps[0:2]:
        cp.start()
    blocks = [pltpu.make_async_remote_copy(dy_out[j - 1], dy_in[j - 1], d_send.at[j - 1], d_recv.at[j - 1],
                                           device_id={"exp": beside(z, j)}, device_id_type=MESH) for j in range(1, size)]
    for cp in blocks:
        cp.start()
    keeps = [pltpu.make_async_copy(weights[k].at[1], other_w[k], o_sem.at[k]) for k in range(6)]
    stores = [pltpu.make_async_copy(held[k], results[k], r_sem.at[k]) for k in range(16)]

    def store(*at):
        for k in at:
            stores[k].start()

    def attention(x, gain, wq, wo, kq, ko, h, qkv, p, o, y, then):
        _, _, n = norm_forward(x(), gain)
        h[...] = n
        per_half = c // LANES
        for side in range(2):
            if side == 0:
                loads[kq].wait()
            else:
                swaps[kq].wait_recv()
                keeps[kq].start()
                for cp in swaps[then : then + 2]:
                    cp.start()
            for k in range(3):
                at = (2 * k + side) * c
                qkv[:, at : at + c] = nn(h[...], wq[side, k]).astype(BF)
            lax.fori_loop(
                0, n_img * per_half,
                lambda i, _, side=side: attend(i // per_half, side * per_half + i % per_half, d, qkv, p, o), 0, unroll=2)
        loads[ko].wait()
        swaps[ko].wait_recv()
        keeps[ko].start()
        y[...] = x() + nn(o[:, :c], wo[0]) + nn(o[:, c:], wo[1])

    fill_rows(x0, 0, images, lax.axis_index("mdl") * n_img, n_img)
    store(15)
    attention(lambda: x0[...].astype(F32), g_ref[0:1, :], q1, w1, 0, 1, h1, qkv1, p1, o1, x1, 2)
    store(0, 1, 2, 3, 4)

    _, _, n = norm_forward(x1[...], g_ref[1:2, :])
    h2[...] = n
    x2[...] = x1[...]
    t = tile_of(f)
    for side in range(2):
        for k in (2, 3):
            if side == 0:
                loads[k].wait()
            else:
                swaps[k].wait_recv()
                keeps[k].start()

        def tile(i, _, side=side):
            at = pl.ds(pl.multiple_of(i * t, t), t)
            a, sl = gelu_parts(nn(h2[...], fi[side, :, at]))
            a = a.astype(BF)
            act[side, :, at] = a
            slope[side, :, at] = sl.astype(BF)
            x2[...] += nn(a, fo[side, at, :])
            return 0

        for cp in swaps[4 + 2 * side : 6 + 2 * side]:
            cp.start()
        lax.fori_loop(0, f // t, tile, 0)
    store(5, 6, 7, 8)

    attention(lambda: x2[...], g_ref[2:3, :], q3, w3, 4, 5, h3, qkv3, p3, o3, x3, 8)
    store(9, 10, 11, 12, 13)
    _, _, n = norm_forward(x3[...], g_ref[3:4, :])
    h4[...] = n
    store(14)
    for cp in blocks:
        cp.wait()
    for cp in keeps + stores:
        cp.wait()
    for cp in swaps[6:]:
        cp.wait_recv()
    for cp in swaps:
        cp.wait_send()


def forward(x, gains, own_w, dy_out, r):
    d = x.shape[2]
    c, f = own_w[0].shape[2], own_w[2].shape[1]
    n_img = r // LP
    heads = d // HDIM
    size = len(dy_out) + 1
    half = dy_out[0].shape[0]
    kept = [out((r, d), F32), out((r, d), BF), out((r, 3 * d), BF), out((n_img * heads, LP, LP), BF), out((r, d), BF)]
    results = kept + [out((r, d), F32), out((r, d), BF), out((2, r, f), BF), out((2, r, f), BF)] + kept + [out((r, d), BF), out((r, d), BF)]
    shapes = results + [out(w.shape, BF) for w in own_w] + [out((half, d), BF)] * (size - 1)
    D, V = pltpu.SemaphoreType.DMA, pltpu.VMEM
    any_ = pl.BlockSpec(memory_space=pl.ANY)
    vm = pl.BlockSpec(memory_space=pltpu.VMEM)
    got = pl.pallas_call(
        functools.partial(forward_body, n_img, size),
        in_specs=[vm] * 2 + [any_] * (len(own_w) + size - 1), out_specs=[any_] * len(shapes), out_shape=shapes,
        scratch_shapes=[V((2,) + w.shape, BF) for w in own_w[:6]] + [V(o.shape, o.dtype) for o in results]
        + [D((6,)), D((8,)), D((8,)), D((6,)), D((len(results),)), D((size - 1,)), D((size - 1,))],
        compiler_params=pltpu.CompilerParams(collective_id=2, has_side_effects=True, vmem_limit_bytes=VMEM_BYTES),
        cost_estimate=pl.CostEstimate(flops=16 * r * d * d + 8 * r * d * f, bytes_accessed=80 * r * d, transcendentals=0),
    )(x, gains, *own_w, *dy_out)
    n = len(results)
    return got[:n], got[n : n + 8], got[n + 8 :]


def routing_body(experts, capacity, half, count_ref, route_ref, prior_ref, router_ref, ga, gb, gc, gd, dy_ref, tr_ref, col_ref, wide_ref,
                 gains_ref, *refs):
    out_refs, (dy_rows, rows_ref, tmp) = refs[:-3], refs[-3:]
    for k, g in enumerate((ga, gb, gc, gd)):
        gains_ref[k : k + 1, :] = g[...].reshape(1, g.shape[0])
    wide_ref[...] = jnp.zeros(wide_ref.shape, BF)
    wide_ref[0:experts, :] = router_ref[...]
    fill_rows(dy_rows, 0, dy_ref, 0, rows_ref.shape[0])
    token = lax.broadcasted_iota(I32, (1, LQ), 1)
    for i in range(rows_ref.shape[0]):
        rows_ref[i] = jnp.zeros((8, LQ), I32)
        rows_ref[i, 0:TOPK, 0:L] = route_ref[i]
        rows_ref[i, 2:3, 0:L] = prior_ref[:, i * L : (i + 1) * L]
        rows_ref[i, 3:4, :] = jnp.where(token < L, (count_ref[0, 0] > i).astype(I32), 0)
    n_img = rows_ref.shape[0]
    slots = experts * half
    core = lax.axis_index("mdl")
    own_img = n_img // 2
    tall = lax.broadcasted_iota(I32, (max(experts, 8), LQ), 0)
    hots, priors = [], []
    for i in range(n_img):
        r = rows_ref[i]
        live = r[3:4, :] > 0
        hots.append((((tall == r[0:1, :]) | (tall == r[1:2, :])) & live).astype(F32).astype(BF))
        priors.append(r.astype(F32).T[:, 2:3])
    for i in range(n_img):
        r = rows_ref[i]
        rank = None
        for k in range(n_img):
            part = nn(hots[k], (priors[k] < r[2:3, :].astype(F32)).astype(F32).astype(BF))
            rank = part if rank is None else rank + part
        for k in range(TOPK):
            e = r[k : k + 1, :]
            mine = jnp.sum(jnp.where(tall == e, rank, 0.0), axis=0, keepdims=True).astype(I32)
            side = (mine >= half).astype(I32)
            slot = side * slots + e * half + mine - side * half
            tr_ref[i, k : k + 1, :] = jnp.where((mine < capacity) & (r[3:4, :] > 0), slot, -1)
        tr_ref[i, TOPK:, :] = jnp.full((8 - TOPK, LQ), -1, I32)
    for i in range(own_img):
        at = core * own_img + i
        for k in range(TOPK):
            t = tr_ref[at, k : k + 1, :]
            there = t - (1 - core) * slots
            tmp[k : k + 1, :] = t - core * slots
            tmp[TOPK + k : TOPK + k + 1, :] = jnp.where(there < slots, there, -1)
        tmp[4:8, :] = rows_ref[at, 0:4, :]
        tmp[6:7, :] = rows_ref[at, 3:4, :]
        col_ref[i * LP : (i + 1) * LP, :] = tmp[...].astype(F32).T[:LP, :].astype(I32)
    z = lax.axis_index("exp")
    for j, o_ref in enumerate(out_refs):
        at = core * slots + (beside(z, j) * half if len(out_refs) > 1 else 0)
        total = None
        for i in range(n_img):
            part = nn(slot_hots(tr_ref[i], at, o_ref.shape[0]), dy_rows[i * LP : (i + 1) * LP, :])
            total = part if total is None else total + part
        o_ref[...] = total.astype(BF)


def slot_hots(t, base, count):
    place = lax.broadcasted_iota(I32, (count, LP), 0) + base
    return ((place == t[0:1, :LP]) | (place == t[1:2, :LP])).astype(F32).astype(BF)


def dispatch_body(experts, half, tr_ref, own_ref, oth_ref, y_ref):
    core = lax.axis_index("mdl")
    own_img = own_ref.shape[0] // LP
    total = None
    for a, v in ((core, own_ref), (1 - core, oth_ref)):
        for i in range(own_img):
            hot = slot_hots(tr_ref[a * own_img + i], core * experts * half, experts * half)
            part = nn(hot, v[i * LP : (i + 1) * LP, :])
            total = part if total is None else total + part
    y_ref[...] = total.astype(BF)


def router_probs(h, router, experts):
    logits = nt(h, router)
    lane = lax.broadcasted_iota(I32, logits.shape, 1)
    logits = jnp.where(lane < experts, logits, -1e30)
    e = jnp.exp(logits - jnp.max(logits, axis=-1, keepdims=True))
    return e / jnp.sum(e, axis=-1, keepdims=True), lane


def expert_body(experts, x_ref, dy_ref, router_ref, im, io, tm, to,
                eout_ref, ret_ref, act_ref, dz_ref, wd_ref, acc_ref, dx_ref):
    step = pl.program_id(0)
    d = x_ref.shape[1]

    @pl.when(step == 0)
    def _():
        probs, lane = router_probs(x_ref[...], router_ref[...], experts)
        gate = jnp.sum(jnp.where(lane == lax.axis_index("exp"), probs, 0.0), axis=-1, keepdims=True)
        wd_ref[...] = (gate * dy_ref[...].astype(F32)).astype(BF)
        acc_ref[...] = jnp.zeros_like(acc_ref)
        dx_ref[...] = jnp.zeros_like(dx_ref)

    for half, (wi, wo) in enumerate(((im, tm), (io, to))):
        a, s = gelu_parts(nn(x_ref[...], wi[...]))
        act = a.astype(BF)
        act_ref[half] = act
        acc_ref[...] += nn(act, wo[...])
        dz = (nt(wd_ref[...], wo[...]) * s).astype(BF)
        dz_ref[half] = dz
        dx_ref[...] += nt(dz, wi[...])

    @pl.when(step == pl.num_programs(0) - 1)
    def _():
        eout = acc_ref[...].astype(BF)
        eout_ref[...] = eout
        ret_ref[:, :d] = dx_ref[...].astype(BF)
        dgate = jnp.sum(dy_ref[...].astype(F32) * eout.astype(F32), axis=-1, keepdims=True)
        high = dgate.astype(BF).astype(F32)
        lane = lax.broadcasted_iota(I32, (x_ref.shape[0], LANES), 1)
        ret_ref[:, d:] = jnp.where(lane < LANES // 2, high, dgate - high).astype(BF)


def expert_forward_backward(x, dy, router, im, io, tm, to, experts):
    r, d = x.shape
    f = im.shape[1]
    t = tile_of(f) // 2
    col = pl.BlockSpec((d, t), lambda i: (0, i))
    row = pl.BlockSpec((t, d), lambda i: (i, 0))
    hid = pl.BlockSpec((2, r, t), lambda i: (0, 0, i))
    return call(
        functools.partial(expert_body, experts),
        [out((r, d), BF), out((r, d + LANES), BF), out((2, r, f), BF), out((2, r, f), BF), out((r, d), BF)],
        x, dy, router, im, io, tm, to, grid=(f // t,),
        in_specs=[whole((r, d)), whole((r, d)), whole(router.shape), col, col, row, row],
        out_specs=[whole((r, d)), whole((r, d + LANES)), hid, hid, whole((r, d))],
        scratch=[pltpu.VMEM((r, d), F32), pltpu.VMEM((r, d), F32)], flops=16 * r * d * f,
    )


def expert_weights_body(x_ref, wd_ref, act_ref, dz_ref, gm_ref, go_ref, xt_ref, wt_ref):
    @pl.when(pl.program_id(0) == 0)
    def _():
        xt_ref[...] = x_ref[...].T
        wt_ref[...] = wd_ref[...].T

    for half, g in enumerate((gm_ref, go_ref)):
        g[0] = nn(xt_ref[...], dz_ref[half]).astype(BF)
        g[1] = nn(wt_ref[...], act_ref[half]).astype(BF)


def expert_weights(x, wd, act, dz):
    r, d = x.shape
    f = act.shape[2]
    t = tile_of(f) // 2
    hid = pl.BlockSpec((2, r, t), lambda i: (0, 0, i))
    grad = pl.BlockSpec((2, d, t), lambda i: (0, 0, i))
    return call(
        expert_weights_body, [out((2, d, f), BF), out((2, d, f), BF)], x, wd, act, dz, grid=(f // t,),
        in_specs=[whole((r, d)), whole((r, d)), hid, hid], out_specs=[grad, grad],
        scratch=[pltpu.VMEM((d, r), BF), pltpu.VMEM((d, r), BF)], flops=8 * r * d * f,
    )


def merge(col_ref, k, ab_ref, n):
    slots = ab_ref.shape[1]
    lane = lax.broadcasted_iota(I32, (n, slots), 1)
    rows = None
    for side in range(2):
        hot = (lane == col_ref[:, 2 * side + k : 2 * side + k + 1]).astype(F32).astype(BF)
        part = nn(hot, ab_ref[side])
        rows = part if rows is None else rows + part
    return rows


def merge_blocks(col_ref, k, blocks, n):
    rows = None
    for side in range(2):
        for e, ref in blocks[side]:
            half = ref.shape[0]
            lane = lax.broadcasted_iota(I32, (n, half), 1) + e * half
            hot = (lane == col_ref[:, 2 * side + k : 2 * side + k + 1]).astype(F32).astype(BF)
            part = nn(hot, ref[...])
            rows = part if rows is None else rows + part
    return rows


def mixture_backward_core(experts, half, x_ref, gain, h_ref, router_ref, dy_ref, col_ref, ab_ref, dgate_ref, dr_ref, dy_rows):
    n, d = x_ref.shape
    n_img = n // LP
    fill_rows(dy_rows, 0, dy_ref, lax.axis_index("mdl") * n_img, n_img)
    probs, lane = router_probs(h_ref[...], router_ref[...], experts)
    dsoft = jnp.zeros(probs.shape, F32)
    dh = jnp.zeros((n, d), F32)
    for k in range(TOPK):
        dh = dh + merge(col_ref, k, ab_ref, n)
        dgate = jnp.zeros((n, 1), F32)
        for side in range(2):
            t = col_ref[:, 2 * side + k : 2 * side + k + 1]
            for e in range(experts):
                line = dgate_ref[side, e, 0:1, :]
                place = lax.broadcasted_iota(I32, (n, line.shape[1]), 1)
                hit = (place + e * half == t) & (place < half)
                dgate = dgate + jnp.sum(jnp.where(hit, line, 0.0), axis=-1, keepdims=True)
        dsoft = dsoft + jnp.where(lane == col_ref[:, 4 + k : 5 + k], dgate, 0.0)
    dlog = (probs * (dsoft - jnp.sum(dsoft * probs, axis=-1, keepdims=True))).astype(BF)
    dr_ref[...] = tn(dlog, h_ref[...])
    dh = dh + nn(dlog, router_ref[...])
    nrm, rr, _ = norm_forward(x_ref[...], gain)
    dv, dw = norm_backward(nrm, rr, gain, dh)
    return dy_rows[...].astype(F32) * col_ref[:, 6:7].astype(F32) + dv, dw


def gate_lines(dgate):
    half = dgate.shape[0]
    wide = -(-half // LANES) * LANES
    tall = jnp.concatenate([dgate, jnp.zeros((wide - half, 1), F32)], axis=0) if wide > half else dgate
    return jnp.broadcast_to(tall, (wide, LANES)).T[0:8, :]


def mixture_attention_backward_body(n_img, experts, half, x3_ref, h4_ref, router_ref, dy_ref, col_ref, ret_ref, dgate_ref, x_ref, g_ref, h_ref,
                                    qkv_ref, p_ref, o_ref, qm, qo, om, oo, dx_ref, dw3_ref, dw4_ref, dr_ref, gm_ref, go_ref,
                                    dx3, dy_rows, do_ref, dqkv_ref, tr_ref):
    grad, dw4 = mixture_backward_core(experts, half, x3_ref, g_ref[3:4, :], h4_ref, router_ref, dy_ref, col_ref, ret_ref, dgate_ref,
                                      dr_ref, dy_rows)
    dx3[...] = grad
    dw4_ref[...] = dw4
    dx, dw3 = attention_backward_core(
        n_img, lambda: dx3[...], x_ref, g_ref[2:3, :], h_ref, qkv_ref, p_ref, o_ref, qm, qo, om, oo,
        gm_ref, go_ref, do_ref, dqkv_ref, tr_ref)
    dx_ref[...] = dx
    dw3_ref[...] = dw3


def mixture_attention_backward(experts, half, x3, h4, router, dy, col, ret, dgate, x, gains, kept, qm, qo, om, oo):
    r, d = x.shape
    c = qm.shape[2]
    n_img = r // LP
    heads = d // HDIM
    shapes = [out((r, d), F32), out((1, d), F32), out((1, d), F32), out(router.shape, F32),
              out((3 * d + d, c), BF), out((3 * d + d, c), BF)]
    return call(functools.partial(mixture_attention_backward_body, n_img, experts, half), shapes,
                x3, h4, router, dy, col, ret, dgate, x, gains, *kept, qm, qo, om, oo,
                scratch=[pltpu.VMEM((r, d), F32), pltpu.VMEM((r, d), BF)] + attention_backward_scratch(r, d),
                flops=4 * r * d * d * 4 + 8 * n_img * heads * LP * LP * LANES + 8 * r * ret.shape[1] * d)


def backward_body(n_img, experts, half, size, *refs):
    refs = list(refs)

    def take(n):
        r = refs[:n]
        del refs[:n]
        return r

    x3, h4, router, cotangent, col, ret, dgate, g_ref = take(8)
    src_two, src_mlp, src_one = take(9), take(8), take(9)
    eouts = take(size - 1)
    dg1, dg2, dg3, dg4, dr, image = take(6)
    out_two, out_mlp, out_one = take(2), take(4), take(2)
    ebacks = take(size - 1)
    attn = take(9)
    x0, x1, h2, act, slope, fi, fo, ga, gi, go, dxs, dy_rows, do, dqkv, tr, da, dh = take(17)
    a_sem, m_sem, b_sem, ga_sem, gi_sem, e_send, e_recv = refs
    d = x3.shape[1]
    f = fi.shape[2]
    t = gi.shape[4]
    z = lax.axis_index("exp")

    def fetch(srcs, dsts, sem):
        return [pltpu.make_async_copy(a, b, sem.at[k]) for k, (a, b) in enumerate(zip(srcs, dsts))]

    two = fetch(src_two, attn, a_sem)
    mlp = fetch(src_mlp, [x1, h2, act, slope, fi.at[0], fi.at[1], fo.at[0], fo.at[1]], m_sem)
    one = fetch(src_one, [x0] + attn[1:], b_sem)
    for cp in two + mlp:
        cp.start()
    barrier = pltpu.get_barrier_semaphore()
    for j in range(1, size):
        pl.semaphore_signal(barrier, inc=1, device_id={"exp": beside(z, j)}, device_id_type=MESH)
    pl.semaphore_wait(barrier, size - 1)
    blocks = [pltpu.make_async_remote_copy(eouts[j - 1], ebacks[j - 1], e_send.at[j - 1], e_recv.at[j - 1],
                                           device_id={"exp": beside(z, j)}, device_id_type=MESH) for j in range(1, size)]
    for cp in blocks:
        cp.start()

    def attention(x, gain, dst):
        leave = []

        def done(part):
            at = slice(part * d, (part + 1) * d)
            for k in range(2):
                leave.append(pltpu.make_async_copy(ga.at[k, at], dst[k].at[at], ga_sem.at[k, part]))
                leave[-1].start()

        dx, dw = attention_backward_core(n_img, lambda: dxs[...], x, gain, *attn[1:], ga.at[0], ga.at[1], do, dqkv, tr, done)
        return dx, dw, leave

    grad, dw4 = mixture_backward_core(experts, half, x3, g_ref[3:4, :], h4, router, cotangent, col, ret, dgate, dr, dy_rows)
    dxs[...] = grad
    dg4[...] = dw4
    for cp in two:
        cp.wait()
    dx, dw, leave = attention(attn[0], g_ref[2:3, :], out_two)
    dxs[...] = dx
    dg3[...] = dw
    for cp in one:
        cp.start()

    da[...] = dxs[...].astype(BF)
    for cp in mlp:
        cp.wait()
    tr[...] = h2[...].T
    dh[...] = jnp.zeros(dh.shape, F32)
    gone = {}
    for i in range(f // t):
        at = slice(i * t, (i + 1) * t)
        slot = i % 2
        for cp in gone.pop(slot, ()):
            cp.wait()
        gone[slot] = []
        for side in range(2):
            dz = (nt(da[...], fo[side, at, :]) * slope[side, :, at].astype(F32)).astype(BF)
            gw = tn(act[side, :, at], da[...]).astype(BF)
            for part in range(d // t):
                go[slot, side, part] = gw[:, part * t : (part + 1) * t]
            gi[slot, side, 0] = nn(tr[...], dz).astype(BF)
            dh[...] += nt(dz, fi[side, :, at])
            gone[slot] += [
                pltpu.make_async_copy(gi.at[slot, side], out_mlp[side].at[i : i + 1], gi_sem.at[slot, side, 0]),
                pltpu.make_async_copy(go.at[slot, side], out_mlp[2 + side].at[:, at], gi_sem.at[slot, side, 1])]
            for cp in gone[slot][-2:]:
                cp.start()
    gain = g_ref[1:2, :]
    n, rr, _ = norm_forward(x1[...], gain)
    dv, dw = norm_backward(n, rr, gain, dh[...])
    dxs[...] += dv
    dg2[...] = dw

    for cp in one + leave:
        cp.wait()
    dx, dw, leave = attention(x0, g_ref[0:1, :], out_one)
    for i in range(n_img):
        image[i] = dx[i * LP : i * LP + L].astype(BF)
    dg1[...] = dw
    for cp in leave + gone[0] + gone[1] + blocks:
        cp.wait()


def backward(experts, half, x3, h4, router, cotangent, col, ret, dgate, gains, x2, kept3, w2, x1, h2, act, slope, mlp_w, x0, kept1,
             w1, eouts):
    r, d = x3.shape
    c, f = w1[0].shape[2], mlp_w[0].shape[1]
    n_img = r // LP
    heads = d // HDIM
    size = len(eouts) + 1
    t = c
    flat = [x2, *kept3, *w2, x1, h2, act, slope, *mlp_w, x0, *kept1, *w1, *eouts]
    near = [x3, h4, router, cotangent, col, ret, dgate, gains]
    D, V = pltpu.SemaphoreType.DMA, pltpu.VMEM
    any_ = pl.BlockSpec(memory_space=pl.ANY)
    vm = pl.BlockSpec(memory_space=pltpu.VMEM)
    shapes = [out((1, d), F32)] * 4 + [out(router.shape, F32), out((n_img, L, d), BF)]
    shapes += [out((4 * d, c), BF)] * 2 + [out((f // t, d, t), BF)] * 2 + [out((d // t, f, t), BF)] * 2 + [out((4 * d, c), BF)] * 2
    shapes += [out(e.shape, BF) for e in eouts]
    like = [V(v.shape, v.dtype) for v in (x2, *kept3, *w2)]
    got = pl.pallas_call(
        functools.partial(backward_body, n_img, experts, half, size),
        in_specs=[vm] * len(near) + [any_] * len(flat), out_specs=[vm] * 6 + [any_] * (len(shapes) - 6), out_shape=shapes,
        scratch_shapes=like + [
            V(x0.shape, x0.dtype), V((r, d), F32), V((r, d), BF), V(act.shape, BF), V(slope.shape, BF), V((2, d, f), BF),
            V((2, f, d), BF), V((2, 4 * d, c), BF), V((2, 2, 1, d, t), BF), V((2, 2, d // t, t, t), BF), V((r, d), F32),
            V((r, d), BF), V((r, d), BF), V((r, 3 * d), BF), V((d, r), BF), V((r, d), BF), V((r, d), F32),
            D((9,)), D((8,)), D((9,)), D((2, 4)), D((2, 2, 2)), D((size - 1,)), D((size - 1,))],
        compiler_params=pltpu.CompilerParams(collective_id=3, has_side_effects=True, vmem_limit_bytes=VMEM_BYTES),
        cost_estimate=pl.CostEstimate(flops=32 * r * d * d + 16 * r * d * f, bytes_accessed=160 * r * d, transcendentals=0),
    )(*near, *flat)
    return got[:6], got[6:14], got[14:]


def mixture_output(experts, x_ref, h_ref, router_ref, col_ref, rows_of):
    n, d = x_ref.shape
    probs, lane = router_probs(h_ref[...], router_ref[...], experts)
    mixed = jnp.zeros((n, d), F32)
    for k in range(TOPK):
        gate = jnp.sum(jnp.where(lane == col_ref[:, 4 + k : 5 + k], probs, 0.0), axis=-1, keepdims=True)
        mixed = mixed + gate * rows_of(k)
    return (col_ref[:, 6:7].astype(F32) * (x_ref[...] + mixed)).astype(BF)


def mixture_output_body(experts, x_ref, h_ref, router_ref, col_ref, ab_ref, y_ref):
    y = mixture_output(experts, x_ref, h_ref, router_ref, col_ref, lambda k: merge(col_ref, k, ab_ref, x_ref.shape[0]))
    for i in range(y_ref.shape[0]):
        y_ref[i] = y[i * LP : i * LP + L]


def widen_body(pieces, n_in, n_slots, *refs):
    src, dst = refs[:n_in], refs[n_in:-2]
    buf, sem = refs[-2:]
    going = []
    for k, (i, a, o, b) in enumerate(pieces):
        slot = k % n_slots
        if k >= n_slots:
            going[k - n_slots].wait()
        value = src[i][a].astype(F32)
        rows, cols = value.shape
        buf[slot, 0:rows, 0:cols] = value
        going.append(pltpu.make_async_copy(buf.at[slot, 0:rows, 0:cols], dst[o].at[b], sem.at[slot]))
        going[k].start()
    for cp in going[max(0, len(pieces) - n_slots) :]:
        cp.wait()


def widen(*vs):
    pieces = []
    for i, v in enumerate(vs):
        if len(v.shape) == 3:
            pieces += [(i, k, i, k) for k in range(v.shape[0])]
        else:
            n = v.shape[0]
            step = min(n, max(16, (1 << 18) // v.shape[1] // 16 * 16))
            while n % step:
                step -= 16
            pieces += [(i, slice(r, r + step), i, slice(r, r + step)) for r in range(0, n, step)]
    rows = max(v.shape[1] if len(v.shape) == 3 else min(v.shape[0], 512) for v in vs)
    rows = max([rows] + [a.stop - a.start for _, a, _, _ in pieces if isinstance(a, slice)])
    cols = max(v.shape[-1] for v in vs)
    n_slots = 4
    any_ = pl.BlockSpec(memory_space=pl.ANY)
    return pl.pallas_call(
        functools.partial(widen_body, tuple(pieces), len(vs), n_slots),
        in_specs=[pl.BlockSpec(memory_space=pltpu.VMEM)] * len(vs), out_specs=[any_] * len(vs),
        out_shape=[out(v.shape, F32) for v in vs],
        scratch_shapes=[pltpu.VMEM((n_slots, rows, cols), F32), pltpu.SemaphoreType.DMA((n_slots,))],
        compiler_params=pltpu.CompilerParams(vmem_limit_bytes=34 * 1024 * 1024),
    )(*vs)


def flip(axis, bit):
    size = lax.axis_size(axis)
    return [(i, i ^ bit) for i in range(size)]


def bits_of(axis):
    size = lax.axis_size(axis)
    return [1 << b for b in range(size.bit_length() - 1)]


def other_core(v):
    return lax.ppermute(v, "mdl", flip("mdl", 1))


def add16(a, b):
    return (a.astype(F32) + b.astype(F32)).astype(BF)


def halve(v, axis, bit):
    side = (lax.axis_index(axis) // bit) % 2
    n = v.shape[0] // 2
    keep = lax.dynamic_slice_in_dim(v, side * n, n)
    send = lax.dynamic_slice_in_dim(v, (1 - side) * n, n)
    return add16(keep, lax.ppermute(send, axis, flip(axis, bit)))


def double(v, axis, bit):
    side = (lax.axis_index(axis) // bit) % 2
    got = lax.ppermute(v, axis, flip(axis, bit))
    return jnp.where(side == 0, jnp.concatenate([v, got]), jnp.concatenate([got, v]))


def sum_everywhere(v):
    n = v.shape[0] // 2
    bits = bits_of("grp")
    parts = []
    for part, order in ((v[:n], bits), (v[n:], bits[::-1])):
        for bit in order:
            part = halve(part, "grp", bit)
        parts.append(part)
    size = lax.axis_size("exp")
    joined = jnp.concatenate(parts)
    rows = joined.shape[0] // size
    spread = lax.all_to_all(joined.reshape(size, rows, -1), "exp", 0, 0, tiled=True)
    mine = jnp.sum(spread.astype(F32), axis=0).astype(BF)
    joined = lax.all_gather(mine, "exp", axis=0, tiled=True)
    h = joined.shape[0] // 2
    done = []
    for part, order in ((joined[:h], bits), (joined[h:], bits[::-1])):
        for bit in order[::-1]:
            part = double(part, "grp", bit)
        done.append(part)
    return jnp.concatenate(done)


def small_sum(v):
    for axis in ("mdl", "grp", "exp"):
        for bit in bits_of(axis):
            v = v + lax.ppermute(v, axis, flip(axis, bit))
    return v


def reduce_body(n_in, per, n_exp, experts, *refs):
    mine = refs[:n_in]
    other = refs[n_in : 2 * n_in]
    dg = refs[2 * n_in : 2 * n_in + 4]
    dr_ref, x3_ref, h4_ref, router_ref, col_ref = refs[2 * n_in + 4 : 2 * n_in + 9]
    eouts = refs[2 * n_in + 9 : 2 * n_in + 13]
    image_ref = refs[2 * n_in + 13]
    outs = refs[2 * n_in + 14 :]
    qkv2, proj2, fc_in, fc_out, qkv1, proj1, sum_ref, y_ref, gx_ref = outs[:9]
    (acc, got, r1, r2, zr, zz, zs, sm, y_own, load_sem, m_send, m_recv, x_send, x_recv, z_send, z_recv, s_send, s_recv,
     i_local, i_send, i_recv, e_oth, e_send, e_recv) = outs[9:]
    out_ref = got
    n = n_in * per
    rows = acc.shape[2]
    h, q = rows // 2, rows // 4
    t = q // n_exp
    g = lax.axis_index("grp")
    z = lax.axis_index("exp")
    core = lax.axis_index("mdl")
    bx, by = g % 2, g // 2
    flat = {"x": g + 1 - 2 * bx, "y": g + 2 - 4 * by}
    order = (("x", "y"), ("y", "x"))
    bits = ((bx, by), (by, bx))

    barrier = pltpu.get_barrier_semaphore()
    others = [{"mdl": 1 - core}, {"grp": flat["x"]}, {"grp": flat["y"]}]
    others += [{"exp": (z + o) % n_exp} for o in range(1, n_exp)]
    for dev in others:
        pl.semaphore_signal(barrier, inc=1, device_id=dev, device_id_type=MESH)
    pl.semaphore_wait(barrier, len(others))

    def load(c):
        i, p = c // per, c % per
        return pltpu.make_async_copy(mine[i].at[p], acc.at[c], load_sem.at[c])

    def swap(c):
        i, p = c // per, c % per
        return pltpu.make_async_remote_copy(other[i].at[p], got.at[c], m_send.at[c], m_recv.at[c],
                                            device_id={"mdl": 1 - core}, device_id_type=MESH)

    for c in range(n):
        swap(c).start()
        load(c).start()

    own_img = image_ref.shape[0]
    places = pl.ds(core * own_img, own_img)

    def image_copies(k, src, dst):
        return (pltpu.make_async_copy(src, dst.at[places], i_local.at[k]),
                pltpu.make_async_remote_copy(src, dst.at[places], i_send.at[k], i_recv.at[k], device_id={"mdl": 1 - core},
                                             device_id_type=MESH))

    def image_come(k, src, dst):
        there = pl.ds((1 - core) * own_img, own_img)
        return pltpu.make_async_remote_copy(src, dst.at[there], i_send.at[k], i_recv.at[k], device_id={"mdl": 1 - core},
                                            device_id_type=MESH)

    for cp in image_copies(0, image_ref, gx_ref):
        cp.start()

    e_copies = [pltpu.make_async_remote_copy(eouts[j], e_oth.at[j], e_send.at[j], e_recv.at[j], device_id={"mdl": 1 - core},
                                             device_id_type=MESH) for j in range(n_exp)]
    for cp in e_copies:
        cp.start()

    def swap_at(c):
        return pltpu.make_async_remote_copy(other[0].at[0], got.at[c], m_send.at[c], m_recv.at[c],
                                            device_id={"mdl": 1 - core}, device_id_type=MESH)

    def load_at(c):
        return pltpu.make_async_copy(mine[0].at[0], acc.at[c], load_sem.at[c])

    def over(u, leg, src, dst, slot, c):
        return pltpu.make_async_remote_copy(src, dst, x_send.at[slot, u, c], x_recv.at[slot, u, c],
                                            device_id={"grp": flat[order[u][leg]]}, device_id_type=MESH)

    def first(u, c):
        return over(u, 0, acc.at[c, u, pl.ds(pl.multiple_of((1 - bits[u][0]) * h, h), h)], r1.at[c, u], 0, c)

    def second(u, c):
        return over(u, 1, r1.at[c, u, pl.ds(pl.multiple_of((1 - bits[u][1]) * q, q), q)], r2.at[c, u], 1, c)

    def along(u, c, o):
        return pltpu.make_async_remote_copy(
            r2.at[c, u, pl.ds(pl.multiple_of(((z + o) % n_exp) * t, t), t)], zr.at[c, u, o - 1],
            z_send.at[0, u, o - 1, c], z_recv.at[0, u, o - 1, c],
            device_id={"exp": (z + o) % n_exp}, device_id_type=MESH)

    def place(u):
        return bits[u][0] * h + bits[u][1] * q

    def back(u, c, o):
        here = out_ref.at[c, u, pl.ds(pl.multiple_of(place(u) + z * t, t), t)]
        return pltpu.make_async_remote_copy(here, here, z_send.at[1, u, o - 1, c], z_recv.at[1, u, o - 1, c],
                                            device_id={"exp": (z + o) % n_exp}, device_id_type=MESH)

    def third(u, c):
        here = out_ref.at[c, u, pl.ds(pl.multiple_of(place(u), q), q)]
        return over(u, 1, here, here, 2, c)

    def fourth(u, c):
        here = out_ref.at[c, u, pl.ds(pl.multiple_of(bits[u][0] * h, h), h)]
        return over(u, 0, here, here, 3, c)

    def plus(a, b):
        return (a.astype(F32) + b.astype(F32)).astype(BF)

    def s1(c):
        load_at(c).wait()
        swap_at(c).wait_recv()
        for u in range(2):
            acc[c, u] = plus(acc[c, u], got[c, u])
            first(u, c).start()

    def s2(c):
        for u in range(2):
            first(u, c).wait_recv()
            keep = acc[c, u, pl.ds(pl.multiple_of(bits[u][0] * h, h), h)]
            r1[c, u] = plus(keep, r1[c, u])
            second(u, c).start()

    def s3(c):
        for u in range(2):
            second(u, c).wait_recv()
            keep = r1[c, u, pl.ds(pl.multiple_of(bits[u][1] * q, q), q)]
            r2[c, u] = plus(keep, r2[c, u])
            for o in range(1, n_exp):
                along(u, c, o).start()

    def s4(c):
        for u in range(2):
            total = r2[c, u, pl.ds(pl.multiple_of(z * t, t), t)].astype(F32)
            for o in range(1, n_exp):
                along(u, c, o).wait_recv()
                total = total + zr[c, u, o - 1].astype(F32)
            out_ref[c, u, pl.ds(pl.multiple_of(place(u) + z * t, t), t)] = total.astype(BF)
            for o in range(1, n_exp):
                back(u, c, o).start()

    def s5(c):
        for u in range(2):
            for o in range(1, n_exp):
                back(u, c, o).wait_recv()
            third(u, c).start()

    def s6(c):
        for u in range(2):
            third(u, c).wait_recv()
            fourth(u, c).start()

    def s7(c):
        for u in range(2):
            fourth(u, c).wait_recv()
        for k in range(n):

            @pl.when(c == k)
            def _(k=k):
                natural(k)

    zc = 0
    e, e2, e4 = rows // n_exp, rows // n_exp // 2, rows // n_exp // 4

    def z_out(u, o):
        return pltpu.make_async_remote_copy(
            acc.at[zc, u, pl.ds(pl.multiple_of(((z + o) % n_exp) * e, e), e)], zz.at[u, o - 1],
            z_send.at[0, u, o - 1, zc], z_recv.at[0, u, o - 1, zc], device_id={"exp": (z + o) % n_exp}, device_id_type=MESH)

    def z_first(u):
        return over(u, 0, zs.at[u, pl.ds(pl.multiple_of((1 - bits[u][0]) * e2, e2), e2)], r1.at[zc, u, 0:e2], 0, zc)

    def z_second(u):
        return over(u, 1, r1.at[zc, u, pl.ds(pl.multiple_of((1 - bits[u][1]) * e4, e4), e4)], r2.at[zc, u, 0:e4], 1, zc)

    def z_third(u):
        here = out_ref.at[zc, u, pl.ds(pl.multiple_of(z * e + bits[u][0] * e2 + bits[u][1] * e4, e4), e4)]
        return over(u, 1, here, here, 2, zc)

    def z_fourth(u):
        here = out_ref.at[zc, u, pl.ds(pl.multiple_of(z * e + bits[u][0] * e2, e2), e2)]
        return over(u, 0, here, here, 3, zc)

    def z_back(u, o):
        here = out_ref.at[zc, u, pl.ds(pl.multiple_of(z * e, e), e)]
        return pltpu.make_async_remote_copy(here, here, z_send.at[1, u, o - 1, zc], z_recv.at[1, u, o - 1, zc],
                                            device_id={"exp": (z + o) % n_exp}, device_id_type=MESH)

    def z1():
        load_at(zc).wait()
        swap_at(zc).wait_recv()
        for u in range(2):
            acc[zc, u] = plus(acc[zc, u], got[zc, u])
            for o in range(1, n_exp):
                z_out(u, o).start()

    def z2():
        for u in range(2):
            total = acc[zc, u, pl.ds(pl.multiple_of(z * e, e), e)].astype(F32)
            for o in range(1, n_exp):
                z_out(u, o).wait_recv()
                total = total + zz[u, o - 1].astype(F32)
            zs[u] = total.astype(BF)
            z_first(u).start()

    def z3():
        for u in range(2):
            z_first(u).wait_recv()
            r1[zc, u, 0:e2] = plus(zs[u, pl.ds(pl.multiple_of(bits[u][0] * e2, e2), e2)], r1[zc, u, 0:e2])
            z_second(u).start()

    def z4():
        for u in range(2):
            z_second(u).wait_recv()
            mine_rows = pl.ds(pl.multiple_of(z * e + bits[u][0] * e2 + bits[u][1] * e4, e4), e4)
            out_ref[zc, u, mine_rows] = plus(r1[zc, u, pl.ds(pl.multiple_of(bits[u][1] * e4, e4), e4)], r2[zc, u, 0:e4])
            z_third(u).start()

    def z5():
        for u in range(2):
            z_third(u).wait_recv()
            z_fourth(u).start()

    def z6():
        for u in range(2):
            z_fourth(u).wait_recv()
            for o in range(1, n_exp):
                z_back(u, o).start()

    def z7():
        for u in range(2):
            for o in range(1, n_exp):
                z_back(u, o).wait_recv()
        natural(zc)

    def drain(c, _):
        swap_at(c).wait_send()
        for u in range(2):
            for make in (first, second, third, fourth):
                make(u, c).wait_send()
            for o in range(1, n_exp):
                along(u, c, o).wait_send()
                back(u, c, o).wait_send()
        return 0

    legs = [({"mdl": 1 - core}), ({"grp": flat["x"]}), ({"grp": flat["y"]})]
    base = 2 * len(legs) + 1

    def small_leg(i):
        return pltpu.make_async_remote_copy(sm.at[2 * i], sm.at[2 * i + 1], s_send.at[i], s_recv.at[i], device_id=legs[i],
                                            device_id_type=MESH)

    def small_along(o):
        return pltpu.make_async_remote_copy(sm.at[base - 1], sm.at[base + z], s_send.at[len(legs) + o - 1],
                                            s_recv.at[len(legs) + o - 1], device_id={"exp": (z + o) % n_exp},
                                            device_id_type=MESH)

    def small_step(i):
        if i == 0:
            sm[0] = jnp.zeros(sm.shape[1:], F32)
            for k in range(4):
                sm[0, k : k + 1, :] = dg[k][...]
            sm[0, 4 : 4 + experts, :] = dr_ref[:experts, :]
        else:
            small_leg(i - 1).wait()
            sm[2 * i] = sm[2 * i - 2] + sm[2 * i - 1]
        if i < len(legs):
            small_leg(i).start()
        else:
            sm[pl.ds(base + z, 1)] = sm[pl.ds(base - 1, 1)]
            for o in range(1, n_exp):
                small_along(o).start()

    def natural(c):
        i, p = c // per, c % per
        wide = out_ref.shape[3]
        piece = wide // 3
        for u in range(2):
            for r0 in range(0, rows, piece):
                at = (2 * p + u) * rows + r0
                value = out_ref[c, u, r0 : r0 + piece]
                if i in (0, 3):
                    qkv, proj = (qkv2, proj2) if i == 0 else (qkv1, proj1)
                    if at < 6 * wide:
                        k, at = divmod(at, 2 * wide)
                        qkv[k, at : at + piece] = value
                    else:
                        k, at = divmod(at - 6 * wide, wide)
                        proj[at : at + piece, k * wide : (k + 1) * wide] = value
                else:
                    to, tall = (fc_in, 2 * wide) if i == 1 else (fc_out, 4 * wide)
                    k, at = divmod(at, tall)
                    to[at : at + piece, k * wide : (k + 1) * wide] = value

    steps = (s1, s2, s3, s4, s5, s6, s7)
    waves = n - 1 + len(steps) - 1
    late = waves - 2
    z_steps = ((0, z1), (2, z2), (3, z3), (4, z4), (5, z5), (6, z6), (late, z7))
    small_steps = {1: 0, 3: 1, 5: 2, 7: 3}

    def wave(tau, _):
        for s, step in enumerate(steps):
            c = tau - s + 1

            @pl.when((c >= 1) & (c < n))
            def _(step=step, c=c):
                step(c)

        for at, step in z_steps:
            pl.when(tau == at)(step)
        for at, i in small_steps.items():
            pl.when(tau == at)(functools.partial(small_step, i))
        return 0

    first_waves = 2
    lax.fori_loop(0, first_waves, wave, 0)
    for cp in e_copies:
        cp.wait_recv()
    blocks = [[(beside(z, j), eouts[j]) for j in range(n_exp)], [(beside(z, j), e_oth.at[j]) for j in range(n_exp)]]
    y = mixture_output(experts, x3_ref, h4_ref, router_ref, col_ref, lambda k: merge_blocks(col_ref, k, blocks, x3_ref.shape[0]))
    for i in range(own_img):
        y_own[i] = y[i * LP : i * LP + L]
    for cp in image_copies(1, y_own, y_ref):
        cp.start()
    lax.fori_loop(first_waves, waves, wave, 0)
    for cp in e_copies:
        cp.wait_send()
    for k, (src, dst) in enumerate(((image_ref, gx_ref), (y_own, y_ref))):
        local, sent = image_copies(k, src, dst)
        local.wait()
        sent.wait_send()
        image_come(k, src, dst).wait_recv()
    lax.fori_loop(1, n, drain, 0)
    swap_at(zc).wait_send()
    for u in range(2):
        for make in (z_first, z_second, z_third, z_fourth):
            make(u).wait_send()
        for o in range(1, n_exp):
            z_out(u, o).wait_send()
            z_back(u, o).wait_send()
    for o in range(1, n_exp):
        small_along(o).wait()
    total = sm[base]
    for k in range(1, n_exp):
        total = total + sm[base + k]
    sum_ref[...] = total


def reduce_all(mine, other, dgs, dr, x3, h4, router, col, eouts, image, n_exp, experts):
    per, _, rows, c = mine[0].shape
    n = len(mine) * per
    d, f = 2 * c, 4 * c
    h, q = rows // 2, rows // 4
    t = q // n_exp
    small = (-(-(4 + experts) // 8) * 8, d)
    n_img, length, _ = image.shape
    D, V = pltpu.SemaphoreType.DMA, pltpu.VMEM
    any_ = pl.BlockSpec(memory_space=pl.ANY)
    vm = pl.BlockSpec(memory_space=pltpu.VMEM)
    return pl.pallas_call(
        functools.partial(reduce_body, len(mine), per, n_exp, experts),
        in_specs=[any_] * (2 * len(mine)) + [vm] * 13 + [any_],
        out_specs=[vm] * 9,
        out_shape=[out((3, d, c), BF), out((c, d), BF), out((d, f), BF), out((f, d), BF), out((3, d, c), BF), out((c, d), BF),
                   out(small, F32), out((2 * n_img, length, d), BF), out((2 * n_img, length, d), BF)],
        scratch_shapes=[
            V((n, 2, rows, c), BF), V((n, 2, rows, c), BF), V((n, 2, h, c), BF), V((n, 2, q, c), BF),
            V((n, 2, n_exp - 1, t, c), BF), V((2, n_exp - 1, rows // n_exp, c), BF), V((2, rows // n_exp, c), BF),
            V((7 + n_exp,) + small, F32), V((n_img, length, d), BF),
            D((n,)), D((n,)), D((n,)), D((4, 2, n)), D((4, 2, n)), D((2, 2, n_exp - 1, n)), D((2, 2, n_exp - 1, n)),
            D((3 + n_exp,)), D((3 + n_exp,)), D((2,)), D((2,)), D((2,)), V((n_exp,) + eouts[0].shape, BF), D((n_exp,)), D((n_exp,)),
        ],
        compiler_params=pltpu.CompilerParams(collective_id=0, has_side_effects=True, vmem_limit_bytes=VMEM_BYTES),
        cost_estimate=pl.CostEstimate(flops=8 * x3.shape[0] * x3.shape[0] * d, bytes_accessed=n * 8 * rows * c, transcendentals=0),
    )(*mine, *other, *dgs, dr, x3, h4, router, col, *eouts, image)


def expert_exchange_body(experts, half, h4_ref, tr_ref, dy0, dy1, dy2, dy3, router_ref, im, io, tm, to,
                         ret_ref, dg_ref, e0, e1, e2, e3, gw_ref,
                         h_oth, part, xo, x, wi, wo, act, dz, wd, acc, dxa, rsend, gscr, ggot, xt, wt,
                         w_sem, swap_sem, x_send, x_recv, r_send, r_recv, f_send, f_recv, g_send, g_recv, g_sem,
                         dgs, l_send, l_recv, k_send, k_recv):
    n, d = h4_ref.shape
    f = im.shape[1]
    t = 256 if f % 256 == 0 else tile_of(f)
    z = lax.axis_index("exp")
    core = lax.axis_index("mdl")
    partner = {"mdl": 1 - core}
    size = experts
    near_first = [1, 3, 2]

    out_grad, eouts = (dy0, dy1, dy2, dy3), (e0, e1, e2, e3)

    def there(j):
        return beside(z, j)

    loads = [pltpu.make_async_copy(src, dst, w_sem.at[k]) for k, (src, dst) in enumerate(
        ((im, wi.at[0]), (io, wi.at[1]), (tm, wo.at[0]), (to, wo.at[1])))]
    for cp in loads:
        cp.start()
    barrier = pltpu.get_barrier_semaphore()
    for dev in [partner] + [{"exp": there(j)} for j in range(1, size)]:
        pl.semaphore_signal(barrier, inc=1, device_id=dev, device_id_type=MESH)
    pl.semaphore_wait(barrier, size)
    swap = pltpu.make_async_remote_copy(h4_ref, h_oth, swap_sem.at[0], swap_sem.at[1], device_id=partner, device_id_type=MESH)
    swap.start()

    own_img = n // LP
    base = core * size * half

    def spread(side, v, j):
        total = None
        for i in range(own_img):
            p = nn(slot_hots(tr_ref[side * own_img + i], base + there(j) * half, half), v[i * LP : (i + 1) * LP, :])
            total = p if total is None else total + p
        return total

    def rows(j):
        return slice(j * half, (j + 1) * half)

    def place(e):
        return pl.ds(pl.multiple_of(e * half, half), half)

    for j in near_first + [0]:
        part[rows(j), :] = spread(core, h4_ref, j)
    swap.wait_recv()
    sends = {}
    for j in near_first + [0]:
        block = (part[rows(j), :] + spread(1 - core, h_oth, j)).astype(BF)
        if j == 0:
            x[rows(0), :] = block
        else:
            xo[rows(j), :] = block
            sends[j] = pltpu.make_async_remote_copy(xo.at[rows(j)], x.at[rows(j)], x_send.at[j], x_recv.at[j],
                                                    device_id={"exp": there(j)}, device_id_type=MESH)
            sends[j].start()

    returns, forwards = {}, {}

    def forward(j):
        here = ret_ref.at[0, place(there(j))]
        forwards[j] = (
            pltpu.make_async_remote_copy(here, ret_ref.at[1, place(there(j))], f_send.at[j], f_recv.at[j],
                                         device_id=partner, device_id_type=MESH),
            pltpu.make_async_remote_copy(dg_ref.at[0, there(j)], dg_ref.at[1, there(j)], k_send.at[j], k_recv.at[j],
                                         device_id=partner, device_id_type=MESH))
        for cp in forwards[j]:
            cp.start()

    def run(blocks):
        r0, r1 = blocks[0] * half, (blocks[-1] + 1) * half
        m = r1 - r0
        for j in blocks:
            probs, lane = router_probs(x[rows(j), :], router_ref[...], experts)
            gate = jnp.sum(jnp.where(lane == z, probs, 0.0), axis=-1, keepdims=True)
            wd[rows(j), :] = (gate * out_grad[j][...].astype(F32)).astype(BF)
        acc[0:m, :] = jnp.zeros((m, d), F32)
        dxa[0:m, :] = jnp.zeros((m, d), F32)

        def tile(i, _):
            at = pl.ds(pl.multiple_of(i * t, t), t)
            for side in range(2):
                a, s = gelu_parts(nn(x[r0:r1, :], wi[side, :, at]))
                a = a.astype(BF)
                act[side, r0:r1, at] = a
                acc[0:m, :] += nn(a, wo[side, at, :])
                g = (nt(wd[r0:r1, :], wo[side, at, :]) * s).astype(BF)
                dz[side, r0:r1, at] = g
                dxa[0:m, :] += nt(g, wi[side, :, at])
            return 0

        lax.fori_loop(0, f // t, tile, 0)
        for b, j in enumerate(blocks):
            here = slice(b * half, (b + 1) * half)
            e_rows = acc[here, :].astype(BF)
            eouts[j][...] = e_rows
            dgate = jnp.sum(out_grad[j][...].astype(F32) * e_rows.astype(F32), axis=-1, keepdims=True)
            lines = gate_lines(dgate)
            if j == 0:
                ret_ref[0, place(z), :] = dxa[here, :].astype(BF)
                dg_ref[0, pl.ds(z, 1)] = lines[None]
                forward(0)
            else:
                rsend[rows(j), :] = dxa[here, :].astype(BF)
                dgs[j] = lines
                returns[j] = (
                    pltpu.make_async_remote_copy(rsend.at[rows(j)], ret_ref.at[0, place(z)], r_send.at[j], r_recv.at[j],
                                                 device_id={"exp": there(j)}, device_id_type=MESH),
                    pltpu.make_async_remote_copy(dgs.at[j], dg_ref.at[0, z], l_send.at[j], l_recv.at[j],
                                                 device_id={"exp": there(j)}, device_id_type=MESH))
                for cp in returns[j]:
                    cp.start()

    for cp in loads:
        cp.wait()
    sends[1].wait_recv()
    run([0, 1])
    for j in near_first[1:]:
        sends[j].wait_recv()
        run([j])

    xt[...] = x[...].T
    wt[...] = wd[...].T

    tiles = f // t

    def cols(i):
        return pl.ds(pl.multiple_of(i * t, t), t)

    def swapped(i):
        return pltpu.make_async_remote_copy(gscr.at[1, :, :, cols(i)], ggot.at[:, :, cols(i)], g_send.at[i], g_recv.at[i],
                                            device_id=partner, device_id_type=MESH)

    def stored(i):
        return pltpu.make_async_copy(gscr.at[0, :, :, cols(i)], gw_ref.at[:, :, cols(i)], g_sem.at[i])

    def weight_tile(i, _):
        for side in (1, 0):
            gscr[side, 0, :, cols(i)] = nn(xt[...], dz[side, :, cols(i)]).astype(BF)
            gscr[side, 1, :, cols(i)] = nn(wt[...], act[side, :, cols(i)]).astype(BF)
            if side == 1:
                swapped(i).start()
        return 0

    lax.fori_loop(0, tiles, weight_tile, 0)

    def sum_tile(i, _):
        swapped(i).wait_recv()
        for k in range(2):
            gscr[0, k, :, cols(i)] = (gscr[0, k, :, cols(i)].astype(F32) + ggot[k, :, cols(i)].astype(F32)).astype(BF)
        stored(i).start()
        return 0

    lax.fori_loop(0, tiles, sum_tile, 0)

    for j in near_first:
        pltpu.make_async_remote_copy(rsend.at[rows(j)], ret_ref.at[0, place(there(j))], r_send.at[j], r_recv.at[j],
                                     device_id={"exp": there(j)}, device_id_type=MESH).wait_recv()
        pltpu.make_async_remote_copy(dgs.at[j], dg_ref.at[0, there(j)], l_send.at[j], l_recv.at[j],
                                     device_id={"exp": there(j)}, device_id_type=MESH).wait_recv()
        forward(j)

    def drain(i, _):
        stored(i).wait()
        swapped(i).wait_send()
        return 0

    lax.fori_loop(0, tiles, drain, 0)
    swap.wait_send()
    for j in range(size):
        if j:
            sends[j].wait_send()
            for cp in returns[j]:
                cp.wait_send()
        for cp in forwards[j]:
            cp.wait()


def expert_exchange(h4, tr, dys, router, im, io, tm, to, experts, half):
    n, d = h4.shape
    f = im.shape[1]
    s = experts * half
    wide = -(-half // LANES) * LANES
    tiles = f // (256 if f % 256 == 0 else tile_of(f))
    D, V = pltpu.SemaphoreType.DMA, pltpu.VMEM
    any_ = pl.BlockSpec(memory_space=pl.ANY)
    vm = pl.BlockSpec(memory_space=pltpu.VMEM)
    return pl.pallas_call(
        functools.partial(expert_exchange_body, experts, half),
        in_specs=[vm] * 7 + [any_] * 4,
        out_specs=[vm] * 6 + [any_],
        out_shape=[out((2, s, d), BF), out((2, experts, 8, wide), F32)] + [out((half, d), BF)] * 4 + [out((2, d, f), BF)],
        scratch_shapes=[
            V((n, d), BF), V((s, d), F32), V((s, d), BF), V((s, d), BF), V((2, d, f), BF), V((2, f, d), BF),
            V((2, s, f), BF), V((2, s, f), BF), V((s, d), BF), V((2 * half, d), F32), V((2 * half, d), F32),
            V((s, d), BF), V((2, 2, d, f), BF), V((2, d, f), BF), V((d, s), BF), V((d, s), BF),
            D((4,)), D((2,)), D((experts,)), D((experts,)), D((experts,)), D((experts,)), D((experts,)), D((experts,)),
            D((tiles,)), D((tiles,)), D((tiles,)),
            V((experts, 8, wide), F32), D((experts,)), D((experts,)), D((experts,)), D((experts,)),
        ],
        compiler_params=pltpu.CompilerParams(collective_id=1, has_side_effects=True, vmem_limit_bytes=VMEM_BYTES),
        cost_estimate=pl.CostEstimate(flops=24 * s * d * f, bytes_accessed=20 * d * f, transcendentals=0),
    )(h4, tr, *dys, router, im, io, tm, to)


FUSED = True
PER = 3


def on_device(images, counts, routes, priority, gain_one, qkv_one, out_one, gain_two, fc_in, fc_out, gain_three,
              qkv_two, out_two, gain_four, router, expert_in, expert_out, cotangent):
    n_slot, length, d = images.shape
    experts = router.shape[1]
    n_mdl = lax.axis_size("mdl")
    peers = lax.axis_size("exp")
    capacity = (25 * L * TOPK + 8 * experts - 1) // (8 * experts)
    half = -(-(-(-capacity // n_mdl)) // 16) * 16
    slots = experts * half
    own_img = n_slot // n_mdl
    f = fc_in.shape[1]
    c = qkv_one.shape[2]
    rows = own_img * LP
    core = lax.axis_index("mdl")
    per = PER
    unit = 4 * d // (2 * per)
    fused = FUSED and (lax.axis_size("grp"), peers, n_mdl) == (4, experts, 2) and peers == 4
    fused = fused and d == 2 * c and f == 4 * c and unit % (64 * peers) == 0 and c % 48 == 0

    def padded(v):
        return jnp.pad(v, ((0, 0), (0, LP - length), (0, 0))).reshape(n_slot * LP, -1)

    qm1, om1, im, tm, qm2, om2, em, fm = halves = (
        qkv_one, out_one, fc_in, fc_out, qkv_two, out_two, expert_in[0], expert_out[0])
    blocks = [(half, d)] * peers if fused else [(slots, d)]
    routing_args = (counts, jnp.transpose(routes, (0, 2, 1)), priority, router.T, gain_one, gain_two, gain_three, gain_four, cotangent)
    slot_rows, col, router_rows, gains, *dy_out = call(
        functools.partial(routing_body, experts, capacity, half),
        [out((n_slot, 8, LQ), I32), out((rows, 8), I32), out((LANES, d), BF), out((4, d), F32)] + [out(b, BF) for b in blocks], *routing_args,
        in_specs=[pl.BlockSpec(memory_space=pltpu.SMEM)] + [whole(v.shape) for v in routing_args[1:]],
        scratch=[pltpu.VMEM((n_slot * LP, d), BF), pltpu.VMEM((n_slot, 8, LQ), I32), pltpu.VMEM((8, LQ), I32)],
        flops=4 * slots * n_slot * LP * d,
    )
    def exchange(v):
        shaped = v.reshape(peers, v.shape[0] // peers, v.shape[1])
        return lax.all_to_all(shaped, "exp", 0, 0, tiled=True).reshape(v.shape)

    if fused:
        got, (qo1, oo1, io, to, qo2, oo2, eo, fo), dy_in = forward(images, gains, halves, dy_out[1:], rows)
        x1, *kept1, x2, h2, act2, slope2, x3 = got[:10]
        kept3, h4, x0 = got[10:14], got[14], got[15]
        dy_in = [dy_out[0], *dy_in]
    else:
        x0 = padded(images)
        qo1, oo1, io, to, qo2, oo2, eo, fo = (other_core(w) for w in halves)
        dy_in = exchange(dy_out[0])
        x1, *kept1 = attention_forward(x0, rows, gains, 0, qm1, qo1, om1, oo1)
        x2, h2, act2, slope2 = mlp_forward(x1, gains, 1, im, io, tm, to)
        x3, *kept3, h4 = attention_forward(x2, rows, gains, 2, qm2, qo2, om2, oo2, tail=3)

    if fused:
        ret, dgate, *eout, ge = expert_exchange(h4, slot_rows, dy_in, router_rows, em, eo, fm, fo, experts, half)
        (dg1, dg2, dg3, dg4, dr, image), grads, eback = backward(
            experts, half, x3, h4, router_rows, cotangent, col, ret, dgate, gains, x2, kept3, (qm2, qo2, om2, oo2),
            x1, h2, act2, slope2, (im, io, tm, to), x0, kept1, (qm1, qo1, om1, oo1), eout[1:])
        a2_mine, a2_other, gim, gio, gtm, gto, a1_mine, a1_other = grads
        eback = [eout[0], *eback]
    else:
        [h4_out] = call(functools.partial(dispatch_body, experts, half), [out((slots, d), BF)], slot_rows, h4, other_core(h4))
        h4_in = exchange(h4_out)
        eout, ret, eact, edz, ewd = expert_forward_backward(h4_in, dy_in, router_rows, em, eo, fm, fo, experts)
        ret, eout = exchange(ret), exchange(eout)
        ret, eback = jnp.stack([ret, other_core(ret)]), jnp.stack([eout, other_core(eout)])
        dgate = ret[:, :, d].astype(F32) + ret[:, :, d + LANES // 2].astype(F32)
        wide = -(-half // LANES) * LANES
        dgate = jnp.pad(dgate.reshape(2, experts, 1, half), ((0, 0), (0, 0), (0, 7), (0, wide - half)))
        ret = ret[:, :, :d]
        ge_mine, ge_other = expert_weights(h4_in, ewd, eact, edz)
        ge = add16(ge_mine, other_core(ge_other))
        dx2, dg3, dg4, dr, a2_mine, a2_other = mixture_attention_backward(
            experts, half, x3, h4, router_rows, cotangent, col, ret, dgate, x2, gains, kept3, qm2, qo2, om2, oo2)
        dx1, dg2, gim, gio, gtm, gto = mlp_backward(dx2, x1, gains, 1, h2, act2, slope2, im, io, tm, to, c)
        image, dg1, a1_mine, a1_other = attention_backward(dx1, x0, gains, 0, kept1, qm1, qo1, om1, oo1)
    expert_sum = lax.psum_scatter(ge, "grp", scatter_dimension=1, tiled=True)

    mines, others = (a2_mine, gim, gtm, a1_mine), (a2_other, gio, gto, a1_other)

    if fused:
        split = [[v.reshape(per, 2, unit, c) for v in side] for side in (mines, others)]
        qkv2, proj2, fi, fo_, qkv1, proj1, small, output, grad_images = reduce_all(
            *split, (dg1, dg2, dg3, dg4), dr, x3, h4, router_rows, col, eback, image, peers, experts)
    else:
        sums = [sum_everywhere(add16(a.reshape(4 * d, c), other_core(b.reshape(4 * d, c)))) for a, b in zip(mines, others)]
        small = small_sum(jnp.concatenate([dg1, dg2, dg3, dg4, dr[:experts]], axis=0))

        def panels(v):
            return jnp.concatenate([v[i] for i in range(v.shape[0])], axis=1)

        (qkv2, proj2), (qkv1, proj1) = (
            (v[: 3 * d].reshape(3, d, c), panels(v[3 * d :].reshape(d // c, c, c))) for v in (sums[0], sums[3]))
        fi, fo_ = panels(sums[1].reshape(f // c, d, c)), panels(sums[2].reshape(d // c, f, c))
        [own_out] = call(
            functools.partial(mixture_output_body, experts), [out((own_img, L, d), BF)], x3, h4, router_rows, col, eback,
            flops=8 * rows * slots * d)

        def both(v):
            there = other_core(v)
            return jnp.where(core == 0, jnp.concatenate([v, there]), jnp.concatenate([there, v]))

        output, grad_images = both(own_out), both(image)
    shared = [v.reshape(v.shape[-2:]) for v in (expert_sum[0], expert_sum[1])]
    wide = widen(qkv1, proj1, fi, fo_, qkv2, proj2, *shared)
    return (
        output, grad_images,
        small[0], wide[0], wide[1], small[1], wide[2], wide[3],
        small[2], wide[4], wide[5], small[3], small[4 : 4 + experts].T,
        wide[6][None], wide[7].T[None],
    )


def solution(mesh):
    token = P(("grp", "exp"), None, None)
    column, line = P(None, None, "mdl"), P("mdl", None)
    return jax.shard_map(
        on_device,
        mesh=mesh,
        in_specs=(token, P("grp", "exp"), token, P(("grp", "exp"), None), P(), column, line, P(), P(None, "mdl"), line,
                  P(), column, line, P(), P(), P("exp", None, "mdl"), P("exp", "mdl", None), token),
        out_specs=(token, token, P(), column, line, P(), P(None, "mdl"), line, P(), column, line, P(), P(),
                   P("exp", "grp", "mdl"), P("exp", "mdl", "grp")),
        check_vma=False,
    )
```

```python
import functools
import math

import jax
import jax.numpy as jnp
from jax import lax
from jax.experimental import pallas as pl
from jax.experimental.pallas import tpu as pltpu
from jax.sharding import PartitionSpec as P

HDIM = 64
L = 197
TOPK = 2
LP = (L + 15) // 16 * 16
LANES = 128
LQ = (L + LANES - 1) // LANES * LANES
BF = jnp.bfloat16
F32 = jnp.float32
I32 = jnp.int32

EPSILON = 1e-06
ROOT_HALF = 0.7071067811865476
DENSITY_FACTOR = 0.3989422804014327
VMEM_BYTES = 60 * 1024 * 1024
MESH = pl.DeviceIdType.MESH


def nn(a, b):
    return lax.dot_general(a, b, (((1,), (0,)), ((), ())), preferred_element_type=F32)


def nt(a, b):
    return lax.dot_general(a, b, (((1,), (1,)), ((), ())), preferred_element_type=F32)


def tn(a, b):
    return lax.dot_general(a, b, (((0,), (0,)), ((), ())), preferred_element_type=F32)


def norm_forward(v, w):
    c = v - jnp.mean(v, axis=-1, keepdims=True)
    r = lax.rsqrt(jnp.mean(c * c, axis=-1, keepdims=True) + EPSILON)
    n = c * r
    return n, r, (n * w).astype(BF)


def norm_backward(n, r, w, dh):
    dn = dh * w
    dw = jnp.sum(dh * n, axis=0, keepdims=True)
    dv = r * (dn - jnp.mean(dn, axis=-1, keepdims=True) - n * jnp.mean(dn * n, axis=-1, keepdims=True))
    return dv, dw


def whole(shape):
    return pl.BlockSpec(shape, lambda *i: (0,) * len(shape))


def call(body, out_shape, *args, grid=(), in_specs=None, out_specs=None, scratch=(), flops=0):
    if in_specs is None:
        in_specs = [whole(a.shape) for a in args]
    if out_specs is None:
        out_specs = [whole(o.shape) for o in out_shape]
    moved = sum(math.prod(a.shape) * a.dtype.itemsize for a in args)
    moved += sum(math.prod(o.shape) * jnp.dtype(o.dtype).itemsize for o in out_shape)
    return pl.pallas_call(
        body,
        grid=grid,
        in_specs=in_specs,
        out_specs=out_specs,
        out_shape=out_shape,
        scratch_shapes=list(scratch),
        cost_estimate=pl.CostEstimate(flops=int(flops), bytes_accessed=int(moved), transcendentals=0),
        compiler_params=pltpu.CompilerParams(vmem_limit_bytes=VMEM_BYTES),
    )(*args)


def out(shape, dtype):
    return jax.ShapeDtypeStruct(shape, dtype)


def head_mask(dtype):
    lane = lax.broadcasted_iota(I32, (LP, LANES), 1)
    return (lane < HDIM).astype(dtype)


def beside(z, j):
    b0, b1 = z % 2, z // 2
    if j & 1:
        b0 = 1 - b0
    if j & 2:
        b1 = 1 - b1
    return b0 + 2 * b1


def fill_rows(ref, at, images, first, count):
    for i in range(count):
        ref[at + i * LP : at + i * LP + L, :] = images[first + i].astype(ref.dtype)
        ref[at + i * LP + L : at + (i + 1) * LP, :] = jnp.zeros((LP - L, ref.shape[1]), ref.dtype)


def own_rows(ref, n):
    if ref.shape[0] == n:
        return ref[...]
    return ref[pl.ds(pl.multiple_of(lax.axis_index("mdl") * n, 16), n), :]


def attend(img, pair, d, qkv_ref, p_ref, o_ref):
    mask = head_mask(BF)
    key_ok = lax.broadcasted_iota(I32, (LP, LP), 1) < L
    rows = pl.ds(pl.multiple_of(img * LP, LP), LP)
    col = pair * LANES
    q = qkv_ref[rows, pl.ds(pl.multiple_of(col, LANES), LANES)]
    ke = qkv_ref[rows, pl.ds(pl.multiple_of(d + col, LANES), LANES)]
    u = qkv_ref[rows, pl.ds(pl.multiple_of(2 * d + col, LANES), LANES)]
    o = jnp.zeros((LP, LANES), F32)
    for hh in range(2):
        mk = mask if hh == 0 else 1 - mask
        s = nt(q * mk, ke) * HDIM ** (-0.5)
        s = jnp.where(key_ok, s, -1e30)
        e = jnp.exp(s - jnp.max(s, axis=-1, keepdims=True))
        p = (e / jnp.sum(e, axis=-1, keepdims=True)).astype(BF)
        p_ref[2 * (img * (d // LANES) + pair) + hh] = p
        o = o + nn(p, u * mk)
    o_ref[rows, pl.ds(pl.multiple_of(col, LANES), LANES)] = o.astype(BF)
    return 0


def attention_forward_body(n_img, g_at, tail, *refs):
    refs = list(refs)
    x_ref, g_ref, qm, qo, om, oo = refs[:6]
    del refs[:6]
    y_ref, h_ref, qkv_ref, p_ref, o_ref = refs[:5]
    del refs[:5]
    h4_ref = refs.pop(0) if tail is not None else None
    rows_all = n_img * LP
    d = x_ref.shape[1]
    c = qm.shape[2]
    pairs = d // LANES
    _, _, h = norm_forward(own_rows(x_ref, rows_all).astype(F32), g_ref[g_at : g_at + 1, :])
    h_ref[...] = h
    for k in range(3):
        for side, w in ((0, qm), (1, qo)):
            at = (2 * k + side) * c
            qkv_ref[:, at : at + c] = nn(h_ref[...], w[k]).astype(BF)
    lax.fori_loop(0, n_img * pairs, lambda i, _: attend(i // pairs, i % pairs, d, qkv_ref, p_ref, o_ref), 0, unroll=2)
    y = own_rows(x_ref, rows_all).astype(F32) + nn(o_ref[:, :c], om[...]) + nn(o_ref[:, c:], oo[...])
    y_ref[...] = y
    if tail is not None:
        _, _, h4 = norm_forward(y, g_ref[tail : tail + 1, :])
        h4_ref[...] = h4


def attention_forward(x, r, gains, g_at, qm, qo, om, oo, tail=None):
    d = x.shape[1]
    n_img = r // LP
    heads = d // HDIM
    shapes = [out((r, d), F32), out((r, d), BF), out((r, 3 * d), BF), out((n_img * heads, LP, LP), BF), out((r, d), BF)]
    if tail is not None:
        shapes.append(out((r, d), BF))
    return call(functools.partial(attention_forward_body, n_img, g_at, tail), shapes, x, gains, qm, qo, om, oo,
                flops=2 * r * d * d * 4 + 4 * n_img * heads * LP * LP * LANES)


def attention_backward_core(n_img, dy, x_ref, gain, h_ref, qkv_ref, p_ref, o_ref, qm, qo, om, oo,
                            gm_ref, go_ref, do_ref, dqkv_ref, tr_ref, done=lambda part: None):
    d = x_ref.shape[1]
    c = qm.shape[2]
    pairs = d // LANES
    da = dy().astype(BF)
    tr_ref[...] = o_ref[...].T
    for side, (w, g) in enumerate(((om, gm_ref), (oo, go_ref))):
        gw = nn(tr_ref[side * c : (side + 1) * c, :], da).astype(BF)
        for part in range(d // c):
            g[3 * d + part * c : 3 * d + (part + 1) * c, :] = gw[:, part * c : (part + 1) * c]
        do_ref[:, side * c : (side + 1) * c] = nt(da, w[...]).astype(BF)
    done(3)
    mask = head_mask(BF)

    def one(i, _):
        rows = pl.ds(pl.multiple_of((i // pairs) * LP, LP), LP)
        col = (i % pairs) * LANES
        cq = pl.ds(pl.multiple_of(col, LANES), LANES)
        ck = pl.ds(pl.multiple_of(d + col, LANES), LANES)
        cu = pl.ds(pl.multiple_of(2 * d + col, LANES), LANES)
        q, ke, u, do = qkv_ref[rows, cq], qkv_ref[rows, ck], qkv_ref[rows, cu], do_ref[rows, cq]
        dq = jnp.zeros((LP, LANES), F32)
        dk = jnp.zeros((LP, LANES), F32)
        du = jnp.zeros((LP, LANES), F32)
        for hh in range(2):
            mk = mask if hh == 0 else 1 - mask
            p = p_ref[2 * i + hh]
            du = du + tn(p, do * mk)
            dp = nt(do * mk, u)
            pf = p.astype(F32)
            ds = (pf * (dp - jnp.sum(dp * pf, axis=-1, keepdims=True))).astype(BF)
            dq = dq + nn(ds, ke * mk)
            dk = dk + tn(ds, q * mk)
        dqkv_ref[rows, cq] = (dq * HDIM ** (-0.5)).astype(BF)
        dqkv_ref[rows, ck] = (dk * HDIM ** (-0.5)).astype(BF)
        dqkv_ref[rows, cu] = du.astype(BF)
        return 0

    lax.fori_loop(0, n_img * pairs, one, 0, unroll=2)
    tr_ref[...] = h_ref[...].T
    dh = jnp.zeros((n_img * LP, d), F32)
    for k in range(3):
        for side, (w, g) in enumerate(((qm, gm_ref), (qo, go_ref))):
            at = (2 * k + side) * c
            g[k * d : (k + 1) * d, :] = nn(tr_ref[...], dqkv_ref[:, at : at + c]).astype(BF)
            dh = dh + nt(dqkv_ref[:, at : at + c], w[k])
        done(k)
    n, rr, _ = norm_forward(own_rows(x_ref, n_img * LP).astype(F32), gain)
    dv, dw = norm_backward(n, rr, gain, dh)
    return dy() + dv, dw


def attention_backward_body(n_img, g_at, dy_ref, x_ref, g_ref, h_ref, qkv_ref, p_ref, o_ref, qm, qo, om, oo,
                            dx_ref, dw_ref, gm_ref, go_ref, do_ref, dqkv_ref, tr_ref):
    dx, dw = attention_backward_core(
        n_img, lambda: dy_ref[...], x_ref, g_ref[g_at : g_at + 1, :], h_ref, qkv_ref, p_ref, o_ref, qm, qo, om, oo,
        gm_ref, go_ref, do_ref, dqkv_ref, tr_ref)
    for i in range(n_img):
        dx_ref[i] = dx[i * LP : i * LP + L].astype(BF)
    dw_ref[...] = dw


def attention_backward_scratch(r, d):
    return [pltpu.VMEM((r, d), BF), pltpu.VMEM((r, 3 * d), BF), pltpu.VMEM((d, r), BF)]


def attention_backward(dy, x, gains, g_at, kept, qm, qo, om, oo):
    r, d = dy.shape
    c = qm.shape[2]
    n_img = r // LP
    heads = d // HDIM
    return call(
        functools.partial(attention_backward_body, n_img, g_at),
        [out((n_img, L, d), BF), out((1, d), F32), out((3 * d + d, c), BF), out((3 * d + d, c), BF)],
        dy, x, gains, *kept, qm, qo, om, oo,
        scratch=attention_backward_scratch(r, d),
        flops=4 * r * d * d * 4 + 8 * n_img * heads * LP * LP * LANES,
    )


def gelu_parts(z):
    phi = 0.5 * (1.0 + lax.erf(z * ROOT_HALF))
    return z * phi, phi + z * jnp.exp(-0.5 * z * z) * DENSITY_FACTOR


def tile_of(f):
    for t in (512, 256, 128):
        if f % t == 0:
            return t
    return f


def mlp_forward_body(g_at, x_ref, g_ref, im, io, tm, to, y_ref, h_ref, act_ref, slope_ref, acc_ref):
    step = pl.program_id(0)

    @pl.when(step == 0)
    def _():
        x = x_ref[...]
        _, _, h = norm_forward(x, g_ref[g_at : g_at + 1, :])
        h_ref[...] = h
        acc_ref[...] = x

    for half, (wi, wo) in enumerate(((im, tm), (io, to))):
        a, s = gelu_parts(nn(h_ref[...], wi[...]))
        act = a.astype(BF)
        act_ref[half] = act
        slope_ref[half] = s.astype(BF)
        acc_ref[...] += nn(act, wo[...])

    @pl.when(step == pl.num_programs(0) - 1)
    def _():
        y_ref[...] = acc_ref[...]


def mlp_forward(x, gains, g_at, im, io, tm, to):
    r, d = x.shape
    f = im.shape[1]
    t = tile_of(f)
    col = pl.BlockSpec((d, t), lambda i: (0, i))
    row = pl.BlockSpec((t, d), lambda i: (i, 0))
    hid = pl.BlockSpec((2, r, t), lambda i: (0, 0, i))
    return call(
        functools.partial(mlp_forward_body, g_at),
        [out((r, d), F32), out((r, d), BF), out((2, r, f), BF), out((2, r, f), BF)],
        x, gains, im, io, tm, to, grid=(f // t,),
        in_specs=[whole((r, d)), whole(gains.shape), col, col, row, row],
        out_specs=[whole((r, d)), whole((r, d)), hid, hid],
        scratch=[pltpu.VMEM((r, d), F32)], flops=8 * r * d * f,
    )


def mlp_backward_body(g_at, dy_ref, x_ref, g_ref, h_ref, act_ref, slope_ref, im, io, tm, to,
                      dx_ref, dw_ref, gim, gio, gtm, gto, da_ref, tr_ref, dh_ref):
    step = pl.program_id(0)

    @pl.when(step == 0)
    def _():
        da_ref[...] = dy_ref[...].astype(BF)
        tr_ref[...] = h_ref[...].T
        dh_ref[...] = jnp.zeros_like(dh_ref)

    for half, (wi, wo, gi, go) in enumerate(((im, tm, gim, gtm), (io, to, gio, gto))):
        dact = nt(da_ref[...], wo[...])
        dz = (dact * slope_ref[half].astype(F32)).astype(BF)
        gw = tn(act_ref[half], da_ref[...]).astype(BF)
        t = gw.shape[0]
        for part in range(gw.shape[1] // t):
            go[part] = gw[:, part * t : (part + 1) * t]
        gi[0] = nn(tr_ref[...], dz).astype(BF)
        dh_ref[...] += nt(dz, wi[...])

    @pl.when(step == pl.num_programs(0) - 1)
    def _():
        gain = g_ref[g_at : g_at + 1, :]
        n, rr, _ = norm_forward(x_ref[...], gain)
        dv, dw = norm_backward(n, rr, gain, dh_ref[...])
        dx_ref[...] = dy_ref[...] + dv
        dw_ref[...] = dw


def mlp_backward(dy, x, gains, g_at, h, act, slope, im, io, tm, to, t):
    r, d = x.shape
    f = im.shape[1]
    col = pl.BlockSpec((d, t), lambda i: (0, i))
    row = pl.BlockSpec((t, d), lambda i: (i, 0))
    hid = pl.BlockSpec((2, r, t), lambda i: (0, 0, i))
    gin = pl.BlockSpec((1, d, t), lambda i: (i, 0, 0))
    gout = pl.BlockSpec((d // t, t, t), lambda i: (0, i, 0))
    return call(
        functools.partial(mlp_backward_body, g_at),
        [out((r, d), F32), out((1, d), F32), out((f // t, d, t), BF), out((f // t, d, t), BF),
         out((d // t, f, t), BF), out((d // t, f, t), BF)],
        dy, x, gains, h, act, slope, im, io, tm, to, grid=(f // t,),
        in_specs=[whole((r, d)), whole((r, d)), whole(gains.shape), whole((r, d)), hid, hid, col, col, row, row],
        out_specs=[whole((r, d)), whole((1, d)), gin, gin, gout, gout],
        scratch=[pltpu.VMEM((r, d), BF), pltpu.VMEM((d, r), BF), pltpu.VMEM((r, d), F32)], flops=16 * r * d * f,
    )


def forward_body(n_img, size, *refs):
    refs = list(refs)

    def take(n):
        r = refs[:n]
        del refs[:n]
        return r

    images, g_ref = take(2)
    own_w = take(8)
    dy_out = take(size - 1)
    results = take(16)
    other_w = take(8)
    dy_in = take(size - 1)
    weights = take(6)
    held = take(16)
    load_sem, w_send, w_recv, o_sem, r_sem, d_send, d_recv = refs
    x1, h1, qkv1, p1, o1, x2, h2, act, slope, x3, h3, qkv3, p3, o3, h4, x0 = held
    q1, w1, fi, fo, q3, w3 = weights
    r = n_img * LP
    d = x0.shape[1]
    c = q1.shape[3]
    f = fi.shape[2]
    z = lax.axis_index("exp")
    partner = {"mdl": 1 - lax.axis_index("mdl")}

    loads = [pltpu.make_async_copy(own_w[k], weights[k].at[0], load_sem.at[k]) for k in range(6)]
    for cp in loads:
        cp.start()
    barrier = pltpu.get_barrier_semaphore()
    for dev in [partner] + [{"exp": beside(z, j)} for j in range(1, size)]:
        pl.semaphore_signal(barrier, inc=1, device_id=dev, device_id_type=MESH)
    pl.semaphore_wait(barrier, size)
    swaps = [pltpu.make_async_remote_copy(own_w[k], weights[k].at[1] if k < 6 else other_w[k], w_send.at[k], w_recv.at[k],
                                          device_id=partner, device_id_type=MESH) for k in range(8)]
    for cp in swaps[0:2]:
        cp.start()
    blocks = [pltpu.make_async_remote_copy(dy_out[j - 1], dy_in[j - 1], d_send.at[j - 1], d_recv.at[j - 1],
                                           device_id={"exp": beside(z, j)}, device_id_type=MESH) for j in range(1, size)]
    for cp in blocks:
        cp.start()
    keeps = [pltpu.make_async_copy(weights[k].at[1], other_w[k], o_sem.at[k]) for k in range(6)]
    stores = [pltpu.make_async_copy(held[k], results[k], r_sem.at[k]) for k in range(16)]

    def store(*at):
        for k in at:
            stores[k].start()

    def attention(x, gain, wq, wo, kq, ko, h, qkv, p, o, y, then):
        _, _, n = norm_forward(x(), gain)
        h[...] = n
        per_half = c // LANES
        for side in range(2):
            if side == 0:
                loads[kq].wait()
            else:
                swaps[kq].wait_recv()
                keeps[kq].start()
                for cp in swaps[then : then + 2]:
                    cp.start()
            for k in range(3):
                at = (2 * k + side) * c
                qkv[:, at : at + c] = nn(h[...], wq[side, k]).astype(BF)
            lax.fori_loop(
                0, n_img * per_half,
                lambda i, _, side=side: attend(i // per_half, side * per_half + i % per_half, d, qkv, p, o), 0, unroll=2)
        loads[ko].wait()
        swaps[ko].wait_recv()
        keeps[ko].start()
        y[...] = x() + nn(o[:, :c], wo[0]) + nn(o[:, c:], wo[1])

    fill_rows(x0, 0, images, lax.axis_index("mdl") * n_img, n_img)
    store(15)
    attention(lambda: x0[...].astype(F32), g_ref[0:1, :], q1, w1, 0, 1, h1, qkv1, p1, o1, x1, 2)
    store(0, 1, 2, 3, 4)

    _, _, n = norm_forward(x1[...], g_ref[1:2, :])
    h2[...] = n
    x2[...] = x1[...]
    t = tile_of(f)
    for side in range(2):
        for k in (2, 3):
            if side == 0:
                loads[k].wait()
            else:
                swaps[k].wait_recv()
                keeps[k].start()

        def tile(i, _, side=side):
            at = pl.ds(pl.multiple_of(i * t, t), t)
            a, sl = gelu_parts(nn(h2[...], fi[side, :, at]))
            a = a.astype(BF)
            act[side, :, at] = a
            slope[side, :, at] = sl.astype(BF)
            x2[...] += nn(a, fo[side, at, :])
            return 0

        for cp in swaps[4 + 2 * side : 6 + 2 * side]:
            cp.start()
        lax.fori_loop(0, f // t, tile, 0)
    store(5, 6, 7, 8)

    attention(lambda: x2[...], g_ref[2:3, :], q3, w3, 4, 5, h3, qkv3, p3, o3, x3, 8)
    store(9, 10, 11, 12, 13)
    _, _, n = norm_forward(x3[...], g_ref[3:4, :])
    h4[...] = n
    store(14)
    for cp in blocks:
        cp.wait()
    for cp in keeps + stores:
        cp.wait()
    for cp in swaps[6:]:
        cp.wait_recv()
    for cp in swaps:
        cp.wait_send()


def forward(x, gains, own_w, dy_out, r):
    d = x.shape[2]
    c, f = own_w[0].shape[2], own_w[2].shape[1]
    n_img = r // LP
    heads = d // HDIM
    size = len(dy_out) + 1
    half = dy_out[0].shape[0]
    kept = [out((r, d), F32), out((r, d), BF), out((r, 3 * d), BF), out((n_img * heads, LP, LP), BF), out((r, d), BF)]
    results = kept + [out((r, d), F32), out((r, d), BF), out((2, r, f), BF), out((2, r, f), BF)] + kept + [out((r, d), BF), out((r, d), BF)]
    shapes = results + [out(w.shape, BF) for w in own_w] + [out((half, d), BF)] * (size - 1)
    D, V = pltpu.SemaphoreType.DMA, pltpu.VMEM
    any_ = pl.BlockSpec(memory_space=pl.ANY)
    vm = pl.BlockSpec(memory_space=pltpu.VMEM)
    got = pl.pallas_call(
        functools.partial(forward_body, n_img, size),
        in_specs=[vm] * 2 + [any_] * (len(own_w) + size - 1), out_specs=[any_] * len(shapes), out_shape=shapes,
        scratch_shapes=[V((2,) + w.shape, BF) for w in own_w[:6]] + [V(o.shape, o.dtype) for o in results]
        + [D((6,)), D((8,)), D((8,)), D((6,)), D((len(results),)), D((size - 1,)), D((size - 1,))],
        compiler_params=pltpu.CompilerParams(collective_id=2, has_side_effects=True, vmem_limit_bytes=VMEM_BYTES),
        cost_estimate=pl.CostEstimate(flops=16 * r * d * d + 8 * r * d * f, bytes_accessed=80 * r * d, transcendentals=0),
    )(x, gains, *own_w, *dy_out)
    n = len(results)
    return got[:n], got[n : n + 8], got[n + 8 :]


def routing_body(experts, capacity, half, count_ref, route_ref, prior_ref, router_ref, ga, gb, gc, gd, dy_ref, tr_ref, col_ref, wide_ref,
                 gains_ref, *refs):
    out_refs, (dy_rows, rows_ref, tmp) = refs[:-3], refs[-3:]
    for k, g in enumerate((ga, gb, gc, gd)):
        gains_ref[k : k + 1, :] = g[...].reshape(1, g.shape[0])
    wide_ref[...] = jnp.zeros(wide_ref.shape, BF)
    wide_ref[0:experts, :] = router_ref[...]
    fill_rows(dy_rows, 0, dy_ref, 0, rows_ref.shape[0])
    token = lax.broadcasted_iota(I32, (1, LQ), 1)
    for i in range(rows_ref.shape[0]):
        rows_ref[i] = jnp.zeros((8, LQ), I32)
        rows_ref[i, 0:TOPK, 0:L] = route_ref[i]
        rows_ref[i, 2:3, 0:L] = prior_ref[:, i * L : (i + 1) * L]
        rows_ref[i, 3:4, :] = jnp.where(token < L, (count_ref[0, 0] > i).astype(I32), 0)
    n_img = rows_ref.shape[0]
    slots = experts * half
    core = lax.axis_index("mdl")
    own_img = n_img // 2
    tall = lax.broadcasted_iota(I32, (max(experts, 8), LQ), 0)
    hots, priors = [], []
    for i in range(n_img):
        r = rows_ref[i]
        live = r[3:4, :] > 0
        hots.append((((tall == r[0:1, :]) | (tall == r[1:2, :])) & live).astype(F32).astype(BF))
        priors.append(r.astype(F32).T[:, 2:3])
    for i in range(n_img):
        r = rows_ref[i]
        rank = None
        for k in range(n_img):
            part = nn(hots[k], (priors[k] < r[2:3, :].astype(F32)).astype(F32).astype(BF))
            rank = part if rank is None else rank + part
        for k in range(TOPK):
            e = r[k : k + 1, :]
            mine = jnp.sum(jnp.where(tall == e, rank, 0.0), axis=0, keepdims=True).astype(I32)
            side = (mine >= half).astype(I32)
            slot = side * slots + e * half + mine - side * half
            tr_ref[i, k : k + 1, :] = jnp.where((mine < capacity) & (r[3:4, :] > 0), slot, -1)
        tr_ref[i, TOPK:, :] = jnp.full((8 - TOPK, LQ), -1, I32)
    for i in range(own_img):
        at = core * own_img + i
        for k in range(TOPK):
            t = tr_ref[at, k : k + 1, :]
            there = t - (1 - core) * slots
            tmp[k : k + 1, :] = t - core * slots
            tmp[TOPK + k : TOPK + k + 1, :] = jnp.where(there < slots, there, -1)
        tmp[4:8, :] = rows_ref[at, 0:4, :]
        tmp[6:7, :] = rows_ref[at, 3:4, :]
        col_ref[i * LP : (i + 1) * LP, :] = tmp[...].astype(F32).T[:LP, :].astype(I32)
    z = lax.axis_index("exp")
    for j, o_ref in enumerate(out_refs):
        at = core * slots + (beside(z, j) * half if len(out_refs) > 1 else 0)
        total = None
        for i in range(n_img):
            part = nn(slot_hots(tr_ref[i], at, o_ref.shape[0]), dy_rows[i * LP : (i + 1) * LP, :])
            total = part if total is None else total + part
        o_ref[...] = total.astype(BF)


def slot_hots(t, base, count):
    place = lax.broadcasted_iota(I32, (count, LP), 0) + base
    return ((place == t[0:1, :LP]) | (place == t[1:2, :LP])).astype(F32).astype(BF)


def dispatch_body(experts, half, tr_ref, own_ref, oth_ref, y_ref):
    core = lax.axis_index("mdl")
    own_img = own_ref.shape[0] // LP
    total = None
    for a, v in ((core, own_ref), (1 - core, oth_ref)):
        for i in range(own_img):
            hot = slot_hots(tr_ref[a * own_img + i], core * experts * half, experts * half)
            part = nn(hot, v[i * LP : (i + 1) * LP, :])
            total = part if total is None else total + part
    y_ref[...] = total.astype(BF)


def router_probs(h, router, experts):
    logits = nt(h, router)
    lane = lax.broadcasted_iota(I32, logits.shape, 1)
    logits = jnp.where(lane < experts, logits, -1e30)
    e = jnp.exp(logits - jnp.max(logits, axis=-1, keepdims=True))
    return e / jnp.sum(e, axis=-1, keepdims=True), lane


def expert_body(experts, x_ref, dy_ref, router_ref, im, io, tm, to,
                eout_ref, ret_ref, act_ref, dz_ref, wd_ref, acc_ref, dx_ref):
    step = pl.program_id(0)
    d = x_ref.shape[1]

    @pl.when(step == 0)
    def _():
        probs, lane = router_probs(x_ref[...], router_ref[...], experts)
        gate = jnp.sum(jnp.where(lane == lax.axis_index("exp"), probs, 0.0), axis=-1, keepdims=True)
        wd_ref[...] = (gate * dy_ref[...].astype(F32)).astype(BF)
        acc_ref[...] = jnp.zeros_like(acc_ref)
        dx_ref[...] = jnp.zeros_like(dx_ref)

    for half, (wi, wo) in enumerate(((im, tm), (io, to))):
        a, s = gelu_parts(nn(x_ref[...], wi[...]))
        act = a.astype(BF)
        act_ref[half] = act
        acc_ref[...] += nn(act, wo[...])
        dz = (nt(wd_ref[...], wo[...]) * s).astype(BF)
        dz_ref[half] = dz
        dx_ref[...] += nt(dz, wi[...])

    @pl.when(step == pl.num_programs(0) - 1)
    def _():
        eout = acc_ref[...].astype(BF)
        eout_ref[...] = eout
        ret_ref[:, :d] = dx_ref[...].astype(BF)
        dgate = jnp.sum(dy_ref[...].astype(F32) * eout.astype(F32), axis=-1, keepdims=True)
        high = dgate.astype(BF).astype(F32)
        lane = lax.broadcasted_iota(I32, (x_ref.shape[0], LANES), 1)
        ret_ref[:, d:] = jnp.where(lane < LANES // 2, high, dgate - high).astype(BF)


def expert_forward_backward(x, dy, router, im, io, tm, to, experts):
    r, d = x.shape
    f = im.shape[1]
    t = tile_of(f) // 2
    col = pl.BlockSpec((d, t), lambda i: (0, i))
    row = pl.BlockSpec((t, d), lambda i: (i, 0))
    hid = pl.BlockSpec((2, r, t), lambda i: (0, 0, i))
    return call(
        functools.partial(expert_body, experts),
        [out((r, d), BF), out((r, d + LANES), BF), out((2, r, f), BF), out((2, r, f), BF), out((r, d), BF)],
        x, dy, router, im, io, tm, to, grid=(f // t,),
        in_specs=[whole((r, d)), whole((r, d)), whole(router.shape), col, col, row, row],
        out_specs=[whole((r, d)), whole((r, d + LANES)), hid, hid, whole((r, d))],
        scratch=[pltpu.VMEM((r, d), F32), pltpu.VMEM((r, d), F32)], flops=16 * r * d * f,
    )


def expert_weights_body(x_ref, wd_ref, act_ref, dz_ref, gm_ref, go_ref, xt_ref, wt_ref):
    @pl.when(pl.program_id(0) == 0)
    def _():
        xt_ref[...] = x_ref[...].T
        wt_ref[...] = wd_ref[...].T

    for half, g in enumerate((gm_ref, go_ref)):
        g[0] = nn(xt_ref[...], dz_ref[half]).astype(BF)
        g[1] = nn(wt_ref[...], act_ref[half]).astype(BF)


def expert_weights(x, wd, act, dz):
    r, d = x.shape
    f = act.shape[2]
    t = tile_of(f) // 2
    hid = pl.BlockSpec((2, r, t), lambda i: (0, 0, i))
    grad = pl.BlockSpec((2, d, t), lambda i: (0, 0, i))
    return call(
        expert_weights_body, [out((2, d, f), BF), out((2, d, f), BF)], x, wd, act, dz, grid=(f // t,),
        in_specs=[whole((r, d)), whole((r, d)), hid, hid], out_specs=[grad, grad],
        scratch=[pltpu.VMEM((d, r), BF), pltpu.VMEM((d, r), BF)], flops=8 * r * d * f,
    )


def merge(col_ref, k, ab_ref, n):
    slots = ab_ref.shape[1]
    lane = lax.broadcasted_iota(I32, (n, slots), 1)
    rows = None
    for side in range(2):
        hot = (lane == col_ref[:, 2 * side + k : 2 * side + k + 1]).astype(F32).astype(BF)
        part = nn(hot, ab_ref[side])
        rows = part if rows is None else rows + part
    return rows


def merge_blocks(col_ref, k, blocks, n):
    rows = None
    for side in range(2):
        for e, ref in blocks[side]:
            half = ref.shape[0]
            lane = lax.broadcasted_iota(I32, (n, half), 1) + e * half
            hot = (lane == col_ref[:, 2 * side + k : 2 * side + k + 1]).astype(F32).astype(BF)
            part = nn(hot, ref[...])
            rows = part if rows is None else rows + part
    return rows


def mixture_backward_core(experts, half, x_ref, gain, h_ref, router_ref, dy_ref, col_ref, ab_ref, dgate_ref, dr_ref, dy_rows):
    n, d = x_ref.shape
    n_img = n // LP
    fill_rows(dy_rows, 0, dy_ref, lax.axis_index("mdl") * n_img, n_img)
    probs, lane = router_probs(h_ref[...], router_ref[...], experts)
    dsoft = jnp.zeros(probs.shape, F32)
    dh = jnp.zeros((n, d), F32)
    for k in range(TOPK):
        dh = dh + merge(col_ref, k, ab_ref, n)
        dgate = jnp.zeros((n, 1), F32)
        for side in range(2):
            t = col_ref[:, 2 * side + k : 2 * side + k + 1]
            for e in range(experts):
                line = dgate_ref[side, e, 0:1, :]
                place = lax.broadcasted_iota(I32, (n, line.shape[1]), 1)
                hit = (place + e * half == t) & (place < half)
                dgate = dgate + jnp.sum(jnp.where(hit, line, 0.0), axis=-1, keepdims=True)
        dsoft = dsoft + jnp.where(lane == col_ref[:, 4 + k : 5 + k], dgate, 0.0)
    dlog = (probs * (dsoft - jnp.sum(dsoft * probs, axis=-1, keepdims=True))).astype(BF)
    dr_ref[...] = tn(dlog, h_ref[...])
    dh = dh + nn(dlog, router_ref[...])
    nrm, rr, _ = norm_forward(x_ref[...], gain)
    dv, dw = norm_backward(nrm, rr, gain, dh)
    return dy_rows[...].astype(F32) * col_ref[:, 6:7].astype(F32) + dv, dw


def gate_lines(dgate):
    half = dgate.shape[0]
    wide = -(-half // LANES) * LANES
    tall = jnp.concatenate([dgate, jnp.zeros((wide - half, 1), F32)], axis=0) if wide > half else dgate
    return jnp.broadcast_to(tall, (wide, LANES)).T[0:8, :]


def mixture_attention_backward_body(n_img, experts, half, x3_ref, h4_ref, router_ref, dy_ref, col_ref, ret_ref, dgate_ref, x_ref, g_ref, h_ref,
                                    qkv_ref, p_ref, o_ref, qm, qo, om, oo, dx_ref, dw3_ref, dw4_ref, dr_ref, gm_ref, go_ref,
                                    dx3, dy_rows, do_ref, dqkv_ref, tr_ref):
    grad, dw4 = mixture_backward_core(experts, half, x3_ref, g_ref[3:4, :], h4_ref, router_ref, dy_ref, col_ref, ret_ref, dgate_ref,
                                      dr_ref, dy_rows)
    dx3[...] = grad
    dw4_ref[...] = dw4
    dx, dw3 = attention_backward_core(
        n_img, lambda: dx3[...], x_ref, g_ref[2:3, :], h_ref, qkv_ref, p_ref, o_ref, qm, qo, om, oo,
        gm_ref, go_ref, do_ref, dqkv_ref, tr_ref)
    dx_ref[...] = dx
    dw3_ref[...] = dw3


def mixture_attention_backward(experts, half, x3, h4, router, dy, col, ret, dgate, x, gains, kept, qm, qo, om, oo):
    r, d = x.shape
    c = qm.shape[2]
    n_img = r // LP
    heads = d // HDIM
    shapes = [out((r, d), F32), out((1, d), F32), out((1, d), F32), out(router.shape, F32),
              out((3 * d + d, c), BF), out((3 * d + d, c), BF)]
    return call(functools.partial(mixture_attention_backward_body, n_img, experts, half), shapes,
                x3, h4, router, dy, col, ret, dgate, x, gains, *kept, qm, qo, om, oo,
                scratch=[pltpu.VMEM((r, d), F32), pltpu.VMEM((r, d), BF)] + attention_backward_scratch(r, d),
                flops=4 * r * d * d * 4 + 8 * n_img * heads * LP * LP * LANES + 8 * r * ret.shape[1] * d)


def backward_body(n_img, experts, half, size, *refs):
    refs = list(refs)

    def take(n):
        r = refs[:n]
        del refs[:n]
        return r

    x3, h4, router, cotangent, col, ret, dgate, g_ref = take(8)
    src_two, src_mlp, src_one = take(9), take(8), take(9)
    eouts = take(size - 1)
    dg1, dg2, dg3, dg4, dr, image = take(6)
    out_two, out_mlp, out_one = take(2), take(4), take(2)
    ebacks = take(size - 1)
    attn = take(9)
    x0, x1, h2, act, slope, fi, fo, ga, gi, go, dxs, dy_rows, do, dqkv, tr, da, dh = take(17)
    a_sem, m_sem, b_sem, ga_sem, gi_sem, e_send, e_recv = refs
    d = x3.shape[1]
    f = fi.shape[2]
    t = gi.shape[4]
    z = lax.axis_index("exp")

    def fetch(srcs, dsts, sem):
        return [pltpu.make_async_copy(a, b, sem.at[k]) for k, (a, b) in enumerate(zip(srcs, dsts))]

    two = fetch(src_two, attn, a_sem)
    mlp = fetch(src_mlp, [x1, h2, act, slope, fi.at[0], fi.at[1], fo.at[0], fo.at[1]], m_sem)
    one = fetch(src_one, [x0] + attn[1:], b_sem)
    for cp in two + mlp:
        cp.start()
    barrier = pltpu.get_barrier_semaphore()
    for j in range(1, size):
        pl.semaphore_signal(barrier, inc=1, device_id={"exp": beside(z, j)}, device_id_type=MESH)
    pl.semaphore_wait(barrier, size - 1)
    blocks = [pltpu.make_async_remote_copy(eouts[j - 1], ebacks[j - 1], e_send.at[j - 1], e_recv.at[j - 1],
                                           device_id={"exp": beside(z, j)}, device_id_type=MESH) for j in range(1, size)]
    for cp in blocks:
        cp.start()

    def attention(x, gain, dst):
        leave = []

        def done(part):
            at = slice(part * d, (part + 1) * d)
            for k in range(2):
                leave.append(pltpu.make_async_copy(ga.at[k, at], dst[k].at[at], ga_sem.at[k, part]))
                leave[-1].start()

        dx, dw = attention_backward_core(n_img, lambda: dxs[...], x, gain, *attn[1:], ga.at[0], ga.at[1], do, dqkv, tr, done)
        return dx, dw, leave

    grad, dw4 = mixture_backward_core(experts, half, x3, g_ref[3:4, :], h4, router, cotangent, col, ret, dgate, dr, dy_rows)
    dxs[...] = grad
    dg4[...] = dw4
    for cp in two:
        cp.wait()
    dx, dw, leave = attention(attn[0], g_ref[2:3, :], out_two)
    dxs[...] = dx
    dg3[...] = dw
    for cp in one:
        cp.start()

    da[...] = dxs[...].astype(BF)
    for cp in mlp:
        cp.wait()
    tr[...] = h2[...].T
    dh[...] = jnp.zeros(dh.shape, F32)
    gone = {}
    for i in range(f // t):
        at = slice(i * t, (i + 1) * t)
        slot = i % 2
        for cp in gone.pop(slot, ()):
            cp.wait()
        gone[slot] = []
        for side in range(2):
            dz = (nt(da[...], fo[side, at, :]) * slope[side, :, at].astype(F32)).astype(BF)
            gw = tn(act[side, :, at], da[...]).astype(BF)
            for part in range(d // t):
                go[slot, side, part] = gw[:, part * t : (part + 1) * t]
            gi[slot, side, 0] = nn(tr[...], dz).astype(BF)
            dh[...] += nt(dz, fi[side, :, at])
            gone[slot] += [
                pltpu.make_async_copy(gi.at[slot, side], out_mlp[side].at[i : i + 1], gi_sem.at[slot, side, 0]),
                pltpu.make_async_copy(go.at[slot, side], out_mlp[2 + side].at[:, at], gi_sem.at[slot, side, 1])]
            for cp in gone[slot][-2:]:
                cp.start()
    gain = g_ref[1:2, :]
    n, rr, _ = norm_forward(x1[...], gain)
    dv, dw = norm_backward(n, rr, gain, dh[...])
    dxs[...] += dv
    dg2[...] = dw

    for cp in one + leave:
        cp.wait()
    dx, dw, leave = attention(x0, g_ref[0:1, :], out_one)
    for i in range(n_img):
        image[i] = dx[i * LP : i * LP + L].astype(BF)
    dg1[...] = dw
    for cp in leave + gone[0] + gone[1] + blocks:
        cp.wait()


def backward(experts, half, x3, h4, router, cotangent, col, ret, dgate, gains, x2, kept3, w2, x1, h2, act, slope, mlp_w, x0, kept1,
             w1, eouts):
    r, d = x3.shape
    c, f = w1[0].shape[2], mlp_w[0].shape[1]
    n_img = r // LP
    heads = d // HDIM
    size = len(eouts) + 1
    t = c
    flat = [x2, *kept3, *w2, x1, h2, act, slope, *mlp_w, x0, *kept1, *w1, *eouts]
    near = [x3, h4, router, cotangent, col, ret, dgate, gains]
    D, V = pltpu.SemaphoreType.DMA, pltpu.VMEM
    any_ = pl.BlockSpec(memory_space=pl.ANY)
    vm = pl.BlockSpec(memory_space=pltpu.VMEM)
    shapes = [out((1, d), F32)] * 4 + [out(router.shape, F32), out((n_img, L, d), BF)]
    shapes += [out((4 * d, c), BF)] * 2 + [out((f // t, d, t), BF)] * 2 + [out((d // t, f, t), BF)] * 2 + [out((4 * d, c), BF)] * 2
    shapes += [out(e.shape, BF) for e in eouts]
    like = [V(v.shape, v.dtype) for v in (x2, *kept3, *w2)]
    got = pl.pallas_call(
        functools.partial(backward_body, n_img, experts, half, size),
        in_specs=[vm] * len(near) + [any_] * len(flat), out_specs=[vm] * 6 + [any_] * (len(shapes) - 6), out_shape=shapes,
        scratch_shapes=like + [
            V(x0.shape, x0.dtype), V((r, d), F32), V((r, d), BF), V(act.shape, BF), V(slope.shape, BF), V((2, d, f), BF),
            V((2, f, d), BF), V((2, 4 * d, c), BF), V((2, 2, 1, d, t), BF), V((2, 2, d // t, t, t), BF), V((r, d), F32),
            V((r, d), BF), V((r, d), BF), V((r, 3 * d), BF), V((d, r), BF), V((r, d), BF), V((r, d), F32),
            D((9,)), D((8,)), D((9,)), D((2, 4)), D((2, 2, 2)), D((size - 1,)), D((size - 1,))],
        compiler_params=pltpu.CompilerParams(collective_id=3, has_side_effects=True, vmem_limit_bytes=VMEM_BYTES),
        cost_estimate=pl.CostEstimate(flops=32 * r * d * d + 16 * r * d * f, bytes_accessed=160 * r * d, transcendentals=0),
    )(*near, *flat)
    return got[:6], got[6:14], got[14:]


def mixture_output(experts, x_ref, h_ref, router_ref, col_ref, rows_of):
    n, d = x_ref.shape
    probs, lane = router_probs(h_ref[...], router_ref[...], experts)
    mixed = jnp.zeros((n, d), F32)
    for k in range(TOPK):
        gate = jnp.sum(jnp.where(lane == col_ref[:, 4 + k : 5 + k], probs, 0.0), axis=-1, keepdims=True)
        mixed = mixed + gate * rows_of(k)
    return (col_ref[:, 6:7].astype(F32) * (x_ref[...] + mixed)).astype(BF)


def mixture_output_body(experts, x_ref, h_ref, router_ref, col_ref, ab_ref, y_ref):
    y = mixture_output(experts, x_ref, h_ref, router_ref, col_ref, lambda k: merge(col_ref, k, ab_ref, x_ref.shape[0]))
    for i in range(y_ref.shape[0]):
        y_ref[i] = y[i * LP : i * LP + L]


def widen_body(pieces, n_in, n_slots, *refs):
    src, dst = refs[:n_in], refs[n_in:-2]
    buf, sem = refs[-2:]
    going = []
    for k, (i, a, o, b) in enumerate(pieces):
        slot = k % n_slots
        if k >= n_slots:
            going[k - n_slots].wait()
        value = src[i][a].astype(F32)
        rows, cols = value.shape
        buf[slot, 0:rows, 0:cols] = value
        going.append(pltpu.make_async_copy(buf.at[slot, 0:rows, 0:cols], dst[o].at[b], sem.at[slot]))
        going[k].start()
    for cp in going[max(0, len(pieces) - n_slots) :]:
        cp.wait()


def widen(pair, *vs):
    pieces = []
    for i, v in enumerate(vs):
        if len(v.shape) == 3:
            pieces += [(i, k, i, k) for k in range(v.shape[0])]
        else:
            n = v.shape[0]
            step = min(n, max(16, (1 << 18) // v.shape[1] // 16 * 16))
            while n % step:
                step -= 16
            pieces += [(i, slice(r, r + step), i, slice(r, r + step)) for r in range(0, n, step)]
    pieces += [(len(vs), k, len(vs) + k, slice(0, pair.shape[1])) for k in range(2)]
    shapes = [v.shape for v in vs] + [pair.shape[1:]] * 2
    vs = (*vs, pair)
    rows = max(v.shape[1] if len(v.shape) == 3 else min(v.shape[0], 512) for v in vs)
    rows = max([rows] + [a.stop - a.start for _, a, _, _ in pieces if isinstance(a, slice)])
    cols = max(v.shape[-1] for v in vs)
    n_slots = 4
    any_ = pl.BlockSpec(memory_space=pl.ANY)
    return pl.pallas_call(
        functools.partial(widen_body, tuple(pieces), len(vs), n_slots),
        in_specs=[pl.BlockSpec(memory_space=pltpu.VMEM)] * len(vs), out_specs=[any_] * len(shapes),
        out_shape=[out(v, F32) for v in shapes],
        scratch_shapes=[pltpu.VMEM((n_slots, rows, cols), F32), pltpu.SemaphoreType.DMA((n_slots,))],
        compiler_params=pltpu.CompilerParams(vmem_limit_bytes=34 * 1024 * 1024),
    )(*vs)


def flip(axis, bit):
    size = lax.axis_size(axis)
    return [(i, i ^ bit) for i in range(size)]


def bits_of(axis):
    size = lax.axis_size(axis)
    return [1 << b for b in range(size.bit_length() - 1)]


def other_core(v):
    return lax.ppermute(v, "mdl", flip("mdl", 1))


def add16(a, b):
    return (a.astype(F32) + b.astype(F32)).astype(BF)


def halve(v, axis, bit):
    side = (lax.axis_index(axis) // bit) % 2
    n = v.shape[0] // 2
    keep = lax.dynamic_slice_in_dim(v, side * n, n)
    send = lax.dynamic_slice_in_dim(v, (1 - side) * n, n)
    return add16(keep, lax.ppermute(send, axis, flip(axis, bit)))


def double(v, axis, bit):
    side = (lax.axis_index(axis) // bit) % 2
    got = lax.ppermute(v, axis, flip(axis, bit))
    return jnp.where(side == 0, jnp.concatenate([v, got]), jnp.concatenate([got, v]))


def sum_everywhere(v):
    n = v.shape[0] // 2
    bits = bits_of("grp")
    parts = []
    for part, order in ((v[:n], bits), (v[n:], bits[::-1])):
        for bit in order:
            part = halve(part, "grp", bit)
        parts.append(part)
    size = lax.axis_size("exp")
    joined = jnp.concatenate(parts)
    rows = joined.shape[0] // size
    spread = lax.all_to_all(joined.reshape(size, rows, -1), "exp", 0, 0, tiled=True)
    mine = jnp.sum(spread.astype(F32), axis=0).astype(BF)
    joined = lax.all_gather(mine, "exp", axis=0, tiled=True)
    h = joined.shape[0] // 2
    done = []
    for part, order in ((joined[:h], bits), (joined[h:], bits[::-1])):
        for bit in order[::-1]:
            part = double(part, "grp", bit)
        done.append(part)
    return jnp.concatenate(done)


def small_sum(v):
    for axis in ("mdl", "grp", "exp"):
        for bit in bits_of(axis):
            v = v + lax.ppermute(v, axis, flip(axis, bit))
    return v


def reduce_body(n_in, per, n_exp, experts, *refs):
    mine = refs[:n_in]
    other = refs[n_in : 2 * n_in]
    dg = refs[2 * n_in : 2 * n_in + 4]
    dr_ref, x3_ref, h4_ref, router_ref, col_ref = refs[2 * n_in + 4 : 2 * n_in + 9]
    eouts = refs[2 * n_in + 9 : 2 * n_in + 13]
    image_ref = refs[2 * n_in + 13]
    outs = refs[2 * n_in + 14 :]
    qkv2, proj2, fc_in, fc_out, qkv1, proj1, sum_ref, y_ref, gx_ref = outs[:9]
    (acc, got, r1, r2, zr, zz, zs, sm, y_own, load_sem, m_send, m_recv, x_send, x_recv, z_send, z_recv, s_send, s_recv,
     i_local, i_send, i_recv, e_oth, e_send, e_recv) = outs[9:]
    out_ref = got
    n = n_in * per
    rows = acc.shape[2]
    h, q = rows // 2, rows // 4
    t = q // n_exp
    g = lax.axis_index("grp")
    z = lax.axis_index("exp")
    core = lax.axis_index("mdl")
    bx, by = g % 2, g // 2
    flat = {"x": g + 1 - 2 * bx, "y": g + 2 - 4 * by}
    order = (("x", "y"), ("y", "x"))
    bits = ((bx, by), (by, bx))

    barrier = pltpu.get_barrier_semaphore()
    others = [{"mdl": 1 - core}, {"grp": flat["x"]}, {"grp": flat["y"]}]
    others += [{"exp": (z + o) % n_exp} for o in range(1, n_exp)]
    for dev in others:
        pl.semaphore_signal(barrier, inc=1, device_id=dev, device_id_type=MESH)
    pl.semaphore_wait(barrier, len(others))

    def load(c):
        i, p = c // per, c % per
        return pltpu.make_async_copy(mine[i].at[p], acc.at[c], load_sem.at[c])

    def swap(c):
        i, p = c // per, c % per
        return pltpu.make_async_remote_copy(other[i].at[p], got.at[c], m_send.at[c], m_recv.at[c],
                                            device_id={"mdl": 1 - core}, device_id_type=MESH)

    for c in range(n):
        swap(c).start()
        load(c).start()

    own_img = image_ref.shape[0]
    places = pl.ds(core * own_img, own_img)

    def image_copies(k, src, dst):
        return (pltpu.make_async_copy(src, dst.at[places], i_local.at[k]),
                pltpu.make_async_remote_copy(src, dst.at[places], i_send.at[k], i_recv.at[k], device_id={"mdl": 1 - core},
                                             device_id_type=MESH))

    def image_come(k, src, dst):
        there = pl.ds((1 - core) * own_img, own_img)
        return pltpu.make_async_remote_copy(src, dst.at[there], i_send.at[k], i_recv.at[k], device_id={"mdl": 1 - core},
                                            device_id_type=MESH)

    for cp in image_copies(0, image_ref, gx_ref):
        cp.start()

    e_copies = [pltpu.make_async_remote_copy(eouts[j], e_oth.at[j], e_send.at[j], e_recv.at[j], device_id={"mdl": 1 - core},
                                             device_id_type=MESH) for j in range(n_exp)]
    for cp in e_copies:
        cp.start()

    def swap_at(c):
        return pltpu.make_async_remote_copy(other[0].at[0], got.at[c], m_send.at[c], m_recv.at[c],
                                            device_id={"mdl": 1 - core}, device_id_type=MESH)

    def load_at(c):
        return pltpu.make_async_copy(mine[0].at[0], acc.at[c], load_sem.at[c])

    def over(u, leg, src, dst, slot, c):
        return pltpu.make_async_remote_copy(src, dst, x_send.at[slot, u, c], x_recv.at[slot, u, c],
                                            device_id={"grp": flat[order[u][leg]]}, device_id_type=MESH)

    def first(u, c):
        return over(u, 0, acc.at[c, u, pl.ds(pl.multiple_of((1 - bits[u][0]) * h, h), h)], r1.at[c, u], 0, c)

    def second(u, c):
        return over(u, 1, r1.at[c, u, pl.ds(pl.multiple_of((1 - bits[u][1]) * q, q), q)], r2.at[c, u], 1, c)

    def along(u, c, o):
        return pltpu.make_async_remote_copy(
            r2.at[c, u, pl.ds(pl.multiple_of(((z + o) % n_exp) * t, t), t)], zr.at[c, u, o - 1],
            z_send.at[0, u, o - 1, c], z_recv.at[0, u, o - 1, c],
            device_id={"exp": (z + o) % n_exp}, device_id_type=MESH)

    def place(u):
        return bits[u][0] * h + bits[u][1] * q

    def back(u, c, o):
        here = out_ref.at[c, u, pl.ds(pl.multiple_of(place(u) + z * t, t), t)]
        return pltpu.make_async_remote_copy(here, here, z_send.at[1, u, o - 1, c], z_recv.at[1, u, o - 1, c],
                                            device_id={"exp": (z + o) % n_exp}, device_id_type=MESH)

    def third(u, c):
        here = out_ref.at[c, u, pl.ds(pl.multiple_of(place(u), q), q)]
        return over(u, 1, here, here, 2, c)

    def fourth(u, c):
        here = out_ref.at[c, u, pl.ds(pl.multiple_of(bits[u][0] * h, h), h)]
        return over(u, 0, here, here, 3, c)

    def plus(a, b):
        return (a.astype(F32) + b.astype(F32)).astype(BF)

    def s1(c):
        load_at(c).wait()
        swap_at(c).wait_recv()
        for u in range(2):
            acc[c, u] = plus(acc[c, u], got[c, u])
            first(u, c).start()

    def s2(c):
        for u in range(2):
            first(u, c).wait_recv()
            keep = acc[c, u, pl.ds(pl.multiple_of(bits[u][0] * h, h), h)]
            r1[c, u] = plus(keep, r1[c, u])
            second(u, c).start()

    def s3(c):
        for u in range(2):
            second(u, c).wait_recv()
            keep = r1[c, u, pl.ds(pl.multiple_of(bits[u][1] * q, q), q)]
            r2[c, u] = plus(keep, r2[c, u])
            for o in range(1, n_exp):
                along(u, c, o).start()

    def s4(c):
        for u in range(2):
            total = r2[c, u, pl.ds(pl.multiple_of(z * t, t), t)].astype(F32)
            for o in range(1, n_exp):
                along(u, c, o).wait_recv()
                total = total + zr[c, u, o - 1].astype(F32)
            out_ref[c, u, pl.ds(pl.multiple_of(place(u) + z * t, t), t)] = total.astype(BF)
            for o in range(1, n_exp):
                back(u, c, o).start()

    def s5(c):
        for u in range(2):
            for o in range(1, n_exp):
                back(u, c, o).wait_recv()
            third(u, c).start()

    def s6(c):
        for u in range(2):
            third(u, c).wait_recv()
            fourth(u, c).start()

    def s7(c):
        for u in range(2):
            fourth(u, c).wait_recv()
        for k in range(n):

            @pl.when(c == k)
            def _(k=k):
                natural(k)

    zc = 0
    e, e2, e4 = rows // n_exp, rows // n_exp // 2, rows // n_exp // 4

    def z_out(u, o):
        return pltpu.make_async_remote_copy(
            acc.at[zc, u, pl.ds(pl.multiple_of(((z + o) % n_exp) * e, e), e)], zz.at[u, o - 1],
            z_send.at[0, u, o - 1, zc], z_recv.at[0, u, o - 1, zc], device_id={"exp": (z + o) % n_exp}, device_id_type=MESH)

    def z_first(u):
        return over(u, 0, zs.at[u, pl.ds(pl.multiple_of((1 - bits[u][0]) * e2, e2), e2)], r1.at[zc, u, 0:e2], 0, zc)

    def z_second(u):
        return over(u, 1, r1.at[zc, u, pl.ds(pl.multiple_of((1 - bits[u][1]) * e4, e4), e4)], r2.at[zc, u, 0:e4], 1, zc)

    def z_third(u):
        here = out_ref.at[zc, u, pl.ds(pl.multiple_of(z * e + bits[u][0] * e2 + bits[u][1] * e4, e4), e4)]
        return over(u, 1, here, here, 2, zc)

    def z_fourth(u):
        here = out_ref.at[zc, u, pl.ds(pl.multiple_of(z * e + bits[u][0] * e2, e2), e2)]
        return over(u, 0, here, here, 3, zc)

    def z_back(u, o):
        here = out_ref.at[zc, u, pl.ds(pl.multiple_of(z * e, e), e)]
        return pltpu.make_async_remote_copy(here, here, z_send.at[1, u, o - 1, zc], z_recv.at[1, u, o - 1, zc],
                                            device_id={"exp": (z + o) % n_exp}, device_id_type=MESH)

    def z1():
        load_at(zc).wait()
        swap_at(zc).wait_recv()
        for u in range(2):
            acc[zc, u] = plus(acc[zc, u], got[zc, u])
            for o in range(1, n_exp):
                z_out(u, o).start()

    def z2():
        for u in range(2):
            total = acc[zc, u, pl.ds(pl.multiple_of(z * e, e), e)].astype(F32)
            for o in range(1, n_exp):
                z_out(u, o).wait_recv()
                total = total + zz[u, o - 1].astype(F32)
            zs[u] = total.astype(BF)
            z_first(u).start()

    def z3():
        for u in range(2):
            z_first(u).wait_recv()
            r1[zc, u, 0:e2] = plus(zs[u, pl.ds(pl.multiple_of(bits[u][0] * e2, e2), e2)], r1[zc, u, 0:e2])
            z_second(u).start()

    def z4():
        for u in range(2):
            z_second(u).wait_recv()
            mine_rows = pl.ds(pl.multiple_of(z * e + bits[u][0] * e2 + bits[u][1] * e4, e4), e4)
            out_ref[zc, u, mine_rows] = plus(r1[zc, u, pl.ds(pl.multiple_of(bits[u][1] * e4, e4), e4)], r2[zc, u, 0:e4])
            z_third(u).start()

    def z5():
        for u in range(2):
            z_third(u).wait_recv()
            z_fourth(u).start()

    def z6():
        for u in range(2):
            z_fourth(u).wait_recv()
            for o in range(1, n_exp):
                z_back(u, o).start()

    def z7():
        for u in range(2):
            for o in range(1, n_exp):
                z_back(u, o).wait_recv()
        natural(zc)

    def drain(c, _):
        swap_at(c).wait_send()
        for u in range(2):
            for make in (first, second, third, fourth):
                make(u, c).wait_send()
            for o in range(1, n_exp):
                along(u, c, o).wait_send()
                back(u, c, o).wait_send()
        return 0

    legs = [({"mdl": 1 - core}), ({"grp": flat["x"]}), ({"grp": flat["y"]})]
    base = 2 * len(legs) + 1

    def small_leg(i):
        return pltpu.make_async_remote_copy(sm.at[2 * i], sm.at[2 * i + 1], s_send.at[i], s_recv.at[i], device_id=legs[i],
                                            device_id_type=MESH)

    def small_along(o):
        return pltpu.make_async_remote_copy(sm.at[base - 1], sm.at[base + z], s_send.at[len(legs) + o - 1],
                                            s_recv.at[len(legs) + o - 1], device_id={"exp": (z + o) % n_exp},
                                            device_id_type=MESH)

    def small_step(i):
        if i == 0:
            sm[0] = jnp.zeros(sm.shape[1:], F32)
            for k in range(4):
                sm[0, k : k + 1, :] = dg[k][...]
            sm[0, 4 : 4 + experts, :] = dr_ref[:experts, :]
        else:
            small_leg(i - 1).wait()
            sm[2 * i] = sm[2 * i - 2] + sm[2 * i - 1]
        if i < len(legs):
            small_leg(i).start()
        else:
            sm[pl.ds(base + z, 1)] = sm[pl.ds(base - 1, 1)]
            for o in range(1, n_exp):
                small_along(o).start()

    def natural(c):
        i, p = c // per, c % per
        wide = out_ref.shape[3]
        piece = wide // 3
        for u in range(2):
            for r0 in range(0, rows, piece):
                at = (2 * p + u) * rows + r0
                value = out_ref[c, u, r0 : r0 + piece]
                if i in (0, 3):
                    qkv, proj = (qkv2, proj2) if i == 0 else (qkv1, proj1)
                    if at < 6 * wide:
                        k, at = divmod(at, 2 * wide)
                        qkv[k, at : at + piece] = value
                    else:
                        k, at = divmod(at - 6 * wide, wide)
                        proj[at : at + piece, k * wide : (k + 1) * wide] = value
                else:
                    to, tall = (fc_in, 2 * wide) if i == 1 else (fc_out, 4 * wide)
                    k, at = divmod(at, tall)
                    to[at : at + piece, k * wide : (k + 1) * wide] = value

    steps = (s1, s2, s3, s4, s5, s6, s7)
    waves = n - 1 + len(steps)
    late = waves - 2
    z_steps = ((0, z1), (3, z2), (4, z3), (5, z4), (6, z5), (7, z6), (late, z7))
    small_steps = {1: 0, 3: 1, 5: 2, 7: 3}

    def wave(tau, _):
        for s, step in enumerate(steps):
            c = tau - s + 1 - (s > 0)

            @pl.when((c >= 1) & (c < n))
            def _(step=step, c=c):
                step(c)

        for at, step in z_steps:
            pl.when(tau == at)(step)
        for at, i in small_steps.items():
            pl.when(tau == at)(functools.partial(small_step, i))
        return 0

    first_waves = 2
    lax.fori_loop(0, first_waves, wave, 0)
    for cp in e_copies:
        cp.wait_recv()
    blocks = [[(beside(z, j), eouts[j]) for j in range(n_exp)], [(beside(z, j), e_oth.at[j]) for j in range(n_exp)]]
    y = mixture_output(experts, x3_ref, h4_ref, router_ref, col_ref, lambda k: merge_blocks(col_ref, k, blocks, x3_ref.shape[0]))
    for i in range(own_img):
        y_own[i] = y[i * LP : i * LP + L]
    for cp in image_copies(1, y_own, y_ref):
        cp.start()
    lax.fori_loop(first_waves, waves, wave, 0)
    for cp in e_copies:
        cp.wait_send()
    for k, (src, dst) in enumerate(((image_ref, gx_ref), (y_own, y_ref))):
        local, sent = image_copies(k, src, dst)
        local.wait()
        sent.wait_send()
        image_come(k, src, dst).wait_recv()
    lax.fori_loop(1, n, drain, 0)
    swap_at(zc).wait_send()
    for u in range(2):
        for make in (z_first, z_second, z_third, z_fourth):
            make(u).wait_send()
        for o in range(1, n_exp):
            z_out(u, o).wait_send()
            z_back(u, o).wait_send()
    for o in range(1, n_exp):
        small_along(o).wait()
    total = sm[base]
    for k in range(1, n_exp):
        total = total + sm[base + k]
    sum_ref[...] = total


def reduce_all(mine, other, dgs, dr, x3, h4, router, col, eouts, image, n_exp, experts):
    per, _, rows, c = mine[0].shape
    n = len(mine) * per
    d, f = 2 * c, 4 * c
    h, q = rows // 2, rows // 4
    t = q // n_exp
    small = (-(-(4 + experts) // 8) * 8, d)
    n_img, length, _ = image.shape
    D, V = pltpu.SemaphoreType.DMA, pltpu.VMEM
    any_ = pl.BlockSpec(memory_space=pl.ANY)
    vm = pl.BlockSpec(memory_space=pltpu.VMEM)
    return pl.pallas_call(
        functools.partial(reduce_body, len(mine), per, n_exp, experts),
        in_specs=[any_] * (2 * len(mine)) + [vm] * 13 + [any_],
        out_specs=[vm] * 9,
        out_shape=[out((3, d, c), BF), out((c, d), BF), out((d, f), BF), out((f, d), BF), out((3, d, c), BF), out((c, d), BF),
                   out(small, F32), out((2 * n_img, length, d), BF), out((2 * n_img, length, d), BF)],
        scratch_shapes=[
            V((n, 2, rows, c), BF), V((n, 2, rows, c), BF), V((n, 2, h, c), BF), V((n, 2, q, c), BF),
            V((n, 2, n_exp - 1, t, c), BF), V((2, n_exp - 1, rows // n_exp, c), BF), V((2, rows // n_exp, c), BF),
            V((7 + n_exp,) + small, F32), V((n_img, length, d), BF),
            D((n,)), D((n,)), D((n,)), D((4, 2, n)), D((4, 2, n)), D((2, 2, n_exp - 1, n)), D((2, 2, n_exp - 1, n)),
            D((3 + n_exp,)), D((3 + n_exp,)), D((2,)), D((2,)), D((2,)), V((n_exp,) + eouts[0].shape, BF), D((n_exp,)), D((n_exp,)),
        ],
        compiler_params=pltpu.CompilerParams(collective_id=0, has_side_effects=True, vmem_limit_bytes=VMEM_BYTES),
        cost_estimate=pl.CostEstimate(flops=8 * x3.shape[0] * x3.shape[0] * d, bytes_accessed=n * 8 * rows * c, transcendentals=0),
    )(*mine, *other, *dgs, dr, x3, h4, router, col, *eouts, image)


def expert_exchange_body(experts, half, h4_ref, tr_ref, dy0, dy1, dy2, dy3, router_ref, im, io, tm, to,
                         ret_ref, dg_ref, e0, e1, e2, e3, gw_ref,
                         h_oth, part, xo, x, wi, wo, act, dz, wd, acc, dxa, rsend, gscr, ggot, xt, wt,
                         w_sem, swap_sem, x_send, x_recv, r_send, r_recv, f_send, f_recv, g_send, g_recv, g_sem,
                         dgs, l_send, l_recv, k_send, k_recv):
    n, d = h4_ref.shape
    f = im.shape[1]
    t = 256 if f % 256 == 0 else tile_of(f)
    z = lax.axis_index("exp")
    core = lax.axis_index("mdl")
    partner = {"mdl": 1 - core}
    size = experts
    near_first = [1, 3, 2]

    out_grad, eouts = (dy0, dy1, dy2, dy3), (e0, e1, e2, e3)

    def there(j):
        return beside(z, j)

    loads = [pltpu.make_async_copy(src, dst, w_sem.at[k]) for k, (src, dst) in enumerate(
        ((im, wi.at[0]), (io, wi.at[1]), (tm, wo.at[0]), (to, wo.at[1])))]
    for cp in loads:
        cp.start()
    barrier = pltpu.get_barrier_semaphore()
    for dev in [partner] + [{"exp": there(j)} for j in range(1, size)]:
        pl.semaphore_signal(barrier, inc=1, device_id=dev, device_id_type=MESH)
    pl.semaphore_wait(barrier, size)
    swap = pltpu.make_async_remote_copy(h4_ref, h_oth, swap_sem.at[0], swap_sem.at[1], device_id=partner, device_id_type=MESH)
    swap.start()

    own_img = n // LP
    base = core * size * half

    def spread(side, v, j):
        total = None
        for i in range(own_img):
            p = nn(slot_hots(tr_ref[side * own_img + i], base + there(j) * half, half), v[i * LP : (i + 1) * LP, :])
            total = p if total is None else total + p
        return total

    def rows(j):
        return slice(j * half, (j + 1) * half)

    def place(e):
        return pl.ds(pl.multiple_of(e * half, half), half)

    for j in near_first + [0]:
        part[rows(j), :] = spread(core, h4_ref, j)
    swap.wait_recv()
    sends = {}
    for j in near_first + [0]:
        block = (part[rows(j), :] + spread(1 - core, h_oth, j)).astype(BF)
        if j == 0:
            x[rows(0), :] = block
        else:
            xo[rows(j), :] = block
            sends[j] = pltpu.make_async_remote_copy(xo.at[rows(j)], x.at[rows(j)], x_send.at[j], x_recv.at[j],
                                                    device_id={"exp": there(j)}, device_id_type=MESH)
            sends[j].start()

    returns, forwards = {}, {}

    def forward(j):
        here = ret_ref.at[0, place(there(j))]
        forwards[j] = (
            pltpu.make_async_remote_copy(here, ret_ref.at[1, place(there(j))], f_send.at[j], f_recv.at[j],
                                         device_id=partner, device_id_type=MESH),
            pltpu.make_async_remote_copy(dg_ref.at[0, there(j)], dg_ref.at[1, there(j)], k_send.at[j], k_recv.at[j],
                                         device_id=partner, device_id_type=MESH))
        for cp in forwards[j]:
            cp.start()

    def run(blocks):
        r0, r1 = blocks[0] * half, (blocks[-1] + 1) * half
        m = r1 - r0
        for j in blocks:
            probs, lane = router_probs(x[rows(j), :], router_ref[...], experts)
            gate = jnp.sum(jnp.where(lane == z, probs, 0.0), axis=-1, keepdims=True)
            wd[rows(j), :] = (gate * out_grad[j][...].astype(F32)).astype(BF)
        acc[0:m, :] = jnp.zeros((m, d), F32)
        dxa[0:m, :] = jnp.zeros((m, d), F32)

        def tile(i, _):
            at = pl.ds(pl.multiple_of(i * t, t), t)
            for side in range(2):
                a, s = gelu_parts(nn(x[r0:r1, :], wi[side, :, at]))
                a = a.astype(BF)
                act[side, r0:r1, at] = a
                acc[0:m, :] += nn(a, wo[side, at, :])
                g = (nt(wd[r0:r1, :], wo[side, at, :]) * s).astype(BF)
                dz[side, r0:r1, at] = g
                dxa[0:m, :] += nt(g, wi[side, :, at])
            return 0

        lax.fori_loop(0, f // t, tile, 0)
        for b, j in enumerate(blocks):
            here = slice(b * half, (b + 1) * half)
            e_rows = acc[here, :].astype(BF)
            eouts[j][...] = e_rows
            dgate = jnp.sum(out_grad[j][...].astype(F32) * e_rows.astype(F32), axis=-1, keepdims=True)
            lines = gate_lines(dgate)
            if j == 0:
                ret_ref[0, place(z), :] = dxa[here, :].astype(BF)
                dg_ref[0, pl.ds(z, 1)] = lines[None]
                forward(0)
            else:
                rsend[rows(j), :] = dxa[here, :].astype(BF)
                dgs[j] = lines
                returns[j] = (
                    pltpu.make_async_remote_copy(rsend.at[rows(j)], ret_ref.at[0, place(z)], r_send.at[j], r_recv.at[j],
                                                 device_id={"exp": there(j)}, device_id_type=MESH),
                    pltpu.make_async_remote_copy(dgs.at[j], dg_ref.at[0, z], l_send.at[j], l_recv.at[j],
                                                 device_id={"exp": there(j)}, device_id_type=MESH))
                for cp in returns[j]:
                    cp.start()

    for cp in loads:
        cp.wait()
    sends[1].wait_recv()
    run([0, 1])
    for j in near_first[1:]:
        sends[j].wait_recv()
        run([j])

    xt[...] = x[...].T
    wt[...] = wd[...].T

    tiles = f // t

    def cols(i):
        return pl.ds(pl.multiple_of(i * t, t), t)

    def swapped(i):
        return pltpu.make_async_remote_copy(gscr.at[1, :, :, cols(i)], ggot.at[:, :, cols(i)], g_send.at[i], g_recv.at[i],
                                            device_id=partner, device_id_type=MESH)

    def stored(i):
        return pltpu.make_async_copy(gscr.at[0, :, :, cols(i)], gw_ref.at[:, :, cols(i)], g_sem.at[i])

    def weight_tile(i, _):
        for side in (1, 0):
            gscr[side, 0, :, cols(i)] = nn(xt[...], dz[side, :, cols(i)]).astype(BF)
            gscr[side, 1, :, cols(i)] = nn(wt[...], act[side, :, cols(i)]).astype(BF)
            if side == 1:
                swapped(i).start()
        return 0

    lax.fori_loop(0, tiles, weight_tile, 0)

    def sum_tile(i, _):
        swapped(i).wait_recv()
        for k in range(2):
            gscr[0, k, :, cols(i)] = (gscr[0, k, :, cols(i)].astype(F32) + ggot[k, :, cols(i)].astype(F32)).astype(BF)
        stored(i).start()
        return 0

    lax.fori_loop(0, tiles, sum_tile, 0)

    for j in near_first:
        pltpu.make_async_remote_copy(rsend.at[rows(j)], ret_ref.at[0, place(there(j))], r_send.at[j], r_recv.at[j],
                                     device_id={"exp": there(j)}, device_id_type=MESH).wait_recv()
        pltpu.make_async_remote_copy(dgs.at[j], dg_ref.at[0, there(j)], l_send.at[j], l_recv.at[j],
                                     device_id={"exp": there(j)}, device_id_type=MESH).wait_recv()
        forward(j)

    def drain(i, _):
        stored(i).wait()
        swapped(i).wait_send()
        return 0

    lax.fori_loop(0, tiles, drain, 0)
    swap.wait_send()
    for j in range(size):
        if j:
            sends[j].wait_send()
            for cp in returns[j]:
                cp.wait_send()
        for cp in forwards[j]:
            cp.wait()


def expert_exchange(h4, tr, dys, router, im, io, tm, to, experts, half):
    n, d = h4.shape
    f = im.shape[1]
    s = experts * half
    wide = -(-half // LANES) * LANES
    tiles = f // (256 if f % 256 == 0 else tile_of(f))
    D, V = pltpu.SemaphoreType.DMA, pltpu.VMEM
    any_ = pl.BlockSpec(memory_space=pl.ANY)
    vm = pl.BlockSpec(memory_space=pltpu.VMEM)
    return pl.pallas_call(
        functools.partial(expert_exchange_body, experts, half),
        in_specs=[vm] * 7 + [any_] * 4,
        out_specs=[vm] * 6 + [any_],
        out_shape=[out((2, s, d), BF), out((2, experts, 8, wide), F32)] + [out((half, d), BF)] * 4 + [out((2, d, f), BF)],
        scratch_shapes=[
            V((n, d), BF), V((s, d), F32), V((s, d), BF), V((s, d), BF), V((2, d, f), BF), V((2, f, d), BF),
            V((2, s, f), BF), V((2, s, f), BF), V((s, d), BF), V((2 * half, d), F32), V((2 * half, d), F32),
            V((s, d), BF), V((2, 2, d, f), BF), V((2, d, f), BF), V((d, s), BF), V((d, s), BF),
            D((4,)), D((2,)), D((experts,)), D((experts,)), D((experts,)), D((experts,)), D((experts,)), D((experts,)),
            D((tiles,)), D((tiles,)), D((tiles,)),
            V((experts, 8, wide), F32), D((experts,)), D((experts,)), D((experts,)), D((experts,)),
        ],
        compiler_params=pltpu.CompilerParams(collective_id=1, has_side_effects=True, vmem_limit_bytes=VMEM_BYTES),
        cost_estimate=pl.CostEstimate(flops=24 * s * d * f, bytes_accessed=20 * d * f, transcendentals=0),
    )(h4, tr, *dys, router, im, io, tm, to)


FUSED = True
PER = 3


def on_device(images, counts, routes, priority, gain_one, qkv_one, out_one, gain_two, fc_in, fc_out, gain_three,
              qkv_two, out_two, gain_four, router, expert_in, expert_out, cotangent):
    n_slot, length, d = images.shape
    experts = router.shape[1]
    n_mdl = lax.axis_size("mdl")
    peers = lax.axis_size("exp")
    capacity = (25 * L * TOPK + 8 * experts - 1) // (8 * experts)
    half = -(-(-(-capacity // n_mdl)) // 16) * 16
    slots = experts * half
    own_img = n_slot // n_mdl
    f = fc_in.shape[1]
    c = qkv_one.shape[2]
    rows = own_img * LP
    core = lax.axis_index("mdl")
    per = PER
    unit = 4 * d // (2 * per)
    fused = FUSED and (lax.axis_size("grp"), peers, n_mdl) == (4, experts, 2) and peers == 4
    fused = fused and d == 2 * c and f == 4 * c and unit % (64 * peers) == 0 and c % 48 == 0

    def padded(v):
        return jnp.pad(v, ((0, 0), (0, LP - length), (0, 0))).reshape(n_slot * LP, -1)

    qm1, om1, im, tm, qm2, om2, em, fm = halves = (
        qkv_one, out_one, fc_in, fc_out, qkv_two, out_two, expert_in[0], expert_out[0])
    blocks = [(half, d)] * peers if fused else [(slots, d)]
    routing_args = (counts, jnp.transpose(routes, (0, 2, 1)), priority, router.T, gain_one, gain_two, gain_three, gain_four, cotangent)
    slot_rows, col, router_rows, gains, *dy_out = call(
        functools.partial(routing_body, experts, capacity, half),
        [out((n_slot, 8, LQ), I32), out((rows, 8), I32), out((LANES, d), BF), out((4, d), F32)] + [out(b, BF) for b in blocks], *routing_args,
        in_specs=[pl.BlockSpec(memory_space=pltpu.SMEM)] + [whole(v.shape) for v in routing_args[1:]],
        scratch=[pltpu.VMEM((n_slot * LP, d), BF), pltpu.VMEM((n_slot, 8, LQ), I32), pltpu.VMEM((8, LQ), I32)],
        flops=4 * slots * n_slot * LP * d,
    )
    def exchange(v):
        shaped = v.reshape(peers, v.shape[0] // peers, v.shape[1])
        return lax.all_to_all(shaped, "exp", 0, 0, tiled=True).reshape(v.shape)

    if fused:
        got, (qo1, oo1, io, to, qo2, oo2, eo, fo), dy_in = forward(images, gains, halves, dy_out[1:], rows)
        x1, *kept1, x2, h2, act2, slope2, x3 = got[:10]
        kept3, h4, x0 = got[10:14], got[14], got[15]
        dy_in = [dy_out[0], *dy_in]
    else:
        x0 = padded(images)
        qo1, oo1, io, to, qo2, oo2, eo, fo = (other_core(w) for w in halves)
        dy_in = exchange(dy_out[0])
        x1, *kept1 = attention_forward(x0, rows, gains, 0, qm1, qo1, om1, oo1)
        x2, h2, act2, slope2 = mlp_forward(x1, gains, 1, im, io, tm, to)
        x3, *kept3, h4 = attention_forward(x2, rows, gains, 2, qm2, qo2, om2, oo2, tail=3)

    if fused:
        ret, dgate, *eout, ge = expert_exchange(h4, slot_rows, dy_in, router_rows, em, eo, fm, fo, experts, half)
        (dg1, dg2, dg3, dg4, dr, image), grads, eback = backward(
            experts, half, x3, h4, router_rows, cotangent, col, ret, dgate, gains, x2, kept3, (qm2, qo2, om2, oo2),
            x1, h2, act2, slope2, (im, io, tm, to), x0, kept1, (qm1, qo1, om1, oo1), eout[1:])
        a2_mine, a2_other, gim, gio, gtm, gto, a1_mine, a1_other = grads
        eback = [eout[0], *eback]
    else:
        [h4_out] = call(functools.partial(dispatch_body, experts, half), [out((slots, d), BF)], slot_rows, h4, other_core(h4))
        h4_in = exchange(h4_out)
        eout, ret, eact, edz, ewd = expert_forward_backward(h4_in, dy_in, router_rows, em, eo, fm, fo, experts)
        ret, eout = exchange(ret), exchange(eout)
        ret, eback = jnp.stack([ret, other_core(ret)]), jnp.stack([eout, other_core(eout)])
        dgate = ret[:, :, d].astype(F32) + ret[:, :, d + LANES // 2].astype(F32)
        wide = -(-half // LANES) * LANES
        dgate = jnp.pad(dgate.reshape(2, experts, 1, half), ((0, 0), (0, 0), (0, 7), (0, wide - half)))
        ret = ret[:, :, :d]
        ge_mine, ge_other = expert_weights(h4_in, ewd, eact, edz)
        ge = add16(ge_mine, other_core(ge_other))
        dx2, dg3, dg4, dr, a2_mine, a2_other = mixture_attention_backward(
            experts, half, x3, h4, router_rows, cotangent, col, ret, dgate, x2, gains, kept3, qm2, qo2, om2, oo2)
        dx1, dg2, gim, gio, gtm, gto = mlp_backward(dx2, x1, gains, 1, h2, act2, slope2, im, io, tm, to, c)
        image, dg1, a1_mine, a1_other = attention_backward(dx1, x0, gains, 0, kept1, qm1, qo1, om1, oo1)
    expert_sum = lax.psum_scatter(ge, "grp", scatter_dimension=1, tiled=True)

    mines, others = (a2_mine, gim, gtm, a1_mine), (a2_other, gio, gto, a1_other)

    if fused:
        split = [[v.reshape(per, 2, unit, c) for v in side] for side in (mines, others)]
        qkv2, proj2, fi, fo_, qkv1, proj1, small, output, grad_images = reduce_all(
            *split, (dg1, dg2, dg3, dg4), dr, x3, h4, router_rows, col, eback, image, peers, experts)
    else:
        sums = [sum_everywhere(add16(a.reshape(4 * d, c), other_core(b.reshape(4 * d, c)))) for a, b in zip(mines, others)]
        small = small_sum(jnp.concatenate([dg1, dg2, dg3, dg4, dr[:experts]], axis=0))

        def panels(v):
            return jnp.concatenate([v[i] for i in range(v.shape[0])], axis=1)

        (qkv2, proj2), (qkv1, proj1) = (
            (v[: 3 * d].reshape(3, d, c), panels(v[3 * d :].reshape(d // c, c, c))) for v in (sums[0], sums[3]))
        fi, fo_ = panels(sums[1].reshape(f // c, d, c)), panels(sums[2].reshape(d // c, f, c))
        [own_out] = call(
            functools.partial(mixture_output_body, experts), [out((own_img, L, d), BF)], x3, h4, router_rows, col, eback,
            flops=8 * rows * slots * d)

        def both(v):
            there = other_core(v)
            return jnp.where(core == 0, jnp.concatenate([v, there]), jnp.concatenate([there, v]))

        output, grad_images = both(own_out), both(image)
    wide = widen(expert_sum, qkv1, proj1, fi, fo_, qkv2, proj2)
    return (
        output, grad_images,
        small[0], wide[0], wide[1], small[1], wide[2], wide[3],
        small[2], wide[4], wide[5], small[3], small[4 : 4 + experts].T,
        wide[6][None], wide[7].T[None],
    )


def solution(mesh):
    token = P(("grp", "exp"), None, None)
    column, line = P(None, None, "mdl"), P("mdl", None)
    return jax.shard_map(
        on_device,
        mesh=mesh,
        in_specs=(token, P("grp", "exp"), token, P(("grp", "exp"), None), P(), column, line, P(), P(None, "mdl"), line,
                  P(), column, line, P(), P(), P("exp", None, "mdl"), P("exp", "mdl", None), token),
        out_specs=(token, token, P(), column, line, P(), P(None, "mdl"), line, P(), column, line, P(), P(),
                   P("exp", "grp", "mdl"), P("exp", "mdl", "grp")),
        check_vma=False,
    )
```
